32 devices in a mesh: gx: 2 (over x), gy: 4 (over y, core), gz: 4 (over z).
Axes of the slice: x: 2, y: 2, z: 4, core: 2. Of those that a mesh axis runs over, the one named last changes fastest.
Arguments:
- facies: int32 [64, 32, 512], P('gz', 'gx', 'gy'), may hold values from 0 to 15
- perm_table: float32 [3, 16], replicated, may hold values from 0.0003 to 3, as said below
- line_breaks: int32 [63], replicated, may hold values 0 or 1
Outputs:
- pressure: float32 [3, 64, 32, 512], P(None, 'gz', 'gx', 'gy')
- residual: float32 [3, 64, 32, 512], P(None, 'gz', 'gx', 'gy')
The draws below stay inside these ranges and needn't reach their ends.
Inputs may be any that keep to these rules, and one draw needn't show every extreme that they name: `perm_table`: positive coefficients.
All inputs are finite; a program needn't handle non-finite values.
Results may differ from the reference program's by a relative error of at most 0.0003.
Values sent between devices are 32-bit elements; how exact they have to be, the bound alone decides.
No kernel may reach another device: no remote copies, remote signals or barrier semaphores. Data moves between devices by JAX's collectives and lax.ppermute only.
A program may use at most 64 MiB of HBM per device.

```python
import math
import jax
import jax.numpy as jnp
from jax import lax

NF = 16
NX = 32
NY = 512
NZ = 64


def draw_perm_table(key, part):
    spread = jax.random.uniform(key, (3, NF), jnp.float32)
    floor = jnp.array([[0.0003], [0.0003], [0.3]], jnp.float32)
    return floor * jnp.exp(spread * math.log(10.0))


def place_ends(values, key, smallest, high):
    longest = values.shape.index(max(values.shape))
    spots = []
    for shift in (0, 1):
        where = [jax.random.randint(jax.random.fold_in(key, axis), (), 0, length) for axis, length in enumerate(values.shape)]
        where[longest] = (where[longest] + shift) % values.shape[longest]
        spots.append(tuple(where))
    return values.at[spots[0]].set(smallest).at[spots[1]].set(high)


def setup_inputs(seed: int = 0) -> dict:
    streams_of = jax.random.split(jax.random.key(seed), 4)
    return {
        "facies": place_ends(jax.random.randint(streams_of[0], (NZ, NX, NY), 0, NF), jax.random.fold_in(streams_of[0], 1), 0, NF - 1).astype(jnp.int32),
        "perm_table": draw_perm_table(jax.random.fold_in(streams_of[3], 71), 0),
        "line_breaks": place_ends((jax.random.randint(streams_of[2], (NZ - 1,), 0, 16) < 1).astype(jnp.int32), jax.random.fold_in(streams_of[2], 1), 0, 1),
    }


def six_sides(padded):
    return (padded[..., :-2, 1:-1, 1:-1], padded[..., 2:, 1:-1, 1:-1],
            padded[..., 1:-1, :-2, 1:-1], padded[..., 1:-1, 2:, 1:-1],
            padded[..., 1:-1, 1:-1, :-2], padded[..., 1:-1, 1:-1, 2:])


def face_pair(centre, beside):
    inside = beside > 0.0
    harmonic = 2.0 * centre * beside / (centre + beside)
    return (jnp.where(inside, harmonic, 2.0 * centre), jnp.where(inside, harmonic, centre),
            jnp.where(inside, harmonic, 0.0))


def assemble(perm, padded):
    z_sides = six_sides(padded[2])
    x_sides = six_sides(padded[0])
    y_sides = six_sides(padded[1])
    z_low = face_pair(perm[2], z_sides[0])
    z_high = face_pair(perm[2], z_sides[1])
    x_low = face_pair(perm[0], x_sides[2])
    x_high = face_pair(perm[0], x_sides[3])
    y_low = face_pair(perm[1], y_sides[4])
    y_high = face_pair(perm[1], y_sides[5])
    taus = (z_low[0], z_high[0], x_low[0], x_high[0], y_low[0], y_high[0])
    source = jnp.stack([x_high[1] - x_low[1], y_high[1] - y_low[1], z_high[1] - z_low[1]])
    centre_sum = taus[0] + taus[1] + taus[2] + taus[3] + taus[4] + taus[5]
    return taus, source, centre_sum, z_low[2], z_high[2]


def explicit_terms(taus, sides, break_low, break_high):
    return (taus[2] * sides[2] + taus[3] * sides[3] + taus[4] * sides[4] + taus[5] * sides[5]
            + taus[0] * break_low * sides[0] + taus[1] * break_high * sides[1])


def residual_of(taus, sides, source, centre_sum, field):
    total = (taus[0] * sides[0] + taus[1] * sides[1] + taus[2] * sides[2]
             + taus[3] * sides[3] + taus[4] * sides[4] + taus[5] * sides[5])
    return source - centre_sum * field + total


def line_solve(sub_diag, main_diag, super_diag, right):
    columns = jnp.moveaxis(right, 1, 0)

    def forward(carry, item):
        ratio_prior, value_prior = carry
        below, centre, above, value = item
        pivot = centre - below * ratio_prior
        ratio = above / pivot
        current = (value - below[None] * value_prior) / pivot[None]
        return (ratio, current), (ratio, current)

    start = (jnp.zeros(main_diag.shape[1:], jnp.float32), jnp.zeros(columns.shape[1:], jnp.float32))
    _, (ratios, partial_value) = lax.scan(forward, start, (sub_diag, main_diag, super_diag, columns))

    def backward(later, item):
        ratio, value = item
        current = value - ratio[None] * later
        return current, current

    _, result = lax.scan(backward, jnp.zeros(columns.shape[1:], jnp.float32), (ratios, partial_value), reverse=True)
    return jnp.moveaxis(result, 0, 1)


def reference(facies, perm_table, line_breaks):
    perm = perm_table[:, facies]
    widths = ((0, 0), (1, 1), (1, 1), (1, 1))
    taus, source, centre_sum, link_low, link_high = assemble(perm, jnp.pad(perm, widths))
    extended = jnp.concatenate([jnp.zeros((1,), jnp.int32), line_breaks, jnp.zeros((1,), jnp.int32)]).astype(jnp.float32)
    break_low = extended[:NZ][:, None, None]
    break_high = extended[1:][:, None, None]
    sub_diag = -link_low * (1.0 - break_low)
    super_diag = -link_high * (1.0 - break_high)
    first = line_solve(sub_diag, centre_sum, super_diag, source)
    right = source + explicit_terms(taus, six_sides(jnp.pad(first, widths)), break_low, break_high)
    second = line_solve(sub_diag, centre_sum, super_diag, right)
    residual = residual_of(taus, six_sides(jnp.pad(second, widths)), source, centre_sum, second)
    return second, residual
```

```python
import functools

import jax
import jax.numpy as jnp
from jax import lax
from jax.experimental import pallas as pl
from jax.experimental.pallas import tpu as pltpu
from jax.sharding import PartitionSpec as P


WIDE = 3
FIRST_COUNT = 11
SECOND_COUNT = 6


def moved(values, amount, axis):
    size = values.shape[axis]
    amount = amount % size
    if amount == 0:
        return values
    return pltpu.roll(values, amount, axis)


def flag(condition):
    return condition.astype(jnp.float32)


def pack_kernel(facies_ref, strip_ref, *row_refs):
    nz, nx, ny = facies_ref.shape
    lane = lax.broadcasted_iota(jnp.int32, (nx, ny), 1)
    strip = jnp.zeros((nx, ny), jnp.int32)
    for z in range(nz):
        strip = jnp.where(lane // 8 == z, moved(facies_ref[z], 8 * z + WIDE, 1), strip)
    strip_ref[...] = strip
    for z in range(nz):
        leading = facies_ref[z, 0:WIDE, :]
        last = facies_ref[z, nx - WIDE : nx, :]
        spot = slice(z * WIDE, (z + 1) * WIDE)
        if len(row_refs) == 1:
            row_refs[0][spot, :] = jnp.where(lax.axis_index("gx") == 0, last, leading)
        else:
            row_refs[0][spot, :] = leading
            row_refs[1][spot, :] = last


def face(a, b):
    product = a * b
    total = a + b
    harmonic = 2.0 * product / total
    inside = product > 0.0
    link = jnp.where(inside, harmonic, 0.0)
    flow = jnp.where(inside, harmonic, total)
    tau = jnp.where(inside, harmonic, 2.0 * total)
    return link, flow, tau


def message_rows(nx, count, halo):
    side_rows = -(-count * 2 * halo // 8) * 8
    return count * nx + nx + 8 + side_rows


def write_message(ref, slabs, nx, ny, halo):
    count = len(slabs)
    row = lax.broadcasted_iota(jnp.int32, (8, ny), 0)
    lane = lax.broadcasted_iota(jnp.int32, (nx + 8, ny), 1)
    per_tile = 8 // (2 * halo)
    strip = jnp.zeros((nx + 8, ny), jnp.float32)
    tile = jnp.zeros((8, ny), jnp.float32)
    base = count * nx + nx + 8
    for q, slab in enumerate(slabs):
        ref[q * nx : (q + 1) * nx, :] = slab[:nx, :ny]
        strip = jnp.where(lane // (2 * halo) == q, moved(slab[:, ny:], 2 * halo * q + halo, 1), strip)
        part = q % per_tile
        tile = jnp.where(
            row // (2 * halo) == part, moved(slab[nx:, :ny], 2 * halo * part + halo, 0), tile
        )
        if part == per_tile - 1 or q == count - 1:
            start = base + (q // per_tile) * 8
            ref[start : start + 8, :] = tile
    ref[count * nx : count * nx + nx + 8, :] = strip


def read_message(ref, q, count, nx, ny, halo):
    per_tile = 8 // (2 * halo)
    part = q % per_tile
    start = count * nx + nx + 8 + (q // per_tile) * 8
    tile = moved(ref[start : start + 8, :], -(2 * halo * part + halo), 0)
    strip = moved(ref[count * nx : count * nx + nx + 8, :], -(2 * halo * q + halo), 1)
    main = jnp.concatenate([ref[q * nx : (q + 1) * nx, :], tile], axis=0)
    return jnp.concatenate([main, strip], axis=1)


def cut_after(breaks_ref, layer):
    spot = jnp.clip(layer, 0, breaks_ref.shape[0] - 1)
    return breaks_ref[spot].astype(jnp.float32)


def eliminate_kernel(
    table_ref, breaks_ref, facies_ref, row_low, row_high, y_low, y_high,
    low_low, low_high, high_low, high_high,
    message_ref, lx_ref, ly_ref, lz_ref, source_ref, centre_ref, d_ref, e_ref, inverse_ref,
    side_ref,
):
    nz, nx, ny = facies_ref.shape
    labels = table_ref.shape[1]
    outside = labels
    at_x, at_y, at_z = lax.axis_index("gx"), lax.axis_index("gy"), lax.axis_index("gz")
    has_x_low, has_x_high = at_x > 0, at_x < lax.axis_size("gx") - 1
    has_y_low, has_y_high = at_y > 0, at_y < lax.axis_size("gy") - 1

    lane8 = lax.broadcasted_iota(jnp.int32, (8, ny), 1)
    row8 = lax.broadcasted_iota(jnp.int32, (8, ny), 0)
    tables = []
    for q in range(3):
        table = jnp.zeros((8, ny), jnp.float32)
        for label in range(labels):
            table = jnp.where(lane8 == label, table_ref[q, label], table)
        tables.append(table)

    side_ref[...] = jnp.full(side_ref.shape, outside, jnp.int32)
    for z in range(nz):
        spot = slice(z * WIDE, (z + 1) * WIDE)
        side_ref[z, 0:WIDE, :] = jnp.where(has_x_high, row_high[spot, :], outside)
        side_ref[z, 8 - WIDE : 8, :] = jnp.where(has_x_low, row_low[spot, :], outside)

    def corner(high_ref, low_ref):
        high = jnp.where(has_x_high, high_ref[0:8, :], outside)
        low = jnp.where(has_x_low, low_ref[nx - 8 : nx, :], outside)
        middle = jnp.where(row8 >= 8 - WIDE, low, outside)
        return jnp.where(row8 < WIDE, high, middle)

    before = jnp.concatenate([y_low[...], corner(low_high, low_low)], axis=0)
    after = jnp.concatenate([y_high[...], corner(high_high, high_low)], axis=0)
    lane = lax.broadcasted_iota(jnp.int32, (nx + 8, ny), 1)
    strip = jnp.where(
        lane % 8 < WIDE,
        jnp.where(has_y_low, before, outside),
        jnp.where(has_y_high, after, outside),
    )
    near = (lane < WIDE) | (lane >= ny - WIDE)

    def lookup(table, index):
        rows = []
        for r in range(0, nx + 8, 8):
            columns = []
            for c in range(0, 2 * ny, ny):
                columns.append(
                    jnp.take_along_axis(table, index[r : r + 8, c : c + ny], axis=1)
                )
            rows.append(jnp.concatenate(columns, axis=1))
        return jnp.concatenate(rows, axis=0)

    def coefficients(z):
        body = jnp.concatenate([facies_ref[z], side_ref[z]], axis=0)
        beside = jnp.where(near, moved(strip, -(8 * z + WIDE), 1), outside)
        label = jnp.concatenate([body, beside], axis=1)
        return [lookup(table, label) for table in tables]

    def open_after(z):
        return 1.0 - cut_after(breaks_ref, at_z * nz + z)

    kz_now = kz_first = None
    link_below = None
    tau_below = flow_below = None
    state = None
    next_k = coefficients(0)
    for z in range(nz):
        kx, ky, kz = next_k
        link_x, flow_x, tau_x = face(kx, moved(kx, -1, 0))
        link_y, flow_y, tau_y = face(ky, moved(ky, -1, 1))
        lx_ref[z] = link_x
        ly_ref[z] = link_y
        centre = tau_x + moved(tau_x, 1, 0) + (tau_y + moved(tau_y, 1, 1))
        sources = [flow_x - moved(flow_x, 1, 0), flow_y - moved(flow_y, 1, 1)]
        source_z = jnp.zeros_like(centre)
        if z > 0:
            centre = centre + link_below
            source_z = source_z - link_below
        else:
            kz_first = kz
        if z < nz - 1:
            next_k = coefficients(z + 1)
            link_z = face(kz, next_k[2])[0]
            lz_ref[z] = link_z
            centre = centre + link_z
            source_z = source_z + link_z
        centre = jnp.where(kz > 0.0, centre, 1.0)
        sources.append(source_z)
        for f in range(3):
            source_ref[f, z] = sources[f]
        centre_ref[z] = centre
        if z == 0:
            s_uu = centre
            g_u = list(sources)
            coupling = link_z * open_after(0)
        elif z < nz - 1:
            if z == 1:
                pivot = centre
                forward = list(sources)
                numerator = coupling
            else:
                pivot = centre - coupling * ratio
                forward = [sources[f] + coupling * value[f] for f in range(3)]
                numerator = coupling * spike
            inverse = 1.0 / pivot
            value = [forward[f] * inverse for f in range(3)]
            spike = numerator * inverse
            s_uu = s_uu - numerator * spike
            g_u = [g_u[f] + spike * forward[f] for f in range(3)]
            coupling = link_z * open_after(z)
            ratio = coupling * inverse
            inverse_ref[z] = inverse
            e_ref[z] = spike
            for f in range(3):
                d_ref[f, z] = value[f]
        else:
            s_vv = centre - coupling * ratio
            s_uv = -coupling * spike
            g_v = [sources[f] + coupling * value[f] for f in range(3)]
        link_below = link_z
    write_message(
        message_ref, [s_uu, s_uv, s_vv, kz_first, kz] + g_u + g_v, nx, ny, 2
    )


def stencil(f_slab, link_x, link_y):
    return (
        link_x * moved(f_slab, -1, 0)
        + moved(link_x * f_slab, 1, 0)
        + (link_y * moved(f_slab, -1, 1) + moved(link_y * f_slab, 1, 1))
    )


def middle_kernel(
    count, breaks_ref, *refs
):
    blocks = refs[:count]
    lx_ref, ly_ref, lz_ref, source_ref, d_ref, e_ref, inverse_ref = refs[count : count + 7]
    message_ref, d2_ref, factor_ref, end_ref, first_ref = refs[count + 7 :]
    nz = lx_ref.shape[0]
    nx, ny = lx_ref.shape[1] - 8, lx_ref.shape[2] // 2
    at_z = lax.axis_index("gz")

    def quantity(block, q):
        return read_message(blocks[block], q, FIRST_COUNT, nx, ny, 2)

    def triple(block, q):
        return [quantity(block, q + f) for f in range(3)]

    def open_after(layer):
        return 1.0 - cut_after(breaks_ref, layer)

    slots = []

    def keep(values):
        factor_ref[len(slots)] = values
        slots.append(None)

    def chain(below):
        near, far, sign = (8, 5, 1.0) if below else (5, 8, -1.0)
        near_s, far_s = (2, 0) if below else (0, 2)
        near_k, far_k = (4, 3) if below else (3, 4)
        carry = None
        for step in range(count - 1, 0, -1):
            block = step if below else count - step
            if carry is None:
                own_k = quantity(block, far_k)
                tau, flow = 2.0 * own_k, own_k
                pivot = quantity(block, far_s) + tau
                right = triple(block, far)
            else:
                pivot = quantity(block, far_s) + tau - coupling * carry[0]
                right = [a + carry[0] * b for a, b in zip(triple(block, far), carry[1])]
            right[2] = right[2] - sign * flow
            s_uv = quantity(block, 1)
            factor = s_uv / pivot
            keep(factor)
            if below:
                exists = at_z >= step
                layer = (at_z - step + 1) * nz - 1
            else:
                exists = at_z + step < count
                layer = (at_z + step) * nz - 1
            k_here = quantity(block, near_k) * flag(exists)
            k_next = quantity((step - 1 if below else (count - step + 1) % count), far_k)
            link, flow, tau = face(k_here, k_next)
            coupling = link * open_after(layer)
            next_pivot = quantity(block, near_s) + tau - s_uv * factor
            next_right = [a - factor * b for a, b in zip(triple(block, near), right)]
            next_right[2] = next_right[2] + sign * flow
            inverse = 1.0 / next_pivot
            carry = (coupling * inverse, next_right)
            keep(carry[0])
        held = inverse * flag(exists)
        keep(held)
        return carry, coupling, held, link, flow, tau

    carry_b, coupling_b, held_b, link_b, flow_b, tau_b = chain(True)
    carry_a, coupling_a, held_a, link_a, flow_a, tau_a = chain(False)
    pivot_u = quantity(0, 0) + tau_b - coupling_b * carry_b[0]
    right_u = [a + carry_b[0] * b for a, b in zip(triple(0, 5), carry_b[1])]
    right_u[2] = right_u[2] - flow_b
    pivot_v = quantity(0, 2) + tau_a - coupling_a * carry_a[0]
    right_v = [a + carry_a[0] * b for a, b in zip(triple(0, 8), carry_a[1])]
    right_v[2] = right_v[2] + flow_a
    s_uv = quantity(0, 1)
    inverse_u = 1.0 / pivot_u
    factor = s_uv * inverse_u
    inverse_v = 1.0 / (pivot_v - s_uv * factor)
    keep(inverse_u)
    keep(factor)
    keep(inverse_v)
    end_ref[0] = link_b
    end_ref[1] = link_a
    end_ref[2] = tau_b
    end_ref[3] = tau_a
    end_ref[4] = flow_b
    end_ref[5] = flow_a

    for f in range(3):
        last = (right_v[f] - factor * right_u[f]) * inverse_v
        first_u = right_u[f] * inverse_u - factor * last
        first_ref[f, 0] = carry_b[1][f] * held_b + carry_b[0] * first_u
        first_ref[f, nz + 1] = carry_a[1][f] * held_a + carry_a[0] * last
        first_ref[f, 1] = first_u
        first_ref[f, nz] = last
    for z in range(nz - 2, 0, -1):
        ratio = lz_ref[z] * open_after(at_z * nz + z) * inverse_ref[z]
        spike = e_ref[z]
        for f in range(3):
            first_ref[f, z + 1] = (
                d_ref[f, z] + spike * first_ref[f, 1] + ratio * first_ref[f, z + 2]
            )

    for z in range(nz):
        link_x, link_y = lx_ref[z], ly_ref[z]
        link_low = link_b if z == 0 else lz_ref[z - 1]
        link_high = link_a if z == nz - 1 else lz_ref[z]
        cut_low = link_low * cut_after(breaks_ref, at_z * nz + z - 1)
        cut_high = link_high * cut_after(breaks_ref, at_z * nz + z)
        right = []
        for f in range(3):
            origin = source_ref[f, z]
            if f == 2 and z == 0:
                origin = origin - flow_b
            if f == 2 and z == nz - 1:
                origin = origin + flow_a
            right.append(
                origin
                + stencil(first_ref[f, z + 1], link_x, link_y)
                + (cut_low * first_ref[f, z] + cut_high * first_ref[f, z + 2])
            )
        if z == 0:
            g_u = list(right)
        else:
            if z == 1:
                forward = right
            else:
                forward = [right[f] + coupling * value[f] for f in range(3)]
            if z < nz - 1:
                inverse, spike = inverse_ref[z], e_ref[z]
                value = [forward[f] * inverse for f in range(3)]
                g_u = [g_u[f] + spike * forward[f] for f in range(3)]
                for f in range(3):
                    d2_ref[f, z] = value[f]
                coupling = lz_ref[z] * open_after(at_z * nz + z)
    write_message(message_ref, g_u + forward, nx, ny, 1)


def final_kernel(count, breaks_ref, *refs):
    blocks = refs[:count]
    lx_ref, ly_ref, lz_ref, source_ref, centre_ref, d2_ref, e_ref, inverse_ref = refs[count : count + 8]
    factor_ref, end_ref, pressure_ref, residual_ref, second_ref = refs[count + 8 :]
    nz = lx_ref.shape[0]
    nx, ny = lx_ref.shape[1] - 8, lx_ref.shape[2] // 2
    at_z = lax.axis_index("gz")

    def triple(block, q):
        return [read_message(blocks[block], q + f, SECOND_COUNT, nx, ny, 1) for f in range(3)]

    slots = []

    def kept():
        slots.append(None)
        return factor_ref[len(slots) - 1]

    def chain(below):
        near, far = (3, 0) if below else (0, 3)
        carry = None
        for step in range(count - 1, 0, -1):
            block = step if below else count - step
            right = triple(block, far)
            if carry is not None:
                right = [a + carry[0] * b for a, b in zip(right, carry[1])]
            factor = kept()
            next_right = [a - factor * b for a, b in zip(triple(block, near), right)]
            carry = (kept(), next_right)
        return carry, kept()

    carry_b, held_b = chain(True)
    carry_a, held_a = chain(False)
    inverse_u, factor, inverse_v = kept(), kept(), kept()
    right_u = [a + carry_b[0] * b for a, b in zip(triple(0, 0), carry_b[1])]
    right_v = [a + carry_a[0] * b for a, b in zip(triple(0, 3), carry_a[1])]
    for f in range(3):
        last = (right_v[f] - factor * right_u[f]) * inverse_v
        first_u = right_u[f] * inverse_u - factor * last
        second_ref[f, 0] = carry_b[1][f] * held_b + carry_b[0] * first_u
        second_ref[f, nz + 1] = carry_a[1][f] * held_a + carry_a[0] * last
        second_ref[f, 1] = first_u
        second_ref[f, nz] = last
    for z in range(nz - 2, 0, -1):
        ratio = lz_ref[z] * (1.0 - cut_after(breaks_ref, at_z * nz + z)) * inverse_ref[z]
        spike = e_ref[z]
        for f in range(3):
            second_ref[f, z + 1] = (
                d2_ref[f, z] + spike * second_ref[f, 1] + ratio * second_ref[f, z + 2]
            )
    own = (slice(0, nx), slice(0, ny))
    for z in range(nz):
        link_x, link_y = lx_ref[z], ly_ref[z]
        link_low = end_ref[0] if z == 0 else lz_ref[z - 1]
        link_high = end_ref[1] if z == nz - 1 else lz_ref[z]
        centre = centre_ref[z]
        if z == 0:
            centre = centre + end_ref[2]
        if z == nz - 1:
            centre = centre + end_ref[3]
        for f in range(3):
            origin = source_ref[f, z]
            if f == 2 and z == 0:
                origin = origin - end_ref[4]
            if f == 2 and z == nz - 1:
                origin = origin + end_ref[5]
            here = second_ref[f, z + 1]
            total = (
                stencil(here, link_x, link_y)
                + (link_low * second_ref[f, z] + link_high * second_ref[f, z + 2])
            )
            pressure_ref[f, z] = here[own]
            residual_ref[f, z] = (origin - centre * here + total)[own]


def kernel_call(kernel, outputs, smem, operands, scratch=()):
    specs = [pl.BlockSpec(memory_space=pltpu.SMEM)] * smem
    specs += [pl.BlockSpec(memory_space=pltpu.VMEM)] * (len(operands) - smem)
    return pl.pallas_call(
        kernel,
        out_shape=[jax.ShapeDtypeStruct(s, t) for s, t in outputs],
        in_specs=specs,
        out_specs=[pl.BlockSpec(memory_space=pltpu.VMEM)] * len(outputs),
        scratch_shapes=list(scratch),
        compiler_params=pltpu.CompilerParams(vmem_limit_bytes=24 * 2**20),
    )(*operands)


def ring(values, axis, distance):
    size = lax.axis_size(axis)
    return lax.ppermute(values, axis, [(i, (i + distance) % size) for i in range(size)])


def diagonal(values, x_distance, y_distance):
    nx, ny = lax.axis_size("gx"), lax.axis_size("gy")
    route = []
    for i in range(nx):
        for j in range(ny):
            target = ((i + x_distance) % nx) * ny + (j + y_distance) % ny
            route.append((i * ny + j, target))
    return lax.ppermute(values, ("gx", "gy"), route)


def per_device(facies, perm_table, line_breaks):
    nz, nx, ny = facies.shape
    gx, gz = lax.axis_size("gx"), lax.axis_size("gz")
    i32, f32 = jnp.int32, jnp.float32
    rows = ((nz * WIDE, ny), i32)
    two = gx == 2
    packed = kernel_call(pack_kernel, [((nx, ny), i32)] + [rows] * (1 if two else 2), 0, [facies])
    strip = packed[0]
    y_low, y_high = ring(strip, "gy", 1), ring(strip, "gy", -1)
    if two:
        row_low = row_high = ring(packed[1], "gx", 1)
        low_low = low_high = diagonal(strip, 1, 1)
        high_low = high_high = diagonal(strip, 1, -1)
    else:
        row_low, row_high = ring(packed[2], "gx", 1), ring(packed[1], "gx", -1)
        low_low, low_high = diagonal(strip, 1, 1), diagonal(strip, -1, 1)
        high_low, high_high = diagonal(strip, 1, -1), diagonal(strip, -1, -1)

    slab = (nx + 8, 2 * ny)
    one, three = ((nz,) + slab, f32), ((3, nz) + slab, f32)
    message, lx, ly, lz, source, centre, d, e, inverse = kernel_call(
        eliminate_kernel,
        [((message_rows(nx, FIRST_COUNT, 2), ny), f32), one, one, one, three, one, three, one, one],
        2,
        [perm_table, line_breaks, facies, row_low, row_high, y_low, y_high,
         low_low, low_high, high_low, high_high],
        [pltpu.VMEM((nz, 8, ny), i32)],
    )
    gathered = [message] + [ring(message, "gz", step) for step in range(1, gz)]
    factors = 2 * (2 * (gz - 1) + 1) + 3
    message, d2, factor, ends = kernel_call(
        functools.partial(middle_kernel, gz),
        [((message_rows(nx, SECOND_COUNT, 1), ny), f32), three, ((factors,) + slab, f32), ((6,) + slab, f32)],
        1,
        [line_breaks] + gathered + [lx, ly, lz, source, d, e, inverse],
        [pltpu.VMEM((3, nz + 2) + slab, f32)],
    )
    gathered = [message] + [ring(message, "gz", step) for step in range(1, gz)]
    out = ((3, nz, nx, ny), f32)
    pressure, residual = kernel_call(
        functools.partial(final_kernel, gz),
        [out, out],
        1,
        [line_breaks] + gathered + [lx, ly, lz, source, centre, d2, e, inverse, factor, ends],
        [pltpu.VMEM((3, nz + 2) + slab, f32)],
    )
    return pressure, residual


def solution(mesh):
    return jax.shard_map(
        per_device,
        mesh=mesh,
        in_specs=(P("gz", "gx", "gy"), P(), P()),
        out_specs=(P(None, "gz", "gx", "gy"), P(None, "gz", "gx", "gy")),
        check_vma=False,
    )
```

```python
import functools

import jax
import jax.numpy as jnp
from jax import lax
from jax.experimental import pallas as pl
from jax.experimental.pallas import tpu as pltpu
from jax.sharding import PartitionSpec as P


WIDE = 3
FIRST_COUNT = 11
LAST_COUNT = 5
SECOND_COUNT = 6
PACK_LIMIT = 24


def moved(values, amount, axis):
    size = values.shape[axis]
    amount = amount % size
    if amount == 0:
        return values
    return pltpu.roll(values, amount, axis)


def flag(condition):
    return condition.astype(jnp.float32)


def iotas(rows, lanes):
    return tuple(lax.broadcasted_iota(jnp.int32, (rows, lanes), d) for d in (0, 1))


def choose(condition, first, second):
    return [jnp.where(condition, a, b) for a, b in zip(first, second)]


def bit_of(stage):
    return (lax.axis_index("gz") >> stage) % 2 == 1


def pack_kernel(stages, facies_in, table_in, breaks_in, facies_ref, table_ref, cut_ref, strip_ref, *refs):
    row_refs, (table, breaks, sems) = refs[:-3], refs[-3:]
    nz, nx, ny = facies_ref.shape
    copies = [
        pltpu.make_async_copy(facies_in, facies_ref, sems.at[0]),
        pltpu.make_async_copy(table_in, table, sems.at[1]),
        pltpu.make_async_copy(breaks_in, breaks, sems.at[2]),
    ]
    for copy in copies:
        copy.start()
    copies[0].wait()
    lane = lax.broadcasted_iota(jnp.int32, (nx, ny), 1)
    strip = jnp.zeros((nx, ny), jnp.int32)
    for z in range(nz):
        strip = jnp.where(lane // 8 == z, moved(facies_ref[z], 8 * z + WIDE, 1), strip)
    strip_ref[...] = strip
    for z in range(nz):
        leading = facies_ref[z, 0:WIDE, :]
        last = facies_ref[z, nx - WIDE : nx, :]
        spot = slice(z * WIDE, (z + 1) * WIDE)
        if len(row_refs) == 1:
            row_refs[0][spot, :] = jnp.where(lax.axis_index("gx") == 0, last, leading)
        else:
            row_refs[0][spot, :] = leading
            row_refs[1][spot, :] = last
    copies[1].wait()
    copies[2].wait()
    lane = iotas(8, ny)[1]
    for q in range(3):
        values = jnp.zeros((8, ny), jnp.float32)
        for label in range(table.shape[1]):
            values = jnp.where(lane == label, table[q, label], values)
        table_ref[q] = values
    at_z = lax.axis_index("gz")
    layers = [at_z * nz + r - 1 for r in range(nz + 1)]
    for s in range(stages):
        base, size = (at_z >> (s + 1)) << (s + 1), 2**s
        layers.append((base + size) * nz - 1)
        layers.append(jnp.where(bit_of(s), base, base + 2 * size) * nz - 1)
    for r, layer in enumerate(layers):
        cut = breaks[jnp.clip(layer, 0, breaks.shape[0] - 1)].astype(jnp.float32)
        cut_ref[r : r + 1, :] = jnp.full((1, ny), cut, jnp.float32)


def face(a, b):
    product = a * b
    total = a + b
    harmonic = 2.0 * product / total
    inside = product > 0.0
    link = jnp.where(inside, harmonic, 0.0)
    flow = jnp.where(inside, harmonic, total)
    tau = jnp.where(inside, harmonic, 2.0 * total)
    return link, flow, tau


class Message:
    def __init__(self, count, halo, nx, ny):
        self.count, self.halo, self.nx, self.ny = count, halo, nx, ny
        self.one_sided = lax.axis_size("gx") == 2
        self.rows_each = halo if self.one_sided else 2 * halo
        self.per_tile = 8 // self.rows_each
        self.tiles = -(-count // self.per_tile)
        self.strip = slice(count * nx, count * nx + nx + 8)
        self.rows = self.strip.stop + 8 * self.tiles

    def tile(self, q):
        start = self.strip.stop + 8 * (q // self.per_tile)
        return slice(start, start + 8)

    def side_moved(self, tile, q, sign):
        part = q % self.per_tile
        if not self.one_sided:
            return moved(tile, sign * (self.rows_each * part + self.halo), 0)
        first = lax.axis_index("gx") == 0
        out = jnp.where(
            first,
            moved(tile, sign * self.halo * part, 0),
            moved(tile, sign * self.halo * (part + 1), 0),
        )
        if sign > 0:
            return out
        row = iotas(8, self.ny)[0]
        return jnp.where(jnp.where(first, row, 7 - row) < self.halo, out, 1.0)

    def write(self, ref, slabs):
        nx, ny, halo = self.nx, self.ny, self.halo
        lane = iotas(nx + 8, ny)[1]
        strip = moved(slabs[0][:, ny:], halo, 1)
        for q in range(1, self.count):
            turned = moved(slabs[q][:, ny:], 2 * halo * q + halo, 1)
            strip = jnp.where(lane < 2 * halo * q, strip, turned)
        ref[self.strip, :] = strip
        row = iotas(8, ny)[0]
        for q, slab in enumerate(slabs):
            ref[q * nx : (q + 1) * nx, :] = slab[:nx, :ny]
            turned = self.side_moved(slab[nx:, :ny], q, 1)
            part = q % self.per_tile
            tile = turned if part == 0 else jnp.where(row < self.rows_each * part, tile, turned)
            if part == self.per_tile - 1 or q == self.count - 1:
                ref[self.tile(q), :] = tile

    def read(self, ref):
        nx, halo = self.nx, self.halo
        strip = ref[self.strip, :]
        slabs = []
        for q in range(self.count):
            side = self.side_moved(ref[self.tile(q), :], q, -1)
            body = jnp.concatenate([ref[q * nx : (q + 1) * nx, :], side], axis=0)
            beside = moved(strip, -(2 * halo * q + halo), 1)
            slabs.append(jnp.concatenate([body, beside], axis=1))
        return slabs


def eliminate_kernel(
    table_ref, cut_ref, facies_ref, row_low, row_high, y_low, y_high,
    low_low, low_high, high_low, high_high,
    message_ref, own_ref, lx_ref, ly_ref, lz_ref, source_ref, centre_ref,
    d_ref, e_ref, inverse_ref, side_ref,
):
    nz, nx, ny = facies_ref.shape
    outside = ny - 1
    at_x, at_y = lax.axis_index("gx"), lax.axis_index("gy")
    has_x_low, has_x_high = at_x > 0, at_x < lax.axis_size("gx") - 1
    has_y_low, has_y_high = at_y > 0, at_y < lax.axis_size("gy") - 1
    tables = [table_ref[q] for q in range(3)]

    side_ref[...] = jnp.full(side_ref.shape, outside, jnp.int32)
    for z in range(nz):
        spot = slice(z * WIDE, (z + 1) * WIDE)
        side_ref[z, 0:WIDE, :] = jnp.where(has_x_high, row_high[spot, :], outside)
        side_ref[z, 8 - WIDE : 8, :] = jnp.where(has_x_low, row_low[spot, :], outside)

    def corner(high_ref, low_ref):
        row = iotas(8, ny)[0]
        high = jnp.where(has_x_high, high_ref[0:8, :], outside)
        low = jnp.where(has_x_low, low_ref[nx - 8 : nx, :], outside)
        middle = jnp.where(row >= 8 - WIDE, low, outside)
        return jnp.where(row < WIDE, high, middle)

    before = jnp.concatenate([y_low[...], corner(low_high, low_low)], axis=0)
    after = jnp.concatenate([y_high[...], corner(high_high, high_low)], axis=0)
    lane = iotas(nx + 8, ny)[1]
    strip = jnp.where(
        lane % 8 < WIDE,
        jnp.where(has_y_low, before, outside),
        jnp.where(has_y_high, after, outside),
    )
    near = (lane < WIDE) | (lane >= ny - WIDE)

    def labels(z):
        beside = jnp.where(near, moved(strip, -(8 * z + WIDE), 1), outside)
        return jnp.concatenate(
            [jnp.concatenate([facies_ref[z], side_ref[z]], axis=0), beside], axis=1
        )

    def lookup(table, index):
        rows = []
        for r in range(0, nx + 8, 8):
            parts = [
                jnp.take_along_axis(table, index[r : r + 8, c : c + ny], axis=1)
                for c in (0, ny)
            ]
            rows.append(jnp.concatenate(parts, axis=1))
        return jnp.concatenate(rows, axis=0)

    def coefficients(label):
        return [lookup(table, label) for table in tables]

    label = labels(0)
    valid = flag(label != outside)
    cell = valid > 0.0
    in_x, in_xp = valid * moved(valid, -1, 0), valid * moved(valid, 1, 0)
    in_y, in_yp = valid * moved(valid, -1, 1), valid * moved(valid, 1, 1)

    def side_faces(here, axis, inside, inside_back):
        there = moved(here, -1, axis)
        total = here + there
        flow = jnp.where(inside > 0.0, 2.0 * (here * there) / total, total)
        flow_back = moved(flow, 1, axis)
        tau = flow * (2.0 - inside) + flow_back * (2.0 - inside_back)
        return flow * inside, tau, flow - flow_back

    next_k = coefficients(label)
    link_below = None
    for z in range(nz):
        kx, ky, kz = next_k
        link_x, tau_x, source_x = side_faces(kx, 0, in_x, in_xp)
        link_y, tau_y, source_y = side_faces(ky, 1, in_y, in_yp)
        lx_ref[z] = link_x
        ly_ref[z] = link_y
        centre = tau_x + tau_y
        if z == 0:
            kz_first = kz
        if z < nz - 1:
            next_k = coefficients(labels(z + 1))
            above = next_k[2]
            link_z = jnp.where(cell, 2.0 * (kz * above) / (kz + above), 0.0)
            lz_ref[z] = link_z
        if z == 0:
            centre = centre + link_z
            source_z = link_z
        elif z == nz - 1:
            centre = centre + link_below
            source_z = -link_below
        else:
            centre = centre + (link_below + link_z)
            source_z = link_z - link_below
        centre = jnp.where(cell, centre, 1.0)
        sources = [source_x, source_y, source_z]
        for f in range(3):
            source_ref[f, z] = sources[f]
        centre_ref[z] = centre
        if z == 0:
            s_uu = centre
            g_u = list(sources)
        elif z < nz - 1:
            if z == 1:
                pivot = centre
                forward = list(sources)
                numerator = coupling
            else:
                pivot = centre - coupling * ratio
                forward = [sources[f] + coupling * value[f] for f in range(3)]
                numerator = coupling * spike
            inverse = 1.0 / pivot
            value = [forward[f] * inverse for f in range(3)]
            spike = numerator * inverse
            s_uu = s_uu - numerator * spike
            g_u = [g_u[f] + spike * forward[f] for f in range(3)]
            inverse_ref[z] = inverse
            e_ref[z] = spike
            for f in range(3):
                d_ref[f, z] = value[f]
        else:
            s_vv = centre - coupling * ratio
            s_uv = -coupling * spike
            g_v = [sources[f] + coupling * value[f] for f in range(3)]
        if z < nz - 1:
            coupling = link_z * open_after(cut_ref, z + 1)
            if z > 0:
                ratio = coupling * inverse
        link_below = link_z
    slabs = [s_uu, s_uv, s_vv, kz_first, kz] + g_u + g_v
    for q, slab in enumerate(slabs):
        own_ref[q] = slab
    Message(FIRST_COUNT, 2, nx, ny).write(message_ref, slabs)


def open_after(cut_ref, r):
    cut = 1.0 - cut_ref[r : r + 1, :]
    return jnp.concatenate([cut, cut], axis=1)


def slab_size(ref):
    return ref.shape[-2] - 8, ref.shape[-1] // 2


def join_kernel(stage, last, nz, cut_ref, own_ref, message_ref, sibling_ref, factor_ref, next_ref, *joined):
    nx, ny = slab_size(own_ref)
    own = [own_ref[q] for q in range(FIRST_COUNT)]
    sibling = Message(FIRST_COUNT, 2, nx, ny).read(message_ref)
    for q, slab in enumerate(sibling):
        sibling_ref[q] = slab
    above = bit_of(stage)
    low, high = choose(above, sibling, own), choose(above, own, sibling)
    link, flow, tau = face(low[4], high[3])
    coupling = link * open_after(cut_ref, nz + 1 + 2 * stage)
    inverse = 1.0 / (low[2] + tau)
    step = coupling * inverse
    last_inverse = 1.0 / (high[0] + tau - coupling * step)
    outer = low[1] * inverse
    weight = step * low[1]
    weight_low, weight_high = weight * last_inverse, high[1] * last_inverse
    right_low = low[8:10] + [low[10] + flow]
    right_high = high[5:7] + [high[7] - flow]
    middle = [b + step * a for a, b in zip(right_low, right_high)]
    s_uu = low[0] - outer * low[1] - weight * weight_low
    s_uv = -weight * weight_high
    s_vv = high[2] - high[1] * weight_high
    g_u = [g - outer * a - weight_low * m for g, a, m in zip(low[5:8], right_low, middle)]
    g_v = [g - weight_high * m for g, m in zip(high[8:11], middle)]
    for n, values in enumerate((outer, step, weight_low, weight_high)):
        factor_ref[n] = values
    if not last:
        slabs = [s_uu, s_uv, s_vv, low[3], high[4]] + g_u + g_v
        for q, slab in enumerate(slabs):
            joined[0][q] = slab
        Message(FIRST_COUNT, 2, nx, ny).write(next_ref, slabs)
        return
    top = bit_of(stage + 1)
    far_s, near_s = choose(top, [s_vv, s_uu], [s_uu, s_vv])
    far_k, near_k = choose(top, [high[4], low[3]], [low[3], high[4]])
    far_g, near_g = choose(top, g_v, g_u), choose(top, g_u, g_v)
    far_g[2] = far_g[2] + far_k * jnp.where(top, 1.0, -1.0)
    factor = s_uv / (far_s + 2.0 * far_k)
    factor_ref[4] = factor
    slabs = [near_s - s_uv * factor, near_k] + [n - factor * g for n, g in zip(near_g, far_g)]
    Message(LAST_COUNT, 2, nx, ny).write(next_ref, slabs)


def join_again_kernel(stage, last, own_ref, message_ref, factor_ref, sibling_ref, next_ref, *joined):
    nx, ny = slab_size(own_ref)
    own = [own_ref[q] for q in range(SECOND_COUNT)]
    sibling = Message(SECOND_COUNT, 1, nx, ny).read(message_ref)
    for q, slab in enumerate(sibling):
        sibling_ref[q] = slab
    above = bit_of(stage)
    low, high = choose(above, sibling, own), choose(above, own, sibling)
    outer, step, weight_low, weight_high = [factor_ref[n] for n in range(4)]
    middle = [b + step * a for a, b in zip(low[3:], high[:3])]
    g_u = [g - outer * a - weight_low * m for g, a, m in zip(low[:3], low[3:], middle)]
    g_v = [g - weight_high * m for g, m in zip(high[3:], middle)]
    if not last:
        for q, slab in enumerate(g_u + g_v):
            joined[0][q] = slab
        Message(SECOND_COUNT, 1, nx, ny).write(next_ref, g_u + g_v)
        return
    top = bit_of(stage + 1)
    factor = factor_ref[4]
    far_g, near_g = choose(top, g_v, g_u), choose(top, g_u, g_v)
    Message(3, 1, nx, ny).write(next_ref, [n - factor * g for n, g in zip(near_g, far_g)])


def stencil(slab, link_x, link_y):
    return (
        link_x * moved(slab, -1, 0)
        + moved(link_x * slab, 1, 0)
        + (link_y * moved(slab, -1, 1) + moved(link_y * slab, 1, 1))
    )


def middle_kernel(stages, cut_ref, *refs):
    own_ref, siblings, message_ref = refs[0], refs[1:stages], refs[stages]
    refs = refs[stages + 1 :]
    lx_ref, ly_ref, lz_ref, source_ref, d_ref, e_ref, inverse_ref = refs[:7]
    next_ref, own2_ref, d2_ref, factor_ref, end_ref, first_ref = refs[7:]
    nz = lx_ref.shape[0]
    nx, ny = slab_size(lx_ref)
    own = [own_ref[q] for q in range(FIRST_COUNT)]
    slots = []

    def keep(values):
        factor_ref[len(slots)] = values
        slots.append(None)

    def attach(state, sign, row, pivot, right, k):
        beside, k_beside, rights, exists = state[0], state[1], state[2:5], state[5]
        link, flow, tau = face(k_beside * exists, k)
        coupling = link * open_after(cut_ref, row)
        rights = rights[:2] + [rights[2] + sign * flow]
        inverse = 1.0 / (beside + tau)
        step = coupling * inverse
        right = [a + step * b for a, b in zip(right, rights)]
        right[2] = right[2] - sign * flow
        return pivot + tau - coupling * step, right, step, inverse, rights, (link, flow, tau)

    far = Message(LAST_COUNT, 2, nx, ny).read(message_ref)
    top = bit_of(stages - 1)
    below, above = far + [flag(top)], far + [flag(jnp.logical_not(top))]
    for s in range(stages - 2, -1, -1):
        up = bit_of(s)
        block = [siblings[s][q] for q in range(FIRST_COUNT)]
        sign = jnp.where(up, 1.0, -1.0)
        state = choose(up, below, above)
        far_s, far_k, near_s, near_k = choose(
            up, [block[0], block[3], block[2], block[4]], [block[2], block[4], block[0], block[3]]
        )
        far_g = choose(up, block[5:8], block[8:11])
        near_g = choose(up, block[8:11], block[5:8])
        pivot, right, step, _, _, _ = attach(state, sign, nz + 2 + 2 * s, far_s, far_g, far_k)
        factor = block[1] / pivot
        keep(step)
        keep(factor)
        state = [near_s - block[1] * factor, near_k]
        state += [n - factor * r for n, r in zip(near_g, right)] + [jnp.float32(1.0)]
        below, above = choose(up, state, below), choose(up, above, state)

    pivot_u, right_u, step_b, inverse_b, rights_b, ends_b = attach(
        below, 1.0, 0, own[0], own[5:8], own[3]
    )
    pivot_v, right_v, step_a, inverse_a, rights_a, ends_a = attach(
        above, -1.0, nz, own[2], own[8:11], own[4]
    )
    held_b, held_a = inverse_b * below[5], inverse_a * above[5]
    inverse_u = 1.0 / pivot_u
    factor = own[1] * inverse_u
    inverse_v = 1.0 / (pivot_v - own[1] * factor)
    for values in (step_b, held_b, step_a, held_a, inverse_u, factor, inverse_v):
        keep(values)
    (link_b, flow_b, tau_b), (link_a, flow_a, tau_a) = ends_b, ends_a
    for n, values in enumerate((link_b, link_a, tau_b, tau_a, flow_b, flow_a)):
        end_ref[n] = values

    for f in range(3):
        last = (right_v[f] - factor * right_u[f]) * inverse_v
        first_u = right_u[f] * inverse_u - factor * last
        first_ref[f, 0] = rights_b[f] * held_b + step_b * first_u
        first_ref[f, nz + 1] = rights_a[f] * held_a + step_a * last
        first_ref[f, 1] = first_u
        first_ref[f, nz] = last
    for z in range(nz - 2, 0, -1):
        ratio = lz_ref[z] * open_after(cut_ref, z + 1) * inverse_ref[z]
        spike = e_ref[z]
        for f in range(3):
            first_ref[f, z + 1] = (
                d_ref[f, z] + spike * first_ref[f, 1] + ratio * first_ref[f, z + 2]
            )

    for z in range(nz):
        link_low = link_b if z == 0 else lz_ref[z - 1]
        link_high = link_a if z == nz - 1 else lz_ref[z]
        cut_low = link_low * (1.0 - open_after(cut_ref, z))
        cut_high = link_high * (1.0 - open_after(cut_ref, z + 1))
        right = []
        for f in range(3):
            origin = source_ref[f, z]
            if f == 2 and z == 0:
                origin = origin - flow_b
            if f == 2 and z == nz - 1:
                origin = origin + flow_a
            right.append(
                origin
                + stencil(first_ref[f, z + 1], lx_ref[z], ly_ref[z])
                + (cut_low * first_ref[f, z] + cut_high * first_ref[f, z + 2])
            )
        if z == 0:
            g_u = list(right)
        else:
            if z == 1:
                forward = right
            else:
                forward = [right[f] + coupling * value[f] for f in range(3)]
            if z < nz - 1:
                inverse, spike = inverse_ref[z], e_ref[z]
                value = [forward[f] * inverse for f in range(3)]
                g_u = [g_u[f] + spike * forward[f] for f in range(3)]
                for f in range(3):
                    d2_ref[f, z] = value[f]
                coupling = lz_ref[z] * open_after(cut_ref, z + 1)
    slabs = g_u + forward
    for q, slab in enumerate(slabs):
        own2_ref[q] = slab
    Message(SECOND_COUNT, 1, nx, ny).write(next_ref, slabs)


def final_kernel(stages, cut_ref, *refs):
    own_ref, siblings, message_ref = refs[0], refs[1:stages], refs[stages]
    refs = refs[stages + 1 :]
    lx_ref, ly_ref, lz_ref, source_ref, centre_ref, d2_ref, e_ref, inverse_ref = refs[:8]
    factor_ref, end_ref, pressure_ref, residual_ref, second_ref = refs[8:]
    nz = lx_ref.shape[0]
    nx, ny = slab_size(lx_ref)
    own = [own_ref[q] for q in range(SECOND_COUNT)]
    slots = []

    def kept():
        slots.append(None)
        return factor_ref[len(slots) - 1]

    below = above = Message(3, 1, nx, ny).read(message_ref)
    for s in range(stages - 2, -1, -1):
        up = bit_of(s)
        block = [siblings[s][q] for q in range(SECOND_COUNT)]
        state = choose(up, below, above)
        far_g = choose(up, block[:3], block[3:])
        near_g = choose(up, block[3:], block[:3])
        step, factor = kept(), kept()
        right = [a + step * b for a, b in zip(far_g, state)]
        state = [n - factor * r for n, r in zip(near_g, right)]
        below, above = choose(up, state, below), choose(up, above, state)
    step_b, held_b, step_a, held_a = kept(), kept(), kept(), kept()
    inverse_u, factor, inverse_v = kept(), kept(), kept()
    for f in range(3):
        right_u = own[f] + step_b * below[f]
        right_v = own[3 + f] + step_a * above[f]
        last = (right_v - factor * right_u) * inverse_v
        first_u = right_u * inverse_u - factor * last
        second_ref[f, 0] = below[f] * held_b + step_b * first_u
        second_ref[f, nz + 1] = above[f] * held_a + step_a * last
        second_ref[f, 1] = first_u
        second_ref[f, nz] = last
    for z in range(nz - 2, 0, -1):
        ratio = lz_ref[z] * open_after(cut_ref, z + 1) * inverse_ref[z]
        spike = e_ref[z]
        for f in range(3):
            second_ref[f, z + 1] = (
                d2_ref[f, z] + spike * second_ref[f, 1] + ratio * second_ref[f, z + 2]
            )
    own_part = (slice(0, nx), slice(0, ny))
    for z in range(nz):
        link_low = end_ref[0] if z == 0 else lz_ref[z - 1]
        link_high = end_ref[1] if z == nz - 1 else lz_ref[z]
        centre = centre_ref[z]
        if z == 0:
            centre = centre + end_ref[2]
        if z == nz - 1:
            centre = centre + end_ref[3]
        for f in range(3):
            origin = source_ref[f, z]
            if f == 2 and z == 0:
                origin = origin - end_ref[4]
            if f == 2 and z == nz - 1:
                origin = origin + end_ref[5]
            here = second_ref[f, z + 1]
            total = stencil(here, lx_ref[z], ly_ref[z]) + (
                link_low * second_ref[f, z] + link_high * second_ref[f, z + 2]
            )
            pressure_ref[f, z] = here[own_part]
            residual_ref[f, z] = (origin - centre * here + total)[own_part]


def kernel_call(kernel, outputs, operands, scratch=(), space=pltpu.VMEM, limit=24):
    return pl.pallas_call(
        kernel,
        out_shape=[jax.ShapeDtypeStruct(s, t) for s, t in outputs],
        in_specs=[pl.BlockSpec(memory_space=space)] * len(operands),
        out_specs=[pl.BlockSpec(memory_space=pltpu.VMEM)] * len(outputs),
        scratch_shapes=list(scratch),
        compiler_params=pltpu.CompilerParams(vmem_limit_bytes=limit * 2**20),
    )(*operands)


def swapped(values, stage):
    size = lax.axis_size("gz")
    return lax.ppermute(values, "gz", [(i, i ^ 2**stage) for i in range(size)])


def ring(values, axis, distance):
    size = lax.axis_size(axis)
    return lax.ppermute(values, axis, [(i, (i + distance) % size) for i in range(size)])


def diagonal(values, x_distance, y_distance):
    nx, ny = lax.axis_size("gx"), lax.axis_size("gy")
    route = []
    for i in range(nx):
        for j in range(ny):
            target = ((i + x_distance) % nx) * ny + (j + y_distance) % ny
            route.append((i * ny + j, target))
    return lax.ppermute(values, ("gx", "gy"), route)


def per_device(facies, perm_table, line_breaks):
    nz, nx, ny = facies.shape
    stages = (lax.axis_size("gz") - 1).bit_length()
    i32, f32 = jnp.int32, jnp.float32
    two = lax.axis_size("gx") == 2
    cut_rows = -(-(nz + 1 + 2 * stages) // 8) * 8
    facies, table, cuts, strip, *rows = kernel_call(
        functools.partial(pack_kernel, stages),
        [((nz, nx, ny), i32), ((3, 8, ny), f32), ((cut_rows, ny), f32), ((nx, ny), i32)]
        + [((nz * WIDE, ny), i32)] * (1 if two else 2),
        [facies, perm_table, line_breaks],
        [
            pltpu.SMEM(perm_table.shape, f32),
            pltpu.SMEM(line_breaks.shape, i32),
            pltpu.SemaphoreType.DMA((3,)),
        ],
        pltpu.HBM,
        PACK_LIMIT,
    )
    y_low, y_high = ring(strip, "gy", 1), ring(strip, "gy", -1)
    if two:
        row_low = row_high = ring(rows[0], "gx", 1)
        low_low = low_high = diagonal(strip, 1, 1)
        high_low = high_high = diagonal(strip, 1, -1)
    else:
        row_low, row_high = ring(rows[1], "gx", 1), ring(rows[0], "gx", -1)
        low_low, low_high = diagonal(strip, 1, 1), diagonal(strip, -1, 1)
        high_low, high_high = diagonal(strip, 1, -1), diagonal(strip, -1, -1)

    slab = (nx + 8, 2 * ny)
    one, three = ((nz,) + slab, f32), ((3, nz) + slab, f32)

    def slabs(count):
        return ((count,) + slab, f32)

    def message_of(count, halo):
        return ((Message(count, halo, nx, ny).rows, ny), f32)

    message, own, lx, ly, lz, source, centre, d, e, inverse = kernel_call(
        eliminate_kernel,
        [message_of(FIRST_COUNT, 2), slabs(FIRST_COUNT)]
        + [one] * 3 + [three, one, three, one, one],
        [table, cuts, facies, row_low, row_high, y_low, y_high,
         low_low, low_high, high_low, high_high],
        [pltpu.VMEM((nz, 8, ny), i32)],
    )
    siblings, factors, group = [], [], own
    for s in range(stages - 1):
        last = s == stages - 2
        outputs = [slabs(FIRST_COUNT), slabs(5), message_of(LAST_COUNT if last else FIRST_COUNT, 2)]
        sibling, factor, message, *joined = kernel_call(
            functools.partial(join_kernel, s, last, nz),
            outputs + ([] if last else [slabs(FIRST_COUNT)]),
            [cuts, group, swapped(message, s)],
        )
        siblings.append(sibling)
        factors.append(factor)
        group = None if last else joined[0]
    message, own, d2, kept, ends = kernel_call(
        functools.partial(middle_kernel, stages),
        [message_of(SECOND_COUNT, 1), slabs(SECOND_COUNT), three, slabs(2 * stages + 5), slabs(6)],
        [cuts, own] + siblings + [swapped(message, stages - 1)]
        + [lx, ly, lz, source, d, e, inverse],
        [pltpu.VMEM((3, nz + 2) + slab, f32)],
    )
    siblings, group = [], own
    for s in range(stages - 1):
        last = s == stages - 2
        outputs = [slabs(SECOND_COUNT), message_of(3 if last else SECOND_COUNT, 1)]
        sibling, message, *joined = kernel_call(
            functools.partial(join_again_kernel, s, last),
            outputs + ([] if last else [slabs(SECOND_COUNT)]),
            [group, swapped(message, s), factors[s]],
        )
        siblings.append(sibling)
        group = None if last else joined[0]
    out = ((3, nz, nx, ny), f32)
    pressure, residual = kernel_call(
        functools.partial(final_kernel, stages),
        [out, out],
        [cuts, own] + siblings + [swapped(message, stages - 1)]
        + [lx, ly, lz, source, centre, d2, e, inverse, kept, ends],
        [pltpu.VMEM((3, nz + 2) + slab, f32)],
    )
    return pressure, residual


def solution(mesh):
    return jax.shard_map(
        per_device,
        mesh=mesh,
        in_specs=(P("gz", "gx", "gy"), P(), P()),
        out_specs=(P(None, "gz", "gx", "gy"), P(None, "gz", "gx", "gy")),
        check_vma=False,
    )
```

```python
import functools

import jax
import jax.numpy as jnp
from jax import lax
from jax.experimental import pallas as pl
from jax.experimental.pallas import tpu as pltpu
from jax.sharding import PartitionSpec as P


WIDE = 3
FIRST_COUNT = 11
LAST_COUNT = 5
SECOND_COUNT = 6


def moved(values, amount, axis):
    size = values.shape[axis]
    amount = amount % size
    if amount == 0:
        return values
    return pltpu.roll(values, amount, axis)


def flag(condition):
    return condition.astype(jnp.float32)


def iotas(rows, lanes):
    return tuple(lax.broadcasted_iota(jnp.int32, (rows, lanes), d) for d in (0, 1))


def choose(condition, first, second):
    return [jnp.where(condition, a, b) for a, b in zip(first, second)]


def bit_of(stage):
    return (lax.axis_index("gz") >> stage) % 2 == 1


def pack_kernel(facies_ref, strip_ref, *row_refs):
    nz, nx, ny = facies_ref.shape
    lane = lax.broadcasted_iota(jnp.int32, (nx, ny), 1)
    strip = jnp.zeros((nx, ny), jnp.int32)
    for z in range(nz):
        strip = jnp.where(lane // 8 == z, moved(facies_ref[z], 8 * z + WIDE, 1), strip)
    strip_ref[...] = strip
    for z in range(nz):
        for i in range(WIDE):
            leading = facies_ref[z, i : i + 1, :]
            last = facies_ref[z, nx - WIDE + i : nx - WIDE + i + 1, :]
            spot = slice(i * nz + z, i * nz + z + 1)
            if len(row_refs) == 1:
                row_refs[0][spot, :] = jnp.where(lax.axis_index("gx") == 0, last, leading)
            else:
                row_refs[0][spot, :] = leading
                row_refs[1][spot, :] = last


def lookup(table, index):
    rows = [
        jnp.take_along_axis(table, index[r : r + 8], axis=1) for r in range(0, index.shape[0], 8)
    ]
    return jnp.concatenate(rows, axis=0)


def prepare_kernel(stages, table, breaks, facies_ref, strip_ref, k_ref, table_ref, cut_ref):
    nz, nx, ny = facies_ref.shape
    lane = iotas(8, ny)[1]
    tables = []
    for q in range(3):
        values = jnp.zeros((8, ny), jnp.float32)
        for label in range(table.shape[1]):
            values = jnp.where(lane == label, table[q, label], values)
        table_ref[q] = values
        tables.append(values)
    for z in range(nz):
        for q in range(3):
            k_ref[q, z] = lookup(tables[q], facies_ref[z])
    at_z = lax.axis_index("gz")
    layers = [at_z * nz + r - 1 for r in range(nz + 1)]
    for s in range(stages):
        base, size = (at_z >> (s + 1)) << (s + 1), 2**s
        layers.append((base + size) * nz - 1)
        layers.append(jnp.where(bit_of(s), base, base + 2 * size) * nz - 1)
    for r, layer in enumerate(layers):
        cut = breaks[jnp.clip(layer, 0, breaks.shape[0] - 1)].astype(jnp.float32)
        cut_ref[r : r + 1, :] = jnp.full((1, ny), cut, jnp.float32)


def face(a, b):
    product = a * b
    total = a + b
    harmonic = 2.0 * product / total
    inside = product > 0.0
    link = jnp.where(inside, harmonic, 0.0)
    flow = jnp.where(inside, harmonic, total)
    tau = jnp.where(inside, harmonic, 2.0 * total)
    return link, flow, tau


class Message:
    def __init__(self, count, halo, nx, ny):
        self.count, self.halo, self.nx, self.ny = count, halo, nx, ny
        self.one_sided = lax.axis_size("gx") == 2
        self.rows_each = halo if self.one_sided else 2 * halo
        self.per_tile = 8 // self.rows_each
        self.tiles = -(-count // self.per_tile)
        self.strip = slice(count * nx, count * nx + nx + 8)
        self.rows = self.strip.stop + 8 * self.tiles

    def tile(self, q):
        start = self.strip.stop + 8 * (q // self.per_tile)
        return slice(start, start + 8)

    def side_moved(self, tile, q, sign):
        part = q % self.per_tile
        if not self.one_sided:
            return moved(tile, sign * (self.rows_each * part + self.halo), 0)
        first = lax.axis_index("gx") == 0
        out = jnp.where(
            first,
            moved(tile, sign * self.halo * part, 0),
            moved(tile, sign * self.halo * (part + 1), 0),
        )
        if sign > 0:
            return out
        row = iotas(8, self.ny)[0]
        return jnp.where(jnp.where(first, row, 7 - row) < self.halo, out, 1.0)

    def write(self, ref, slabs):
        nx, ny, halo = self.nx, self.ny, self.halo
        lane = iotas(nx + 8, ny)[1]
        strip = moved(slabs[0][:, ny:], halo, 1)
        for q in range(1, self.count):
            turned = moved(slabs[q][:, ny:], 2 * halo * q + halo, 1)
            strip = jnp.where(lane < 2 * halo * q, strip, turned)
        ref[self.strip, :] = strip
        row = iotas(8, ny)[0]
        for q, slab in enumerate(slabs):
            ref[q * nx : (q + 1) * nx, :] = slab[:nx, :ny]
            turned = self.side_moved(slab[nx:, :ny], q, 1)
            part = q % self.per_tile
            tile = turned if part == 0 else jnp.where(row < self.rows_each * part, tile, turned)
            if part == self.per_tile - 1 or q == self.count - 1:
                ref[self.tile(q), :] = tile

    def read(self, ref):
        nx, halo = self.nx, self.halo
        strip = ref[self.strip, :]
        slabs = []
        for q in range(self.count):
            side = self.side_moved(ref[self.tile(q), :], q, -1)
            body = jnp.concatenate([ref[q * nx : (q + 1) * nx, :], side], axis=0)
            beside = moved(strip, -(2 * halo * q + halo), 1)
            slabs.append(jnp.concatenate([body, beside], axis=1))
        return slabs


def eliminate_kernel(
    table_ref, cut_ref, k_ref, row_low, row_high, y_low, y_high,
    low_low, low_high, high_low, high_high,
    message_ref, own_ref, lx_ref, ly_ref, lz_ref, source_ref, centre_ref,
    d_ref, e_ref, inverse_ref, low_ref, high_ref,
):
    nz, nx, ny = k_ref.shape[1:]
    at_x, at_y = lax.axis_index("gx"), lax.axis_index("gy")
    has_x_low, has_x_high = at_x > 0, at_x < lax.axis_size("gx") - 1
    has_y_low, has_y_high = at_y > 0, at_y < lax.axis_size("gy") - 1
    tables = [table_ref[q] for q in range(3)]

    row, lane = iotas(nx + 8, 2 * ny)
    x_in = (row < nx) | ((row < nx + WIDE) & has_x_high) | ((row >= nx + 8 - WIDE) & has_x_low)
    y_in = (lane < ny) | ((lane < ny + WIDE) & has_y_high)
    y_in = y_in | ((lane >= 2 * ny - WIDE) & has_y_low)
    cell = x_in & y_in
    valid = flag(cell)
    in_x, in_xp = valid * moved(valid, -1, 0), valid * moved(valid, 1, 0)
    in_y, in_yp = valid * moved(valid, -1, 1), valid * moved(valid, 1, 1)
    row_in, strip_in = cell[nx:, :ny], cell[:, ny:]

    row = iotas(8, ny)[0]
    lane = iotas(nx + 8, ny)[1]

    def corner(high, low):
        return jnp.where(row < WIDE, high[0:8, :], low[nx - 8 : nx, :])

    before = jnp.concatenate([y_low[...], corner(low_high, low_low)], axis=0)
    after = jnp.concatenate([y_high[...], corner(high_high, high_low)], axis=0)
    strip = jnp.where(lane % 8 < WIDE, before, after)
    strips = [lookup(table, strip) for table in tables]
    for q in range(3):
        low_ref[q] = lookup(tables[q], row_low[...])
        high_ref[q] = lookup(tables[q], row_high[...])

    def coefficients(z):
        out = []
        for q in range(3):
            side = jnp.zeros((8, ny), jnp.float32)
            for i in range(WIDE):
                spot = slice(i * nz + z, i * nz + z + 1)
                side = jnp.where(row == i, high_ref[q, spot, :], side)
                side = jnp.where(row == 8 - WIDE + i, low_ref[q, spot, :], side)
            side = jnp.where(row_in, side, 0.0)
            body = jnp.concatenate([k_ref[q, z], side], axis=0)
            beside = jnp.where(strip_in, moved(strips[q], -(8 * z + WIDE), 1), 0.0)
            out.append(jnp.concatenate([body, beside], axis=1))
        return out

    def side_faces(here, axis, inside, inside_back):
        there = moved(here, -1, axis)
        total = here + there
        flow = jnp.where(inside > 0.0, 2.0 * (here * there) / total, total)
        flow_back = moved(flow, 1, axis)
        tau = flow * (2.0 - inside) + flow_back * (2.0 - inside_back)
        return flow * inside, tau, flow - flow_back

    next_k = coefficients(0)
    link_below = None
    for z in range(nz):
        kx, ky, kz = next_k
        link_x, tau_x, source_x = side_faces(kx, 0, in_x, in_xp)
        link_y, tau_y, source_y = side_faces(ky, 1, in_y, in_yp)
        lx_ref[z] = link_x
        ly_ref[z] = link_y
        centre = tau_x + tau_y
        if z == 0:
            kz_first = kz
        if z < nz - 1:
            next_k = coefficients(z + 1)
            above = next_k[2]
            link_z = jnp.where(cell, 2.0 * (kz * above) / (kz + above), 0.0)
            lz_ref[z] = link_z
        if z == 0:
            centre = centre + link_z
            source_z = link_z
        elif z == nz - 1:
            centre = centre + link_below
            source_z = -link_below
        else:
            centre = centre + (link_below + link_z)
            source_z = link_z - link_below
        centre = jnp.where(cell, centre, 1.0)
        sources = [source_x, source_y, source_z]
        for f in range(3):
            source_ref[f, z] = sources[f]
        centre_ref[z] = centre
        if z == 0:
            s_uu = centre
            g_u = list(sources)
        elif z < nz - 1:
            if z == 1:
                pivot = centre
                forward = list(sources)
                numerator = coupling
            else:
                pivot = centre - coupling * ratio
                forward = [sources[f] + coupling * value[f] for f in range(3)]
                numerator = coupling * spike
            inverse = 1.0 / pivot
            value = [forward[f] * inverse for f in range(3)]
            spike = numerator * inverse
            s_uu = s_uu - numerator * spike
            g_u = [g_u[f] + spike * forward[f] for f in range(3)]
            inverse_ref[z] = inverse
            e_ref[z] = spike
            for f in range(3):
                d_ref[f, z] = value[f]
        else:
            s_vv = centre - coupling * ratio
            s_uv = -coupling * spike
            g_v = [sources[f] + coupling * value[f] for f in range(3)]
        if z < nz - 1:
            coupling = link_z * open_after(cut_ref, z + 1)
            if z > 0:
                ratio = coupling * inverse
        link_below = link_z
    slabs = [s_uu, s_uv, s_vv, kz_first, kz] + g_u + g_v
    for q, slab in enumerate(slabs):
        own_ref[q] = slab
    Message(FIRST_COUNT, 2, nx, ny).write(message_ref, slabs)


def open_after(cut_ref, r):
    cut = 1.0 - cut_ref[r : r + 1, :]
    return jnp.concatenate([cut, cut], axis=1)


def slab_size(ref):
    return ref.shape[-2] - 8, ref.shape[-1] // 2


def join_kernel(stage, last, nz, cut_ref, own_ref, message_ref, sibling_ref, factor_ref, next_ref, *joined):
    nx, ny = slab_size(own_ref)
    own = [own_ref[q] for q in range(FIRST_COUNT)]
    sibling = Message(FIRST_COUNT, 2, nx, ny).read(message_ref)
    for q, slab in enumerate(sibling):
        sibling_ref[q] = slab
    above = bit_of(stage)
    low, high = choose(above, sibling, own), choose(above, own, sibling)
    link, flow, tau = face(low[4], high[3])
    coupling = link * open_after(cut_ref, nz + 1 + 2 * stage)
    inverse = 1.0 / (low[2] + tau)
    step = coupling * inverse
    last_inverse = 1.0 / (high[0] + tau - coupling * step)
    outer = low[1] * inverse
    weight = step * low[1]
    weight_low, weight_high = weight * last_inverse, high[1] * last_inverse
    right_low = low[8:10] + [low[10] + flow]
    right_high = high[5:7] + [high[7] - flow]
    middle = [b + step * a for a, b in zip(right_low, right_high)]
    s_uu = low[0] - outer * low[1] - weight * weight_low
    s_uv = -weight * weight_high
    s_vv = high[2] - high[1] * weight_high
    g_u = [g - outer * a - weight_low * m for g, a, m in zip(low[5:8], right_low, middle)]
    g_v = [g - weight_high * m for g, m in zip(high[8:11], middle)]
    for n, values in enumerate((outer, step, weight_low, weight_high)):
        factor_ref[n] = values
    if not last:
        slabs = [s_uu, s_uv, s_vv, low[3], high[4]] + g_u + g_v
        for q, slab in enumerate(slabs):
            joined[0][q] = slab
        Message(FIRST_COUNT, 2, nx, ny).write(next_ref, slabs)
        return
    top = bit_of(stage + 1)
    far_s, near_s = choose(top, [s_vv, s_uu], [s_uu, s_vv])
    far_k, near_k = choose(top, [high[4], low[3]], [low[3], high[4]])
    far_g, near_g = choose(top, g_v, g_u), choose(top, g_u, g_v)
    far_g[2] = far_g[2] + far_k * jnp.where(top, 1.0, -1.0)
    factor = s_uv / (far_s + 2.0 * far_k)
    factor_ref[4] = factor
    slabs = [near_s - s_uv * factor, near_k] + [n - factor * g for n, g in zip(near_g, far_g)]
    Message(LAST_COUNT, 2, nx, ny).write(next_ref, slabs)


def join_again_kernel(stage, last, own_ref, message_ref, factor_ref, sibling_ref, next_ref, *joined):
    nx, ny = slab_size(own_ref)
    own = [own_ref[q] for q in range(SECOND_COUNT)]
    sibling = Message(SECOND_COUNT, 1, nx, ny).read(message_ref)
    for q, slab in enumerate(sibling):
        sibling_ref[q] = slab
    above = bit_of(stage)
    low, high = choose(above, sibling, own), choose(above, own, sibling)
    outer, step, weight_low, weight_high = [factor_ref[n] for n in range(4)]
    middle = [b + step * a for a, b in zip(low[3:], high[:3])]
    g_u = [g - outer * a - weight_low * m for g, a, m in zip(low[:3], low[3:], middle)]
    g_v = [g - weight_high * m for g, m in zip(high[3:], middle)]
    if not last:
        for q, slab in enumerate(g_u + g_v):
            joined[0][q] = slab
        Message(SECOND_COUNT, 1, nx, ny).write(next_ref, g_u + g_v)
        return
    top = bit_of(stage + 1)
    factor = factor_ref[4]
    far_g, near_g = choose(top, g_v, g_u), choose(top, g_u, g_v)
    Message(3, 1, nx, ny).write(next_ref, [n - factor * g for n, g in zip(near_g, far_g)])


def stencil(slab, link_x, link_y):
    return (
        link_x * moved(slab, -1, 0)
        + moved(link_x * slab, 1, 0)
        + (link_y * moved(slab, -1, 1) + moved(link_y * slab, 1, 1))
    )


def middle_kernel(stages, cut_ref, *refs):
    own_ref, siblings, message_ref = refs[0], refs[1:stages], refs[stages]
    refs = refs[stages + 1 :]
    lx_ref, ly_ref, lz_ref, source_ref, d_ref, e_ref, inverse_ref = refs[:7]
    next_ref, own2_ref, d2_ref, factor_ref, end_ref, first_ref = refs[7:]
    nz = lx_ref.shape[0]
    nx, ny = slab_size(lx_ref)
    own = [own_ref[q] for q in range(FIRST_COUNT)]
    slots = []

    def keep(values):
        factor_ref[len(slots)] = values
        slots.append(None)

    def attach(state, sign, row, pivot, right, k):
        beside, k_beside, rights, exists = state[0], state[1], state[2:5], state[5]
        link, flow, tau = face(k_beside * exists, k)
        coupling = link * open_after(cut_ref, row)
        rights = rights[:2] + [rights[2] + sign * flow]
        inverse = 1.0 / (beside + tau)
        step = coupling * inverse
        right = [a + step * b for a, b in zip(right, rights)]
        right[2] = right[2] - sign * flow
        return pivot + tau - coupling * step, right, step, inverse, rights, (link, flow, tau)

    far = Message(LAST_COUNT, 2, nx, ny).read(message_ref)
    top = bit_of(stages - 1)
    below, above = far + [flag(top)], far + [flag(jnp.logical_not(top))]
    for s in range(stages - 2, -1, -1):
        up = bit_of(s)
        block = [siblings[s][q] for q in range(FIRST_COUNT)]
        sign = jnp.where(up, 1.0, -1.0)
        state = choose(up, below, above)
        far_s, far_k, near_s, near_k = choose(
            up, [block[0], block[3], block[2], block[4]], [block[2], block[4], block[0], block[3]]
        )
        far_g = choose(up, block[5:8], block[8:11])
        near_g = choose(up, block[8:11], block[5:8])
        pivot, right, step, _, _, _ = attach(state, sign, nz + 2 + 2 * s, far_s, far_g, far_k)
        factor = block[1] / pivot
        keep(step)
        keep(factor)
        state = [near_s - block[1] * factor, near_k]
        state += [n - factor * r for n, r in zip(near_g, right)] + [jnp.float32(1.0)]
        below, above = choose(up, state, below), choose(up, above, state)

    pivot_u, right_u, step_b, inverse_b, rights_b, ends_b = attach(
        below, 1.0, 0, own[0], own[5:8], own[3]
    )
    pivot_v, right_v, step_a, inverse_a, rights_a, ends_a = attach(
        above, -1.0, nz, own[2], own[8:11], own[4]
    )
    held_b, held_a = inverse_b * below[5], inverse_a * above[5]
    inverse_u = 1.0 / pivot_u
    factor = own[1] * inverse_u
    inverse_v = 1.0 / (pivot_v - own[1] * factor)
    for values in (step_b, held_b, step_a, held_a, inverse_u, factor, inverse_v):
        keep(values)
    (link_b, flow_b, tau_b), (link_a, flow_a, tau_a) = ends_b, ends_a
    for n, values in enumerate((link_b, link_a, tau_b, tau_a, flow_b, flow_a)):
        end_ref[n] = values

    for f in range(3):
        last = (right_v[f] - factor * right_u[f]) * inverse_v
        first_u = right_u[f] * inverse_u - factor * last
        first_ref[f, 0] = rights_b[f] * held_b + step_b * first_u
        first_ref[f, nz + 1] = rights_a[f] * held_a + step_a * last
        first_ref[f, 1] = first_u
        first_ref[f, nz] = last
    for z in range(nz - 2, 0, -1):
        ratio = lz_ref[z] * open_after(cut_ref, z + 1) * inverse_ref[z]
        spike = e_ref[z]
        for f in range(3):
            first_ref[f, z + 1] = (
                d_ref[f, z] + spike * first_ref[f, 1] + ratio * first_ref[f, z + 2]
            )

    for z in range(nz):
        link_low = link_b if z == 0 else lz_ref[z - 1]
        link_high = link_a if z == nz - 1 else lz_ref[z]
        cut_low = link_low * (1.0 - open_after(cut_ref, z))
        cut_high = link_high * (1.0 - open_after(cut_ref, z + 1))
        right = []
        for f in range(3):
            origin = source_ref[f, z]
            if f == 2 and z == 0:
                origin = origin - flow_b
            if f == 2 and z == nz - 1:
                origin = origin + flow_a
            right.append(
                origin
                + stencil(first_ref[f, z + 1], lx_ref[z], ly_ref[z])
                + (cut_low * first_ref[f, z] + cut_high * first_ref[f, z + 2])
            )
        if z == 0:
            g_u = list(right)
        else:
            if z == 1:
                forward = right
            else:
                forward = [right[f] + coupling * value[f] for f in range(3)]
            if z < nz - 1:
                inverse, spike = inverse_ref[z], e_ref[z]
                value = [forward[f] * inverse for f in range(3)]
                g_u = [g_u[f] + spike * forward[f] for f in range(3)]
                for f in range(3):
                    d2_ref[f, z] = value[f]
                coupling = lz_ref[z] * open_after(cut_ref, z + 1)
    slabs = g_u + forward
    for q, slab in enumerate(slabs):
        own2_ref[q] = slab
    Message(SECOND_COUNT, 1, nx, ny).write(next_ref, slabs)


def final_kernel(stages, cut_ref, *refs):
    own_ref, siblings, message_ref = refs[0], refs[1:stages], refs[stages]
    refs = refs[stages + 1 :]
    lx_ref, ly_ref, lz_ref, source_ref, centre_ref, d2_ref, e_ref, inverse_ref = refs[:8]
    factor_ref, end_ref, pressure_ref, residual_ref, second_ref = refs[8:]
    nz = lx_ref.shape[0]
    nx, ny = slab_size(lx_ref)
    own = [own_ref[q] for q in range(SECOND_COUNT)]
    slots = []

    def kept():
        slots.append(None)
        return factor_ref[len(slots) - 1]

    below = above = Message(3, 1, nx, ny).read(message_ref)
    for s in range(stages - 2, -1, -1):
        up = bit_of(s)
        block = [siblings[s][q] for q in range(SECOND_COUNT)]
        state = choose(up, below, above)
        far_g = choose(up, block[:3], block[3:])
        near_g = choose(up, block[3:], block[:3])
        step, factor = kept(), kept()
        right = [a + step * b for a, b in zip(far_g, state)]
        state = [n - factor * r for n, r in zip(near_g, right)]
        below, above = choose(up, state, below), choose(up, above, state)
    step_b, held_b, step_a, held_a = kept(), kept(), kept(), kept()
    inverse_u, factor, inverse_v = kept(), kept(), kept()
    for f in range(3):
        right_u = own[f] + step_b * below[f]
        right_v = own[3 + f] + step_a * above[f]
        last = (right_v - factor * right_u) * inverse_v
        first_u = right_u * inverse_u - factor * last
        second_ref[f, 0] = below[f] * held_b + step_b * first_u
        second_ref[f, nz + 1] = above[f] * held_a + step_a * last
        second_ref[f, 1] = first_u
        second_ref[f, nz] = last
    for z in range(nz - 2, 0, -1):
        ratio = lz_ref[z] * open_after(cut_ref, z + 1) * inverse_ref[z]
        spike = e_ref[z]
        for f in range(3):
            second_ref[f, z + 1] = (
                d2_ref[f, z] + spike * second_ref[f, 1] + ratio * second_ref[f, z + 2]
            )
    own_part = (slice(0, nx), slice(0, ny))
    for z in range(nz):
        link_low = end_ref[0] if z == 0 else lz_ref[z - 1]
        link_high = end_ref[1] if z == nz - 1 else lz_ref[z]
        centre = centre_ref[z]
        if z == 0:
            centre = centre + end_ref[2]
        if z == nz - 1:
            centre = centre + end_ref[3]
        for f in range(3):
            origin = source_ref[f, z]
            if f == 2 and z == 0:
                origin = origin - end_ref[4]
            if f == 2 and z == nz - 1:
                origin = origin + end_ref[5]
            here = second_ref[f, z + 1]
            total = stencil(here, lx_ref[z], ly_ref[z]) + (
                link_low * second_ref[f, z] + link_high * second_ref[f, z + 2]
            )
            pressure_ref[f, z] = here[own_part]
            residual_ref[f, z] = (origin - centre * here + total)[own_part]


def kernel_call(kernel, outputs, operands, scratch=(), smem=0, cost=None):
    specs = [pl.BlockSpec(memory_space=pltpu.SMEM)] * smem
    specs += [pl.BlockSpec(memory_space=pltpu.VMEM)] * (len(operands) - smem)
    return pl.pallas_call(
        kernel,
        out_shape=[jax.ShapeDtypeStruct(s, t) for s, t in outputs],
        in_specs=specs,
        out_specs=[pl.BlockSpec(memory_space=pltpu.VMEM)] * len(outputs),
        scratch_shapes=list(scratch),
        compiler_params=pltpu.CompilerParams(vmem_limit_bytes=24 * 2**20),
        cost_estimate=cost,
    )(*operands)


def swapped(values, stage):
    size = lax.axis_size("gz")
    return lax.ppermute(values, "gz", [(i, i ^ 2**stage) for i in range(size)])


def ring(values, axis, distance):
    size = lax.axis_size(axis)
    return lax.ppermute(values, axis, [(i, (i + distance) % size) for i in range(size)])


def diagonal(values, x_distance, y_distance):
    nx, ny = lax.axis_size("gx"), lax.axis_size("gy")
    route = []
    for i in range(nx):
        for j in range(ny):
            target = ((i + x_distance) % nx) * ny + (j + y_distance) % ny
            route.append((i * ny + j, target))
    return lax.ppermute(values, ("gx", "gy"), route)


def per_device(facies, perm_table, line_breaks):
    nz, nx, ny = facies.shape
    stages = (lax.axis_size("gz") - 1).bit_length()
    i32, f32 = jnp.int32, jnp.float32
    two = lax.axis_size("gx") == 2
    cut_rows = -(-(nz + 1 + 2 * stages) // 8) * 8
    strip, *rows = kernel_call(
        pack_kernel,
        [((nx, ny), i32)] + [((nz * WIDE, ny), i32)] * (1 if two else 2),
        [facies],
    )
    k, table, cuts = kernel_call(
        functools.partial(prepare_kernel, stages),
        [((3, nz, nx, ny), f32), ((3, 8, ny), f32), ((cut_rows, ny), f32)],
        [perm_table, line_breaks, facies, strip],
        smem=2,
        cost=pl.CostEstimate(flops=10**7, bytes_accessed=10**6, transcendentals=0),
    )
    y_low, y_high = ring(strip, "gy", 1), ring(strip, "gy", -1)
    if two:
        row_low = row_high = ring(rows[0], "gx", 1)
        low_low = low_high = diagonal(strip, 1, 1)
        high_low = high_high = diagonal(strip, 1, -1)
    else:
        row_low, row_high = ring(rows[1], "gx", 1), ring(rows[0], "gx", -1)
        low_low, low_high = diagonal(strip, 1, 1), diagonal(strip, -1, 1)
        high_low, high_high = diagonal(strip, 1, -1), diagonal(strip, -1, -1)

    slab = (nx + 8, 2 * ny)
    one, three = ((nz,) + slab, f32), ((3, nz) + slab, f32)

    def slabs(count):
        return ((count,) + slab, f32)

    def message_of(count, halo):
        return ((Message(count, halo, nx, ny).rows, ny), f32)

    message, own, lx, ly, lz, source, centre, d, e, inverse = kernel_call(
        eliminate_kernel,
        [message_of(FIRST_COUNT, 2), slabs(FIRST_COUNT)]
        + [one] * 3 + [three, one, three, one, one],
        [table, cuts, k, row_low, row_high, y_low, y_high,
         low_low, low_high, high_low, high_high],
        [pltpu.VMEM((3, nz * WIDE, ny), f32)] * 2,
    )
    siblings, factors, group = [], [], own
    for s in range(stages - 1):
        last = s == stages - 2
        outputs = [slabs(FIRST_COUNT), slabs(5), message_of(LAST_COUNT if last else FIRST_COUNT, 2)]
        sibling, factor, message, *joined = kernel_call(
            functools.partial(join_kernel, s, last, nz),
            outputs + ([] if last else [slabs(FIRST_COUNT)]),
            [cuts, group, swapped(message, s)],
        )
        siblings.append(sibling)
        factors.append(factor)
        group = None if last else joined[0]
    message, own, d2, kept, ends = kernel_call(
        functools.partial(middle_kernel, stages),
        [message_of(SECOND_COUNT, 1), slabs(SECOND_COUNT), three, slabs(2 * stages + 5), slabs(6)],
        [cuts, own] + siblings + [swapped(message, stages - 1)]
        + [lx, ly, lz, source, d, e, inverse],
        [pltpu.VMEM((3, nz + 2) + slab, f32)],
    )
    siblings, group = [], own
    for s in range(stages - 1):
        last = s == stages - 2
        outputs = [slabs(SECOND_COUNT), message_of(3 if last else SECOND_COUNT, 1)]
        sibling, message, *joined = kernel_call(
            functools.partial(join_again_kernel, s, last),
            outputs + ([] if last else [slabs(SECOND_COUNT)]),
            [group, swapped(message, s), factors[s]],
        )
        siblings.append(sibling)
        group = None if last else joined[0]
    out = ((3, nz, nx, ny), f32)
    pressure, residual = kernel_call(
        functools.partial(final_kernel, stages),
        [out, out],
        [cuts, own] + siblings + [swapped(message, stages - 1)]
        + [lx, ly, lz, source, centre, d2, e, inverse, kept, ends],
        [pltpu.VMEM((3, nz + 2) + slab, f32)],
    )
    return pressure, residual


def solution(mesh):
    return jax.shard_map(
        per_device,
        mesh=mesh,
        in_specs=(P("gz", "gx", "gy"), P(), P()),
        out_specs=(P(None, "gz", "gx", "gy"), P(None, "gz", "gx", "gy")),
        check_vma=False,
    )
```

```python
import functools

import jax
import jax.numpy as jnp
from jax import lax
from jax.experimental import pallas as pl
from jax.experimental.pallas import tpu as pltpu
from jax.sharding import PartitionSpec as P


WIDE = 3
FIRST_COUNT = 11
LAST_COUNT = 5
SECOND_COUNT = 6
PAIR_COUNT = 16
CHUNK = 4


def moved(values, amount, axis):
    size = values.shape[axis]
    amount = amount % size
    if amount == 0:
        return values
    return pltpu.roll(values, amount, axis)


def flag(condition):
    return condition.astype(jnp.float32)


def iotas(rows, lanes):
    return tuple(lax.broadcasted_iota(jnp.int32, (rows, lanes), d) for d in (0, 1))


def choose(condition, first, second):
    return [jnp.where(condition, a, b) for a, b in zip(first, second)]


def is_high(stage):
    return (lax.axis_index("gz") >> (stage + 1)) % 2 == 1


def own_start(nz):
    return (lax.axis_index("gz") % 2) * nz


def pack_kernel(own_ref, other_ref, table_ref, strip_ref, *row_refs):
    nz, nx, ny = own_ref.shape
    lane = lax.broadcasted_iota(jnp.int32, (nx, ny), 1)
    row = iotas(8, ny)[0]
    swap = own_start(nz) > 0
    for b in range(2):
        strip = jnp.zeros((nx, ny), jnp.int32)
        for z in range(0, nz, 2):
            pair = []
            for at in (z, z + 1):
                layer = jnp.where(swap == (b == 1), own_ref[at], other_ref[at])
                pair.append(layer)
                strip = jnp.where(lane // 8 == at, moved(layer, 8 * at + WIDE, 1), strip)
            first = jnp.where(row < 4, pair[0][:8], moved(pair[1][:8], 4, 0))
            last = jnp.where(row < 4, moved(pair[0][nx - 8 :], 4, 0), pair[1][nx - 8 :])
            start = (b * nz + z) * 4
            spot = slice(start, start + 8)
            if len(row_refs) == 1:
                row_refs[0][spot, :] = jnp.where(lax.axis_index("gx") == 0, last, first)
            else:
                row_refs[0][spot, :] = first
                row_refs[1][spot, :] = last
        strip_ref[b * nx : (b + 1) * nx, :] = strip


def lookup(table, index):
    rows = [
        jnp.take_along_axis(table, index[r : r + 8], axis=1) for r in range(0, index.shape[0], 8)
    ]
    return jnp.concatenate(rows, axis=0)


def prepare_kernel(stages, table, breaks, facies_ref, k_ref, table_ref, cut_ref):
    nz, nx, ny = facies_ref.shape
    lane = iotas(8, ny)[1]
    tables = []
    for q in range(3):
        values = jnp.zeros((8, ny), jnp.float32)
        for label in range(table.shape[1]):
            values = jnp.where(lane == label, table[q, label], values)
        table_ref[q] = values
        tables.append(values)
    for z in range(nz):
        for q in range(3):
            k_ref[q, z] = lookup(tables[q], facies_ref[z])
    pair = lax.axis_index("gz") // 2
    layers = [pair * 2 * nz + r - 1 for r in range(2 * nz + 1)]
    for s in range(stages):
        base, size = (pair >> (s + 1)) << (s + 1), 2**s
        layers.append((base + size) * 2 * nz - 1)
        layers.append(jnp.where(is_high(s), base, base + 2 * size) * 2 * nz - 1)
    for r, layer in enumerate(layers):
        cut = breaks[jnp.clip(layer, 0, breaks.shape[0] - 1)].astype(jnp.float32)
        cut_ref[r : r + 1, :] = jnp.full((1, ny), cut, jnp.float32)


def prepare_other_kernel(table_ref, own_ref, other_ref, strip_ref, k_ref):
    nz = other_ref.shape[0]
    start = own_start(nz)
    for q in range(3):
        k_ref[q, pl.ds(start, nz)] = own_ref[q]
        for z in range(nz):
            k_ref[q, nz - start + z] = lookup(table_ref[q], other_ref[z])


def face(a, b):
    product = a * b
    total = a + b
    harmonic = 2.0 * product / total
    inside = product > 0.0
    link = jnp.where(inside, harmonic, 0.0)
    flow = jnp.where(inside, harmonic, total)
    tau = jnp.where(inside, harmonic, 2.0 * total)
    return link, flow, tau


class Message:
    def __init__(self, count, halo, nx, ny):
        self.count, self.halo, self.nx, self.ny = count, halo, nx, ny
        self.one_sided = lax.axis_size("gx") == 2
        self.rows_each = halo if self.one_sided else 2 * halo
        self.per_tile = 8 // self.rows_each
        self.tiles = -(-count // self.per_tile)
        self.strip = slice(count * nx, count * nx + nx + 8)
        self.rows = self.strip.stop + 8 * self.tiles

    def tile(self, q):
        start = self.strip.stop + 8 * (q // self.per_tile)
        return slice(start, start + 8)

    def side_moved(self, tile, q, sign):
        part = q % self.per_tile
        if not self.one_sided:
            return moved(tile, sign * (self.rows_each * part + self.halo), 0)
        first = lax.axis_index("gx") == 0
        out = jnp.where(
            first,
            moved(tile, sign * self.halo * part, 0),
            moved(tile, sign * self.halo * (part + 1), 0),
        )
        if sign > 0:
            return out
        row = iotas(8, self.ny)[0]
        return jnp.where(jnp.where(first, row, 7 - row) < self.halo, out, 1.0)

    def write(self, ref, slabs):
        nx, ny, halo = self.nx, self.ny, self.halo
        lane = iotas(nx + 8, ny)[1]
        strip = moved(slabs[0][:, ny:], halo, 1)
        for q in range(1, self.count):
            turned = moved(slabs[q][:, ny:], 2 * halo * q + halo, 1)
            strip = jnp.where(lane < 2 * halo * q, strip, turned)
        ref[self.strip, :] = strip
        row = iotas(8, ny)[0]
        for q, slab in enumerate(slabs):
            ref[q * nx : (q + 1) * nx, :] = slab[:nx, :ny]
            turned = self.side_moved(slab[nx:, :ny], q, 1)
            part = q % self.per_tile
            tile = turned if part == 0 else jnp.where(row < self.rows_each * part, tile, turned)
            if part == self.per_tile - 1 or q == self.count - 1:
                ref[self.tile(q), :] = tile

    def read(self, ref):
        nx, halo = self.nx, self.halo
        strip = ref[self.strip, :]
        slabs = []
        for q in range(self.count):
            side = self.side_moved(ref[self.tile(q), :], q, -1)
            body = jnp.concatenate([ref[q * nx : (q + 1) * nx, :], side], axis=0)
            beside = moved(strip, -(2 * halo * q + halo), 1)
            slabs.append(jnp.concatenate([body, beside], axis=1))
        return slabs


def open_after(cut_ref, r):
    cut = 1.0 - cut_ref[r : r + 1, :]
    return jnp.concatenate([cut, cut], axis=1)


def slab_size(ref):
    return ref.shape[-2] - 8, ref.shape[-1] // 2


def join(low, high, opened):
    ends = link, flow, tau = face(low[4], high[3])
    coupling = link * opened
    inverse = 1.0 / (low[2] + tau)
    step = coupling * inverse
    last_inverse = 1.0 / (high[0] + tau - coupling * step)
    outer = low[1] * inverse
    weight = step * low[1]
    weight_low, weight_high = weight * last_inverse, high[1] * last_inverse
    right_low = low[8:10] + [low[10] + flow]
    right_high = high[5:7] + [high[7] - flow]
    s_uu = low[0] - outer * low[1] - weight * weight_low
    s_uv = -weight * weight_high
    s_vv = high[2] - high[1] * weight_high
    factors = [outer, step, weight_low, weight_high, inverse, last_inverse]
    g_u, g_v, middle = join_right(factors, low[5:8], right_low, right_high, high[8:11])
    return [s_uu, s_uv, s_vv, low[3], high[4]] + g_u + g_v, factors, right_low + middle, ends


def join_right(factors, low_u, low_v, high_u, high_v):
    outer, step, weight_low, weight_high = factors[:4]
    middle = [b + step * a for a, b in zip(low_v, high_u)]
    g_u = [g - outer * a - weight_low * m for g, a, m in zip(low_u, low_v, middle)]
    g_v = [g - weight_high * m for g, m in zip(high_v, middle)]
    return g_u, g_v, middle


def join_inner(factors, right_low, middle, first, last):
    outer, step, weight_low, weight_high, inverse, last_inverse = factors
    high = last_inverse * middle - weight_low * first - weight_high * last
    return inverse * right_low - outer * first + step * high, high


def reduce_end(slabs, top):
    s_uu, s_uv, s_vv, k_u, k_v = slabs[:5]
    far_s, near_s = choose(top, [s_vv, s_uu], [s_uu, s_vv])
    far_k, near_k = choose(top, [k_v, k_u], [k_u, k_v])
    sign = jnp.where(top, 1.0, -1.0)
    factor = s_uv / (far_s + 2.0 * far_k)
    g_u, g_v = slabs[5:8], slabs[8:11]
    far_g, near_g = choose(top, g_v, g_u), choose(top, g_u, g_v)
    far_g[2] = far_g[2] + far_k * sign
    return [near_s - s_uv * factor, near_k] + [n - factor * g for n, g in zip(near_g, far_g)], factor


def reduce_end_right(factor, g_u, g_v, top):
    far_g, near_g = choose(top, g_v, g_u), choose(top, g_u, g_v)
    return [n - factor * g for n, g in zip(near_g, far_g)]


def eliminate_kernel(
    stages, table_ref, cut_ref, k_ref, row_low, row_high, y_low, y_high,
    low_low, low_high, high_low, high_high,
    message_ref, own_ref, pair_ref, lx_ref, ly_ref, lz_ref, d_ref, e_ref, inverse_ref,
    all_ref, flow_ref, source_ref, centre_ref, low_ref, high_ref=None,
):
    high_ref = low_ref if high_ref is None else high_ref
    layers, nx, ny = k_ref.shape[1:]
    nz = layers // 2
    at_x, at_y = lax.axis_index("gx"), lax.axis_index("gy")
    has_x_low, has_x_high = at_x > 0, at_x < lax.axis_size("gx") - 1
    has_y_low, has_y_high = at_y > 0, at_y < lax.axis_size("gy") - 1
    tables = [table_ref[q] for q in range(3)]

    row, lane = iotas(nx + 8, 2 * ny)
    x_in = (row < nx) | ((row < nx + WIDE) & has_x_high) | ((row >= nx + 8 - WIDE) & has_x_low)
    y_in = (lane < ny) | ((lane < ny + WIDE) & has_y_high)
    y_in = y_in | ((lane >= 2 * ny - WIDE) & has_y_low)
    cell = x_in & y_in
    valid = flag(cell)
    in_x, in_xp = valid * moved(valid, -1, 0), valid * moved(valid, 1, 0)
    in_y, in_yp = valid * moved(valid, -1, 1), valid * moved(valid, 1, 1)
    row_in, strip_in = cell[nx:, :ny], cell[:, ny:]

    row = iotas(8, ny)[0]
    lane = iotas(nx + 8, ny)[1]
    strips = []
    for b in range(2):
        part = slice(b * nx, (b + 1) * nx)

        def whole(own, high, low):
            side = jnp.where(row < WIDE, high[part, :][0:8], low[part, :][nx - 8 :])
            return jnp.concatenate([own[part, :], side], axis=0)

        before, after = whole(y_low, low_high, low_low), whole(y_high, high_high, high_low)
        strip = jnp.where(lane % 8 < WIDE, before, after)
        strips.append([lookup(table, strip) for table in tables])
    for q in range(3):
        low_ref[q] = lookup(tables[q], row_low[...])
        if high_ref is not low_ref:
            high_ref[q] = lookup(tables[q], row_high[...])

    for b in range(2):
        for z in range(nz):
            at = b * nz + z
            start = at // 2 * 8
            for q in range(3):
                low, high = low_ref[q, start : start + 8, :], high_ref[q, start : start + 8, :]
                if z % 2 == 0:
                    low = moved(low, 4, 0)
                else:
                    high = moved(high, 4, 0)
                side = jnp.where(row_in, jnp.where(row < 4, high, low), 0.0)
                beside = jnp.where(strip_in, moved(strips[b][q], -(8 * z + WIDE), 1), 0.0)
                all_ref[q, at, :nx, :ny] = k_ref[q, at]
                all_ref[q, at, nx:, :ny] = side
                all_ref[q, at, :, ny:] = beside

    def flow_after(here, axis, inside):
        there = moved(here, -1, axis)
        total = here + there
        return jnp.where(inside > 0.0, 2.0 * (here * there) / total, total)

    def tau_and_source(flow, axis, inside, inside_back):
        back = moved(flow, 1, axis)
        return flow * (2.0 - inside) + back * (2.0 - inside_back), flow - back

    for at in range(layers):
        flow_x = flow_after(all_ref[0, at], 0, in_x)
        flow_ref[at] = flow_after(all_ref[1, at], 1, in_y)
        lx_ref[at] = flow_x * in_x
        centre_ref[at], source_ref[0, at] = tau_and_source(flow_x, 0, in_x, in_xp)
        if at % nz < nz - 1:
            kz, above = all_ref[2, at], all_ref[2, at + 1]
            lz_ref[at] = jnp.where(cell, 2.0 * (kz * above) / (kz + above), 0.0)
    for at in range(layers):
        flow_y = flow_ref[at]
        ly_ref[at] = flow_y * in_y
        tau_y, source_ref[1, at] = tau_and_source(flow_y, 1, in_y, in_yp)
        centre = centre_ref[at] + tau_y
        if at % nz > 0:
            centre = centre + lz_ref[at - 1]
        if at % nz < nz - 1:
            centre = centre + lz_ref[at]
        centre_ref[at] = jnp.where(cell, centre, 1.0)

    states = [{}, {}]
    for z in range(nz):
        for b in range(2):
            at, v = b * nz + z, states[b]
            centre = centre_ref[at]
            sources = [source_ref[0, at], source_ref[1, at]]
            if z == 0:
                v["source"] = sources + [lz_ref[at]]
                v["s_uu"], v["g_u"] = centre, v["source"]
            elif z == nz - 1:
                sources = sources + [-lz_ref[at - 1]]
                v["s_vv"] = centre - v["coupling"] * v["ratio"]
                v["s_uv"] = -v["coupling"] * v["spike"]
                v["g_v"] = [a + v["coupling"] * d for a, d in zip(sources, v["value"])]
            else:
                forward = sources + [lz_ref[at] - lz_ref[at - 1]]
                if z == 1:
                    pivot, numerator = centre, v["coupling"]
                else:
                    pivot = centre - v["coupling"] * v["ratio"]
                    forward = [a + v["coupling"] * d for a, d in zip(forward, v["value"])]
                    numerator = v["coupling"] * v["spike"]
                inverse = 1.0 / pivot
                v["value"] = [a * inverse for a in forward]
                v["spike"] = numerator * inverse
                v["s_uu"] = v["s_uu"] - numerator * v["spike"]
                v["g_u"] = [g + v["spike"] * a for g, a in zip(v["g_u"], forward)]
                inverse_ref[at] = inverse
                e_ref[at] = v["spike"]
                for f in range(3):
                    d_ref[f, at] = v["value"][f]
            if z < nz - 1:
                v["coupling"] = lz_ref[at] * open_after(cut_ref, at + 1)
                if z > 0:
                    v["ratio"] = v["coupling"] * inverse

    def block(b):
        v = states[b]
        k_ends = [all_ref[2, b * nz], all_ref[2, b * nz + nz - 1]]
        return [v["s_uu"], v["s_uv"], v["s_vv"]] + k_ends + v["g_u"] + v["g_v"]

    slabs, factors, rights, ends = join(block(0), block(1), open_after(cut_ref, nz))
    for q, slab in enumerate(slabs):
        own_ref[q] = slab
    for n, slab in enumerate(factors + rights + list(ends)):
        pair_ref[n] = slab
    if stages == 1:
        slabs, pair_ref[PAIR_COUNT - 1] = reduce_end(slabs, is_high(0))
    Message(len(slabs), 2, nx, ny).write(message_ref, slabs)


def join_kernel(stage, last, base, cut_ref, own_ref, message_ref, sibling_ref, factor_ref, next_ref, *joined):
    nx, ny = slab_size(own_ref)
    own = [own_ref[q] for q in range(FIRST_COUNT)]
    sibling = Message(FIRST_COUNT, 2, nx, ny).read(message_ref)
    for q, slab in enumerate(sibling):
        sibling_ref[q] = slab
    high = is_high(stage)
    slabs, factors, _, _ = join(
        choose(high, sibling, own),
        choose(high, own, sibling),
        open_after(cut_ref, base + 2 * stage),
    )
    for n, values in enumerate(factors):
        factor_ref[n] = values
    if last:
        slabs, factor_ref[6] = reduce_end(slabs, is_high(stage + 1))
    else:
        for q, slab in enumerate(slabs):
            joined[0][q] = slab
    Message(len(slabs), 2, nx, ny).write(next_ref, slabs)


def join_again_kernel(stage, last, own_ref, message_ref, factor_ref, sibling_ref, next_ref, *joined):
    nx, ny = slab_size(own_ref)
    own = [own_ref[q] for q in range(SECOND_COUNT)]
    sibling = Message(SECOND_COUNT, 1, nx, ny).read(message_ref)
    for q, slab in enumerate(sibling):
        sibling_ref[q] = slab
    above = is_high(stage)
    low, high = choose(above, sibling, own), choose(above, own, sibling)
    factors = [factor_ref[n] for n in range(6)]
    g_u, g_v, _ = join_right(factors, low[:3], low[3:], high[:3], high[3:])
    slabs = g_u + g_v
    if last:
        slabs = reduce_end_right(factor_ref[6], g_u, g_v, is_high(stage + 1))
    else:
        for q, slab in enumerate(slabs):
            joined[0][q] = slab
    Message(len(slabs), 1, nx, ny).write(next_ref, slabs)


def stencil(slab, link_x, link_y):
    return (
        link_x * moved(slab, -1, 0)
        + moved(link_x * slab, 1, 0)
        + (link_y * moved(slab, -1, 1) + moved(link_y * slab, 1, 1))
    )


def beyond_cuts(cut_ref, at, link_low, link_high):
    low, high = cut_ref[pl.ds(at, 1), :], cut_ref[pl.ds(at + 1, 1), :]
    return (
        link_low * jnp.concatenate([low, low], axis=1),
        link_high * jnp.concatenate([high, high], axis=1),
    )


def left_out(field_ref, f, at, link_x, link_y, cuts):
    return stencil(field_ref[f, at + 1], link_x, link_y) + (
        cuts[0] * field_ref[f, at] + cuts[1] * field_ref[f, at + 2]
    )


def middle_kernel(stages, cut_ref, *refs):
    own_ref, pair_ref, siblings, message_ref = refs[0], refs[1], refs[2 : stages + 1], refs[stages + 1]
    refs = refs[stages + 2 :]
    lx_ref, ly_ref, lz_ref, d_ref, e_ref, inverse_ref = refs[:6]
    next_ref, own2_ref, right_ref, d2_ref, factor_ref, end_ref, first_ref = refs[6:]
    layers = lx_ref.shape[0]
    nz = layers // 2
    nx, ny = slab_size(lx_ref)
    own = [own_ref[q] for q in range(FIRST_COUNT)]
    slots = []

    def keep(values):
        factor_ref[len(slots)] = values
        slots.append(None)

    def attach(state, sign, row, pivot, right, k):
        beside, k_beside, rights, exists = state[0], state[1], state[2:5], state[5]
        link, flow, tau = face(k_beside * exists, k)
        coupling = link * open_after(cut_ref, row)
        rights = rights[:2] + [rights[2] + sign * flow]
        inverse = 1.0 / (beside + tau)
        step = coupling * inverse
        right = [a + step * b for a, b in zip(right, rights)]
        right[2] = right[2] - sign * flow
        return pivot + tau - coupling * step, right, step, inverse, rights, (link, flow, tau)

    far = Message(LAST_COUNT, 2, nx, ny).read(message_ref)
    top = is_high(stages - 1)
    below, above = far + [flag(top)], far + [flag(jnp.logical_not(top))]
    for s in range(stages - 2, -1, -1):
        up = is_high(s)
        block = [siblings[s][q] for q in range(FIRST_COUNT)]
        sign = jnp.where(up, 1.0, -1.0)
        state = choose(up, below, above)
        far_s, far_k, near_s, near_k = choose(
            up, [block[0], block[3], block[2], block[4]], [block[2], block[4], block[0], block[3]]
        )
        far_g = choose(up, block[5:8], block[8:11])
        near_g = choose(up, block[8:11], block[5:8])
        row = layers + 2 + 2 * s
        pivot, right, step, _, _, _ = attach(state, sign, row, far_s, far_g, far_k)
        factor = block[1] / pivot
        keep(step)
        keep(factor)
        state = [near_s - block[1] * factor, near_k]
        state += [n - factor * r for n, r in zip(near_g, right)] + [jnp.float32(1.0)]
        below, above = choose(up, state, below), choose(up, above, state)

    pivot_u, right_u, step_b, inverse_b, rights_b, ends_b = attach(
        below, 1.0, 0, own[0], own[5:8], own[3]
    )
    pivot_v, right_v, step_a, inverse_a, rights_a, ends_a = attach(
        above, -1.0, layers, own[2], own[8:11], own[4]
    )
    held_b, held_a = inverse_b * below[5], inverse_a * above[5]
    inverse_u = 1.0 / pivot_u
    factor = own[1] * inverse_u
    inverse_v = 1.0 / (pivot_v - own[1] * factor)
    for values in (step_b, held_b, step_a, held_a, inverse_u, factor, inverse_v):
        keep(values)
    pair = [pair_ref[n] for n in range(PAIR_COUNT)]
    inner = pair[:6]
    ends = [ends_b[0], pair[12], ends_a[0]]
    for n, values in enumerate(ends):
        end_ref[n] = values

    for f in range(3):
        last = (right_v[f] - factor * right_u[f]) * inverse_v
        first_u = right_u[f] * inverse_u - factor * last
        low_v, high_u = join_inner(inner, pair[6 + f], pair[9 + f], first_u, last)
        first_ref[f, 0] = rights_b[f] * held_b + step_b * first_u
        first_ref[f, layers + 1] = rights_a[f] * held_a + step_a * last
        first_ref[f, 1] = first_u
        first_ref[f, nz] = low_v
        first_ref[f, nz + 1] = high_u
        first_ref[f, layers] = last
    for z in range(nz - 2, 0, -1):
        for at in (z, nz + z):
            ratio = lz_ref[at] * open_after(cut_ref, at + 1) * inverse_ref[at]
            spike = e_ref[at]
            for f in range(3):
                first_ref[f, at + 1] = (
                    d_ref[f, at]
                    + spike * first_ref[f, 1 + at - z]
                    + ratio * first_ref[f, at + 2]
                )

    def block(b):
        for z in range(nz):
            at = b * nz + z
            cuts = beyond_cuts(
                cut_ref, at,
                ends[b] if z == 0 else lz_ref[at - 1],
                ends[b + 1] if z == nz - 1 else lz_ref[at],
            )
            right = [left_out(first_ref, f, at, lx_ref[at], ly_ref[at], cuts) for f in range(3)]
            if z == 0:
                g_u = list(right)
            else:
                if z == 1:
                    forward = right
                else:
                    forward = [right[f] + coupling * value[f] for f in range(3)]
                if z < nz - 1:
                    inverse, spike = inverse_ref[at], e_ref[at]
                    value = [forward[f] * inverse for f in range(3)]
                    g_u = [g_u[f] + spike * forward[f] for f in range(3)]
                    for f in range(3):
                        d2_ref[f, at] = value[f]
                    coupling = lz_ref[at] * open_after(cut_ref, at + 1)
        return g_u, forward

    (low_u, low_v), (high_u, high_v) = block(0), block(1)
    g_u, g_v, middle = join_right(inner, low_u, low_v, high_u, high_v)
    for n, slab in enumerate(low_v + middle):
        right_ref[n] = slab
    for q, slab in enumerate(g_u + g_v):
        own2_ref[q] = slab
    slabs = g_u + g_v
    if stages == 1:
        slabs = reduce_end_right(pair[PAIR_COUNT - 1], g_u, g_v, is_high(0))
    Message(len(slabs), 1, nx, ny).write(next_ref, slabs)


def final_kernel(stages, cut_ref, *refs):
    own_ref, pair_ref, siblings, message_ref = refs[0], refs[1], refs[2 : stages + 1], refs[stages + 1]
    refs = refs[stages + 2 :]
    lx_ref, ly_ref, lz_ref, first_ref, right_ref, d2_ref, e_ref, inverse_ref = refs[:8]
    factor_ref, end_ref, pressure_out, residual_out = refs[8:12]
    change_ref, pressure_ref, residual_ref, sems = refs[12:]
    nz = lx_ref.shape[0] // 2
    nx, ny = slab_size(lx_ref)
    own = [own_ref[q] for q in range(SECOND_COUNT)]
    slots = []

    def kept():
        slots.append(None)
        return factor_ref[len(slots) - 1]

    below = above = Message(3, 1, nx, ny).read(message_ref)
    for s in range(stages - 2, -1, -1):
        up = is_high(s)
        block = [siblings[s][q] for q in range(SECOND_COUNT)]
        state = choose(up, below, above)
        far_g = choose(up, block[:3], block[3:])
        near_g = choose(up, block[3:], block[:3])
        step, factor = kept(), kept()
        right = [a + step * b for a, b in zip(far_g, state)]
        state = [n - factor * r for n, r in zip(near_g, right)]
        below, above = choose(up, state, below), choose(up, above, state)
    step_b, held_b, step_a, held_a = kept(), kept(), kept(), kept()
    inverse_u, factor, inverse_v = kept(), kept(), kept()
    inner = [pair_ref[n] for n in range(6)]
    start = own_start(nz)
    high = start > 0
    for f in range(3):
        right_u = own[f] + step_b * below[f]
        right_v = own[3 + f] + step_a * above[f]
        last = (right_v - factor * right_u) * inverse_v
        first = right_u * inverse_u - factor * last
        low_v, high_u = join_inner(inner, right_ref[f], right_ref[3 + f], first, last)
        beyond_b = below[f] * held_b + step_b * first
        beyond_a = above[f] * held_a + step_a * last
        values = choose(high, [low_v, high_u, last, beyond_a], [beyond_b, first, low_v, high_u])
        for at, slab in zip((0, 1, nz, nz + 1), values):
            change_ref[f, at] = slab
    ends = choose(high, [end_ref[1], end_ref[2]], [end_ref[0], end_ref[1]])
    for z in range(nz - 2, 0, -1):
        at = start + z
        opened = 1.0 - cut_ref[pl.ds(at + 1, 1), :]
        opened = jnp.concatenate([opened, opened], axis=1)
        ratio = lz_ref[at] * opened * inverse_ref[at]
        spike = e_ref[at]
        for f in range(3):
            change_ref[f, z + 1] = (
                d2_ref[f, at] + spike * change_ref[f, 1] + ratio * change_ref[f, z + 2]
            )
    own_part = (slice(0, nx), slice(0, ny))
    copies = []
    for z in range(nz):
        at = start + z
        cuts = beyond_cuts(
            cut_ref, at,
            ends[0] if z == 0 else lz_ref[at - 1],
            ends[1] if z == nz - 1 else lz_ref[at],
        )
        link_x, link_y = lx_ref[at], ly_ref[at]
        for f in range(3):
            pressure_ref[f, z] = (first_ref[f, at + 1] + change_ref[f, z + 1])[own_part]
            residual_ref[f, z] = left_out(change_ref, f, z, link_x, link_y, cuts)[own_part]
        if (z + 1) % CHUNK == 0:
            part = (slice(None), slice(z + 1 - CHUNK, z + 1))
            for n, (buffer, out) in enumerate(
                ((pressure_ref, pressure_out), (residual_ref, residual_out))
            ):
                copy = pltpu.make_async_copy(
                    buffer.at[part], out.at[part], sems.at[n, z // CHUNK]
                )
                copy.start()
                copies.append(copy)
    for copy in copies:
        copy.wait()


def kernel_call(kernel, outputs, operands, scratch=(), smem=0, cost=None, space=pltpu.VMEM):
    specs = [pl.BlockSpec(memory_space=pltpu.SMEM)] * smem
    specs += [pl.BlockSpec(memory_space=pltpu.VMEM)] * (len(operands) - smem)
    return pl.pallas_call(
        kernel,
        out_shape=[jax.ShapeDtypeStruct(s, t) for s, t in outputs],
        in_specs=specs,
        out_specs=[pl.BlockSpec(memory_space=space)] * len(outputs),
        scratch_shapes=list(scratch),
        compiler_params=pltpu.CompilerParams(vmem_limit_bytes=24 * 2**20),
        cost_estimate=cost,
    )(*operands)


def swapped(values, stage):
    size = lax.axis_size("gz")
    return lax.ppermute(values, "gz", [(i, i ^ 2**stage) for i in range(size)])


def ring(values, axis, distance):
    size = lax.axis_size(axis)
    return lax.ppermute(values, axis, [(i, (i + distance) % size) for i in range(size)])


def diagonal(values, x_distance, y_distance):
    nx, ny = lax.axis_size("gx"), lax.axis_size("gy")
    route = []
    for i in range(nx):
        for j in range(ny):
            target = ((i + x_distance) % nx) * ny + (j + y_distance) % ny
            route.append((i * ny + j, target))
    return lax.ppermute(values, ("gx", "gy"), route)


def per_device(facies, perm_table, line_breaks):
    nz, nx, ny = facies.shape
    stages = (lax.axis_size("gz") - 1).bit_length() - 1
    i32, f32 = jnp.int32, jnp.float32
    two = lax.axis_size("gx") == 2
    layers = 2 * nz
    cut_rows = -(-(layers + 1 + 2 * stages) // 8) * 8
    other = swapped(facies, 0)
    k, table, cuts = kernel_call(
        functools.partial(prepare_kernel, stages),
        [((3, nz, nx, ny), f32), ((3, 8, ny), f32), ((cut_rows, ny), f32)],
        [perm_table, line_breaks, facies],
        smem=2,
        cost=pl.CostEstimate(flops=10**7, bytes_accessed=10**6, transcendentals=0),
    )
    strip, *rows = kernel_call(
        pack_kernel,
        [((2 * nx, ny), i32)] + [((layers * 4, ny), i32)] * (1 if two else 2),
        [facies, other, table],
    )
    k, = kernel_call(
        prepare_other_kernel,
        [((3, layers, nx, ny), f32)],
        [table, k, other, strip],
        cost=pl.CostEstimate(flops=10**7, bytes_accessed=10**6, transcendentals=0),
    )
    y_low, y_high = ring(strip, "gy", 1), ring(strip, "gy", -1)
    if two:
        row_low = row_high = ring(rows[0], "gx", 1)
        low_low = low_high = diagonal(strip, 1, 1)
        high_low = high_high = diagonal(strip, 1, -1)
    else:
        row_low, row_high = ring(rows[1], "gx", 1), ring(rows[0], "gx", -1)
        low_low, low_high = diagonal(strip, 1, 1), diagonal(strip, -1, 1)
        high_low, high_high = diagonal(strip, 1, -1), diagonal(strip, -1, -1)

    slab = (nx + 8, 2 * ny)
    one, three = ((layers,) + slab, f32), ((3, layers) + slab, f32)

    def slabs(count):
        return ((count,) + slab, f32)

    def message_of(count, halo):
        return ((Message(count, halo, nx, ny).rows, ny), f32)

    message, own, pair, lx, ly, lz, d, e, inverse = kernel_call(
        functools.partial(eliminate_kernel, stages),
        [message_of(LAST_COUNT if stages == 1 else FIRST_COUNT, 2)]
        + [slabs(FIRST_COUNT), slabs(PAIR_COUNT)]
        + [one] * 3 + [three, one, one],
        [table, cuts, k, row_low, row_high, y_low, y_high,
         low_low, low_high, high_low, high_high],
        [pltpu.VMEM(s, f32) for s in (three[0], one[0], (2,) + one[0], one[0])]
        + [pltpu.VMEM((3, layers * 4, ny), f32)] * (1 if two else 2),
    )
    siblings, factors, group = [], [], own
    for s in range(stages - 1):
        last = s == stages - 2
        outputs = [slabs(FIRST_COUNT), slabs(7), message_of(LAST_COUNT if last else FIRST_COUNT, 2)]
        sibling, factor, message, *joined = kernel_call(
            functools.partial(join_kernel, s, last, layers + 1),
            outputs + ([] if last else [slabs(FIRST_COUNT)]),
            [cuts, group, swapped(message, s + 1)],
        )
        siblings.append(sibling)
        factors.append(factor)
        group = None if last else joined[0]
    fields = ((3, layers + 2) + slab, f32)
    message, own, rights, d2, kept, ends, first = kernel_call(
        functools.partial(middle_kernel, stages),
        [message_of(3 if stages == 1 else SECOND_COUNT, 1), slabs(SECOND_COUNT), slabs(6), three,
         slabs(2 * stages + 5), slabs(3), fields],
        [cuts, own, pair] + siblings + [swapped(message, stages)]
        + [lx, ly, lz, d, e, inverse],
    )
    siblings, group = [], own
    for s in range(stages - 1):
        last = s == stages - 2
        outputs = [slabs(SECOND_COUNT), message_of(3 if last else SECOND_COUNT, 1)]
        sibling, message, *joined = kernel_call(
            functools.partial(join_again_kernel, s, last),
            outputs + ([] if last else [slabs(SECOND_COUNT)]),
            [group, swapped(message, s + 1), factors[s]],
        )
        siblings.append(sibling)
        group = None if last else joined[0]
    out = ((3, nz, nx, ny), f32)
    pressure, residual = kernel_call(
        functools.partial(final_kernel, stages),
        [out, out],
        [cuts, own, pair] + siblings + [swapped(message, stages)]
        + [lx, ly, lz, first, rights, d2, e, inverse, kept, ends],
        [pltpu.VMEM((3, nz + 2) + slab, f32)]
        + [pltpu.VMEM((3, nz, nx, ny), f32)] * 2
        + [pltpu.SemaphoreType.DMA((2, nz // CHUNK))],
        space=pl.ANY,
    )
    return pressure, residual


def solution(mesh):
    return jax.shard_map(
        per_device,
        mesh=mesh,
        in_specs=(P("gz", "gx", "gy"), P(), P()),
        out_specs=(P(None, "gz", "gx", "gy"), P(None, "gz", "gx", "gy")),
        check_vma=False,
    )
```

```python
import functools

import jax
import jax.numpy as jnp
from jax import lax
from jax.experimental import pallas as pl
from jax.experimental.pallas import tpu as pltpu
from jax.sharding import PartitionSpec as P


WIDE = 3
FIRST_COUNT = 11
LAST_COUNT = 5
SECOND_COUNT = 6
PAIR_COUNT = 16
CHUNK = 4


def moved(values, amount, axis):
    size = values.shape[axis]
    amount = amount % size
    if amount == 0:
        return values
    return pltpu.roll(values, amount, axis)


def flag(condition):
    return condition.astype(jnp.float32)


def iotas(rows, lanes):
    return tuple(lax.broadcasted_iota(jnp.int32, (rows, lanes), d) for d in (0, 1))


def choose(condition, first, second):
    return [jnp.where(condition, a, b) for a, b in zip(first, second)]


def is_high(stage):
    return (lax.axis_index("gz") >> (stage + 1)) % 2 == 1


def own_start(nz):
    return (lax.axis_index("gz") % 2) * nz


def pack_kernel(facies_ref, copy_ref, rims_ref):
    nz, nx, ny = facies_ref.shape
    copy_ref[...] = facies_ref[...]
    lane = lax.broadcasted_iota(jnp.int32, (nx, ny), 1)
    row = iotas(8, ny)[0]
    strip = jnp.zeros((nx, ny), jnp.int32)
    for z in range(0, nz, 2):
        pair = [facies_ref[z], facies_ref[z + 1]]
        for at in (z, z + 1):
            strip = jnp.where(lane // 8 == at, moved(pair[at - z], 8 * at + WIDE, 1), strip)
        first = jnp.where(row < 4, pair[0][:8], moved(pair[1][:8], 4, 0))
        last = jnp.where(row < 4, moved(pair[0][nx - 8 :], 4, 0), pair[1][nx - 8 :])
        start = nx + 4 * z
        if rims_ref.shape[0] == nx + 4 * nz:
            rims_ref[start : start + 8, :] = jnp.where(lax.axis_index("gx") == 0, last, first)
        else:
            rims_ref[start : start + 8, :] = first
            rims_ref[start + 4 * nz : start + 4 * nz + 8, :] = last
    rims_ref[0:nx, :] = strip


def merge_kernel(facies_ref, own_ref, other_ref, table_ref, copy_ref, strip_ref, *row_refs):
    nz = facies_ref.shape[0]
    size, ny = own_ref.shape
    copy_ref[...] = facies_ref[...]
    nx = size - 4 * nz * len(row_refs)
    swap = own_start(nz) > 0
    for b in range(2):
        rims = jnp.where(swap == (b == 1), own_ref[...], other_ref[...])
        strip_ref[b * nx : (b + 1) * nx, :] = rims[:nx]
        for n, ref in enumerate(row_refs):
            start = nx + 4 * nz * n
            ref[4 * nz * b : 4 * nz * (b + 1), :] = rims[start : start + 4 * nz]


def lookup(table, index):
    rows = [
        jnp.take_along_axis(table, index[r : r + 8], axis=1) for r in range(0, index.shape[0], 8)
    ]
    return jnp.concatenate(rows, axis=0)


def prepare_kernel(stages, table, breaks, facies_ref, k_ref, table_ref, cut_ref):
    nz, nx, ny = facies_ref.shape
    lane = iotas(8, ny)[1]
    tables = []
    for q in range(3):
        values = jnp.zeros((8, ny), jnp.float32)
        for label in range(table.shape[1]):
            values = jnp.where(lane == label, table[q, label], values)
        table_ref[q] = values
        tables.append(values)
    for z in range(nz):
        for q in range(3):
            k_ref[q, z] = lookup(tables[q], facies_ref[z])
    pair = lax.axis_index("gz") // 2
    layers = [pair * 2 * nz + r - 1 for r in range(2 * nz + 1)]
    if stages == 1:
        high = is_high(0)
        layers = [
            pair * 2 * nz + jnp.where(high, 2 * nz - 1 - r, r - 1) for r in range(2 * nz + 1)
        ]
    for s in range(stages if stages > 1 else 0):
        base, size = (pair >> (s + 1)) << (s + 1), 2**s
        layers.append((base + size) * 2 * nz - 1)
        layers.append(jnp.where(is_high(s), base, base + 2 * size) * 2 * nz - 1)
    for r, layer in enumerate(layers):
        cut = breaks[jnp.clip(layer, 0, breaks.shape[0] - 1)].astype(jnp.float32)
        cut_ref[r : r + 1, :] = jnp.full((1, ny), cut, jnp.float32)


def prepare_other_kernel(table_ref, own_ref, other_ref, strip_ref, k_ref):
    nz = other_ref.shape[0]
    start = own_start(nz)
    for q in range(3):
        k_ref[q, pl.ds(start, nz)] = own_ref[q]
        for z in range(nz):
            k_ref[q, nz - start + z] = lookup(table_ref[q], other_ref[z])


def face(a, b):
    product = a * b
    total = a + b
    harmonic = 2.0 * product / total
    inside = product > 0.0
    link = jnp.where(inside, harmonic, 0.0)
    flow = jnp.where(inside, harmonic, total)
    tau = jnp.where(inside, harmonic, 2.0 * total)
    return link, flow, tau


class Message:
    def __init__(self, count, halo, nx, ny):
        self.count, self.halo, self.nx, self.ny = count, halo, nx, ny
        self.one_sided = lax.axis_size("gx") == 2
        self.rows_each = halo if self.one_sided else 2 * halo
        self.per_tile = 8 // self.rows_each
        self.tiles = -(-count // self.per_tile)
        self.abreast = ny // (2 * halo * count)
        strips = -(-(nx // 8 + 1) // self.abreast)
        self.sides = count * nx + 8 * strips
        self.rows = self.sides + 8 * self.tiles

    def strip(self, t, q):
        start = self.count * self.nx + 8 * (t // self.abreast)
        shift = 2 * self.halo * (self.count * (t % self.abreast) + q) + self.halo
        return slice(start, start + 8), shift

    def tile(self, q):
        start = self.sides + 8 * (q // self.per_tile)
        return slice(start, start + 8)

    def side_moved(self, tile, q, sign):
        part = q % self.per_tile
        if not self.one_sided:
            return moved(tile, sign * (self.rows_each * part + self.halo), 0)
        first = lax.axis_index("gx") == 0
        out = jnp.where(
            first,
            moved(tile, sign * self.halo * part, 0),
            moved(tile, sign * self.halo * (part + 1), 0),
        )
        if sign > 0:
            return out
        row = iotas(8, self.ny)[0]
        return jnp.where(jnp.where(first, row, 7 - row) < self.halo, out, 1.0)

    def write(self, ref, slabs):
        nx, ny, halo = self.nx, self.ny, self.halo
        row, lane = iotas(8, ny)
        strips = {}
        for t in range(nx // 8 + 1):
            for q, slab in enumerate(slabs):
                spot, shift = self.strip(t, q)
                turned = moved(slab[8 * t : 8 * t + 8, ny:], shift, 1)
                held = strips.get(spot.start, turned)
                strips[spot.start] = jnp.where(lane < shift - halo, held, turned)
        for start, strip in strips.items():
            ref[start : start + 8, :] = strip
        for q, slab in enumerate(slabs):
            ref[q * nx : (q + 1) * nx, :] = slab[:nx, :ny]
            turned = self.side_moved(slab[nx:, :ny], q, 1)
            part = q % self.per_tile
            tile = turned if part == 0 else jnp.where(row < self.rows_each * part, tile, turned)
            if part == self.per_tile - 1 or q == self.count - 1:
                ref[self.tile(q), :] = tile

    def read(self, ref):
        nx = self.nx
        slabs = []
        for q in range(self.count):
            side = self.side_moved(ref[self.tile(q), :], q, -1)
            body = jnp.concatenate([ref[q * nx : (q + 1) * nx, :], side], axis=0)
            beside = []
            for t in range(nx // 8 + 1):
                spot, shift = self.strip(t, q)
                beside.append(moved(ref[spot, :], -shift, 1))
            slabs.append(jnp.concatenate([body, jnp.concatenate(beside, axis=0)], axis=1))
        return slabs


def open_after(cut_ref, r):
    cut = 1.0 - cut_ref[r : r + 1, :]
    return jnp.concatenate([cut, cut], axis=1)


def slab_size(ref):
    return ref.shape[-2] - 8, ref.shape[-1] // 2


def join(low, high, opened):
    ends = link, flow, tau = face(low[4], high[3])
    coupling = link * opened
    inverse = 1.0 / (low[2] + tau)
    step = coupling * inverse
    last_inverse = 1.0 / (high[0] + tau - coupling * step)
    outer = low[1] * inverse
    weight = step * low[1]
    weight_low, weight_high = weight * last_inverse, high[1] * last_inverse
    right_low = low[8:10] + [low[10] + flow]
    right_high = high[5:7] + [high[7] - flow]
    s_uu = low[0] - outer * low[1] - weight * weight_low
    s_uv = -weight * weight_high
    s_vv = high[2] - high[1] * weight_high
    factors = [outer, step, weight_low, weight_high, inverse, last_inverse]
    g_u, g_v, middle = join_right(factors, low[5:8], right_low, right_high, high[8:11])
    return [s_uu, s_uv, s_vv, low[3], high[4]] + g_u + g_v, factors, right_low + middle, ends


def join_right(factors, low_u, low_v, high_u, high_v):
    outer, step, weight_low, weight_high = factors[:4]
    middle = [b + step * a for a, b in zip(low_v, high_u)]
    g_u = [g - outer * a - weight_low * m for g, a, m in zip(low_u, low_v, middle)]
    g_v = [g - weight_high * m for g, m in zip(high_v, middle)]
    return g_u, g_v, middle


def join_inner(factors, right_low, middle, first, last):
    outer, step, weight_low, weight_high, inverse, last_inverse = factors
    high = last_inverse * middle - weight_low * first - weight_high * last
    return inverse * right_low - outer * first + step * high, high


def reduce_end(slabs, top):
    s_uu, s_uv, s_vv, k_u, k_v = slabs[:5]
    far_s, near_s = choose(top, [s_vv, s_uu], [s_uu, s_vv])
    far_k, near_k = choose(top, [k_v, k_u], [k_u, k_v])
    sign = jnp.where(top, 1.0, -1.0)
    factor = s_uv / (far_s + 2.0 * far_k)
    g_u, g_v = slabs[5:8], slabs[8:11]
    far_g, near_g = choose(top, g_v, g_u), choose(top, g_u, g_v)
    far_g[2] = far_g[2] + far_k * sign
    return [near_s - s_uv * factor, near_k] + [n - factor * g for n, g in zip(near_g, far_g)], factor


def reduce_end_right(factor, g_u, g_v, top):
    far_g, near_g = choose(top, g_v, g_u), choose(top, g_u, g_v)
    return [n - factor * g for n, g in zip(near_g, far_g)]


def assemble_slabs(k_ref, tables, rims, low_ref, high_ref, store):
    row_low, row_high, y_low, y_high, low_low, low_high, high_low, high_high = rims
    layers, nx, ny = k_ref.shape[1:]
    nz = layers // 2
    at_x, at_y = lax.axis_index("gx"), lax.axis_index("gy")
    has_x_low, has_x_high = at_x > 0, at_x < lax.axis_size("gx") - 1
    has_y_low, has_y_high = at_y > 0, at_y < lax.axis_size("gy") - 1

    row, lane = iotas(nx + 8, 2 * ny)
    x_in = (row < nx) | ((row < nx + WIDE) & has_x_high) | ((row >= nx + 8 - WIDE) & has_x_low)
    y_in = (lane < ny) | ((lane < ny + WIDE) & has_y_high)
    y_in = y_in | ((lane >= 2 * ny - WIDE) & has_y_low)
    cell = x_in & y_in
    valid = flag(cell)
    in_x, in_xp = valid * moved(valid, -1, 0), valid * moved(valid, 1, 0)
    in_y, in_yp = valid * moved(valid, -1, 1), valid * moved(valid, 1, 1)
    row_in, strip_in = cell[nx:, :ny], cell[:, ny:]

    row = iotas(8, ny)[0]
    lane = iotas(nx + 8, ny)[1]
    strips = []
    for b in range(2):
        part = slice(b * nx, (b + 1) * nx)

        def whole(own, high, low):
            side = jnp.where(row < WIDE, high[part, :][0:8], low[part, :][nx - 8 :])
            return jnp.concatenate([own[part, :], side], axis=0)

        before, after = whole(y_low, low_high, low_low), whole(y_high, high_high, high_low)
        strip = jnp.where(lane % 8 < WIDE, before, after)
        strips.append([lookup(table, strip) for table in tables])
    for q in range(3):
        low_ref[q] = lookup(tables[q], row_low[...])
        if high_ref is not low_ref:
            high_ref[q] = lookup(tables[q], row_high[...])

    for b in range(2):
        for z in range(nz):
            at = b * nz + z
            start = at // 2 * 8
            for q in range(3):
                low, high = low_ref[q, start : start + 8, :], high_ref[q, start : start + 8, :]
                if z % 2 == 0:
                    low = moved(low, 4, 0)
                else:
                    high = moved(high, 4, 0)
                side = jnp.where(row_in, jnp.where(row < 4, high, low), 0.0)
                beside = jnp.where(strip_in, moved(strips[b][q], -(8 * z + WIDE), 1), 0.0)
                body = jnp.concatenate([k_ref[q, at], side], axis=0)
                store(q, at, jnp.concatenate([body, beside], axis=1))

    return cell, in_x, in_xp, in_y, in_yp


def flow_after(here, there, inside):
    total = here + there
    return jnp.where(inside > 0.0, 2.0 * (here * there) / total, total)


def tau_and_source(flow, back, inside, inside_back):
    return flow * (2.0 - inside) + back * (2.0 - inside_back), flow - back


def eliminate_kernel(
    stages, table_ref, cut_ref, k_ref, row_low, row_high, y_low, y_high,
    low_low, low_high, high_low, high_high,
    message_ref, own_ref, pair_ref, lx_ref, ly_ref, lz_ref, d_ref, e_ref, inverse_ref,
    all_ref, flow_ref, source_ref, centre_ref, low_ref, high_ref=None,
):
    layers, nx, ny = k_ref.shape[1:]
    nz = layers // 2
    rims = row_low, row_high, y_low, y_high, low_low, low_high, high_low, high_high

    def store(q, at, slab):
        all_ref[q, at] = slab

    cell, in_x, in_xp, in_y, in_yp = assemble_slabs(
        k_ref, [table_ref[q] for q in range(3)], rims, low_ref,
        low_ref if high_ref is None else high_ref, store,
    )
    for at in range(layers):
        kx, ky = all_ref[0, at], all_ref[1, at]
        flow_x = flow_after(kx, moved(kx, -1, 0), in_x)
        flow_ref[at] = flow_after(ky, moved(ky, -1, 1), in_y)
        lx_ref[at] = flow_x * in_x
        centre_ref[at], source_ref[0, at] = tau_and_source(
            flow_x, moved(flow_x, 1, 0), in_x, in_xp
        )
        if at % nz < nz - 1:
            kz, above = all_ref[2, at], all_ref[2, at + 1]
            lz_ref[at] = jnp.where(cell, 2.0 * (kz * above) / (kz + above), 0.0)
    for at in range(layers):
        flow_y = flow_ref[at]
        ly_ref[at] = flow_y * in_y
        tau_y, source_ref[1, at] = tau_and_source(
            flow_y, moved(flow_y, 1, 1), in_y, in_yp
        )
        centre = centre_ref[at] + tau_y
        if at % nz > 0:
            centre = centre + lz_ref[at - 1]
        if at % nz < nz - 1:
            centre = centre + lz_ref[at]
        centre_ref[at] = jnp.where(cell, centre, 1.0)

    states = [{}, {}]
    for z in range(nz):
        for b in range(2):
            at, v = b * nz + z, states[b]
            centre = centre_ref[at]
            sources = [source_ref[0, at], source_ref[1, at]]
            if z == 0:
                v["source"] = sources + [lz_ref[at]]
                v["s_uu"], v["g_u"] = centre, v["source"]
            elif z == nz - 1:
                sources = sources + [-lz_ref[at - 1]]
                v["s_vv"] = centre - v["coupling"] * v["ratio"]
                v["s_uv"] = -v["coupling"] * v["spike"]
                v["g_v"] = [a + v["coupling"] * d for a, d in zip(sources, v["value"])]
            else:
                forward = sources + [lz_ref[at] - lz_ref[at - 1]]
                if z == 1:
                    pivot, numerator = centre, v["coupling"]
                else:
                    pivot = centre - v["coupling"] * v["ratio"]
                    forward = [a + v["coupling"] * d for a, d in zip(forward, v["value"])]
                    numerator = v["coupling"] * v["spike"]
                inverse = 1.0 / pivot
                v["value"] = [a * inverse for a in forward]
                v["spike"] = numerator * inverse
                v["s_uu"] = v["s_uu"] - numerator * v["spike"]
                v["g_u"] = [g + v["spike"] * a for g, a in zip(v["g_u"], forward)]
                inverse_ref[at] = inverse
                e_ref[at] = v["spike"]
                for f in range(3):
                    d_ref[f, at] = v["value"][f]
            if z < nz - 1:
                v["coupling"] = lz_ref[at] * open_after(cut_ref, at + 1)
                if z > 0:
                    v["ratio"] = v["coupling"] * inverse

    def block(b):
        v = states[b]
        k_ends = [all_ref[2, b * nz], all_ref[2, b * nz + nz - 1]]
        return [v["s_uu"], v["s_uv"], v["s_vv"]] + k_ends + v["g_u"] + v["g_v"]

    slabs, factors, rights, ends = join(block(0), block(1), open_after(cut_ref, nz))
    for q, slab in enumerate(slabs):
        own_ref[q] = slab
    for n, slab in enumerate(factors + rights + list(ends)):
        pair_ref[n] = slab
    if stages == 1:
        slabs, pair_ref[PAIR_COUNT - 1] = reduce_end(slabs, is_high(0))
    Message(len(slabs), 2, nx, ny).write(message_ref, slabs)


def join_kernel(stage, last, base, cut_ref, own_ref, message_ref, sibling_ref, factor_ref, next_ref, *joined):
    nx, ny = slab_size(own_ref)
    own = [own_ref[q] for q in range(FIRST_COUNT)]
    sibling = Message(FIRST_COUNT, 2, nx, ny).read(message_ref)
    for q, slab in enumerate(sibling):
        sibling_ref[q] = slab
    high = is_high(stage)
    slabs, factors, _, _ = join(
        choose(high, sibling, own),
        choose(high, own, sibling),
        open_after(cut_ref, base + 2 * stage),
    )
    for n, values in enumerate(factors):
        factor_ref[n] = values
    if last:
        slabs, factor_ref[6] = reduce_end(slabs, is_high(stage + 1))
    else:
        for q, slab in enumerate(slabs):
            joined[0][q] = slab
    Message(len(slabs), 2, nx, ny).write(next_ref, slabs)


def join_again_kernel(stage, last, own_ref, message_ref, factor_ref, sibling_ref, next_ref, *joined):
    nx, ny = slab_size(own_ref)
    own = [own_ref[q] for q in range(SECOND_COUNT)]
    sibling = Message(SECOND_COUNT, 1, nx, ny).read(message_ref)
    for q, slab in enumerate(sibling):
        sibling_ref[q] = slab
    above = is_high(stage)
    low, high = choose(above, sibling, own), choose(above, own, sibling)
    factors = [factor_ref[n] for n in range(6)]
    g_u, g_v, _ = join_right(factors, low[:3], low[3:], high[:3], high[3:])
    slabs = g_u + g_v
    if last:
        slabs = reduce_end_right(factor_ref[6], g_u, g_v, is_high(stage + 1))
    else:
        for q, slab in enumerate(slabs):
            joined[0][q] = slab
    Message(len(slabs), 1, nx, ny).write(next_ref, slabs)


def stencil(slab, link_x, link_y):
    return (
        link_x * moved(slab, -1, 0)
        + moved(link_x * slab, 1, 0)
        + (link_y * moved(slab, -1, 1) + moved(link_y * slab, 1, 1))
    )


def beyond_cuts(cut_ref, at, link_low, link_high):
    low, high = cut_ref[pl.ds(at, 1), :], cut_ref[pl.ds(at + 1, 1), :]
    return (
        link_low * jnp.concatenate([low, low], axis=1),
        link_high * jnp.concatenate([high, high], axis=1),
    )


def left_out(field_ref, f, at, link_x, link_y, cuts):
    return stencil(field_ref[f, at + 1], link_x, link_y) + (
        cuts[0] * field_ref[f, at] + cuts[1] * field_ref[f, at + 2]
    )


def middle_kernel(stages, cut_ref, *refs):
    own_ref, pair_ref, siblings, message_ref = refs[0], refs[1], refs[2 : stages + 1], refs[stages + 1]
    refs = refs[stages + 2 :]
    lx_ref, ly_ref, lz_ref, d_ref, e_ref, inverse_ref = refs[:6]
    next_ref, own2_ref, right_ref, d2_ref, factor_ref, end_ref, first_ref = refs[6:]
    layers = lx_ref.shape[0]
    nz = layers // 2
    nx, ny = slab_size(lx_ref)
    own = [own_ref[q] for q in range(FIRST_COUNT)]
    slots = []

    def keep(values):
        factor_ref[len(slots)] = values
        slots.append(None)

    def attach(state, sign, row, pivot, right, k):
        beside, k_beside, rights, exists = state[0], state[1], state[2:5], state[5]
        link, flow, tau = face(k_beside * exists, k)
        coupling = link * open_after(cut_ref, row)
        rights = rights[:2] + [rights[2] + sign * flow]
        inverse = 1.0 / (beside + tau)
        step = coupling * inverse
        right = [a + step * b for a, b in zip(right, rights)]
        right[2] = right[2] - sign * flow
        return pivot + tau - coupling * step, right, step, inverse, rights, (link, flow, tau)

    far = Message(LAST_COUNT, 2, nx, ny).read(message_ref)
    top = is_high(stages - 1)
    below, above = far + [flag(top)], far + [flag(jnp.logical_not(top))]
    for s in range(stages - 2, -1, -1):
        up = is_high(s)
        block = [siblings[s][q] for q in range(FIRST_COUNT)]
        sign = jnp.where(up, 1.0, -1.0)
        state = choose(up, below, above)
        far_s, far_k, near_s, near_k = choose(
            up, [block[0], block[3], block[2], block[4]], [block[2], block[4], block[0], block[3]]
        )
        far_g = choose(up, block[5:8], block[8:11])
        near_g = choose(up, block[8:11], block[5:8])
        row = layers + 2 + 2 * s
        pivot, right, step, _, _, _ = attach(state, sign, row, far_s, far_g, far_k)
        factor = block[1] / pivot
        keep(step)
        keep(factor)
        state = [near_s - block[1] * factor, near_k]
        state += [n - factor * r for n, r in zip(near_g, right)] + [jnp.float32(1.0)]
        below, above = choose(up, state, below), choose(up, above, state)

    pivot_u, right_u, step_b, inverse_b, rights_b, ends_b = attach(
        below, 1.0, 0, own[0], own[5:8], own[3]
    )
    pivot_v, right_v, step_a, inverse_a, rights_a, ends_a = attach(
        above, -1.0, layers, own[2], own[8:11], own[4]
    )
    held_b, held_a = inverse_b * below[5], inverse_a * above[5]
    inverse_u = 1.0 / pivot_u
    factor = own[1] * inverse_u
    inverse_v = 1.0 / (pivot_v - own[1] * factor)
    for values in (step_b, held_b, step_a, held_a, inverse_u, factor, inverse_v):
        keep(values)
    pair = [pair_ref[n] for n in range(PAIR_COUNT)]
    inner = pair[:6]
    ends = [ends_b[0], pair[12], ends_a[0]]
    for n, values in enumerate(ends):
        end_ref[n] = values

    for f in range(3):
        last = (right_v[f] - factor * right_u[f]) * inverse_v
        first_u = right_u[f] * inverse_u - factor * last
        low_v, high_u = join_inner(inner, pair[6 + f], pair[9 + f], first_u, last)
        first_ref[f, 0] = rights_b[f] * held_b + step_b * first_u
        first_ref[f, layers + 1] = rights_a[f] * held_a + step_a * last
        first_ref[f, 1] = first_u
        first_ref[f, nz] = low_v
        first_ref[f, nz + 1] = high_u
        first_ref[f, layers] = last
    for z in range(nz - 2, 0, -1):
        for at in (z, nz + z):
            ratio = lz_ref[at] * open_after(cut_ref, at + 1) * inverse_ref[at]
            spike = e_ref[at]
            for f in range(3):
                first_ref[f, at + 1] = (
                    d_ref[f, at]
                    + spike * first_ref[f, 1 + at - z]
                    + ratio * first_ref[f, at + 2]
                )

    def block(b):
        for z in range(nz):
            at = b * nz + z
            cuts = beyond_cuts(
                cut_ref, at,
                ends[b] if z == 0 else lz_ref[at - 1],
                ends[b + 1] if z == nz - 1 else lz_ref[at],
            )
            right = [left_out(first_ref, f, at, lx_ref[at], ly_ref[at], cuts) for f in range(3)]
            if z == 0:
                g_u = list(right)
            else:
                if z == 1:
                    forward = right
                else:
                    forward = [right[f] + coupling * value[f] for f in range(3)]
                if z < nz - 1:
                    inverse, spike = inverse_ref[at], e_ref[at]
                    value = [forward[f] * inverse for f in range(3)]
                    g_u = [g_u[f] + spike * forward[f] for f in range(3)]
                    for f in range(3):
                        d2_ref[f, at] = value[f]
                    coupling = lz_ref[at] * open_after(cut_ref, at + 1)
        return g_u, forward

    (low_u, low_v), (high_u, high_v) = block(0), block(1)
    g_u, g_v, middle = join_right(inner, low_u, low_v, high_u, high_v)
    for n, slab in enumerate(low_v + middle):
        right_ref[n] = slab
    for q, slab in enumerate(g_u + g_v):
        own2_ref[q] = slab
    slabs = g_u + g_v
    if stages == 1:
        slabs = reduce_end_right(pair[PAIR_COUNT - 1], g_u, g_v, is_high(0))
    Message(len(slabs), 1, nx, ny).write(next_ref, slabs)


def final_kernel(stages, cut_ref, *refs):
    own_ref, pair_ref, siblings, message_ref = refs[0], refs[1], refs[2 : stages + 1], refs[stages + 1]
    refs = refs[stages + 2 :]
    lx_ref, ly_ref, lz_ref, first_ref, right_ref, d2_ref, e_ref, inverse_ref = refs[:8]
    factor_ref, end_ref, pressure_out, residual_out = refs[8:12]
    change_ref, pressure_ref, residual_ref, sems = refs[12:]
    nz = lx_ref.shape[0] // 2
    nx, ny = slab_size(lx_ref)
    own = [own_ref[q] for q in range(SECOND_COUNT)]
    slots = []

    def kept():
        slots.append(None)
        return factor_ref[len(slots) - 1]

    below = above = Message(3, 1, nx, ny).read(message_ref)
    for s in range(stages - 2, -1, -1):
        up = is_high(s)
        block = [siblings[s][q] for q in range(SECOND_COUNT)]
        state = choose(up, below, above)
        far_g = choose(up, block[:3], block[3:])
        near_g = choose(up, block[3:], block[:3])
        step, factor = kept(), kept()
        right = [a + step * b for a, b in zip(far_g, state)]
        state = [n - factor * r for n, r in zip(near_g, right)]
        below, above = choose(up, state, below), choose(up, above, state)
    step_b, held_b, step_a, held_a = kept(), kept(), kept(), kept()
    inverse_u, factor, inverse_v = kept(), kept(), kept()
    inner = [pair_ref[n] for n in range(6)]
    start = own_start(nz)
    high = start > 0
    for f in range(3):
        right_u = own[f] + step_b * below[f]
        right_v = own[3 + f] + step_a * above[f]
        last = (right_v - factor * right_u) * inverse_v
        first = right_u * inverse_u - factor * last
        low_v, high_u = join_inner(inner, right_ref[f], right_ref[3 + f], first, last)
        beyond_b = below[f] * held_b + step_b * first
        beyond_a = above[f] * held_a + step_a * last
        values = choose(high, [low_v, high_u, last, beyond_a], [beyond_b, first, low_v, high_u])
        for at, slab in zip((0, 1, nz, nz + 1), values):
            change_ref[f, at] = slab
    ends = choose(high, [end_ref[1], end_ref[2]], [end_ref[0], end_ref[1]])
    for z in range(nz - 2, 0, -1):
        at = start + z
        opened = 1.0 - cut_ref[pl.ds(at + 1, 1), :]
        opened = jnp.concatenate([opened, opened], axis=1)
        ratio = lz_ref[at] * opened * inverse_ref[at]
        spike = e_ref[at]
        for f in range(3):
            change_ref[f, z + 1] = (
                d2_ref[f, at] + spike * change_ref[f, 1] + ratio * change_ref[f, z + 2]
            )
    own_part = (slice(0, nx), slice(0, ny))
    copies = []
    for z in range(nz):
        at = start + z
        cuts = beyond_cuts(
            cut_ref, at,
            ends[0] if z == 0 else lz_ref[at - 1],
            ends[1] if z == nz - 1 else lz_ref[at],
        )
        link_x, link_y = lx_ref[at], ly_ref[at]
        for f in range(3):
            pressure_ref[f, z] = (first_ref[f, at + 1] + change_ref[f, z + 1])[own_part]
            residual_ref[f, z] = left_out(change_ref, f, z, link_x, link_y, cuts)[own_part]
        if (z + 1) % CHUNK == 0:
            part = (slice(None), slice(z + 1 - CHUNK, z + 1))
            for n, (buffer, out) in enumerate(
                ((pressure_ref, pressure_out), (residual_ref, residual_out))
            ):
                copy = pltpu.make_async_copy(
                    buffer.at[part], out.at[part], sems.at[n, z // CHUNK]
                )
                copy.start()
                copies.append(copy)
    for copy in copies:
        copy.wait()


def put(ref, index, slab):
    rows, ny = slab.shape[0], slab.shape[1] // 2
    for h in range(2):
        half = slab[:, h * ny : (h + 1) * ny]
        ref[index + (h, slice(8, 8 + rows))] = half
        ref[index + (h, slice(0, 8))] = half[rows - 8 :]
        ref[index + (h, slice(8 + rows, 16 + rows))] = half[:8]


def get(ref, index, shift=0):
    rows = ref.shape[-2] - 16
    halves = [ref[index + (h, slice(8 + shift, 8 + shift + rows))] for h in range(2)]
    return jnp.concatenate(halves, axis=1)


def signed():
    return jnp.where(is_high(0), -1.0, 1.0)


def both_halves(ref, r):
    values = ref[pl.ds(r, 1), :]
    return jnp.concatenate([values, values], axis=1)


def beside_sum(field_ref, index, lx_ref, ly_ref, j):
    here, link_y = get(field_ref, index), ly_ref[j]
    return (
        get(lx_ref, (j,)) * get(field_ref, index, 1)
        + get(lx_ref, (j,), -1) * get(field_ref, index, -1)
        + (link_y * moved(here, -1, 1) + moved(link_y * here, 1, 1))
    )


def end_eliminate_kernel(
    table_ref, cut_ref, k_ref, row_low, row_high, y_low, y_high,
    low_low, low_high, high_low, high_high,
    message_ref, own_ref, lx_ref, ly_ref, lz_ref, d_ref, ratio_ref, inverse_ref,
    kx_ref, fx_ref, ky_ref, kz_ref, source_ref, centre_ref, low_ref, high_ref=None,
):
    layers, nx, ny = k_ref.shape[1:]
    rims = row_low, row_high, y_low, y_high, low_low, low_high, high_low, high_high
    high, sign = is_high(0), signed()

    def store(q, at, slab):
        j = jnp.where(high, layers - 1 - at, at)
        if q == 0:
            put(kx_ref, (j,), slab)
        else:
            (ky_ref, kz_ref)[q - 1][j] = slab

    cell, in_x, in_xp, in_y, in_yp = assemble_slabs(
        k_ref, [table_ref[q] for q in range(3)], rims, low_ref,
        low_ref if high_ref is None else high_ref, store,
    )
    zero = jnp.zeros((nx + 8, 2 * ny), jnp.float32)
    lz_ref[0] = zero
    lz_ref[layers] = zero
    for j in range(layers):
        flow_x = flow_after(get(kx_ref, (j,)), get(kx_ref, (j,), 1), in_x)
        put(fx_ref, (j,), flow_x)
        put(lx_ref, (j,), flow_x * in_x)
        ky = ky_ref[j]
        ky_ref[j] = flow_after(ky, moved(ky, -1, 1), in_y)
        if j < layers - 1:
            kz, above = kz_ref[j], kz_ref[j + 1]
            lz_ref[j + 1] = jnp.where(cell, 2.0 * (kz * above) / (kz + above), 0.0)
    for j in range(layers):
        flow_y = ky_ref[j]
        ly_ref[j] = flow_y * in_y
        tau_x, source_ref[0, j] = tau_and_source(
            get(fx_ref, (j,)), get(fx_ref, (j,), -1), in_x, in_xp
        )
        tau_y, source_ref[1, j] = tau_and_source(flow_y, moved(flow_y, 1, 1), in_y, in_yp)
        centre = tau_x + tau_y + (2.0 * kz_ref[0] if j == 0 else lz_ref[j])
        if j < layers - 1:
            centre = centre + lz_ref[j + 1]
        centre_ref[j] = jnp.where(cell, centre, 1.0)
    for j in range(layers):
        flow_z = -kz_ref[0] if j == 0 else -lz_ref[j]
        if j < layers - 1:
            flow_z = flow_z + lz_ref[j + 1]
        forward = [source_ref[0, j], source_ref[1, j], sign * flow_z]
        pivot = centre_ref[j]
        if j > 0:
            pivot = pivot - coupling * ratio
            forward = [a + coupling * d for a, d in zip(forward, value)]
        if j < layers - 1:
            inverse = 1.0 / pivot
            coupling = lz_ref[j + 1] * (1.0 - both_halves(cut_ref, j + 1))
            ratio = coupling * inverse
            value = [a * inverse for a in forward]
            inverse_ref[j] = inverse
            ratio_ref[j] = ratio
            for f in range(3):
                d_ref[f, j] = value[f]
    slabs = [pivot, kz_ref[layers - 1]] + forward
    for q, slab in enumerate(slabs):
        own_ref[q] = slab
    Message(LAST_COUNT, 2, nx, ny).write(message_ref, slabs)


def expand_kernel(
    cut_ref, lx_ref, ly_ref, lz_ref, d_ref, ratio_ref, base_ref, phi_ref, part_ref
):
    layers = ly_ref.shape[0]
    zero = jnp.zeros(ly_ref.shape[1:], jnp.float32)
    phi, base = zero + 1.0, [zero] * 3
    put(phi_ref, (layers - 1,), phi)
    for f in range(3):
        put(base_ref, (f, layers - 1), zero)
    for j in range(layers - 2, -1, -1):
        ratio = ratio_ref[j]
        phi = ratio * phi
        put(phi_ref, (j,), phi)
        for f in range(3):
            base[f] = d_ref[f, j] + ratio * base[f]
            put(base_ref, (f, j), base[f])
    along_x = along_y = along_z = zero
    parts = [zero] * 3
    for j in range(layers):
        phi = get(phi_ref, (j,))
        along_x = along_x + (get(lx_ref, (j,)) * phi) * get(phi_ref, (j,), 1)
        along_y = along_y + (ly_ref[j] * phi) * moved(phi, -1, 1)
        cut_low = lz_ref[j] * both_halves(cut_ref, j)
        if j < layers - 1:
            cut_high = lz_ref[j + 1] * both_halves(cut_ref, j + 1)
            along_z = along_z + (cut_high * phi) * get(phi_ref, (j + 1,))
        for f in range(3):
            right = beside_sum(base_ref, (f, j), lx_ref, ly_ref, j)
            if j > 0:
                right = right + cut_low * get(base_ref, (f, j - 1))
            if j < layers - 1:
                right = right + cut_high * get(base_ref, (f, j + 1))
            parts[f] = parts[f] + phi * right
    for n, slab in enumerate(parts + [along_x, along_y, 2.0 * along_z]):
        part_ref[n] = slab


def end_join_kernel(layers, cut_ref, own_ref, message_ref, part_ref, next_ref, near_ref):
    nx, ny = slab_size(own_ref)
    own = [own_ref[q] for q in range(LAST_COUNT)]
    other = Message(LAST_COUNT, 2, nx, ny).read(message_ref)
    sign = signed()
    cut = both_halves(cut_ref, layers)
    link, flow, tau = face(own[1], other[1])
    coupling = link * (1.0 - cut)
    inverse_other = 1.0 / (other[0] + tau)
    step = coupling * inverse_other
    inverse = 1.0 / (own[0] + tau - coupling * step)
    right_own = own[2:4] + [own[4] + sign * flow]
    right_other = other[2:4] + [other[4] - sign * flow]
    cut_near = link * cut
    along_x, along_y, along_z = [part_ref[3 + n] for n in range(3)]
    slabs = []
    for f in range(3):
        near = (right_own[f] + step * right_other[f]) * inverse
        beyond = right_other[f] * inverse_other + step * near
        near_ref[f], near_ref[3 + f] = near, beyond
        right = part_ref[f] + stencil(near, along_x, along_y)
        slabs.append(right + (along_z * near + cut_near * beyond))
        near_ref[6 + f] = slabs[f]
    near_ref[9], near_ref[10], near_ref[11], near_ref[12] = step, inverse, inverse_other, link
    Message(3, 1, nx, ny).write(next_ref, slabs)


def correct_kernel(
    cut_ref, near_ref, lx_ref, ly_ref, lz_ref, ratio_ref, inverse_ref, base_ref, phi_ref,
    first_ref, change_ref, d_ref,
):
    layers = ly_ref.shape[0]
    for j in range(layers):
        phi = get(phi_ref, (j,))
        for f in range(3):
            put(first_ref, (f, j), get(base_ref, (f, j)) + phi * near_ref[f])
    for j in range(layers - 1):
        cut_low = lz_ref[j] * both_halves(cut_ref, j)
        cut_high = lz_ref[j + 1] * both_halves(cut_ref, j + 1)
        inverse = inverse_ref[j]
        if j > 0:
            coupling = lz_ref[j] * (1.0 - both_halves(cut_ref, j))
        for f in range(3):
            right = beside_sum(first_ref, (f, j), lx_ref, ly_ref, j)
            right = right + cut_high * get(first_ref, (f, j + 1))
            if j > 0:
                right = right + cut_low * get(first_ref, (f, j - 1)) + coupling * d_ref[f, j - 1]
            d_ref[f, j] = right * inverse
    change = [jnp.zeros(ly_ref.shape[1:], jnp.float32)] * 3
    for f in range(3):
        change_ref[f, layers - 1] = change[f]
    for j in range(layers - 2, -1, -1):
        ratio = ratio_ref[j]
        for f in range(3):
            change[f] = d_ref[f, j] + ratio * change[f]
            change_ref[f, j] = change[f]


def end_final_kernel(
    cut_ref, message_ref, near_ref, lx_ref, ly_ref, lz_ref, phi_ref, first_ref, base_ref,
    pressure_out, residual_out, change_ref, pressure_ref, residual_ref, sems,
):
    layers = ly_ref.shape[0]
    nz = layers // 2
    nx, ny = slab_size(ly_ref)
    high = is_high(0)
    start = jnp.where(high, nz - own_start(nz), own_start(nz))
    beside_other = start > 0
    other = Message(3, 1, nx, ny).read(message_ref)
    step, inverse, inverse_other, link_near = [near_ref[9 + n] for n in range(4)]
    near = [(near_ref[6 + f] + step * other[f]) * inverse for f in range(3)]
    for i in range(-1, nz + 1):
        j = jnp.clip(start + i, 0, layers - 1)
        phi = get(phi_ref, (j,))
        for f in range(3):
            change = base_ref[f, j] + phi * near[f]
            if i == -1:
                change = jnp.where(beside_other, change, 0.0)
            if i == nz:
                beyond = other[f] * inverse_other + step * near[f]
                change = jnp.where(beside_other, beyond, change)
            put(change_ref, (f, i + 1), change)
    own_part = (slice(0, nx), slice(0, ny))
    copies = []
    for i in range(nz):
        j = start + i
        z = jnp.where(high, nz - 1 - i, i)
        link_high = lz_ref[j + 1]
        if i == nz - 1:
            link_high = jnp.where(beside_other, link_near, link_high)
        cut_low = lz_ref[j] * both_halves(cut_ref, j)
        cut_high = link_high * both_halves(cut_ref, j + 1)
        for f in range(3):
            left_out = beside_sum(change_ref, (f, i + 1), lx_ref, ly_ref, j) + (
                cut_low * get(change_ref, (f, i)) + cut_high * get(change_ref, (f, i + 2))
            )
            pressure = get(first_ref, (f, j)) + get(change_ref, (f, i + 1))
            pressure_ref[f, z] = pressure[own_part]
            residual_ref[f, z] = left_out[own_part]
        if (i + 1) % CHUNK == 0:
            part = (slice(None), pl.ds(jnp.where(high, nz - 1 - i, i + 1 - CHUNK), CHUNK))
            for n, (buffer, out) in enumerate(
                ((pressure_ref, pressure_out), (residual_ref, residual_out))
            ):
                copy = pltpu.make_async_copy(
                    buffer.at[part], out.at[part], sems.at[n, i // CHUNK]
                )
                copy.start()
                copies.append(copy)
    for copy in copies:
        copy.wait()


def kernel_call(kernel, outputs, operands, scratch=(), smem=0, cost=None, space=pltpu.VMEM):
    specs = [pl.BlockSpec(memory_space=pltpu.SMEM)] * smem
    specs += [pl.BlockSpec(memory_space=pltpu.VMEM)] * (len(operands) - smem)
    return pl.pallas_call(
        kernel,
        out_shape=[jax.ShapeDtypeStruct(s, t) for s, t in outputs],
        in_specs=specs,
        out_specs=[pl.BlockSpec(memory_space=space)] * len(outputs),
        scratch_shapes=list(scratch),
        compiler_params=pltpu.CompilerParams(vmem_limit_bytes=32 * 2**20),
        cost_estimate=cost,
    )(*operands)


def swapped(values, stage):
    size = lax.axis_size("gz")
    return lax.ppermute(values, "gz", [(i, i ^ 2**stage) for i in range(size)])


def ring(values, axis, distance):
    size = lax.axis_size(axis)
    return lax.ppermute(values, axis, [(i, (i + distance) % size) for i in range(size)])


def diagonal(values, x_distance, y_distance):
    nx, ny = lax.axis_size("gx"), lax.axis_size("gy")
    route = []
    for i in range(nx):
        for j in range(ny):
            target = ((i + x_distance) % nx) * ny + (j + y_distance) % ny
            route.append((i * ny + j, target))
    return lax.ppermute(values, ("gx", "gy"), route)


def per_device(facies, perm_table, line_breaks):
    nz, nx, ny = facies.shape
    stages = (lax.axis_size("gz") - 1).bit_length() - 1
    i32, f32 = jnp.int32, jnp.float32
    two = lax.axis_size("gx") == 2
    layers = 2 * nz
    cut_rows = -(-(layers + 1 + 2 * stages) // 8) * 8
    sides = 1 if two else 2
    facies, rims = kernel_call(
        pack_kernel,
        [((nz, nx, ny), i32), ((nx + 4 * nz * sides, ny), i32)],
        [facies],
    )
    other_rims = swapped(rims, 0)
    k, table, cuts = kernel_call(
        functools.partial(prepare_kernel, stages),
        [((3, nz, nx, ny), f32), ((3, 8, ny), f32), ((cut_rows, ny), f32)],
        [perm_table, line_breaks, facies],
        smem=2,
        cost=pl.CostEstimate(flops=10**7, bytes_accessed=10**6, transcendentals=0),
    )
    facies, strip, *rows = kernel_call(
        merge_kernel,
        [((nz, nx, ny), i32), ((2 * nx, ny), i32)] + [((layers * 4, ny), i32)] * sides,
        [facies, rims, other_rims, table],
    )
    other = swapped(facies, 0)
    k, = kernel_call(
        prepare_other_kernel,
        [((3, layers, nx, ny), f32)],
        [table, k, other, strip],
        cost=pl.CostEstimate(flops=10**7, bytes_accessed=10**6, transcendentals=0),
    )
    y_low, y_high = ring(strip, "gy", 1), ring(strip, "gy", -1)
    if two:
        row_low = row_high = ring(rows[0], "gx", 1)
        low_low = low_high = diagonal(strip, 1, 1)
        high_low = high_high = diagonal(strip, 1, -1)
    else:
        row_low, row_high = ring(rows[1], "gx", 1), ring(rows[0], "gx", -1)
        low_low, low_high = diagonal(strip, 1, 1), diagonal(strip, -1, 1)
        high_low, high_high = diagonal(strip, 1, -1), diagonal(strip, -1, -1)

    sizes = nz, nx, ny
    operands = [table, cuts, k, row_low, row_high, y_low, y_high,
                low_low, low_high, high_low, high_high]
    scratch = [pltpu.VMEM((3, layers * 4, ny), f32)] * sides
    return (sweep_ends if stages == 1 else sweep_tree)(sizes, stages, operands, scratch)


def sweep_ends(sizes, stages, operands, scratch):
    nz, nx, ny = sizes
    layers, f32 = 2 * nz, jnp.float32
    cuts = operands[1]
    slab, tall = (nx + 8, 2 * ny), (2, nx + 24, ny)

    def slabs(*count):
        return (count + slab, f32)

    def talls(*count):
        return (count + tall, f32)

    def message_of(count, halo):
        return ((Message(count, halo, nx, ny).rows, ny), f32)

    def filler(flops):
        return pl.CostEstimate(flops=flops, bytes_accessed=10**6, transcendentals=0)

    message, own, lx, ly, lz, d, ratio, inverse = kernel_call(
        end_eliminate_kernel,
        [message_of(LAST_COUNT, 2), slabs(LAST_COUNT), talls(layers), slabs(layers),
         slabs(layers + 1), slabs(3, layers), slabs(layers), slabs(layers)],
        operands,
        [pltpu.VMEM(*s) for s in (talls(layers), talls(layers), slabs(layers), slabs(layers),
                                  slabs(2, layers), slabs(layers))] + scratch,
    )
    other = swapped(message, stages)
    base, phi, parts = kernel_call(
        expand_kernel,
        [talls(3, layers), talls(layers), slabs(6)],
        [cuts, lx, ly, lz, d, ratio],
        cost=filler(10**7),
    )
    message, near = kernel_call(
        functools.partial(end_join_kernel, layers),
        [message_of(3, 1), slabs(13)],
        [cuts, own, other, parts],
    )
    other = swapped(message, stages)
    first, change = kernel_call(
        correct_kernel,
        [talls(3, layers), slabs(3, layers)],
        [cuts, near, lx, ly, lz, ratio, inverse, base, phi],
        [pltpu.VMEM(*slabs(3, layers))],
        cost=filler(10**7),
    )
    out = ((3, nz, nx, ny), f32)
    return tuple(kernel_call(
        end_final_kernel,
        [out, out],
        [cuts, other, near, lx, ly, lz, phi, first, change],
        [pltpu.VMEM(*talls(3, nz + 2)), pltpu.VMEM(*out), pltpu.VMEM(*out),
         pltpu.SemaphoreType.DMA((2, nz // CHUNK))],
        space=pl.ANY,
    ))


def sweep_tree(sizes, stages, operands, scratch):
    nz, nx, ny = sizes
    layers, f32 = 2 * nz, jnp.float32
    cuts = operands[1]
    slab = (nx + 8, 2 * ny)
    one, three = ((layers,) + slab, f32), ((3, layers) + slab, f32)

    def slabs(count):
        return ((count,) + slab, f32)

    def message_of(count, halo):
        return ((Message(count, halo, nx, ny).rows, ny), f32)

    message, own, pair, lx, ly, lz, d, e, inverse = kernel_call(
        functools.partial(eliminate_kernel, stages),
        [message_of(LAST_COUNT if stages == 1 else FIRST_COUNT, 2)]
        + [slabs(FIRST_COUNT), slabs(PAIR_COUNT)]
        + [one] * 3 + [three, one, one],
        operands,
        [pltpu.VMEM(s, f32) for s in (three[0], one[0], (2,) + one[0], one[0])]
        + scratch,
    )
    siblings, factors, group = [], [], own
    for s in range(stages - 1):
        last = s == stages - 2
        outputs = [slabs(FIRST_COUNT), slabs(7), message_of(LAST_COUNT if last else FIRST_COUNT, 2)]
        sibling, factor, message, *joined = kernel_call(
            functools.partial(join_kernel, s, last, layers + 1),
            outputs + ([] if last else [slabs(FIRST_COUNT)]),
            [cuts, group, swapped(message, s + 1)],
        )
        siblings.append(sibling)
        factors.append(factor)
        group = None if last else joined[0]
    fields = ((3, layers + 2) + slab, f32)
    message, own, rights, d2, kept, ends, first = kernel_call(
        functools.partial(middle_kernel, stages),
        [message_of(3 if stages == 1 else SECOND_COUNT, 1), slabs(SECOND_COUNT), slabs(6), three,
         slabs(2 * stages + 5), slabs(3), fields],
        [cuts, own, pair] + siblings + [swapped(message, stages)]
        + [lx, ly, lz, d, e, inverse],
    )
    siblings, group = [], own
    for s in range(stages - 1):
        last = s == stages - 2
        outputs = [slabs(SECOND_COUNT), message_of(3 if last else SECOND_COUNT, 1)]
        sibling, message, *joined = kernel_call(
            functools.partial(join_again_kernel, s, last),
            outputs + ([] if last else [slabs(SECOND_COUNT)]),
            [group, swapped(message, s + 1), factors[s]],
        )
        siblings.append(sibling)
        group = None if last else joined[0]
    out = ((3, nz, nx, ny), f32)
    pressure, residual = kernel_call(
        functools.partial(final_kernel, stages),
        [out, out],
        [cuts, own, pair] + siblings + [swapped(message, stages)]
        + [lx, ly, lz, first, rights, d2, e, inverse, kept, ends],
        [pltpu.VMEM((3, nz + 2) + slab, f32)]
        + [pltpu.VMEM((3, nz, nx, ny), f32)] * 2
        + [pltpu.SemaphoreType.DMA((2, nz // CHUNK))],
        space=pl.ANY,
    )
    return pressure, residual


def solution(mesh):
    return jax.shard_map(
        per_device,
        mesh=mesh,
        in_specs=(P("gz", "gx", "gy"), P(), P()),
        out_specs=(P(None, "gz", "gx", "gy"), P(None, "gz", "gx", "gy")),
        check_vma=False,
    )
```

```python
import functools

import jax
import jax.numpy as jnp
from jax import lax
from jax.experimental import pallas as pl
from jax.experimental.pallas import tpu as pltpu
from jax.sharding import PartitionSpec as P


WIDE = 3
FIRST_COUNT = 11
LAST_COUNT = 5
SECOND_COUNT = 6
PAIR_COUNT = 16
CHUNK = 4


def moved(values, amount, axis):
    size = values.shape[axis]
    amount = amount % size
    if amount == 0:
        return values
    return pltpu.roll(values, amount, axis)


def flag(condition):
    return condition.astype(jnp.float32)


def iotas(rows, lanes):
    return tuple(lax.broadcasted_iota(jnp.int32, (rows, lanes), d) for d in (0, 1))


def choose(condition, first, second):
    return [jnp.where(condition, a, b) for a, b in zip(first, second)]


def is_high(stage):
    return (lax.axis_index("gz") >> (stage + 1)) % 2 == 1


def own_start(nz):
    return (lax.axis_index("gz") % 2) * nz


def pack_kernel(facies_ref, copy_ref, *row_refs):
    nz, nx, ny = facies_ref.shape
    copy_ref[...] = facies_ref[...]
    row = iotas(8, ny)[0]
    for z in range(0, nz, 2):
        pair = [facies_ref[z], facies_ref[z + 1]]
        first = jnp.where(row < 4, pair[0][:8], moved(pair[1][:8], 4, 0))
        last = jnp.where(row < 4, moved(pair[0][nx - 8 :], 4, 0), pair[1][nx - 8 :])
        spot = slice(4 * z, 4 * z + 8)
        if len(row_refs) == 1:
            row_refs[0][spot, :] = jnp.where(lax.axis_index("gx") == 0, last, first)
        else:
            row_refs[0][spot, :] = first
            row_refs[1][spot, :] = last


def rim_tile(low, high, layer):
    row = iotas(8, low.shape[1])[0]
    if layer % 2 == 0:
        return jnp.where(row < 4, high, moved(low, 4, 0))
    return jnp.where(row < 4, moved(high, 4, 0), low)


def merge_kernel(own_ref, other_ref, table_ref, *refs):
    sides = (len(refs) - 1) // 3
    ins, strip_ref, row_refs = refs[: 2 * sides], refs[2 * sides], refs[2 * sides + 1 :]
    nz, nx, ny = own_ref.shape
    swap = own_start(nz) > 0
    lane = lax.broadcasted_iota(jnp.int32, (nx + 8, ny), 1)
    for b in range(2):
        own = swap == (b == 1)
        for n, ref in enumerate(row_refs):
            ref[4 * nz * b : 4 * nz * (b + 1), :] = jnp.where(own, ins[n][...], ins[sides + n][...])
        strip = jnp.zeros((nx + 8, ny), jnp.int32)
        for z in range(nz):
            start = 4 * nz * b + z // 2 * 8
            low, high = [ref[start : start + 8, :] for ref in (row_refs[0], row_refs[-1])]
            layer = jnp.where(own, own_ref[z], other_ref[z])
            layer = jnp.concatenate([layer, rim_tile(low, high, z)], axis=0)
            strip = jnp.where(lane // 8 == z, moved(layer, 8 * z + WIDE, 1), strip)
        strip_ref[b * (nx + 8) : (b + 1) * (nx + 8), :] = strip


def lookup(table, index):
    rows = [
        jnp.take_along_axis(table, index[r : r + 8], axis=1) for r in range(0, index.shape[0], 8)
    ]
    return jnp.concatenate(rows, axis=0)


def prepare_kernel(stages, table, breaks, facies_ref, k_ref, table_ref, cut_ref):
    nz, nx, ny = facies_ref.shape
    lane = iotas(8, ny)[1]
    tables = []
    for q in range(3):
        values = jnp.zeros((8, ny), jnp.float32)
        for label in range(table.shape[1]):
            values = jnp.where(lane == label, table[q, label], values)
        table_ref[q] = values
        tables.append(values)
    for z in range(nz):
        for q in range(3):
            k_ref[q, z] = lookup(tables[q], facies_ref[z])
    pair = lax.axis_index("gz") // 2
    layers = [pair * 2 * nz + r - 1 for r in range(2 * nz + 1)]
    if stages == 1:
        high = is_high(0)
        layers = [
            pair * 2 * nz + jnp.where(high, 2 * nz - 1 - r, r - 1) for r in range(2 * nz + 1)
        ]
    for s in range(stages if stages > 1 else 0):
        base, size = (pair >> (s + 1)) << (s + 1), 2**s
        layers.append((base + size) * 2 * nz - 1)
        layers.append(jnp.where(is_high(s), base, base + 2 * size) * 2 * nz - 1)
    for r, layer in enumerate(layers):
        cut = breaks[jnp.clip(layer, 0, breaks.shape[0] - 1)].astype(jnp.float32)
        cut_ref[r : r + 1, :] = jnp.full((1, ny), cut, jnp.float32)


def prepare_other_kernel(table_ref, own_ref, other_ref, strip_ref, k_ref):
    nz = other_ref.shape[0]
    start = own_start(nz)
    for q in range(3):
        k_ref[q, pl.ds(start, nz)] = own_ref[q]
        for z in range(nz):
            k_ref[q, nz - start + z] = lookup(table_ref[q], other_ref[z])


def face(a, b):
    product = a * b
    total = a + b
    harmonic = 2.0 * product / total
    inside = product > 0.0
    link = jnp.where(inside, harmonic, 0.0)
    flow = jnp.where(inside, harmonic, total)
    tau = jnp.where(inside, harmonic, 2.0 * total)
    return link, flow, tau


class Message:
    def __init__(self, count, halo, nx, ny):
        self.count, self.halo, self.nx, self.ny = count, halo, nx, ny
        self.one_sided = lax.axis_size("gx") == 2
        self.rows_each = halo if self.one_sided else 2 * halo
        self.per_tile = 8 // self.rows_each
        self.tiles = -(-count // self.per_tile)
        self.abreast = ny // (2 * halo * count)
        strips = -(-(nx // 8 + 1) // self.abreast)
        self.sides = count * nx + 8 * strips
        self.rows = self.sides + 8 * self.tiles

    def strip(self, t, q):
        start = self.count * self.nx + 8 * (t // self.abreast)
        shift = 2 * self.halo * (self.count * (t % self.abreast) + q) + self.halo
        return slice(start, start + 8), shift

    def tile(self, q):
        start = self.sides + 8 * (q // self.per_tile)
        return slice(start, start + 8)

    def side_moved(self, tile, q, sign):
        part = q % self.per_tile
        if not self.one_sided:
            return moved(tile, sign * (self.rows_each * part + self.halo), 0)
        first = lax.axis_index("gx") == 0
        out = jnp.where(
            first,
            moved(tile, sign * self.halo * part, 0),
            moved(tile, sign * self.halo * (part + 1), 0),
        )
        if sign > 0:
            return out
        row = iotas(8, self.ny)[0]
        return jnp.where(jnp.where(first, row, 7 - row) < self.halo, out, 1.0)

    def write(self, ref, slabs):
        nx, ny, halo = self.nx, self.ny, self.halo
        row, lane = iotas(8, ny)
        strips = {}
        for t in range(nx // 8 + 1):
            for q, slab in enumerate(slabs):
                spot, shift = self.strip(t, q)
                turned = moved(slab[8 * t : 8 * t + 8, ny:], shift, 1)
                held = strips.get(spot.start, turned)
                strips[spot.start] = jnp.where(lane < shift - halo, held, turned)
        for start, strip in strips.items():
            ref[start : start + 8, :] = strip
        for q, slab in enumerate(slabs):
            ref[q * nx : (q + 1) * nx, :] = slab[:nx, :ny]
            turned = self.side_moved(slab[nx:, :ny], q, 1)
            part = q % self.per_tile
            tile = turned if part == 0 else jnp.where(row < self.rows_each * part, tile, turned)
            if part == self.per_tile - 1 or q == self.count - 1:
                ref[self.tile(q), :] = tile

    def read(self, ref):
        nx = self.nx
        slabs = []
        for q in range(self.count):
            side = self.side_moved(ref[self.tile(q), :], q, -1)
            body = jnp.concatenate([ref[q * nx : (q + 1) * nx, :], side], axis=0)
            beside = []
            for t in range(nx // 8 + 1):
                spot, shift = self.strip(t, q)
                beside.append(moved(ref[spot, :], -shift, 1))
            slabs.append(jnp.concatenate([body, jnp.concatenate(beside, axis=0)], axis=1))
        return slabs


def open_after(cut_ref, r):
    cut = 1.0 - cut_ref[r : r + 1, :]
    return jnp.concatenate([cut, cut], axis=1)


def slab_size(ref):
    return ref.shape[-2] - 8, ref.shape[-1] // 2


def join(low, high, opened):
    ends = link, flow, tau = face(low[4], high[3])
    coupling = link * opened
    inverse = 1.0 / (low[2] + tau)
    step = coupling * inverse
    last_inverse = 1.0 / (high[0] + tau - coupling * step)
    outer = low[1] * inverse
    weight = step * low[1]
    weight_low, weight_high = weight * last_inverse, high[1] * last_inverse
    right_low = low[8:10] + [low[10] + flow]
    right_high = high[5:7] + [high[7] - flow]
    s_uu = low[0] - outer * low[1] - weight * weight_low
    s_uv = -weight * weight_high
    s_vv = high[2] - high[1] * weight_high
    factors = [outer, step, weight_low, weight_high, inverse, last_inverse]
    g_u, g_v, middle = join_right(factors, low[5:8], right_low, right_high, high[8:11])
    return [s_uu, s_uv, s_vv, low[3], high[4]] + g_u + g_v, factors, right_low + middle, ends


def join_right(factors, low_u, low_v, high_u, high_v):
    outer, step, weight_low, weight_high = factors[:4]
    middle = [b + step * a for a, b in zip(low_v, high_u)]
    g_u = [g - outer * a - weight_low * m for g, a, m in zip(low_u, low_v, middle)]
    g_v = [g - weight_high * m for g, m in zip(high_v, middle)]
    return g_u, g_v, middle


def join_inner(factors, right_low, middle, first, last):
    outer, step, weight_low, weight_high, inverse, last_inverse = factors
    high = last_inverse * middle - weight_low * first - weight_high * last
    return inverse * right_low - outer * first + step * high, high


def reduce_end(slabs, top):
    s_uu, s_uv, s_vv, k_u, k_v = slabs[:5]
    far_s, near_s = choose(top, [s_vv, s_uu], [s_uu, s_vv])
    far_k, near_k = choose(top, [k_v, k_u], [k_u, k_v])
    sign = jnp.where(top, 1.0, -1.0)
    factor = s_uv / (far_s + 2.0 * far_k)
    g_u, g_v = slabs[5:8], slabs[8:11]
    far_g, near_g = choose(top, g_v, g_u), choose(top, g_u, g_v)
    far_g[2] = far_g[2] + far_k * sign
    return [near_s - s_uv * factor, near_k] + [n - factor * g for n, g in zip(near_g, far_g)], factor


def reduce_end_right(factor, g_u, g_v, top):
    far_g, near_g = choose(top, g_v, g_u), choose(top, g_u, g_v)
    return [n - factor * g for n, g in zip(near_g, far_g)]


def assemble_slabs(k_ref, tables, rims, low_ref, high_ref, store):
    row_low, row_high, y_low, y_high = rims
    layers, nx, ny = k_ref.shape[1:]
    nz = layers // 2
    at_x, at_y = lax.axis_index("gx"), lax.axis_index("gy")
    has_x_low, has_x_high = at_x > 0, at_x < lax.axis_size("gx") - 1
    has_y_low, has_y_high = at_y > 0, at_y < lax.axis_size("gy") - 1

    row, lane = iotas(nx + 8, 2 * ny)
    x_in = (row < nx) | ((row < nx + WIDE) & has_x_high) | ((row >= nx + 8 - WIDE) & has_x_low)
    y_in = (lane < ny) | ((lane < ny + WIDE) & has_y_high)
    y_in = y_in | ((lane >= 2 * ny - WIDE) & has_y_low)
    cell = x_in & y_in
    valid = flag(cell)
    in_x, in_xp = valid * moved(valid, -1, 0), valid * moved(valid, 1, 0)
    in_y, in_yp = valid * moved(valid, -1, 1), valid * moved(valid, 1, 1)
    row_in, strip_in = cell[nx:, :ny], cell[:, ny:]

    lane = iotas(nx + 8, ny)[1]
    strips = []
    for b in range(2):
        part = slice(b * (nx + 8), (b + 1) * (nx + 8))
        strip = jnp.where(lane % 8 < WIDE, y_low[part, :], y_high[part, :])
        strips.append([lookup(table, strip) for table in tables])
    for q in range(3):
        low_ref[q] = lookup(tables[q], row_low[...])
        if high_ref is not low_ref:
            high_ref[q] = lookup(tables[q], row_high[...])

    for b in range(2):
        for z in range(nz):
            at = b * nz + z
            start = at // 2 * 8
            for q in range(3):
                low, high = low_ref[q, start : start + 8, :], high_ref[q, start : start + 8, :]
                side = jnp.where(row_in, rim_tile(low, high, z), 0.0)
                beside = jnp.where(strip_in, moved(strips[b][q], -(8 * z + WIDE), 1), 0.0)
                body = jnp.concatenate([k_ref[q, at], side], axis=0)
                store(q, at, jnp.concatenate([body, beside], axis=1))

    return cell, in_x, in_xp, in_y, in_yp


def flow_after(here, there, inside):
    total = here + there
    return jnp.where(inside > 0.0, 2.0 * (here * there) / total, total)


def tau_and_source(flow, back, inside, inside_back):
    return flow * (2.0 - inside) + back * (2.0 - inside_back), flow - back


def eliminate_kernel(
    stages, table_ref, cut_ref, k_ref, row_low, row_high, y_low, y_high,
    message_ref, own_ref, pair_ref, lx_ref, ly_ref, lz_ref, d_ref, e_ref, inverse_ref,
    all_ref, flow_ref, source_ref, centre_ref, low_ref, high_ref=None,
):
    layers, nx, ny = k_ref.shape[1:]
    nz = layers // 2
    rims = row_low, row_high, y_low, y_high

    def store(q, at, slab):
        all_ref[q, at] = slab

    cell, in_x, in_xp, in_y, in_yp = assemble_slabs(
        k_ref, [table_ref[q] for q in range(3)], rims, low_ref,
        low_ref if high_ref is None else high_ref, store,
    )
    for at in range(layers):
        kx, ky = all_ref[0, at], all_ref[1, at]
        flow_x = flow_after(kx, moved(kx, -1, 0), in_x)
        flow_ref[at] = flow_after(ky, moved(ky, -1, 1), in_y)
        lx_ref[at] = flow_x * in_x
        centre_ref[at], source_ref[0, at] = tau_and_source(
            flow_x, moved(flow_x, 1, 0), in_x, in_xp
        )
        if at % nz < nz - 1:
            kz, above = all_ref[2, at], all_ref[2, at + 1]
            lz_ref[at] = jnp.where(cell, 2.0 * (kz * above) / (kz + above), 0.0)
    for at in range(layers):
        flow_y = flow_ref[at]
        ly_ref[at] = flow_y * in_y
        tau_y, source_ref[1, at] = tau_and_source(
            flow_y, moved(flow_y, 1, 1), in_y, in_yp
        )
        centre = centre_ref[at] + tau_y
        if at % nz > 0:
            centre = centre + lz_ref[at - 1]
        if at % nz < nz - 1:
            centre = centre + lz_ref[at]
        centre_ref[at] = jnp.where(cell, centre, 1.0)

    states = [{}, {}]
    for z in range(nz):
        for b in range(2):
            at, v = b * nz + z, states[b]
            centre = centre_ref[at]
            sources = [source_ref[0, at], source_ref[1, at]]
            if z == 0:
                v["source"] = sources + [lz_ref[at]]
                v["s_uu"], v["g_u"] = centre, v["source"]
            elif z == nz - 1:
                sources = sources + [-lz_ref[at - 1]]
                v["s_vv"] = centre - v["coupling"] * v["ratio"]
                v["s_uv"] = -v["coupling"] * v["spike"]
                v["g_v"] = [a + v["coupling"] * d for a, d in zip(sources, v["value"])]
            else:
                forward = sources + [lz_ref[at] - lz_ref[at - 1]]
                if z == 1:
                    pivot, numerator = centre, v["coupling"]
                else:
                    pivot = centre - v["coupling"] * v["ratio"]
                    forward = [a + v["coupling"] * d for a, d in zip(forward, v["value"])]
                    numerator = v["coupling"] * v["spike"]
                inverse = 1.0 / pivot
                v["value"] = [a * inverse for a in forward]
                v["spike"] = numerator * inverse
                v["s_uu"] = v["s_uu"] - numerator * v["spike"]
                v["g_u"] = [g + v["spike"] * a for g, a in zip(v["g_u"], forward)]
                inverse_ref[at] = inverse
                e_ref[at] = v["spike"]
                for f in range(3):
                    d_ref[f, at] = v["value"][f]
            if z < nz - 1:
                v["coupling"] = lz_ref[at] * open_after(cut_ref, at + 1)
                if z > 0:
                    v["ratio"] = v["coupling"] * inverse

    def block(b):
        v = states[b]
        k_ends = [all_ref[2, b * nz], all_ref[2, b * nz + nz - 1]]
        return [v["s_uu"], v["s_uv"], v["s_vv"]] + k_ends + v["g_u"] + v["g_v"]

    slabs, factors, rights, ends = join(block(0), block(1), open_after(cut_ref, nz))
    for q, slab in enumerate(slabs):
        own_ref[q] = slab
    for n, slab in enumerate(factors + rights + list(ends)):
        pair_ref[n] = slab
    if stages == 1:
        slabs, pair_ref[PAIR_COUNT - 1] = reduce_end(slabs, is_high(0))
    Message(len(slabs), 2, nx, ny).write(message_ref, slabs)


def join_kernel(stage, last, base, cut_ref, own_ref, message_ref, sibling_ref, factor_ref, next_ref, *joined):
    nx, ny = slab_size(own_ref)
    own = [own_ref[q] for q in range(FIRST_COUNT)]
    sibling = Message(FIRST_COUNT, 2, nx, ny).read(message_ref)
    for q, slab in enumerate(sibling):
        sibling_ref[q] = slab
    high = is_high(stage)
    slabs, factors, _, _ = join(
        choose(high, sibling, own),
        choose(high, own, sibling),
        open_after(cut_ref, base + 2 * stage),
    )
    for n, values in enumerate(factors):
        factor_ref[n] = values
    if last:
        slabs, factor_ref[6] = reduce_end(slabs, is_high(stage + 1))
    else:
        for q, slab in enumerate(slabs):
            joined[0][q] = slab
    Message(len(slabs), 2, nx, ny).write(next_ref, slabs)


def join_again_kernel(stage, last, own_ref, message_ref, factor_ref, sibling_ref, next_ref, *joined):
    nx, ny = slab_size(own_ref)
    own = [own_ref[q] for q in range(SECOND_COUNT)]
    sibling = Message(SECOND_COUNT, 1, nx, ny).read(message_ref)
    for q, slab in enumerate(sibling):
        sibling_ref[q] = slab
    above = is_high(stage)
    low, high = choose(above, sibling, own), choose(above, own, sibling)
    factors = [factor_ref[n] for n in range(6)]
    g_u, g_v, _ = join_right(factors, low[:3], low[3:], high[:3], high[3:])
    slabs = g_u + g_v
    if last:
        slabs = reduce_end_right(factor_ref[6], g_u, g_v, is_high(stage + 1))
    else:
        for q, slab in enumerate(slabs):
            joined[0][q] = slab
    Message(len(slabs), 1, nx, ny).write(next_ref, slabs)


def stencil(slab, link_x, link_y):
    return (
        link_x * moved(slab, -1, 0)
        + moved(link_x * slab, 1, 0)
        + (link_y * moved(slab, -1, 1) + moved(link_y * slab, 1, 1))
    )


def beyond_cuts(cut_ref, at, link_low, link_high):
    low, high = cut_ref[pl.ds(at, 1), :], cut_ref[pl.ds(at + 1, 1), :]
    return (
        link_low * jnp.concatenate([low, low], axis=1),
        link_high * jnp.concatenate([high, high], axis=1),
    )


def left_out(field_ref, f, at, link_x, link_y, cuts):
    return stencil(field_ref[f, at + 1], link_x, link_y) + (
        cuts[0] * field_ref[f, at] + cuts[1] * field_ref[f, at + 2]
    )


def middle_kernel(stages, cut_ref, *refs):
    own_ref, pair_ref, siblings, message_ref = refs[0], refs[1], refs[2 : stages + 1], refs[stages + 1]
    refs = refs[stages + 2 :]
    lx_ref, ly_ref, lz_ref, d_ref, e_ref, inverse_ref = refs[:6]
    next_ref, own2_ref, right_ref, d2_ref, factor_ref, end_ref, first_ref = refs[6:]
    layers = lx_ref.shape[0]
    nz = layers // 2
    nx, ny = slab_size(lx_ref)
    own = [own_ref[q] for q in range(FIRST_COUNT)]
    slots = []

    def keep(values):
        factor_ref[len(slots)] = values
        slots.append(None)

    def attach(state, sign, row, pivot, right, k):
        beside, k_beside, rights, exists = state[0], state[1], state[2:5], state[5]
        link, flow, tau = face(k_beside * exists, k)
        coupling = link * open_after(cut_ref, row)
        rights = rights[:2] + [rights[2] + sign * flow]
        inverse = 1.0 / (beside + tau)
        step = coupling * inverse
        right = [a + step * b for a, b in zip(right, rights)]
        right[2] = right[2] - sign * flow
        return pivot + tau - coupling * step, right, step, inverse, rights, (link, flow, tau)

    far = Message(LAST_COUNT, 2, nx, ny).read(message_ref)
    top = is_high(stages - 1)
    below, above = far + [flag(top)], far + [flag(jnp.logical_not(top))]
    for s in range(stages - 2, -1, -1):
        up = is_high(s)
        block = [siblings[s][q] for q in range(FIRST_COUNT)]
        sign = jnp.where(up, 1.0, -1.0)
        state = choose(up, below, above)
        far_s, far_k, near_s, near_k = choose(
            up, [block[0], block[3], block[2], block[4]], [block[2], block[4], block[0], block[3]]
        )
        far_g = choose(up, block[5:8], block[8:11])
        near_g = choose(up, block[8:11], block[5:8])
        row = layers + 2 + 2 * s
        pivot, right, step, _, _, _ = attach(state, sign, row, far_s, far_g, far_k)
        factor = block[1] / pivot
        keep(step)
        keep(factor)
        state = [near_s - block[1] * factor, near_k]
        state += [n - factor * r for n, r in zip(near_g, right)] + [jnp.float32(1.0)]
        below, above = choose(up, state, below), choose(up, above, state)

    pivot_u, right_u, step_b, inverse_b, rights_b, ends_b = attach(
        below, 1.0, 0, own[0], own[5:8], own[3]
    )
    pivot_v, right_v, step_a, inverse_a, rights_a, ends_a = attach(
        above, -1.0, layers, own[2], own[8:11], own[4]
    )
    held_b, held_a = inverse_b * below[5], inverse_a * above[5]
    inverse_u = 1.0 / pivot_u
    factor = own[1] * inverse_u
    inverse_v = 1.0 / (pivot_v - own[1] * factor)
    for values in (step_b, held_b, step_a, held_a, inverse_u, factor, inverse_v):
        keep(values)
    pair = [pair_ref[n] for n in range(PAIR_COUNT)]
    inner = pair[:6]
    ends = [ends_b[0], pair[12], ends_a[0]]
    for n, values in enumerate(ends):
        end_ref[n] = values

    for f in range(3):
        last = (right_v[f] - factor * right_u[f]) * inverse_v
        first_u = right_u[f] * inverse_u - factor * last
        low_v, high_u = join_inner(inner, pair[6 + f], pair[9 + f], first_u, last)
        first_ref[f, 0] = rights_b[f] * held_b + step_b * first_u
        first_ref[f, layers + 1] = rights_a[f] * held_a + step_a * last
        first_ref[f, 1] = first_u
        first_ref[f, nz] = low_v
        first_ref[f, nz + 1] = high_u
        first_ref[f, layers] = last
    for z in range(nz - 2, 0, -1):
        for at in (z, nz + z):
            ratio = lz_ref[at] * open_after(cut_ref, at + 1) * inverse_ref[at]
            spike = e_ref[at]
            for f in range(3):
                first_ref[f, at + 1] = (
                    d_ref[f, at]
                    + spike * first_ref[f, 1 + at - z]
                    + ratio * first_ref[f, at + 2]
                )

    def block(b):
        for z in range(nz):
            at = b * nz + z
            cuts = beyond_cuts(
                cut_ref, at,
                ends[b] if z == 0 else lz_ref[at - 1],
                ends[b + 1] if z == nz - 1 else lz_ref[at],
            )
            right = [left_out(first_ref, f, at, lx_ref[at], ly_ref[at], cuts) for f in range(3)]
            if z == 0:
                g_u = list(right)
            else:
                if z == 1:
                    forward = right
                else:
                    forward = [right[f] + coupling * value[f] for f in range(3)]
                if z < nz - 1:
                    inverse, spike = inverse_ref[at], e_ref[at]
                    value = [forward[f] * inverse for f in range(3)]
                    g_u = [g_u[f] + spike * forward[f] for f in range(3)]
                    for f in range(3):
                        d2_ref[f, at] = value[f]
                    coupling = lz_ref[at] * open_after(cut_ref, at + 1)
        return g_u, forward

    (low_u, low_v), (high_u, high_v) = block(0), block(1)
    g_u, g_v, middle = join_right(inner, low_u, low_v, high_u, high_v)
    for n, slab in enumerate(low_v + middle):
        right_ref[n] = slab
    for q, slab in enumerate(g_u + g_v):
        own2_ref[q] = slab
    slabs = g_u + g_v
    if stages == 1:
        slabs = reduce_end_right(pair[PAIR_COUNT - 1], g_u, g_v, is_high(0))
    Message(len(slabs), 1, nx, ny).write(next_ref, slabs)


def final_kernel(stages, cut_ref, *refs):
    own_ref, pair_ref, siblings, message_ref = refs[0], refs[1], refs[2 : stages + 1], refs[stages + 1]
    refs = refs[stages + 2 :]
    lx_ref, ly_ref, lz_ref, first_ref, right_ref, d2_ref, e_ref, inverse_ref = refs[:8]
    factor_ref, end_ref, pressure_out, residual_out = refs[8:12]
    change_ref, pressure_ref, residual_ref, sems = refs[12:]
    nz = lx_ref.shape[0] // 2
    nx, ny = slab_size(lx_ref)
    own = [own_ref[q] for q in range(SECOND_COUNT)]
    slots = []

    def kept():
        slots.append(None)
        return factor_ref[len(slots) - 1]

    below = above = Message(3, 1, nx, ny).read(message_ref)
    for s in range(stages - 2, -1, -1):
        up = is_high(s)
        block = [siblings[s][q] for q in range(SECOND_COUNT)]
        state = choose(up, below, above)
        far_g = choose(up, block[:3], block[3:])
        near_g = choose(up, block[3:], block[:3])
        step, factor = kept(), kept()
        right = [a + step * b for a, b in zip(far_g, state)]
        state = [n - factor * r for n, r in zip(near_g, right)]
        below, above = choose(up, state, below), choose(up, above, state)
    step_b, held_b, step_a, held_a = kept(), kept(), kept(), kept()
    inverse_u, factor, inverse_v = kept(), kept(), kept()
    inner = [pair_ref[n] for n in range(6)]
    start = own_start(nz)
    high = start > 0
    for f in range(3):
        right_u = own[f] + step_b * below[f]
        right_v = own[3 + f] + step_a * above[f]
        last = (right_v - factor * right_u) * inverse_v
        first = right_u * inverse_u - factor * last
        low_v, high_u = join_inner(inner, right_ref[f], right_ref[3 + f], first, last)
        beyond_b = below[f] * held_b + step_b * first
        beyond_a = above[f] * held_a + step_a * last
        values = choose(high, [low_v, high_u, last, beyond_a], [beyond_b, first, low_v, high_u])
        for at, slab in zip((0, 1, nz, nz + 1), values):
            change_ref[f, at] = slab
    ends = choose(high, [end_ref[1], end_ref[2]], [end_ref[0], end_ref[1]])
    for z in range(nz - 2, 0, -1):
        at = start + z
        opened = 1.0 - cut_ref[pl.ds(at + 1, 1), :]
        opened = jnp.concatenate([opened, opened], axis=1)
        ratio = lz_ref[at] * opened * inverse_ref[at]
        spike = e_ref[at]
        for f in range(3):
            change_ref[f, z + 1] = (
                d2_ref[f, at] + spike * change_ref[f, 1] + ratio * change_ref[f, z + 2]
            )
    own_part = (slice(0, nx), slice(0, ny))
    copies = []
    for z in range(nz):
        at = start + z
        cuts = beyond_cuts(
            cut_ref, at,
            ends[0] if z == 0 else lz_ref[at - 1],
            ends[1] if z == nz - 1 else lz_ref[at],
        )
        link_x, link_y = lx_ref[at], ly_ref[at]
        for f in range(3):
            pressure_ref[f, z] = (first_ref[f, at + 1] + change_ref[f, z + 1])[own_part]
            residual_ref[f, z] = left_out(change_ref, f, z, link_x, link_y, cuts)[own_part]
        if (z + 1) % CHUNK == 0:
            part = (slice(None), slice(z + 1 - CHUNK, z + 1))
            for n, (buffer, out) in enumerate(
                ((pressure_ref, pressure_out), (residual_ref, residual_out))
            ):
                copy = pltpu.make_async_copy(
                    buffer.at[part], out.at[part], sems.at[n, z // CHUNK]
                )
                copy.start()
                copies.append(copy)
    for copy in copies:
        copy.wait()


def put(ref, index, slab):
    rows, ny = slab.shape[0], slab.shape[1] // 2
    for h in range(2):
        half = slab[:, h * ny : (h + 1) * ny]
        ref[index + (h, slice(8, 8 + rows))] = half
        ref[index + (h, slice(0, 8))] = half[rows - 8 :]
        ref[index + (h, slice(8 + rows, 16 + rows))] = half[:8]


def get(ref, index, shift=0):
    rows = ref.shape[-2] - 16
    halves = [ref[index + (h, slice(8 + shift, 8 + shift + rows))] for h in range(2)]
    return jnp.concatenate(halves, axis=1)


def signed():
    return jnp.where(is_high(0), -1.0, 1.0)


def both_halves(ref, r):
    values = ref[pl.ds(r, 1), :]
    return jnp.concatenate([values, values], axis=1)


def beside_sum(field_ref, index, lx_ref, ly_ref, j):
    here, link_y = get(field_ref, index), ly_ref[j]
    return (
        get(lx_ref, (j,)) * get(field_ref, index, 1)
        + get(lx_ref, (j,), -1) * get(field_ref, index, -1)
        + (link_y * moved(here, -1, 1) + moved(link_y * here, 1, 1))
    )


def end_eliminate_kernel(
    table_ref, cut_ref, k_ref, row_low, row_high, y_low, y_high,
    message_ref, own_ref, lx_ref, ly_ref, lz_ref, d_ref, ratio_ref, inverse_ref,
    kx_ref, fx_ref, ky_ref, kz_ref, source_ref, centre_ref, low_ref, high_ref=None,
):
    layers, nx, ny = k_ref.shape[1:]
    rims = row_low, row_high, y_low, y_high
    high, sign = is_high(0), signed()

    def store(q, at, slab):
        j = jnp.where(high, layers - 1 - at, at)
        if q == 0:
            put(kx_ref, (j,), slab)
        else:
            (ky_ref, kz_ref)[q - 1][j] = slab

    cell, in_x, in_xp, in_y, in_yp = assemble_slabs(
        k_ref, [table_ref[q] for q in range(3)], rims, low_ref,
        low_ref if high_ref is None else high_ref, store,
    )
    zero = jnp.zeros((nx + 8, 2 * ny), jnp.float32)
    lz_ref[0] = zero
    lz_ref[layers] = zero
    for j in range(layers):
        flow_x = flow_after(get(kx_ref, (j,)), get(kx_ref, (j,), 1), in_x)
        put(fx_ref, (j,), flow_x)
        put(lx_ref, (j,), flow_x * in_x)
        ky = ky_ref[j]
        ky_ref[j] = flow_after(ky, moved(ky, -1, 1), in_y)
        if j < layers - 1:
            kz, above = kz_ref[j], kz_ref[j + 1]
            lz_ref[j + 1] = jnp.where(cell, 2.0 * (kz * above) / (kz + above), 0.0)
    for j in range(layers):
        flow_y = ky_ref[j]
        ly_ref[j] = flow_y * in_y
        tau_x, source_ref[0, j] = tau_and_source(
            get(fx_ref, (j,)), get(fx_ref, (j,), -1), in_x, in_xp
        )
        tau_y, source_ref[1, j] = tau_and_source(flow_y, moved(flow_y, 1, 1), in_y, in_yp)
        centre = tau_x + tau_y + (2.0 * kz_ref[0] if j == 0 else lz_ref[j])
        if j < layers - 1:
            centre = centre + lz_ref[j + 1]
        centre_ref[j] = jnp.where(cell, centre, 1.0)
    for j in range(layers):
        flow_z = -kz_ref[0] if j == 0 else -lz_ref[j]
        if j < layers - 1:
            flow_z = flow_z + lz_ref[j + 1]
        forward = [source_ref[0, j], source_ref[1, j], sign * flow_z]
        pivot = centre_ref[j]
        if j > 0:
            pivot = pivot - coupling * ratio
            forward = [a + coupling * d for a, d in zip(forward, value)]
        if j < layers - 1:
            inverse = 1.0 / pivot
            coupling = lz_ref[j + 1] * (1.0 - both_halves(cut_ref, j + 1))
            ratio = coupling * inverse
            value = [a * inverse for a in forward]
            inverse_ref[j] = inverse
            ratio_ref[j] = ratio
            for f in range(3):
                d_ref[f, j] = value[f]
    slabs = [pivot, kz_ref[layers - 1]] + forward
    for q, slab in enumerate(slabs):
        own_ref[q] = slab
    Message(LAST_COUNT, 2, nx, ny).write(message_ref, slabs)


def expand_kernel(
    cut_ref, lx_ref, ly_ref, lz_ref, d_ref, ratio_ref, base_ref, phi_ref, part_ref
):
    layers = ly_ref.shape[0]
    zero = jnp.zeros(ly_ref.shape[1:], jnp.float32)
    phi, base = zero + 1.0, [zero] * 3
    put(phi_ref, (layers - 1,), phi)
    for f in range(3):
        put(base_ref, (f, layers - 1), zero)
    for j in range(layers - 2, -1, -1):
        ratio = ratio_ref[j]
        phi = ratio * phi
        put(phi_ref, (j,), phi)
        for f in range(3):
            base[f] = d_ref[f, j] + ratio * base[f]
            put(base_ref, (f, j), base[f])
    along_x = along_y = along_z = zero
    parts = [zero] * 3
    for j in range(layers):
        phi = get(phi_ref, (j,))
        along_x = along_x + (get(lx_ref, (j,)) * phi) * get(phi_ref, (j,), 1)
        along_y = along_y + (ly_ref[j] * phi) * moved(phi, -1, 1)
        cut_low = lz_ref[j] * both_halves(cut_ref, j)
        if j < layers - 1:
            cut_high = lz_ref[j + 1] * both_halves(cut_ref, j + 1)
            along_z = along_z + (cut_high * phi) * get(phi_ref, (j + 1,))
        for f in range(3):
            right = beside_sum(base_ref, (f, j), lx_ref, ly_ref, j)
            if j > 0:
                right = right + cut_low * get(base_ref, (f, j - 1))
            if j < layers - 1:
                right = right + cut_high * get(base_ref, (f, j + 1))
            parts[f] = parts[f] + phi * right
    for n, slab in enumerate(parts + [along_x, along_y, 2.0 * along_z]):
        part_ref[n] = slab


def end_join_kernel(layers, cut_ref, own_ref, message_ref, part_ref, next_ref, near_ref):
    nx, ny = slab_size(own_ref)
    own = [own_ref[q] for q in range(LAST_COUNT)]
    other = Message(LAST_COUNT, 2, nx, ny).read(message_ref)
    sign = signed()
    cut = both_halves(cut_ref, layers)
    link, flow, tau = face(own[1], other[1])
    coupling = link * (1.0 - cut)
    inverse_other = 1.0 / (other[0] + tau)
    step = coupling * inverse_other
    inverse = 1.0 / (own[0] + tau - coupling * step)
    right_own = own[2:4] + [own[4] + sign * flow]
    right_other = other[2:4] + [other[4] - sign * flow]
    cut_near = link * cut
    along_x, along_y, along_z = [part_ref[3 + n] for n in range(3)]
    slabs = []
    for f in range(3):
        near = (right_own[f] + step * right_other[f]) * inverse
        beyond = right_other[f] * inverse_other + step * near
        near_ref[f], near_ref[3 + f] = near, beyond
        right = part_ref[f] + stencil(near, along_x, along_y)
        slabs.append(right + (along_z * near + cut_near * beyond))
        near_ref[6 + f] = slabs[f]
    near_ref[9], near_ref[10], near_ref[11], near_ref[12] = step, inverse, inverse_other, link
    Message(3, 1, nx, ny).write(next_ref, slabs)


def correct_kernel(
    cut_ref, near_ref, lx_ref, ly_ref, lz_ref, ratio_ref, inverse_ref, base_ref, phi_ref,
    first_ref, change_ref, d_ref,
):
    layers = ly_ref.shape[0]
    for j in range(layers):
        phi = get(phi_ref, (j,))
        for f in range(3):
            put(first_ref, (f, j), get(base_ref, (f, j)) + phi * near_ref[f])
    for j in range(layers - 1):
        cut_low = lz_ref[j] * both_halves(cut_ref, j)
        cut_high = lz_ref[j + 1] * both_halves(cut_ref, j + 1)
        inverse = inverse_ref[j]
        if j > 0:
            coupling = lz_ref[j] * (1.0 - both_halves(cut_ref, j))
        for f in range(3):
            right = beside_sum(first_ref, (f, j), lx_ref, ly_ref, j)
            right = right + cut_high * get(first_ref, (f, j + 1))
            if j > 0:
                right = right + cut_low * get(first_ref, (f, j - 1)) + coupling * d_ref[f, j - 1]
            d_ref[f, j] = right * inverse
    change = [jnp.zeros(ly_ref.shape[1:], jnp.float32)] * 3
    for f in range(3):
        change_ref[f, layers - 1] = change[f]
    for j in range(layers - 2, -1, -1):
        ratio = ratio_ref[j]
        for f in range(3):
            change[f] = d_ref[f, j] + ratio * change[f]
            change_ref[f, j] = change[f]


def end_final_kernel(
    cut_ref, message_ref, near_ref, lx_ref, ly_ref, lz_ref, phi_ref, first_ref, base_ref,
    pressure_out, residual_out, change_ref, pressure_ref, residual_ref, sems,
):
    layers = ly_ref.shape[0]
    nz = layers // 2
    nx, ny = slab_size(ly_ref)
    high = is_high(0)
    start = jnp.where(high, nz - own_start(nz), own_start(nz))
    beside_other = start > 0
    other = Message(3, 1, nx, ny).read(message_ref)
    step, inverse, inverse_other, link_near = [near_ref[9 + n] for n in range(4)]
    near = [(near_ref[6 + f] + step * other[f]) * inverse for f in range(3)]
    for i in range(-1, nz + 1):
        j = jnp.clip(start + i, 0, layers - 1)
        phi = get(phi_ref, (j,))
        for f in range(3):
            change = base_ref[f, j] + phi * near[f]
            if i == -1:
                change = jnp.where(beside_other, change, 0.0)
            if i == nz:
                beyond = other[f] * inverse_other + step * near[f]
                change = jnp.where(beside_other, beyond, change)
            put(change_ref, (f, i + 1), change)
    own_part = (slice(0, nx), slice(0, ny))
    copies = []
    for i in range(nz):
        j = start + i
        z = jnp.where(high, nz - 1 - i, i)
        link_high = lz_ref[j + 1]
        if i == nz - 1:
            link_high = jnp.where(beside_other, link_near, link_high)
        cut_low = lz_ref[j] * both_halves(cut_ref, j)
        cut_high = link_high * both_halves(cut_ref, j + 1)
        for f in range(3):
            left_out = beside_sum(change_ref, (f, i + 1), lx_ref, ly_ref, j) + (
                cut_low * get(change_ref, (f, i)) + cut_high * get(change_ref, (f, i + 2))
            )
            pressure = get(first_ref, (f, j)) + get(change_ref, (f, i + 1))
            pressure_ref[f, z] = pressure[own_part]
            residual_ref[f, z] = left_out[own_part]
        if (i + 1) % CHUNK == 0:
            part = (slice(None), pl.ds(jnp.where(high, nz - 1 - i, i + 1 - CHUNK), CHUNK))
            for n, (buffer, out) in enumerate(
                ((pressure_ref, pressure_out), (residual_ref, residual_out))
            ):
                copy = pltpu.make_async_copy(
                    buffer.at[part], out.at[part], sems.at[n, i // CHUNK]
                )
                copy.start()
                copies.append(copy)
    for copy in copies:
        copy.wait()


def kernel_call(kernel, outputs, operands, scratch=(), smem=0, cost=None, space=pltpu.VMEM):
    specs = [pl.BlockSpec(memory_space=pltpu.SMEM)] * smem
    specs += [pl.BlockSpec(memory_space=pltpu.VMEM)] * (len(operands) - smem)
    return pl.pallas_call(
        kernel,
        out_shape=[jax.ShapeDtypeStruct(s, t) for s, t in outputs],
        in_specs=specs,
        out_specs=[pl.BlockSpec(memory_space=space)] * len(outputs),
        scratch_shapes=list(scratch),
        compiler_params=pltpu.CompilerParams(vmem_limit_bytes=32 * 2**20),
        cost_estimate=cost,
    )(*operands)


def swapped(values, stage):
    size = lax.axis_size("gz")
    return lax.ppermute(values, "gz", [(i, i ^ 2**stage) for i in range(size)])


def ring(values, axis, distance):
    size = lax.axis_size(axis)
    return lax.ppermute(values, axis, [(i, (i + distance) % size) for i in range(size)])


def slanted(values, x_distance):
    nx, nz = lax.axis_size("gx"), lax.axis_size("gz")
    route = []
    for i in range(nx):
        for k in range(nz):
            route.append((i * nz + k, (i + x_distance) % nx * nz + (k ^ 1)))
    return lax.ppermute(values, ("gx", "gz"), route)


def per_device(facies, perm_table, line_breaks):
    nz, nx, ny = facies.shape
    stages = (lax.axis_size("gz") - 1).bit_length() - 1
    i32, f32 = jnp.int32, jnp.float32
    two = lax.axis_size("gx") == 2
    layers = 2 * nz
    cut_rows = -(-(layers + 1 + 2 * stages) // 8) * 8
    sides = 1 if two else 2
    facies, *rows = kernel_call(
        pack_kernel,
        [((nz, nx, ny), i32)] + [((nz * 4, ny), i32)] * sides,
        [facies],
    )
    other = swapped(facies, 0)
    if two:
        rims = [ring(rows[0], "gx", 1), slanted(rows[0], 1)]
    else:
        rims = [ring(rows[1], "gx", 1), ring(rows[0], "gx", -1)]
        rims += [slanted(rows[1], 1), slanted(rows[0], -1)]
    k, table, cuts = kernel_call(
        functools.partial(prepare_kernel, stages),
        [((3, nz, nx, ny), f32), ((3, 8, ny), f32), ((cut_rows, ny), f32)],
        [perm_table, line_breaks, facies],
        smem=2,
        cost=pl.CostEstimate(flops=10**7, bytes_accessed=10**6, transcendentals=0),
    )
    strip, *rows = kernel_call(
        merge_kernel,
        [((2 * nx + 16, ny), i32)] + [((layers * 4, ny), i32)] * sides,
        [facies, other, table] + rims,
    )
    k, = kernel_call(
        prepare_other_kernel,
        [((3, layers, nx, ny), f32)],
        [table, k, other, strip],
        cost=pl.CostEstimate(flops=10**7, bytes_accessed=10**6, transcendentals=0),
    )
    y_low, y_high = ring(strip, "gy", 1), ring(strip, "gy", -1)
    sizes = nz, nx, ny
    operands = [table, cuts, k, rows[0], rows[-1], y_low, y_high]
    scratch = [pltpu.VMEM((3, layers * 4, ny), f32)] * sides
    return (sweep_ends if stages == 1 else sweep_tree)(sizes, stages, operands, scratch)


def sweep_ends(sizes, stages, operands, scratch):
    nz, nx, ny = sizes
    layers, f32 = 2 * nz, jnp.float32
    cuts = operands[1]
    slab, tall = (nx + 8, 2 * ny), (2, nx + 24, ny)

    def slabs(*count):
        return (count + slab, f32)

    def talls(*count):
        return (count + tall, f32)

    def message_of(count, halo):
        return ((Message(count, halo, nx, ny).rows, ny), f32)

    def filler(flops):
        return pl.CostEstimate(flops=flops, bytes_accessed=10**6, transcendentals=0)

    message, own, lx, ly, lz, d, ratio, inverse = kernel_call(
        end_eliminate_kernel,
        [message_of(LAST_COUNT, 2), slabs(LAST_COUNT), talls(layers), slabs(layers),
         slabs(layers + 1), slabs(3, layers), slabs(layers), slabs(layers)],
        operands,
        [pltpu.VMEM(*s) for s in (talls(layers), talls(layers), slabs(layers), slabs(layers),
                                  slabs(2, layers), slabs(layers))] + scratch,
    )
    other = swapped(message, stages)
    base, phi, parts = kernel_call(
        expand_kernel,
        [talls(3, layers), talls(layers), slabs(6)],
        [cuts, lx, ly, lz, d, ratio],
        cost=filler(10**7),
    )
    message, near = kernel_call(
        functools.partial(end_join_kernel, layers),
        [message_of(3, 1), slabs(13)],
        [cuts, own, other, parts],
    )
    other = swapped(message, stages)
    first, change = kernel_call(
        correct_kernel,
        [talls(3, layers), slabs(3, layers)],
        [cuts, near, lx, ly, lz, ratio, inverse, base, phi],
        [pltpu.VMEM(*slabs(3, layers))],
        cost=filler(10**7),
    )
    out = ((3, nz, nx, ny), f32)
    return tuple(kernel_call(
        end_final_kernel,
        [out, out],
        [cuts, other, near, lx, ly, lz, phi, first, change],
        [pltpu.VMEM(*talls(3, nz + 2)), pltpu.VMEM(*out), pltpu.VMEM(*out),
         pltpu.SemaphoreType.DMA((2, nz // CHUNK))],
        space=pl.ANY,
    ))


def sweep_tree(sizes, stages, operands, scratch):
    nz, nx, ny = sizes
    layers, f32 = 2 * nz, jnp.float32
    cuts = operands[1]
    slab = (nx + 8, 2 * ny)
    one, three = ((layers,) + slab, f32), ((3, layers) + slab, f32)

    def slabs(count):
        return ((count,) + slab, f32)

    def message_of(count, halo):
        return ((Message(count, halo, nx, ny).rows, ny), f32)

    message, own, pair, lx, ly, lz, d, e, inverse = kernel_call(
        functools.partial(eliminate_kernel, stages),
        [message_of(LAST_COUNT if stages == 1 else FIRST_COUNT, 2)]
        + [slabs(FIRST_COUNT), slabs(PAIR_COUNT)]
        + [one] * 3 + [three, one, one],
        operands,
        [pltpu.VMEM(s, f32) for s in (three[0], one[0], (2,) + one[0], one[0])]
        + scratch,
    )
    siblings, factors, group = [], [], own
    for s in range(stages - 1):
        last = s == stages - 2
        outputs = [slabs(FIRST_COUNT), slabs(7), message_of(LAST_COUNT if last else FIRST_COUNT, 2)]
        sibling, factor, message, *joined = kernel_call(
            functools.partial(join_kernel, s, last, layers + 1),
            outputs + ([] if last else [slabs(FIRST_COUNT)]),
            [cuts, group, swapped(message, s + 1)],
        )
        siblings.append(sibling)
        factors.append(factor)
        group = None if last else joined[0]
    fields = ((3, layers + 2) + slab, f32)
    message, own, rights, d2, kept, ends, first = kernel_call(
        functools.partial(middle_kernel, stages),
        [message_of(3 if stages == 1 else SECOND_COUNT, 1), slabs(SECOND_COUNT), slabs(6), three,
         slabs(2 * stages + 5), slabs(3), fields],
        [cuts, own, pair] + siblings + [swapped(message, stages)]
        + [lx, ly, lz, d, e, inverse],
    )
    siblings, group = [], own
    for s in range(stages - 1):
        last = s == stages - 2
        outputs = [slabs(SECOND_COUNT), message_of(3 if last else SECOND_COUNT, 1)]
        sibling, message, *joined = kernel_call(
            functools.partial(join_again_kernel, s, last),
            outputs + ([] if last else [slabs(SECOND_COUNT)]),
            [group, swapped(message, s + 1), factors[s]],
        )
        siblings.append(sibling)
        group = None if last else joined[0]
    out = ((3, nz, nx, ny), f32)
    pressure, residual = kernel_call(
        functools.partial(final_kernel, stages),
        [out, out],
        [cuts, own, pair] + siblings + [swapped(message, stages)]
        + [lx, ly, lz, first, rights, d2, e, inverse, kept, ends],
        [pltpu.VMEM((3, nz + 2) + slab, f32)]
        + [pltpu.VMEM((3, nz, nx, ny), f32)] * 2
        + [pltpu.SemaphoreType.DMA((2, nz // CHUNK))],
        space=pl.ANY,
    )
    return pressure, residual


def solution(mesh):
    return jax.shard_map(
        per_device,
        mesh=mesh,
        in_specs=(P("gz", "gx", "gy"), P(), P()),
        out_specs=(P(None, "gz", "gx", "gy"), P(None, "gz", "gx", "gy")),
        check_vma=False,
    )
```

```python
import functools

import jax
import jax.numpy as jnp
from jax import lax
from jax.experimental import pallas as pl
from jax.experimental.pallas import tpu as pltpu
from jax.sharding import PartitionSpec as P


WIDE = 3
FIRST_COUNT = 11
LAST_COUNT = 5
SECOND_COUNT = 6
PAIR_COUNT = 16
CHUNK = 4


def moved(values, amount, axis):
    size = values.shape[axis]
    amount = amount % size
    if amount == 0:
        return values
    return pltpu.roll(values, amount, axis)


def flag(condition):
    return condition.astype(jnp.float32)


def iotas(rows, lanes):
    return tuple(lax.broadcasted_iota(jnp.int32, (rows, lanes), d) for d in (0, 1))


def choose(condition, first, second):
    return [jnp.where(condition, a, b) for a, b in zip(first, second)]


def flipped(flips):
    return is_high(0) if flips else False


def is_high(stage):
    return (lax.axis_index("gz") >> (stage + 1)) % 2 == 1


def own_start(nz):
    return (lax.axis_index("gz") % 2) * nz


def pack_kernel(facies_ref, copy_ref, *row_refs):
    nz, nx, ny = facies_ref.shape
    copy_ref[...] = facies_ref[...]
    row = iotas(8, ny)[0]
    for z in range(0, nz, 2):
        pair = [facies_ref[z], facies_ref[z + 1]]
        first = jnp.where(row < 4, pair[0][:8], moved(pair[1][:8], 4, 0))
        last = jnp.where(row < 4, moved(pair[0][nx - 8 :], 4, 0), pair[1][nx - 8 :])
        spot = slice(4 * z, 4 * z + 8)
        if len(row_refs) == 1:
            row_refs[0][spot, :] = jnp.where(lax.axis_index("gx") == 0, last, first)
        else:
            row_refs[0][spot, :] = first
            row_refs[1][spot, :] = last


def rim_tile(low, high, layer):
    row = iotas(8, low.shape[1])[0]
    if layer % 2 == 0:
        return jnp.where(row < 4, high, moved(low, 4, 0))
    return jnp.where(row < 4, moved(high, 4, 0), low)


def merge_kernel(own_ref, other_ref, table_ref, *refs):
    sides = (len(refs) - 1) // 3
    ins, strip_ref, row_refs = refs[: 2 * sides], refs[2 * sides], refs[2 * sides + 1 :]
    nz, nx, ny = own_ref.shape
    swap = own_start(nz) > 0
    lane = lax.broadcasted_iota(jnp.int32, (nx + 8, ny), 1)
    for b in range(2):
        own = swap == (b == 1)
        for n, ref in enumerate(row_refs):
            ref[4 * nz * b : 4 * nz * (b + 1), :] = jnp.where(own, ins[n][...], ins[sides + n][...])
        strip = jnp.zeros((nx + 8, ny), jnp.int32)
        for z in range(nz):
            start = 4 * nz * b + z // 2 * 8
            low, high = [ref[start : start + 8, :] for ref in (row_refs[0], row_refs[-1])]
            layer = jnp.where(own, own_ref[z], other_ref[z])
            layer = jnp.concatenate([layer, rim_tile(low, high, z)], axis=0)
            strip = jnp.where(lane // 8 == z, moved(layer, 8 * z + WIDE, 1), strip)
        strip_ref[b * (nx + 8) : (b + 1) * (nx + 8), :] = strip


def lookup(table, index):
    rows = [
        jnp.take_along_axis(table, index[r : r + 8], axis=1) for r in range(0, index.shape[0], 8)
    ]
    return jnp.concatenate(rows, axis=0)


def prepare_kernel(stages, table, breaks, facies_ref, k_ref, table_ref, cut_ref):
    nz, nx, ny = facies_ref.shape
    lane = iotas(8, ny)[1]
    tables = []
    for q in range(3):
        values = jnp.zeros((8, ny), jnp.float32)
        for label in range(table.shape[1]):
            values = jnp.where(lane == label, table[q, label], values)
        if stages == 1:
            values = 2.0 * values
        table_ref[q] = values
        tables.append(values)
    for z in range(nz):
        for q in range(3):
            k_ref[q, z] = lookup(tables[q], facies_ref[z])
    pair = lax.axis_index("gz") // 2
    layers = [pair * 2 * nz + r - 1 for r in range(2 * nz + 1)]
    if stages == 1:
        high = is_high(0)
        layers = [
            pair * 2 * nz + jnp.where(high, 2 * nz - 1 - r, r - 1) for r in range(2 * nz + 1)
        ]
    for s in range(stages if stages > 1 else 0):
        base, size = (pair >> (s + 1)) << (s + 1), 2**s
        layers.append((base + size) * 2 * nz - 1)
        layers.append(jnp.where(is_high(s), base, base + 2 * size) * 2 * nz - 1)
    for r, layer in enumerate(layers):
        cut = breaks[jnp.clip(layer, 0, breaks.shape[0] - 1)].astype(jnp.float32)
        cut_ref[r : r + 1, :] = jnp.full((1, ny), cut, jnp.float32)


def prepare_other_kernel(sides, flips, table_ref, own_ref, other_ref, *refs):
    rows, k_ref, row_refs = refs[:sides], refs[sides], refs[sides + 1 :]
    nz, _, ny = other_ref.shape
    start, flip = own_start(nz), flipped(flips)

    def spot(at, count):
        return jnp.where(flip, count - 1 - at, at)

    for q in range(3):
        for z in range(nz):
            k_ref[q, spot(start + z, 2 * nz)] = own_ref[q, z]
            k_ref[q, spot(nz - start + z, 2 * nz)] = lookup(table_ref[q], other_ref[z])
        for n in range(sides):
            for t in range(nz):
                tile = lookup(table_ref[q], rows[n][8 * t : 8 * t + 8, :])
                tile = jnp.where(flip, moved(tile, 4, 0), tile)
                row_refs[n][q, pl.ds(pl.multiple_of(8 * spot(t, nz), 8), 8), :] = tile


def face(a, b):
    product = a * b
    total = a + b
    harmonic = 2.0 * product / total
    inside = product > 0.0
    link = jnp.where(inside, harmonic, 0.0)
    flow = jnp.where(inside, harmonic, total)
    tau = jnp.where(inside, harmonic, 2.0 * total)
    return link, flow, tau


class Message:
    def __init__(self, count, halo, nx, ny):
        self.count, self.halo, self.nx, self.ny = count, halo, nx, ny
        self.one_sided = lax.axis_size("gx") == 2
        self.rows_each = halo if self.one_sided else 2 * halo
        self.per_tile = 8 // self.rows_each
        self.tiles = -(-count // self.per_tile)
        self.abreast = ny // (2 * halo * count)
        strips = -(-(nx // 8 + 1) // self.abreast)
        self.sides = count * nx + 8 * strips
        self.rows = self.sides + 8 * self.tiles

    def strip(self, t, q):
        start = self.count * self.nx + 8 * (t // self.abreast)
        shift = 2 * self.halo * (self.count * (t % self.abreast) + q) + self.halo
        return slice(start, start + 8), shift

    def tile(self, q):
        start = self.sides + 8 * (q // self.per_tile)
        return slice(start, start + 8)

    def side_moved(self, tile, q, sign):
        part = q % self.per_tile
        if not self.one_sided:
            return moved(tile, sign * (self.rows_each * part + self.halo), 0)
        first = lax.axis_index("gx") == 0
        out = jnp.where(
            first,
            moved(tile, sign * self.halo * part, 0),
            moved(tile, sign * self.halo * (part + 1), 0),
        )
        if sign > 0:
            return out
        row = iotas(8, self.ny)[0]
        return jnp.where(jnp.where(first, row, 7 - row) < self.halo, out, 1.0)

    def write(self, ref, slabs):
        nx, ny, halo = self.nx, self.ny, self.halo
        row, lane = iotas(8, ny)
        strips = {}
        for t in range(nx // 8 + 1):
            for q, slab in enumerate(slabs):
                spot, shift = self.strip(t, q)
                turned = moved(slab[8 * t : 8 * t + 8, ny:], shift, 1)
                held = strips.get(spot.start, turned)
                strips[spot.start] = jnp.where(lane < shift - halo, held, turned)
        for start, strip in strips.items():
            ref[start : start + 8, :] = strip
        for q, slab in enumerate(slabs):
            ref[q * nx : (q + 1) * nx, :] = slab[:nx, :ny]
            turned = self.side_moved(slab[nx:, :ny], q, 1)
            part = q % self.per_tile
            tile = turned if part == 0 else jnp.where(row < self.rows_each * part, tile, turned)
            if part == self.per_tile - 1 or q == self.count - 1:
                ref[self.tile(q), :] = tile

    def read(self, ref):
        nx = self.nx
        slabs = []
        for q in range(self.count):
            side = self.side_moved(ref[self.tile(q), :], q, -1)
            body = jnp.concatenate([ref[q * nx : (q + 1) * nx, :], side], axis=0)
            beside = []
            for t in range(nx // 8 + 1):
                spot, shift = self.strip(t, q)
                beside.append(moved(ref[spot, :], -shift, 1))
            slabs.append(jnp.concatenate([body, jnp.concatenate(beside, axis=0)], axis=1))
        return slabs


def open_after(cut_ref, r):
    cut = 1.0 - cut_ref[r : r + 1, :]
    return jnp.concatenate([cut, cut], axis=1)


def slab_size(ref):
    return ref.shape[-2] - 8, ref.shape[-1] // 2


def join(low, high, opened):
    ends = link, flow, tau = face(low[4], high[3])
    coupling = link * opened
    inverse = 1.0 / (low[2] + tau)
    step = coupling * inverse
    last_inverse = 1.0 / (high[0] + tau - coupling * step)
    outer = low[1] * inverse
    weight = step * low[1]
    weight_low, weight_high = weight * last_inverse, high[1] * last_inverse
    right_low = low[8:10] + [low[10] + flow]
    right_high = high[5:7] + [high[7] - flow]
    s_uu = low[0] - outer * low[1] - weight * weight_low
    s_uv = -weight * weight_high
    s_vv = high[2] - high[1] * weight_high
    factors = [outer, step, weight_low, weight_high, inverse, last_inverse]
    g_u, g_v, middle = join_right(factors, low[5:8], right_low, right_high, high[8:11])
    return [s_uu, s_uv, s_vv, low[3], high[4]] + g_u + g_v, factors, right_low + middle, ends


def join_right(factors, low_u, low_v, high_u, high_v):
    outer, step, weight_low, weight_high = factors[:4]
    middle = [b + step * a for a, b in zip(low_v, high_u)]
    g_u = [g - outer * a - weight_low * m for g, a, m in zip(low_u, low_v, middle)]
    g_v = [g - weight_high * m for g, m in zip(high_v, middle)]
    return g_u, g_v, middle


def join_inner(factors, right_low, middle, first, last):
    outer, step, weight_low, weight_high, inverse, last_inverse = factors
    high = last_inverse * middle - weight_low * first - weight_high * last
    return inverse * right_low - outer * first + step * high, high


def reduce_end(slabs, top):
    s_uu, s_uv, s_vv, k_u, k_v = slabs[:5]
    far_s, near_s = choose(top, [s_vv, s_uu], [s_uu, s_vv])
    far_k, near_k = choose(top, [k_v, k_u], [k_u, k_v])
    sign = jnp.where(top, 1.0, -1.0)
    factor = s_uv / (far_s + 2.0 * far_k)
    g_u, g_v = slabs[5:8], slabs[8:11]
    far_g, near_g = choose(top, g_v, g_u), choose(top, g_u, g_v)
    far_g[2] = far_g[2] + far_k * sign
    return [near_s - s_uv * factor, near_k] + [n - factor * g for n, g in zip(near_g, far_g)], factor


def reduce_end_right(factor, g_u, g_v, top):
    far_g, near_g = choose(top, g_v, g_u), choose(top, g_u, g_v)
    return [n - factor * g for n, g in zip(near_g, far_g)]


def grid_masks(nx, ny):
    at_x, at_y = lax.axis_index("gx"), lax.axis_index("gy")
    has_x_low, has_x_high = at_x > 0, at_x < lax.axis_size("gx") - 1
    has_y_low, has_y_high = at_y > 0, at_y < lax.axis_size("gy") - 1
    row, lane = iotas(nx + 8, 2 * ny)
    x_in = (row < nx) | ((row < nx + WIDE) & has_x_high) | ((row >= nx + 8 - WIDE) & has_x_low)
    y_in = (lane < ny) | ((lane < ny + WIDE) & has_y_high)
    y_in = y_in | ((lane >= 2 * ny - WIDE) & has_y_low)
    cell = x_in & y_in
    valid = flag(cell)
    in_x, in_xp = valid * moved(valid, -1, 0), valid * moved(valid, 1, 0)
    in_y, in_yp = valid * moved(valid, -1, 1), valid * moved(valid, 1, 1)
    return cell, in_x, in_xp, in_y, in_yp


def rim_columns(flips, tables, y_low, y_high, cell):
    ny = cell.shape[1] // 2
    size = cell.shape[0]
    strip_in = cell[:, ny:]
    lane = iotas(size, ny)[1]
    strips = []
    for b in range(2):
        part = slice(b * size, (b + 1) * size)
        strips.append(jnp.where(lane % 8 < WIDE, y_low[part, :], y_high[part, :]))
    flip, nz = flipped(flips), ny // 8
    if flips:
        strips = choose(flip, strips[::-1], strips)
    strips = [[lookup(table, strip) for table in tables] for strip in strips]

    def beside(q, at):
        z, strip = at % nz, strips[at // nz][q]
        if flips:
            turned = pltpu.roll(strip, ny - WIDE - 8 * jnp.where(flip, nz - 1 - z, z), 1)
        else:
            turned = moved(strip, -(8 * z + WIDE), 1)
        return jnp.where(strip_in, turned, 0.0)

    return beside


def body_rows(k_ref, low_ref, high_ref, q, at, row_in):
    spot = slice(at // 2 * 8, at // 2 * 8 + 8)
    side = rim_tile(low_ref[q, spot, :], high_ref[q, spot, :], at)
    return jnp.concatenate([k_ref[q, at], jnp.where(row_in, side, 0.0)], axis=0)


def flow_after(here, there, inside):
    total = here + there
    return jnp.where(inside > 0.0, 2.0 * (here * there) / total, total)


def tau_and_source(flow, back, inside, inside_back):
    return flow * (2.0 - inside) + back * (2.0 - inside_back), flow - back


def eliminate_kernel(
    stages, table_ref, cut_ref, k_ref, row_low, row_high, y_low, y_high,
    message_ref, own_ref, pair_ref, lx_ref, ly_ref, lz_ref, d_ref, e_ref, inverse_ref,
    all_ref, flow_ref, source_ref, centre_ref,
):
    layers, nx, ny = k_ref.shape[1:]
    nz = layers // 2
    cell, in_x, in_xp, in_y, in_yp = grid_masks(nx, ny)
    beside = rim_columns(False, [table_ref[q] for q in range(3)], y_low, y_high, cell)
    for at in range(layers):
        for q in range(3):
            body = body_rows(k_ref, row_low, row_high, q, at, cell[nx:, :ny])
            all_ref[q, at] = jnp.concatenate([body, beside(q, at)], axis=1)
    for at in range(layers):
        kx, ky = all_ref[0, at], all_ref[1, at]
        flow_x = flow_after(kx, moved(kx, -1, 0), in_x)
        flow_ref[at] = flow_after(ky, moved(ky, -1, 1), in_y)
        lx_ref[at] = flow_x * in_x
        centre_ref[at], source_ref[0, at] = tau_and_source(
            flow_x, moved(flow_x, 1, 0), in_x, in_xp
        )
        if at % nz < nz - 1:
            kz, above = all_ref[2, at], all_ref[2, at + 1]
            lz_ref[at] = jnp.where(cell, 2.0 * (kz * above) / (kz + above), 0.0)
    for at in range(layers):
        flow_y = flow_ref[at]
        ly_ref[at] = flow_y * in_y
        tau_y, source_ref[1, at] = tau_and_source(
            flow_y, moved(flow_y, 1, 1), in_y, in_yp
        )
        centre = centre_ref[at] + tau_y
        if at % nz > 0:
            centre = centre + lz_ref[at - 1]
        if at % nz < nz - 1:
            centre = centre + lz_ref[at]
        centre_ref[at] = jnp.where(cell, centre, 1.0)

    states = [{}, {}]
    for z in range(nz):
        for b in range(2):
            at, v = b * nz + z, states[b]
            centre = centre_ref[at]
            sources = [source_ref[0, at], source_ref[1, at]]
            if z == 0:
                v["source"] = sources + [lz_ref[at]]
                v["s_uu"], v["g_u"] = centre, v["source"]
            elif z == nz - 1:
                sources = sources + [-lz_ref[at - 1]]
                v["s_vv"] = centre - v["coupling"] * v["ratio"]
                v["s_uv"] = -v["coupling"] * v["spike"]
                v["g_v"] = [a + v["coupling"] * d for a, d in zip(sources, v["value"])]
            else:
                forward = sources + [lz_ref[at] - lz_ref[at - 1]]
                if z == 1:
                    pivot, numerator = centre, v["coupling"]
                else:
                    pivot = centre - v["coupling"] * v["ratio"]
                    forward = [a + v["coupling"] * d for a, d in zip(forward, v["value"])]
                    numerator = v["coupling"] * v["spike"]
                inverse = 1.0 / pivot
                v["value"] = [a * inverse for a in forward]
                v["spike"] = numerator * inverse
                v["s_uu"] = v["s_uu"] - numerator * v["spike"]
                v["g_u"] = [g + v["spike"] * a for g, a in zip(v["g_u"], forward)]
                inverse_ref[at] = inverse
                e_ref[at] = v["spike"]
                for f in range(3):
                    d_ref[f, at] = v["value"][f]
            if z < nz - 1:
                v["coupling"] = lz_ref[at] * open_after(cut_ref, at + 1)
                if z > 0:
                    v["ratio"] = v["coupling"] * inverse

    def block(b):
        v = states[b]
        k_ends = [all_ref[2, b * nz], all_ref[2, b * nz + nz - 1]]
        return [v["s_uu"], v["s_uv"], v["s_vv"]] + k_ends + v["g_u"] + v["g_v"]

    slabs, factors, rights, ends = join(block(0), block(1), open_after(cut_ref, nz))
    for q, slab in enumerate(slabs):
        own_ref[q] = slab
    for n, slab in enumerate(factors + rights + list(ends)):
        pair_ref[n] = slab
    if stages == 1:
        slabs, pair_ref[PAIR_COUNT - 1] = reduce_end(slabs, is_high(0))
    Message(len(slabs), 2, nx, ny).write(message_ref, slabs)


def join_kernel(stage, last, base, cut_ref, own_ref, message_ref, sibling_ref, factor_ref, next_ref, *joined):
    nx, ny = slab_size(own_ref)
    own = [own_ref[q] for q in range(FIRST_COUNT)]
    sibling = Message(FIRST_COUNT, 2, nx, ny).read(message_ref)
    for q, slab in enumerate(sibling):
        sibling_ref[q] = slab
    high = is_high(stage)
    slabs, factors, _, _ = join(
        choose(high, sibling, own),
        choose(high, own, sibling),
        open_after(cut_ref, base + 2 * stage),
    )
    for n, values in enumerate(factors):
        factor_ref[n] = values
    if last:
        slabs, factor_ref[6] = reduce_end(slabs, is_high(stage + 1))
    else:
        for q, slab in enumerate(slabs):
            joined[0][q] = slab
    Message(len(slabs), 2, nx, ny).write(next_ref, slabs)


def join_again_kernel(stage, last, own_ref, message_ref, factor_ref, sibling_ref, next_ref, *joined):
    nx, ny = slab_size(own_ref)
    own = [own_ref[q] for q in range(SECOND_COUNT)]
    sibling = Message(SECOND_COUNT, 1, nx, ny).read(message_ref)
    for q, slab in enumerate(sibling):
        sibling_ref[q] = slab
    above = is_high(stage)
    low, high = choose(above, sibling, own), choose(above, own, sibling)
    factors = [factor_ref[n] for n in range(6)]
    g_u, g_v, _ = join_right(factors, low[:3], low[3:], high[:3], high[3:])
    slabs = g_u + g_v
    if last:
        slabs = reduce_end_right(factor_ref[6], g_u, g_v, is_high(stage + 1))
    else:
        for q, slab in enumerate(slabs):
            joined[0][q] = slab
    Message(len(slabs), 1, nx, ny).write(next_ref, slabs)


def stencil(slab, link_x, link_y):
    return (
        link_x * moved(slab, -1, 0)
        + moved(link_x * slab, 1, 0)
        + (link_y * moved(slab, -1, 1) + moved(link_y * slab, 1, 1))
    )


def beyond_cuts(cut_ref, at, link_low, link_high):
    low, high = cut_ref[pl.ds(at, 1), :], cut_ref[pl.ds(at + 1, 1), :]
    return (
        link_low * jnp.concatenate([low, low], axis=1),
        link_high * jnp.concatenate([high, high], axis=1),
    )


def left_out(field_ref, f, at, link_x, link_y, cuts):
    return stencil(field_ref[f, at + 1], link_x, link_y) + (
        cuts[0] * field_ref[f, at] + cuts[1] * field_ref[f, at + 2]
    )


def middle_kernel(stages, cut_ref, *refs):
    own_ref, pair_ref, siblings, message_ref = refs[0], refs[1], refs[2 : stages + 1], refs[stages + 1]
    refs = refs[stages + 2 :]
    lx_ref, ly_ref, lz_ref, d_ref, e_ref, inverse_ref = refs[:6]
    next_ref, own2_ref, right_ref, d2_ref, factor_ref, end_ref, first_ref = refs[6:]
    layers = lx_ref.shape[0]
    nz = layers // 2
    nx, ny = slab_size(lx_ref)
    own = [own_ref[q] for q in range(FIRST_COUNT)]
    slots = []

    def keep(values):
        factor_ref[len(slots)] = values
        slots.append(None)

    def attach(state, sign, row, pivot, right, k):
        beside, k_beside, rights, exists = state[0], state[1], state[2:5], state[5]
        link, flow, tau = face(k_beside * exists, k)
        coupling = link * open_after(cut_ref, row)
        rights = rights[:2] + [rights[2] + sign * flow]
        inverse = 1.0 / (beside + tau)
        step = coupling * inverse
        right = [a + step * b for a, b in zip(right, rights)]
        right[2] = right[2] - sign * flow
        return pivot + tau - coupling * step, right, step, inverse, rights, (link, flow, tau)

    far = Message(LAST_COUNT, 2, nx, ny).read(message_ref)
    top = is_high(stages - 1)
    below, above = far + [flag(top)], far + [flag(jnp.logical_not(top))]
    for s in range(stages - 2, -1, -1):
        up = is_high(s)
        block = [siblings[s][q] for q in range(FIRST_COUNT)]
        sign = jnp.where(up, 1.0, -1.0)
        state = choose(up, below, above)
        far_s, far_k, near_s, near_k = choose(
            up, [block[0], block[3], block[2], block[4]], [block[2], block[4], block[0], block[3]]
        )
        far_g = choose(up, block[5:8], block[8:11])
        near_g = choose(up, block[8:11], block[5:8])
        row = layers + 2 + 2 * s
        pivot, right, step, _, _, _ = attach(state, sign, row, far_s, far_g, far_k)
        factor = block[1] / pivot
        keep(step)
        keep(factor)
        state = [near_s - block[1] * factor, near_k]
        state += [n - factor * r for n, r in zip(near_g, right)] + [jnp.float32(1.0)]
        below, above = choose(up, state, below), choose(up, above, state)

    pivot_u, right_u, step_b, inverse_b, rights_b, ends_b = attach(
        below, 1.0, 0, own[0], own[5:8], own[3]
    )
    pivot_v, right_v, step_a, inverse_a, rights_a, ends_a = attach(
        above, -1.0, layers, own[2], own[8:11], own[4]
    )
    held_b, held_a = inverse_b * below[5], inverse_a * above[5]
    inverse_u = 1.0 / pivot_u
    factor = own[1] * inverse_u
    inverse_v = 1.0 / (pivot_v - own[1] * factor)
    for values in (step_b, held_b, step_a, held_a, inverse_u, factor, inverse_v):
        keep(values)
    pair = [pair_ref[n] for n in range(PAIR_COUNT)]
    inner = pair[:6]
    ends = [ends_b[0], pair[12], ends_a[0]]
    for n, values in enumerate(ends):
        end_ref[n] = values

    for f in range(3):
        last = (right_v[f] - factor * right_u[f]) * inverse_v
        first_u = right_u[f] * inverse_u - factor * last
        low_v, high_u = join_inner(inner, pair[6 + f], pair[9 + f], first_u, last)
        first_ref[f, 0] = rights_b[f] * held_b + step_b * first_u
        first_ref[f, layers + 1] = rights_a[f] * held_a + step_a * last
        first_ref[f, 1] = first_u
        first_ref[f, nz] = low_v
        first_ref[f, nz + 1] = high_u
        first_ref[f, layers] = last
    for z in range(nz - 2, 0, -1):
        for at in (z, nz + z):
            ratio = lz_ref[at] * open_after(cut_ref, at + 1) * inverse_ref[at]
            spike = e_ref[at]
            for f in range(3):
                first_ref[f, at + 1] = (
                    d_ref[f, at]
                    + spike * first_ref[f, 1 + at - z]
                    + ratio * first_ref[f, at + 2]
                )

    def block(b):
        for z in range(nz):
            at = b * nz + z
            cuts = beyond_cuts(
                cut_ref, at,
                ends[b] if z == 0 else lz_ref[at - 1],
                ends[b + 1] if z == nz - 1 else lz_ref[at],
            )
            right = [left_out(first_ref, f, at, lx_ref[at], ly_ref[at], cuts) for f in range(3)]
            if z == 0:
                g_u = list(right)
            else:
                if z == 1:
                    forward = right
                else:
                    forward = [right[f] + coupling * value[f] for f in range(3)]
                if z < nz - 1:
                    inverse, spike = inverse_ref[at], e_ref[at]
                    value = [forward[f] * inverse for f in range(3)]
                    g_u = [g_u[f] + spike * forward[f] for f in range(3)]
                    for f in range(3):
                        d2_ref[f, at] = value[f]
                    coupling = lz_ref[at] * open_after(cut_ref, at + 1)
        return g_u, forward

    (low_u, low_v), (high_u, high_v) = block(0), block(1)
    g_u, g_v, middle = join_right(inner, low_u, low_v, high_u, high_v)
    for n, slab in enumerate(low_v + middle):
        right_ref[n] = slab
    for q, slab in enumerate(g_u + g_v):
        own2_ref[q] = slab
    slabs = g_u + g_v
    if stages == 1:
        slabs = reduce_end_right(pair[PAIR_COUNT - 1], g_u, g_v, is_high(0))
    Message(len(slabs), 1, nx, ny).write(next_ref, slabs)


def final_kernel(stages, cut_ref, *refs):
    own_ref, pair_ref, siblings, message_ref = refs[0], refs[1], refs[2 : stages + 1], refs[stages + 1]
    refs = refs[stages + 2 :]
    lx_ref, ly_ref, lz_ref, first_ref, right_ref, d2_ref, e_ref, inverse_ref = refs[:8]
    factor_ref, end_ref, pressure_out, residual_out = refs[8:12]
    change_ref, pressure_ref, residual_ref, sems = refs[12:]
    nz = lx_ref.shape[0] // 2
    nx, ny = slab_size(lx_ref)
    own = [own_ref[q] for q in range(SECOND_COUNT)]
    slots = []

    def kept():
        slots.append(None)
        return factor_ref[len(slots) - 1]

    below = above = Message(3, 1, nx, ny).read(message_ref)
    for s in range(stages - 2, -1, -1):
        up = is_high(s)
        block = [siblings[s][q] for q in range(SECOND_COUNT)]
        state = choose(up, below, above)
        far_g = choose(up, block[:3], block[3:])
        near_g = choose(up, block[3:], block[:3])
        step, factor = kept(), kept()
        right = [a + step * b for a, b in zip(far_g, state)]
        state = [n - factor * r for n, r in zip(near_g, right)]
        below, above = choose(up, state, below), choose(up, above, state)
    step_b, held_b, step_a, held_a = kept(), kept(), kept(), kept()
    inverse_u, factor, inverse_v = kept(), kept(), kept()
    inner = [pair_ref[n] for n in range(6)]
    start = own_start(nz)
    high = start > 0
    for f in range(3):
        right_u = own[f] + step_b * below[f]
        right_v = own[3 + f] + step_a * above[f]
        last = (right_v - factor * right_u) * inverse_v
        first = right_u * inverse_u - factor * last
        low_v, high_u = join_inner(inner, right_ref[f], right_ref[3 + f], first, last)
        beyond_b = below[f] * held_b + step_b * first
        beyond_a = above[f] * held_a + step_a * last
        values = choose(high, [low_v, high_u, last, beyond_a], [beyond_b, first, low_v, high_u])
        for at, slab in zip((0, 1, nz, nz + 1), values):
            change_ref[f, at] = slab
    ends = choose(high, [end_ref[1], end_ref[2]], [end_ref[0], end_ref[1]])
    for z in range(nz - 2, 0, -1):
        at = start + z
        opened = 1.0 - cut_ref[pl.ds(at + 1, 1), :]
        opened = jnp.concatenate([opened, opened], axis=1)
        ratio = lz_ref[at] * opened * inverse_ref[at]
        spike = e_ref[at]
        for f in range(3):
            change_ref[f, z + 1] = (
                d2_ref[f, at] + spike * change_ref[f, 1] + ratio * change_ref[f, z + 2]
            )
    own_part = (slice(0, nx), slice(0, ny))
    copies = []
    for z in range(nz):
        at = start + z
        cuts = beyond_cuts(
            cut_ref, at,
            ends[0] if z == 0 else lz_ref[at - 1],
            ends[1] if z == nz - 1 else lz_ref[at],
        )
        link_x, link_y = lx_ref[at], ly_ref[at]
        for f in range(3):
            pressure_ref[f, z] = (first_ref[f, at + 1] + change_ref[f, z + 1])[own_part]
            residual_ref[f, z] = left_out(change_ref, f, z, link_x, link_y, cuts)[own_part]
        if (z + 1) % CHUNK == 0:
            part = (slice(None), slice(z + 1 - CHUNK, z + 1))
            for n, (buffer, out) in enumerate(
                ((pressure_ref, pressure_out), (residual_ref, residual_out))
            ):
                copy = pltpu.make_async_copy(
                    buffer.at[part], out.at[part], sems.at[n, z // CHUNK]
                )
                copy.start()
                copies.append(copy)
    for copy in copies:
        copy.wait()


def put(ref, index, slab):
    rows, ny = slab.shape[0], slab.shape[1] // 2
    for h in range(2):
        half = slab[:, h * ny : (h + 1) * ny]
        ref[index + (h, slice(8, 8 + rows))] = half
        ref[index + (h, slice(0, 8))] = half[rows - 8 :]
        ref[index + (h, slice(8 + rows, 16 + rows))] = half[:8]


def get(ref, index, shift=0):
    rows = ref.shape[-2] - 16
    halves = [ref[index + (h, slice(8 + shift, 8 + shift + rows))] for h in range(2)]
    return jnp.concatenate(halves, axis=1)


def signed():
    return jnp.where(is_high(0), -1.0, 1.0)


def both_halves(ref, r):
    values = ref[pl.ds(r, 1), :]
    return jnp.concatenate([values, values], axis=1)


def beside_sum(field_ref, index, lx_ref, ly_ref, j):
    here, link_y = get(field_ref, index), ly_ref[j]
    return (
        get(lx_ref, (j,)) * get(field_ref, index, 1)
        + get(lx_ref, (j,), -1) * get(field_ref, index, -1)
        + (link_y * moved(here, -1, 1) + moved(link_y * here, 1, 1))
    )


def put_half(ref, index, half):
    rows = half.shape[0]
    ref[index + (slice(8, 8 + rows),)] = half
    ref[index + (slice(0, 8),)] = half[rows - 8 :]
    ref[index + (slice(8 + rows, 16 + rows),)] = half[:8]


def harmonic(here, there):
    return here * there / (here + there)


def tau_after(here, there, inside):
    return jnp.where(inside > 0.0, harmonic(here, there), here + there)


def body_kernel(k_ref, row_low, row_high, lx_ref, tau_ref, source_ref, ky_ref, kz_ref, lz_ref):
    layers, nx, ny = k_ref.shape[1:]
    cell, in_x, in_xp = [mask[:, :ny] for mask in grid_masks(nx, ny)[:3]]
    share, share_back = 0.5 + 0.5 * in_x, 0.5 + 0.5 * in_xp
    zero = jnp.zeros((nx + 8, ny), jnp.float32)
    lz_ref[0] = zero
    lz_ref[layers] = zero
    for j in range(layers):
        kx, ky, kz = [body_rows(k_ref, row_low, row_high, q, j, cell[nx:]) for q in range(3)]
        tau = tau_after(kx, moved(kx, -1, 0), in_x)
        back = moved(tau, 1, 0)
        put_half(lx_ref, (j,), tau * in_x)
        tau_ref[j] = tau + back
        source_ref[j] = tau * share - back * share_back
        ky_ref[j] = ky
        kz_ref[j] = kz
        if j > 0:
            lz_ref[j] = jnp.where(cell, harmonic(below, kz), 0.0)
        below = kz


def end_eliminate_kernel(
    table_ref, cut_ref, y_low, y_high, lx_body, tau_body, source_body, ky_body, kz_body, lz_body,
    message_ref, own_ref, lx_ref, ly_ref, lz_ref, d_ref, ratio_ref, inverse_ref,
    kx_ref, tx_ref, ky_ref, kz_ref, source_ref, centre_ref,
):
    layers, size, ny = ky_body.shape
    nx = size - 8
    sign = signed()
    cell, in_x, in_xp, in_y, in_yp = grid_masks(nx, ny)
    share_x, share_xp = 0.5 + 0.5 * in_x[:, ny:], 0.5 + 0.5 * in_xp[:, ny:]
    share_y, share_yp = 0.5 + 0.5 * in_y, 0.5 + 0.5 * in_yp
    side_x, side_in = in_x[:, ny:], cell[:, ny:]
    rows = slice(8, 8 + size)

    def whole(body, side):
        return jnp.concatenate([body, side], axis=1)

    beside = rim_columns(True, [table_ref[q] for q in range(3)], y_low, y_high, cell)
    for j in range(layers):
        put_half(kx_ref, (j,), beside(0, j))
        ky_ref[j] = whole(ky_body[j], beside(1, j))
        kz_ref[j] = beside(2, j)
    lz_ref[0] = jnp.zeros((size, 2 * ny), jnp.float32)
    lz_ref[layers] = jnp.zeros((size, 2 * ny), jnp.float32)
    for j in range(layers):
        tau = tau_after(kx_ref[j, rows, :], kx_ref[j, slice(9, 9 + size), :], side_x)
        put_half(tx_ref, (j,), tau)
        put_half(lx_ref, (j, 1), tau * side_x)
        lx_ref[j, 0] = lx_body[j]
        ky = ky_ref[j]
        ky_ref[j] = tau_after(ky, moved(ky, -1, 1), in_y)
        if j < layers - 1:
            side = jnp.where(side_in, harmonic(kz_ref[j], kz_ref[j + 1]), 0.0)
            lz_ref[j + 1] = whole(lz_body[j + 1], side)
    for j in range(layers):
        tau, back = tx_ref[j, rows, :], tx_ref[j, slice(7, 7 + size), :]
        source_ref[0, j] = whole(source_body[j], tau * share_x - back * share_xp)
        centre = whole(tau_body[j], tau + back)
        tau = ky_ref[j]
        back = moved(tau, 1, 1)
        ly_ref[j] = tau * in_y
        source_ref[1, j] = tau * share_y - back * share_yp
        centre = centre + (tau + back)
        centre = centre + (whole(kz_body[0], kz_ref[0]) if j == 0 else lz_ref[j])
        if j < layers - 1:
            centre = centre + lz_ref[j + 1]
        centre_ref[j] = jnp.where(cell, centre, 1.0)
    for j in range(layers):
        flow_z = -0.5 * whole(kz_body[0], kz_ref[0]) if j == 0 else -lz_ref[j]
        if j < layers - 1:
            flow_z = flow_z + lz_ref[j + 1]
        forward = [source_ref[0, j], source_ref[1, j], sign * flow_z]
        pivot = centre_ref[j]
        if j > 0:
            pivot = pivot - coupling * ratio
            forward = [a + coupling * d for a, d in zip(forward, value)]
        if j < layers - 1:
            inverse = 1.0 / pivot
            coupling = lz_ref[j + 1] * (1.0 - both_halves(cut_ref, j + 1))
            ratio = coupling * inverse
            value = [a * inverse for a in forward]
            inverse_ref[j] = inverse
            ratio_ref[j] = ratio
            for f in range(3):
                d_ref[f, j] = value[f]
    slabs = [pivot, 0.5 * whole(kz_body[layers - 1], kz_ref[layers - 1])] + forward
    for q, slab in enumerate(slabs):
        own_ref[q] = slab
    Message(LAST_COUNT, 2, nx, ny).write(message_ref, slabs)


def expand_kernel(
    cut_ref, lx_ref, ly_ref, lz_ref, d_ref, ratio_ref, base_ref, phi_ref, part_ref
):
    layers = ly_ref.shape[0]
    zero = jnp.zeros(ly_ref.shape[1:], jnp.float32)
    phi, base = zero + 1.0, [zero] * 3
    put(phi_ref, (layers - 1,), phi)
    for f in range(3):
        put(base_ref, (f, layers - 1), zero)
    for j in range(layers - 2, -1, -1):
        ratio = ratio_ref[j]
        phi = ratio * phi
        put(phi_ref, (j,), phi)
        for f in range(3):
            base[f] = d_ref[f, j] + ratio * base[f]
            put(base_ref, (f, j), base[f])
    along_x = along_y = along_z = zero
    parts = [zero] * 3
    for j in range(layers):
        phi = get(phi_ref, (j,))
        along_x = along_x + (get(lx_ref, (j,)) * phi) * get(phi_ref, (j,), 1)
        along_y = along_y + (ly_ref[j] * phi) * moved(phi, -1, 1)
        cut_low = lz_ref[j] * both_halves(cut_ref, j)
        if j < layers - 1:
            cut_high = lz_ref[j + 1] * both_halves(cut_ref, j + 1)
            along_z = along_z + (cut_high * phi) * get(phi_ref, (j + 1,))
        for f in range(3):
            right = beside_sum(base_ref, (f, j), lx_ref, ly_ref, j)
            if j > 0:
                right = right + cut_low * get(base_ref, (f, j - 1))
            if j < layers - 1:
                right = right + cut_high * get(base_ref, (f, j + 1))
            parts[f] = parts[f] + phi * right
    for n, slab in enumerate(parts + [along_x, along_y, 2.0 * along_z]):
        part_ref[n] = slab


def end_join_kernel(layers, cut_ref, own_ref, message_ref, part_ref, next_ref, near_ref):
    nx, ny = slab_size(own_ref)
    own = [own_ref[q] for q in range(LAST_COUNT)]
    other = Message(LAST_COUNT, 2, nx, ny).read(message_ref)
    sign = signed()
    cut = both_halves(cut_ref, layers)
    link, flow, tau = face(own[1], other[1])
    coupling = link * (1.0 - cut)
    inverse_other = 1.0 / (other[0] + tau)
    step = coupling * inverse_other
    inverse = 1.0 / (own[0] + tau - coupling * step)
    right_own = own[2:4] + [own[4] + sign * flow]
    right_other = other[2:4] + [other[4] - sign * flow]
    cut_near = link * cut
    along_x, along_y, along_z = [part_ref[3 + n] for n in range(3)]
    slabs = []
    for f in range(3):
        near = (right_own[f] + step * right_other[f]) * inverse
        beyond = right_other[f] * inverse_other + step * near
        near_ref[f], near_ref[3 + f] = near, beyond
        right = part_ref[f] + stencil(near, along_x, along_y)
        slabs.append(right + (along_z * near + cut_near * beyond))
        near_ref[6 + f] = slabs[f]
    near_ref[9], near_ref[10], near_ref[11], near_ref[12] = step, inverse, inverse_other, link
    Message(3, 1, nx, ny).write(next_ref, slabs)


def correct_kernel(
    cut_ref, near_ref, lx_ref, ly_ref, lz_ref, ratio_ref, inverse_ref, base_ref, phi_ref,
    first_ref, change_ref, d_ref,
):
    layers = ly_ref.shape[0]
    for j in range(layers):
        phi = get(phi_ref, (j,))
        for f in range(3):
            put(first_ref, (f, j), get(base_ref, (f, j)) + phi * near_ref[f])
    for j in range(layers - 1):
        cut_low = lz_ref[j] * both_halves(cut_ref, j)
        cut_high = lz_ref[j + 1] * both_halves(cut_ref, j + 1)
        inverse = inverse_ref[j]
        if j > 0:
            coupling = lz_ref[j] * (1.0 - both_halves(cut_ref, j))
        for f in range(3):
            right = beside_sum(first_ref, (f, j), lx_ref, ly_ref, j)
            right = right + cut_high * get(first_ref, (f, j + 1))
            if j > 0:
                right = right + cut_low * get(first_ref, (f, j - 1)) + coupling * d_ref[f, j - 1]
            d_ref[f, j] = right * inverse
    change = [jnp.zeros(ly_ref.shape[1:], jnp.float32)] * 3
    for f in range(3):
        change_ref[f, layers - 1] = change[f]
    for j in range(layers - 2, -1, -1):
        ratio = ratio_ref[j]
        for f in range(3):
            change[f] = d_ref[f, j] + ratio * change[f]
            change_ref[f, j] = change[f]


def end_final_kernel(
    cut_ref, message_ref, near_ref, lx_ref, ly_ref, lz_ref, phi_ref, first_ref, base_ref,
    pressure_out, residual_out, change_ref, pressure_ref, residual_ref, sems,
):
    layers = ly_ref.shape[0]
    nz = layers // 2
    nx, ny = slab_size(ly_ref)
    high = is_high(0)
    start = jnp.where(high, nz - own_start(nz), own_start(nz))
    beside_other = start > 0
    other = Message(3, 1, nx, ny).read(message_ref)
    step, inverse, inverse_other, link_near = [near_ref[9 + n] for n in range(4)]
    near = [(near_ref[6 + f] + step * other[f]) * inverse for f in range(3)]
    for i in range(-1, nz + 1):
        j = jnp.clip(start + i, 0, layers - 1)
        phi = get(phi_ref, (j,))
        for f in range(3):
            change = base_ref[f, j] + phi * near[f]
            if i == -1:
                change = jnp.where(beside_other, change, 0.0)
            if i == nz:
                beyond = other[f] * inverse_other + step * near[f]
                change = jnp.where(beside_other, beyond, change)
            put(change_ref, (f, i + 1), change)
    lane = iotas(nx, ny)[1]
    first_lane, last_lane = lane == 0, lane == ny - 1

    def body(ref, index, shift=0):
        return ref[index + (0, slice(8 + shift, 8 + shift + nx))]

    def edge(ref, index):
        return ref[index + (1, slice(8, 8 + nx))]

    copies = []
    for i in range(nz):
        j = start + i
        z = jnp.where(high, nz - 1 - i, i)
        link_high = lz_ref[j + 1][:nx, :ny]
        if i == nz - 1:
            link_high = jnp.where(beside_other, link_near[:nx, :ny], link_high)
        cut_low = lz_ref[j][:nx, :ny] * cut_ref[pl.ds(j, 1), :]
        cut_high = link_high * cut_ref[pl.ds(j + 1, 1), :]
        link_x, link_xp = body(lx_ref, (j,)), body(lx_ref, (j,), -1)
        link_y = ly_ref[j][:nx]
        link_yp = moved(jnp.where(last_lane, link_y[:, ny:], link_y[:, :ny]), 1, 1)
        for f in range(3):
            at = (f, i + 1)
            here, side = body(change_ref, at), edge(change_ref, at)
            left_out = (
                link_x * body(change_ref, at, 1)
                + link_xp * body(change_ref, at, -1)
                + link_y[:, :ny] * moved(jnp.where(first_lane, side, here), -1, 1)
                + link_yp * moved(jnp.where(last_lane, side, here), 1, 1)
            )
            beyond = cut_low * body(change_ref, (f, i)) + cut_high * body(change_ref, (f, i + 2))
            pressure_ref[f, z] = body(first_ref, (f, j)) + here
            residual_ref[f, z] = left_out + beyond
        if (i + 1) % CHUNK == 0:
            part = (slice(None), pl.ds(jnp.where(high, nz - 1 - i, i + 1 - CHUNK), CHUNK))
            for n, (buffer, out) in enumerate(
                ((pressure_ref, pressure_out), (residual_ref, residual_out))
            ):
                copy = pltpu.make_async_copy(
                    buffer.at[part], out.at[part], sems.at[n, i // CHUNK]
                )
                copy.start()
                copies.append(copy)
    for copy in copies:
        copy.wait()


def kernel_call(kernel, outputs, operands, scratch=(), smem=0, cost=None, space=pltpu.VMEM):
    specs = [pl.BlockSpec(memory_space=pltpu.SMEM)] * smem
    specs += [pl.BlockSpec(memory_space=pltpu.VMEM)] * (len(operands) - smem)
    return pl.pallas_call(
        kernel,
        out_shape=[jax.ShapeDtypeStruct(s, t) for s, t in outputs],
        in_specs=specs,
        out_specs=[pl.BlockSpec(memory_space=space)] * len(outputs),
        scratch_shapes=list(scratch),
        compiler_params=pltpu.CompilerParams(vmem_limit_bytes=32 * 2**20),
        cost_estimate=cost,
    )(*operands)


def swapped(values, stage):
    size = lax.axis_size("gz")
    return lax.ppermute(values, "gz", [(i, i ^ 2**stage) for i in range(size)])


def ring(values, axis, distance):
    size = lax.axis_size(axis)
    return lax.ppermute(values, axis, [(i, (i + distance) % size) for i in range(size)])


def slanted(values, x_distance):
    nx, nz = lax.axis_size("gx"), lax.axis_size("gz")
    route = []
    for i in range(nx):
        for k in range(nz):
            route.append((i * nz + k, (i + x_distance) % nx * nz + (k ^ 1)))
    return lax.ppermute(values, ("gx", "gz"), route)


def per_device(facies, perm_table, line_breaks):
    nz, nx, ny = facies.shape
    stages = (lax.axis_size("gz") - 1).bit_length() - 1
    i32, f32 = jnp.int32, jnp.float32
    two = lax.axis_size("gx") == 2
    layers = 2 * nz
    cut_rows = -(-(layers + 1 + 2 * stages) // 8) * 8
    sides = 1 if two else 2
    facies, *rows = kernel_call(
        pack_kernel,
        [((nz, nx, ny), i32)] + [((nz * 4, ny), i32)] * sides,
        [facies],
    )
    other = swapped(facies, 0)
    if two:
        rims = [ring(rows[0], "gx", 1), slanted(rows[0], 1)]
    else:
        rims = [ring(rows[1], "gx", 1), ring(rows[0], "gx", -1)]
        rims += [slanted(rows[1], 1), slanted(rows[0], -1)]
    k, table, cuts = kernel_call(
        functools.partial(prepare_kernel, stages),
        [((3, nz, nx, ny), f32), ((3, 8, ny), f32), ((cut_rows, ny), f32)],
        [perm_table, line_breaks, facies],
        smem=2,
        cost=pl.CostEstimate(flops=10**7, bytes_accessed=10**6, transcendentals=0),
    )
    strip, *rows = kernel_call(
        merge_kernel,
        [((2 * nx + 16, ny), i32)] + [((layers * 4, ny), i32)] * sides,
        [facies, other, table] + rims,
    )
    k, *rows = kernel_call(
        functools.partial(prepare_other_kernel, sides, stages == 1),
        [((3, layers, nx, ny), f32)] + [((3, layers * 4, ny), f32)] * sides,
        [table, k, other] + rows,
        cost=pl.CostEstimate(flops=10**7, bytes_accessed=10**6, transcendentals=0),
    )
    y_low, y_high = ring(strip, "gy", 1), ring(strip, "gy", -1)
    sizes = nz, nx, ny
    operands = [table, cuts, k, rows[0], rows[-1], y_low, y_high]
    return (sweep_ends if stages == 1 else sweep_tree)(sizes, stages, operands)


def sweep_ends(sizes, stages, operands):
    nz, nx, ny = sizes
    layers, f32 = 2 * nz, jnp.float32
    slab, tall = (nx + 8, 2 * ny), (2, nx + 24, ny)

    def slabs(*count):
        return (count + slab, f32)

    def talls(*count):
        return (count + tall, f32)

    def message_of(count, halo):
        return ((Message(count, halo, nx, ny).rows, ny), f32)

    def filler(flops):
        return pl.CostEstimate(flops=flops, bytes_accessed=10**6, transcendentals=0)

    half, tall_half = (nx + 8, ny), (nx + 24, ny)
    table, cuts, k, row_low, row_high, y_low, y_high = operands
    body = kernel_call(
        body_kernel,
        [((layers,) + tall_half, f32)] + [((layers,) + half, f32)] * 4
        + [((layers + 1,) + half, f32)],
        [k, row_low, row_high],
        cost=filler(10**7),
    )
    message, own, lx, ly, lz, d, ratio, inverse = kernel_call(
        end_eliminate_kernel,
        [message_of(LAST_COUNT, 2), slabs(LAST_COUNT), talls(layers), slabs(layers),
         slabs(layers + 1), slabs(3, layers), slabs(layers), slabs(layers)],
        [table, cuts, y_low, y_high] + list(body),
        [pltpu.VMEM((layers,) + tall_half, f32), pltpu.VMEM((layers,) + tall_half, f32),
         pltpu.VMEM(*slabs(layers)), pltpu.VMEM((layers,) + half, f32),
         pltpu.VMEM(*slabs(2, layers)), pltpu.VMEM(*slabs(layers))],
    )
    other = swapped(message, stages)
    base, phi, parts = kernel_call(
        expand_kernel,
        [talls(3, layers), talls(layers), slabs(6)],
        [cuts, lx, ly, lz, d, ratio],
        cost=filler(10**7),
    )
    message, near = kernel_call(
        functools.partial(end_join_kernel, layers),
        [message_of(3, 1), slabs(13)],
        [cuts, own, other, parts],
    )
    other = swapped(message, stages)
    first, change = kernel_call(
        correct_kernel,
        [talls(3, layers), slabs(3, layers)],
        [cuts, near, lx, ly, lz, ratio, inverse, base, phi],
        [pltpu.VMEM(*slabs(3, layers))],
        cost=filler(10**7),
    )
    out = ((3, nz, nx, ny), f32)
    return tuple(kernel_call(
        end_final_kernel,
        [out, out],
        [cuts, other, near, lx, ly, lz, phi, first, change],
        [pltpu.VMEM(*talls(3, nz + 2)), pltpu.VMEM(*out), pltpu.VMEM(*out),
         pltpu.SemaphoreType.DMA((2, nz // CHUNK))],
        space=pl.ANY,
    ))


def sweep_tree(sizes, stages, operands):
    nz, nx, ny = sizes
    layers, f32 = 2 * nz, jnp.float32
    cuts = operands[1]
    slab = (nx + 8, 2 * ny)
    one, three = ((layers,) + slab, f32), ((3, layers) + slab, f32)

    def slabs(count):
        return ((count,) + slab, f32)

    def message_of(count, halo):
        return ((Message(count, halo, nx, ny).rows, ny), f32)

    message, own, pair, lx, ly, lz, d, e, inverse = kernel_call(
        functools.partial(eliminate_kernel, stages),
        [message_of(LAST_COUNT if stages == 1 else FIRST_COUNT, 2)]
        + [slabs(FIRST_COUNT), slabs(PAIR_COUNT)]
        + [one] * 3 + [three, one, one],
        operands,
        [pltpu.VMEM(s, f32) for s in (three[0], one[0], (2,) + one[0], one[0])],
    )
    siblings, factors, group = [], [], own
    for s in range(stages - 1):
        last = s == stages - 2
        outputs = [slabs(FIRST_COUNT), slabs(7), message_of(LAST_COUNT if last else FIRST_COUNT, 2)]
        sibling, factor, message, *joined = kernel_call(
            functools.partial(join_kernel, s, last, layers + 1),
            outputs + ([] if last else [slabs(FIRST_COUNT)]),
            [cuts, group, swapped(message, s + 1)],
        )
        siblings.append(sibling)
        factors.append(factor)
        group = None if last else joined[0]
    fields = ((3, layers + 2) + slab, f32)
    message, own, rights, d2, kept, ends, first = kernel_call(
        functools.partial(middle_kernel, stages),
        [message_of(3 if stages == 1 else SECOND_COUNT, 1), slabs(SECOND_COUNT), slabs(6), three,
         slabs(2 * stages + 5), slabs(3), fields],
        [cuts, own, pair] + siblings + [swapped(message, stages)]
        + [lx, ly, lz, d, e, inverse],
    )
    siblings, group = [], own
    for s in range(stages - 1):
        last = s == stages - 2
        outputs = [slabs(SECOND_COUNT), message_of(3 if last else SECOND_COUNT, 1)]
        sibling, message, *joined = kernel_call(
            functools.partial(join_again_kernel, s, last),
            outputs + ([] if last else [slabs(SECOND_COUNT)]),
            [group, swapped(message, s + 1), factors[s]],
        )
        siblings.append(sibling)
        group = None if last else joined[0]
    out = ((3, nz, nx, ny), f32)
    pressure, residual = kernel_call(
        functools.partial(final_kernel, stages),
        [out, out],
        [cuts, own, pair] + siblings + [swapped(message, stages)]
        + [lx, ly, lz, first, rights, d2, e, inverse, kept, ends],
        [pltpu.VMEM((3, nz + 2) + slab, f32)]
        + [pltpu.VMEM((3, nz, nx, ny), f32)] * 2
        + [pltpu.SemaphoreType.DMA((2, nz // CHUNK))],
        space=pl.ANY,
    )
    return pressure, residual


def solution(mesh):
    return jax.shard_map(
        per_device,
        mesh=mesh,
        in_specs=(P("gz", "gx", "gy"), P(), P()),
        out_specs=(P(None, "gz", "gx", "gy"), P(None, "gz", "gx", "gy")),
        check_vma=False,
    )
```

```python
import functools

import jax
import jax.numpy as jnp
from jax import lax
from jax.experimental import pallas as pl
from jax.experimental.pallas import tpu as pltpu
from jax.sharding import PartitionSpec as P


WIDE = 3
FIRST_COUNT = 11
LAST_COUNT = 5
SECOND_COUNT = 6
PAIR_COUNT = 16
CHUNK = 4


def moved(values, amount, axis):
    size = values.shape[axis]
    amount = amount % size
    if amount == 0:
        return values
    return pltpu.roll(values, amount, axis)


def flag(condition):
    return condition.astype(jnp.float32)


def iotas(rows, lanes):
    return tuple(lax.broadcasted_iota(jnp.int32, (rows, lanes), d) for d in (0, 1))


def choose(condition, first, second):
    return [jnp.where(condition, a, b) for a, b in zip(first, second)]


def flipped(flips):
    return is_high(0) if flips else False


def is_high(stage):
    return (lax.axis_index("gz") >> (stage + 1)) % 2 == 1


def own_start(nz):
    return (lax.axis_index("gz") % 2) * nz


def pack_kernel(facies_ref, copy_ref, *row_refs):
    nz, nx, ny = facies_ref.shape
    copy_ref[...] = facies_ref[...]
    row = iotas(8, ny)[0]
    for z in range(0, nz, 2):
        pair = [facies_ref[z], facies_ref[z + 1]]
        first = jnp.where(row < 4, pair[0][:8], moved(pair[1][:8], 4, 0))
        last = jnp.where(row < 4, moved(pair[0][nx - 8 :], 4, 0), pair[1][nx - 8 :])
        spot = slice(4 * z, 4 * z + 8)
        if len(row_refs) == 1:
            row_refs[0][spot, :] = jnp.where(lax.axis_index("gx") == 0, last, first)
        else:
            row_refs[0][spot, :] = first
            row_refs[1][spot, :] = last


def rim_tile(low, high, layer):
    row = iotas(8, low.shape[1])[0]
    if layer % 2 == 0:
        return jnp.where(row < 4, high, moved(low, 4, 0))
    return jnp.where(row < 4, moved(high, 4, 0), low)


def merge_kernel(own_ref, other_ref, *refs):
    sides = (len(refs) - 1) // 3
    ins, strip_ref, row_refs = refs[: 2 * sides], refs[2 * sides], refs[2 * sides + 1 :]
    nz, nx, ny = own_ref.shape
    swap = own_start(nz) > 0
    lane = lax.broadcasted_iota(jnp.int32, (nx + 8, ny), 1)
    for b in range(2):
        own = swap == (b == 1)
        for n, ref in enumerate(row_refs):
            ref[4 * nz * b : 4 * nz * (b + 1), :] = jnp.where(own, ins[n][...], ins[sides + n][...])
        strip = jnp.zeros((nx + 8, ny), jnp.int32)
        for z in range(nz):
            start = 4 * nz * b + z // 2 * 8
            low, high = [ref[start : start + 8, :] for ref in (row_refs[0], row_refs[-1])]
            layer = jnp.where(own, own_ref[z], other_ref[z])
            layer = jnp.concatenate([layer, rim_tile(low, high, z)], axis=0)
            strip = jnp.where(lane // 8 == z, moved(layer, 8 * z + WIDE, 1), strip)
        strip_ref[b * (nx + 8) : (b + 1) * (nx + 8), :] = strip


def lookup(table, index):
    rows = [
        jnp.take_along_axis(table, index[r : r + 8], axis=1) for r in range(0, index.shape[0], 8)
    ]
    return jnp.concatenate(rows, axis=0)


def prepare_kernel(stages, table, breaks, facies_ref, k_ref, table_ref, cut_ref):
    nz, nx, ny = facies_ref.shape
    lane = iotas(8, ny)[1]
    tables = []
    for q in range(3):
        values = jnp.zeros((8, ny), jnp.float32)
        for label in range(table.shape[1]):
            values = jnp.where(lane == label, table[q, label], values)
        if stages == 1:
            values = 2.0 * values
        table_ref[q] = values
        tables.append(values)
    for z in range(nz):
        for q in range(3):
            k_ref[q, z] = lookup(tables[q], facies_ref[z])
    pair = lax.axis_index("gz") // 2
    layers = [pair * 2 * nz + r - 1 for r in range(2 * nz + 1)]
    if stages == 1:
        high = is_high(0)
        layers = [
            pair * 2 * nz + jnp.where(high, 2 * nz - 1 - r, r - 1) for r in range(2 * nz + 1)
        ]
    for s in range(stages if stages > 1 else 0):
        base, size = (pair >> (s + 1)) << (s + 1), 2**s
        layers.append((base + size) * 2 * nz - 1)
        layers.append(jnp.where(is_high(s), base, base + 2 * size) * 2 * nz - 1)
    for r, layer in enumerate(layers):
        cut = breaks[jnp.clip(layer, 0, breaks.shape[0] - 1)].astype(jnp.float32)
        cut_ref[r : r + 1, :] = jnp.full((1, ny), cut, jnp.float32)


def prepare_other_kernel(sides, flips, table_ref, own_ref, other_ref, *refs):
    rows, k_ref, row_refs = refs[:sides], refs[sides], refs[sides + 1 :]
    nz, _, ny = other_ref.shape
    start, flip = own_start(nz), flipped(flips)

    def spot(at, count):
        return jnp.where(flip, count - 1 - at, at)

    for q in range(3):
        for z in range(nz):
            k_ref[q, spot(start + z, 2 * nz)] = own_ref[q, z]
            k_ref[q, spot(nz - start + z, 2 * nz)] = lookup(table_ref[q], other_ref[z])
        for n in range(sides):
            for t in range(nz):
                tile = lookup(table_ref[q], rows[n][8 * t : 8 * t + 8, :])
                tile = jnp.where(flip, moved(tile, 4, 0), tile)
                row_refs[n][q, pl.ds(pl.multiple_of(8 * spot(t, nz), 8), 8), :] = tile


def face(a, b):
    product = a * b
    total = a + b
    harmonic = 2.0 * product / total
    inside = product > 0.0
    link = jnp.where(inside, harmonic, 0.0)
    flow = jnp.where(inside, harmonic, total)
    tau = jnp.where(inside, harmonic, 2.0 * total)
    return link, flow, tau


class Message:
    def __init__(self, count, halo, nx, ny):
        self.count, self.halo, self.nx, self.ny = count, halo, nx, ny
        self.one_sided = lax.axis_size("gx") == 2
        self.rows_each = halo if self.one_sided else 2 * halo
        self.per_tile = 8 // self.rows_each
        self.tiles = -(-count // self.per_tile)
        self.abreast = ny // (2 * halo * count)
        strips = -(-(nx // 8 + 1) // self.abreast)
        self.sides = count * nx + 8 * strips
        self.rows = self.sides + 8 * self.tiles

    def strip(self, t, q):
        start = self.count * self.nx + 8 * (t // self.abreast)
        shift = 2 * self.halo * (self.count * (t % self.abreast) + q) + self.halo
        return slice(start, start + 8), shift

    def tile(self, q):
        start = self.sides + 8 * (q // self.per_tile)
        return slice(start, start + 8)

    def side_moved(self, tile, q, sign):
        part = q % self.per_tile
        if not self.one_sided:
            return moved(tile, sign * (self.rows_each * part + self.halo), 0)
        first = lax.axis_index("gx") == 0
        out = jnp.where(
            first,
            moved(tile, sign * self.halo * part, 0),
            moved(tile, sign * self.halo * (part + 1), 0),
        )
        if sign > 0:
            return out
        row = iotas(8, self.ny)[0]
        return jnp.where(jnp.where(first, row, 7 - row) < self.halo, out, 1.0)

    def write(self, ref, slabs):
        nx, ny, halo = self.nx, self.ny, self.halo
        row, lane = iotas(8, ny)
        strips = {}
        for t in range(nx // 8 + 1):
            for q, slab in enumerate(slabs):
                spot, shift = self.strip(t, q)
                turned = moved(slab[8 * t : 8 * t + 8, ny:], shift, 1)
                held = strips.get(spot.start, turned)
                strips[spot.start] = jnp.where(lane < shift - halo, held, turned)
        for start, strip in strips.items():
            ref[start : start + 8, :] = strip
        for q, slab in enumerate(slabs):
            ref[q * nx : (q + 1) * nx, :] = slab[:nx, :ny]
            turned = self.side_moved(slab[nx:, :ny], q, 1)
            part = q % self.per_tile
            tile = turned if part == 0 else jnp.where(row < self.rows_each * part, tile, turned)
            if part == self.per_tile - 1 or q == self.count - 1:
                ref[self.tile(q), :] = tile

    def read(self, ref):
        nx = self.nx
        slabs = []
        for q in range(self.count):
            side = self.side_moved(ref[self.tile(q), :], q, -1)
            body = jnp.concatenate([ref[q * nx : (q + 1) * nx, :], side], axis=0)
            beside = []
            for t in range(nx // 8 + 1):
                spot, shift = self.strip(t, q)
                beside.append(moved(ref[spot, :], -shift, 1))
            slabs.append(jnp.concatenate([body, jnp.concatenate(beside, axis=0)], axis=1))
        return slabs


def open_after(cut_ref, r):
    cut = 1.0 - cut_ref[r : r + 1, :]
    return jnp.concatenate([cut, cut], axis=1)


def slab_size(ref):
    return ref.shape[-2] - 8, ref.shape[-1] // 2


def join(low, high, opened):
    ends = link, flow, tau = face(low[4], high[3])
    coupling = link * opened
    inverse = 1.0 / (low[2] + tau)
    step = coupling * inverse
    last_inverse = 1.0 / (high[0] + tau - coupling * step)
    outer = low[1] * inverse
    weight = step * low[1]
    weight_low, weight_high = weight * last_inverse, high[1] * last_inverse
    right_low = low[8:10] + [low[10] + flow]
    right_high = high[5:7] + [high[7] - flow]
    s_uu = low[0] - outer * low[1] - weight * weight_low
    s_uv = -weight * weight_high
    s_vv = high[2] - high[1] * weight_high
    factors = [outer, step, weight_low, weight_high, inverse, last_inverse]
    g_u, g_v, middle = join_right(factors, low[5:8], right_low, right_high, high[8:11])
    return [s_uu, s_uv, s_vv, low[3], high[4]] + g_u + g_v, factors, right_low + middle, ends


def join_right(factors, low_u, low_v, high_u, high_v):
    outer, step, weight_low, weight_high = factors[:4]
    middle = [b + step * a for a, b in zip(low_v, high_u)]
    g_u = [g - outer * a - weight_low * m for g, a, m in zip(low_u, low_v, middle)]
    g_v = [g - weight_high * m for g, m in zip(high_v, middle)]
    return g_u, g_v, middle


def join_inner(factors, right_low, middle, first, last):
    outer, step, weight_low, weight_high, inverse, last_inverse = factors
    high = last_inverse * middle - weight_low * first - weight_high * last
    return inverse * right_low - outer * first + step * high, high


def reduce_end(slabs, top):
    s_uu, s_uv, s_vv, k_u, k_v = slabs[:5]
    far_s, near_s = choose(top, [s_vv, s_uu], [s_uu, s_vv])
    far_k, near_k = choose(top, [k_v, k_u], [k_u, k_v])
    sign = jnp.where(top, 1.0, -1.0)
    factor = s_uv / (far_s + 2.0 * far_k)
    g_u, g_v = slabs[5:8], slabs[8:11]
    far_g, near_g = choose(top, g_v, g_u), choose(top, g_u, g_v)
    far_g[2] = far_g[2] + far_k * sign
    return [near_s - s_uv * factor, near_k] + [n - factor * g for n, g in zip(near_g, far_g)], factor


def reduce_end_right(factor, g_u, g_v, top):
    far_g, near_g = choose(top, g_v, g_u), choose(top, g_u, g_v)
    return [n - factor * g for n, g in zip(near_g, far_g)]


def grid_masks(nx, ny):
    at_x, at_y = lax.axis_index("gx"), lax.axis_index("gy")
    has_x_low, has_x_high = at_x > 0, at_x < lax.axis_size("gx") - 1
    has_y_low, has_y_high = at_y > 0, at_y < lax.axis_size("gy") - 1
    row, lane = iotas(nx + 8, 2 * ny)
    x_in = (row < nx) | ((row < nx + WIDE) & has_x_high) | ((row >= nx + 8 - WIDE) & has_x_low)
    y_in = (lane < ny) | ((lane < ny + WIDE) & has_y_high)
    y_in = y_in | ((lane >= 2 * ny - WIDE) & has_y_low)
    cell = x_in & y_in
    valid = flag(cell)
    in_x, in_xp = valid * moved(valid, -1, 0), valid * moved(valid, 1, 0)
    in_y, in_yp = valid * moved(valid, -1, 1), valid * moved(valid, 1, 1)
    return cell, in_x, in_xp, in_y, in_yp


def rim_columns(flips, tables, y_low, y_high, cell):
    ny = cell.shape[1] // 2
    size = cell.shape[0]
    strip_in = cell[:, ny:]
    lane = iotas(size, ny)[1]
    strips = []
    for b in range(2):
        part = slice(b * size, (b + 1) * size)
        strips.append(jnp.where(lane % 8 < WIDE, y_low[part, :], y_high[part, :]))
    flip, nz = flipped(flips), ny // 8
    if flips:
        strips = choose(flip, strips[::-1], strips)
    strips = [[lookup(table, strip) for table in tables] for strip in strips]

    def beside(q, at):
        z, strip = at % nz, strips[at // nz][q]
        if flips:
            turned = pltpu.roll(strip, ny - WIDE - 8 * jnp.where(flip, nz - 1 - z, z), 1)
        else:
            turned = moved(strip, -(8 * z + WIDE), 1)
        return jnp.where(strip_in, turned, 0.0)

    return beside


def body_rows(k_ref, low_ref, high_ref, q, at, row_in):
    spot = slice(at // 2 * 8, at // 2 * 8 + 8)
    side = rim_tile(low_ref[q, spot, :], high_ref[q, spot, :], at)
    return jnp.concatenate([k_ref[q, at], jnp.where(row_in, side, 0.0)], axis=0)


def flow_after(here, there, inside):
    total = here + there
    return jnp.where(inside > 0.0, 2.0 * (here * there) / total, total)


def tau_and_source(flow, back, inside, inside_back):
    return flow * (2.0 - inside) + back * (2.0 - inside_back), flow - back


def eliminate_kernel(
    stages, table_ref, cut_ref, k_ref, row_low, row_high, y_low, y_high,
    message_ref, own_ref, pair_ref, lx_ref, ly_ref, lz_ref, d_ref, e_ref, inverse_ref,
    all_ref, flow_ref, source_ref, centre_ref,
):
    layers, nx, ny = k_ref.shape[1:]
    nz = layers // 2
    cell, in_x, in_xp, in_y, in_yp = grid_masks(nx, ny)
    beside = rim_columns(False, [table_ref[q] for q in range(3)], y_low, y_high, cell)
    for at in range(layers):
        for q in range(3):
            body = body_rows(k_ref, row_low, row_high, q, at, cell[nx:, :ny])
            all_ref[q, at] = jnp.concatenate([body, beside(q, at)], axis=1)
    for at in range(layers):
        kx, ky = all_ref[0, at], all_ref[1, at]
        flow_x = flow_after(kx, moved(kx, -1, 0), in_x)
        flow_ref[at] = flow_after(ky, moved(ky, -1, 1), in_y)
        lx_ref[at] = flow_x * in_x
        centre_ref[at], source_ref[0, at] = tau_and_source(
            flow_x, moved(flow_x, 1, 0), in_x, in_xp
        )
        if at % nz < nz - 1:
            kz, above = all_ref[2, at], all_ref[2, at + 1]
            lz_ref[at] = jnp.where(cell, 2.0 * (kz * above) / (kz + above), 0.0)
    for at in range(layers):
        flow_y = flow_ref[at]
        ly_ref[at] = flow_y * in_y
        tau_y, source_ref[1, at] = tau_and_source(
            flow_y, moved(flow_y, 1, 1), in_y, in_yp
        )
        centre = centre_ref[at] + tau_y
        if at % nz > 0:
            centre = centre + lz_ref[at - 1]
        if at % nz < nz - 1:
            centre = centre + lz_ref[at]
        centre_ref[at] = jnp.where(cell, centre, 1.0)

    states = [{}, {}]
    for z in range(nz):
        for b in range(2):
            at, v = b * nz + z, states[b]
            centre = centre_ref[at]
            sources = [source_ref[0, at], source_ref[1, at]]
            if z == 0:
                v["source"] = sources + [lz_ref[at]]
                v["s_uu"], v["g_u"] = centre, v["source"]
            elif z == nz - 1:
                sources = sources + [-lz_ref[at - 1]]
                v["s_vv"] = centre - v["coupling"] * v["ratio"]
                v["s_uv"] = -v["coupling"] * v["spike"]
                v["g_v"] = [a + v["coupling"] * d for a, d in zip(sources, v["value"])]
            else:
                forward = sources + [lz_ref[at] - lz_ref[at - 1]]
                if z == 1:
                    pivot, numerator = centre, v["coupling"]
                else:
                    pivot = centre - v["coupling"] * v["ratio"]
                    forward = [a + v["coupling"] * d for a, d in zip(forward, v["value"])]
                    numerator = v["coupling"] * v["spike"]
                inverse = 1.0 / pivot
                v["value"] = [a * inverse for a in forward]
                v["spike"] = numerator * inverse
                v["s_uu"] = v["s_uu"] - numerator * v["spike"]
                v["g_u"] = [g + v["spike"] * a for g, a in zip(v["g_u"], forward)]
                inverse_ref[at] = inverse
                e_ref[at] = v["spike"]
                for f in range(3):
                    d_ref[f, at] = v["value"][f]
            if z < nz - 1:
                v["coupling"] = lz_ref[at] * open_after(cut_ref, at + 1)
                if z > 0:
                    v["ratio"] = v["coupling"] * inverse

    def block(b):
        v = states[b]
        k_ends = [all_ref[2, b * nz], all_ref[2, b * nz + nz - 1]]
        return [v["s_uu"], v["s_uv"], v["s_vv"]] + k_ends + v["g_u"] + v["g_v"]

    slabs, factors, rights, ends = join(block(0), block(1), open_after(cut_ref, nz))
    for q, slab in enumerate(slabs):
        own_ref[q] = slab
    for n, slab in enumerate(factors + rights + list(ends)):
        pair_ref[n] = slab
    if stages == 1:
        slabs, pair_ref[PAIR_COUNT - 1] = reduce_end(slabs, is_high(0))
    Message(len(slabs), 2, nx, ny).write(message_ref, slabs)


def join_kernel(stage, last, base, cut_ref, own_ref, message_ref, sibling_ref, factor_ref, next_ref, *joined):
    nx, ny = slab_size(own_ref)
    own = [own_ref[q] for q in range(FIRST_COUNT)]
    sibling = Message(FIRST_COUNT, 2, nx, ny).read(message_ref)
    for q, slab in enumerate(sibling):
        sibling_ref[q] = slab
    high = is_high(stage)
    slabs, factors, _, _ = join(
        choose(high, sibling, own),
        choose(high, own, sibling),
        open_after(cut_ref, base + 2 * stage),
    )
    for n, values in enumerate(factors):
        factor_ref[n] = values
    if last:
        slabs, factor_ref[6] = reduce_end(slabs, is_high(stage + 1))
    else:
        for q, slab in enumerate(slabs):
            joined[0][q] = slab
    Message(len(slabs), 2, nx, ny).write(next_ref, slabs)


def join_again_kernel(stage, last, own_ref, message_ref, factor_ref, sibling_ref, next_ref, *joined):
    nx, ny = slab_size(own_ref)
    own = [own_ref[q] for q in range(SECOND_COUNT)]
    sibling = Message(SECOND_COUNT, 1, nx, ny).read(message_ref)
    for q, slab in enumerate(sibling):
        sibling_ref[q] = slab
    above = is_high(stage)
    low, high = choose(above, sibling, own), choose(above, own, sibling)
    factors = [factor_ref[n] for n in range(6)]
    g_u, g_v, _ = join_right(factors, low[:3], low[3:], high[:3], high[3:])
    slabs = g_u + g_v
    if last:
        slabs = reduce_end_right(factor_ref[6], g_u, g_v, is_high(stage + 1))
    else:
        for q, slab in enumerate(slabs):
            joined[0][q] = slab
    Message(len(slabs), 1, nx, ny).write(next_ref, slabs)


def stencil(slab, link_x, link_y):
    return (
        link_x * moved(slab, -1, 0)
        + moved(link_x * slab, 1, 0)
        + (link_y * moved(slab, -1, 1) + moved(link_y * slab, 1, 1))
    )


def beyond_cuts(cut_ref, at, link_low, link_high):
    low, high = cut_ref[pl.ds(at, 1), :], cut_ref[pl.ds(at + 1, 1), :]
    return (
        link_low * jnp.concatenate([low, low], axis=1),
        link_high * jnp.concatenate([high, high], axis=1),
    )


def left_out(field_ref, f, at, link_x, link_y, cuts):
    return stencil(field_ref[f, at + 1], link_x, link_y) + (
        cuts[0] * field_ref[f, at] + cuts[1] * field_ref[f, at + 2]
    )


def middle_kernel(stages, cut_ref, *refs):
    own_ref, pair_ref, siblings, message_ref = refs[0], refs[1], refs[2 : stages + 1], refs[stages + 1]
    refs = refs[stages + 2 :]
    lx_ref, ly_ref, lz_ref, d_ref, e_ref, inverse_ref = refs[:6]
    next_ref, own2_ref, right_ref, d2_ref, factor_ref, end_ref, first_ref = refs[6:]
    layers = lx_ref.shape[0]
    nz = layers // 2
    nx, ny = slab_size(lx_ref)
    own = [own_ref[q] for q in range(FIRST_COUNT)]
    slots = []

    def keep(values):
        factor_ref[len(slots)] = values
        slots.append(None)

    def attach(state, sign, row, pivot, right, k):
        beside, k_beside, rights, exists = state[0], state[1], state[2:5], state[5]
        link, flow, tau = face(k_beside * exists, k)
        coupling = link * open_after(cut_ref, row)
        rights = rights[:2] + [rights[2] + sign * flow]
        inverse = 1.0 / (beside + tau)
        step = coupling * inverse
        right = [a + step * b for a, b in zip(right, rights)]
        right[2] = right[2] - sign * flow
        return pivot + tau - coupling * step, right, step, inverse, rights, (link, flow, tau)

    far = Message(LAST_COUNT, 2, nx, ny).read(message_ref)
    top = is_high(stages - 1)
    below, above = far + [flag(top)], far + [flag(jnp.logical_not(top))]
    for s in range(stages - 2, -1, -1):
        up = is_high(s)
        block = [siblings[s][q] for q in range(FIRST_COUNT)]
        sign = jnp.where(up, 1.0, -1.0)
        state = choose(up, below, above)
        far_s, far_k, near_s, near_k = choose(
            up, [block[0], block[3], block[2], block[4]], [block[2], block[4], block[0], block[3]]
        )
        far_g = choose(up, block[5:8], block[8:11])
        near_g = choose(up, block[8:11], block[5:8])
        row = layers + 2 + 2 * s
        pivot, right, step, _, _, _ = attach(state, sign, row, far_s, far_g, far_k)
        factor = block[1] / pivot
        keep(step)
        keep(factor)
        state = [near_s - block[1] * factor, near_k]
        state += [n - factor * r for n, r in zip(near_g, right)] + [jnp.float32(1.0)]
        below, above = choose(up, state, below), choose(up, above, state)

    pivot_u, right_u, step_b, inverse_b, rights_b, ends_b = attach(
        below, 1.0, 0, own[0], own[5:8], own[3]
    )
    pivot_v, right_v, step_a, inverse_a, rights_a, ends_a = attach(
        above, -1.0, layers, own[2], own[8:11], own[4]
    )
    held_b, held_a = inverse_b * below[5], inverse_a * above[5]
    inverse_u = 1.0 / pivot_u
    factor = own[1] * inverse_u
    inverse_v = 1.0 / (pivot_v - own[1] * factor)
    for values in (step_b, held_b, step_a, held_a, inverse_u, factor, inverse_v):
        keep(values)
    pair = [pair_ref[n] for n in range(PAIR_COUNT)]
    inner = pair[:6]
    ends = [ends_b[0], pair[12], ends_a[0]]
    for n, values in enumerate(ends):
        end_ref[n] = values

    for f in range(3):
        last = (right_v[f] - factor * right_u[f]) * inverse_v
        first_u = right_u[f] * inverse_u - factor * last
        low_v, high_u = join_inner(inner, pair[6 + f], pair[9 + f], first_u, last)
        first_ref[f, 0] = rights_b[f] * held_b + step_b * first_u
        first_ref[f, layers + 1] = rights_a[f] * held_a + step_a * last
        first_ref[f, 1] = first_u
        first_ref[f, nz] = low_v
        first_ref[f, nz + 1] = high_u
        first_ref[f, layers] = last
    for z in range(nz - 2, 0, -1):
        for at in (z, nz + z):
            ratio = lz_ref[at] * open_after(cut_ref, at + 1) * inverse_ref[at]
            spike = e_ref[at]
            for f in range(3):
                first_ref[f, at + 1] = (
                    d_ref[f, at]
                    + spike * first_ref[f, 1 + at - z]
                    + ratio * first_ref[f, at + 2]
                )

    def block(b):
        for z in range(nz):
            at = b * nz + z
            cuts = beyond_cuts(
                cut_ref, at,
                ends[b] if z == 0 else lz_ref[at - 1],
                ends[b + 1] if z == nz - 1 else lz_ref[at],
            )
            right = [left_out(first_ref, f, at, lx_ref[at], ly_ref[at], cuts) for f in range(3)]
            if z == 0:
                g_u = list(right)
            else:
                if z == 1:
                    forward = right
                else:
                    forward = [right[f] + coupling * value[f] for f in range(3)]
                if z < nz - 1:
                    inverse, spike = inverse_ref[at], e_ref[at]
                    value = [forward[f] * inverse for f in range(3)]
                    g_u = [g_u[f] + spike * forward[f] for f in range(3)]
                    for f in range(3):
                        d2_ref[f, at] = value[f]
                    coupling = lz_ref[at] * open_after(cut_ref, at + 1)
        return g_u, forward

    (low_u, low_v), (high_u, high_v) = block(0), block(1)
    g_u, g_v, middle = join_right(inner, low_u, low_v, high_u, high_v)
    for n, slab in enumerate(low_v + middle):
        right_ref[n] = slab
    for q, slab in enumerate(g_u + g_v):
        own2_ref[q] = slab
    slabs = g_u + g_v
    if stages == 1:
        slabs = reduce_end_right(pair[PAIR_COUNT - 1], g_u, g_v, is_high(0))
    Message(len(slabs), 1, nx, ny).write(next_ref, slabs)


def final_kernel(stages, cut_ref, *refs):
    own_ref, pair_ref, siblings, message_ref = refs[0], refs[1], refs[2 : stages + 1], refs[stages + 1]
    refs = refs[stages + 2 :]
    lx_ref, ly_ref, lz_ref, first_ref, right_ref, d2_ref, e_ref, inverse_ref = refs[:8]
    factor_ref, end_ref, pressure_out, residual_out = refs[8:12]
    change_ref, pressure_ref, residual_ref, sems = refs[12:]
    nz = lx_ref.shape[0] // 2
    nx, ny = slab_size(lx_ref)
    own = [own_ref[q] for q in range(SECOND_COUNT)]
    slots = []

    def kept():
        slots.append(None)
        return factor_ref[len(slots) - 1]

    below = above = Message(3, 1, nx, ny).read(message_ref)
    for s in range(stages - 2, -1, -1):
        up = is_high(s)
        block = [siblings[s][q] for q in range(SECOND_COUNT)]
        state = choose(up, below, above)
        far_g = choose(up, block[:3], block[3:])
        near_g = choose(up, block[3:], block[:3])
        step, factor = kept(), kept()
        right = [a + step * b for a, b in zip(far_g, state)]
        state = [n - factor * r for n, r in zip(near_g, right)]
        below, above = choose(up, state, below), choose(up, above, state)
    step_b, held_b, step_a, held_a = kept(), kept(), kept(), kept()
    inverse_u, factor, inverse_v = kept(), kept(), kept()
    inner = [pair_ref[n] for n in range(6)]
    start = own_start(nz)
    high = start > 0
    for f in range(3):
        right_u = own[f] + step_b * below[f]
        right_v = own[3 + f] + step_a * above[f]
        last = (right_v - factor * right_u) * inverse_v
        first = right_u * inverse_u - factor * last
        low_v, high_u = join_inner(inner, right_ref[f], right_ref[3 + f], first, last)
        beyond_b = below[f] * held_b + step_b * first
        beyond_a = above[f] * held_a + step_a * last
        values = choose(high, [low_v, high_u, last, beyond_a], [beyond_b, first, low_v, high_u])
        for at, slab in zip((0, 1, nz, nz + 1), values):
            change_ref[f, at] = slab
    ends = choose(high, [end_ref[1], end_ref[2]], [end_ref[0], end_ref[1]])
    for z in range(nz - 2, 0, -1):
        at = start + z
        opened = 1.0 - cut_ref[pl.ds(at + 1, 1), :]
        opened = jnp.concatenate([opened, opened], axis=1)
        ratio = lz_ref[at] * opened * inverse_ref[at]
        spike = e_ref[at]
        for f in range(3):
            change_ref[f, z + 1] = (
                d2_ref[f, at] + spike * change_ref[f, 1] + ratio * change_ref[f, z + 2]
            )
    own_part = (slice(0, nx), slice(0, ny))
    copies = []
    for z in range(nz):
        at = start + z
        cuts = beyond_cuts(
            cut_ref, at,
            ends[0] if z == 0 else lz_ref[at - 1],
            ends[1] if z == nz - 1 else lz_ref[at],
        )
        link_x, link_y = lx_ref[at], ly_ref[at]
        for f in range(3):
            pressure_ref[f, z] = (first_ref[f, at + 1] + change_ref[f, z + 1])[own_part]
            residual_ref[f, z] = left_out(change_ref, f, z, link_x, link_y, cuts)[own_part]
        if (z + 1) % CHUNK == 0:
            part = (slice(None), slice(z + 1 - CHUNK, z + 1))
            for n, (buffer, out) in enumerate(
                ((pressure_ref, pressure_out), (residual_ref, residual_out))
            ):
                copy = pltpu.make_async_copy(
                    buffer.at[part], out.at[part], sems.at[n, z // CHUNK]
                )
                copy.start()
                copies.append(copy)
    for copy in copies:
        copy.wait()


def put(ref, index, slab):
    rows, ny = slab.shape[0], slab.shape[1] // 2
    for h in range(2):
        half = slab[:, h * ny : (h + 1) * ny]
        ref[index + (h, slice(8, 8 + rows))] = half
        ref[index + (h, slice(0, 8))] = half[rows - 8 :]
        ref[index + (h, slice(8 + rows, 16 + rows))] = half[:8]


def get(ref, index, shift=0):
    rows = ref.shape[-2] - 16
    halves = [ref[index + (h, slice(8 + shift, 8 + shift + rows))] for h in range(2)]
    return jnp.concatenate(halves, axis=1)


def signed():
    return jnp.where(is_high(0), -1.0, 1.0)


def both_halves(ref, r):
    values = ref[pl.ds(r, 1), :]
    return jnp.concatenate([values, values], axis=1)


def beside_sum(field_ref, index, lx_ref, ly_ref, j):
    here, link_y = get(field_ref, index), ly_ref[j]
    return (
        get(lx_ref, (j,)) * get(field_ref, index, 1)
        + get(lx_ref, (j,), -1) * get(field_ref, index, -1)
        + (link_y * moved(here, -1, 1) + moved(link_y * here, 1, 1))
    )


def put_half(ref, index, half):
    rows = half.shape[0]
    ref[index + (slice(8, 8 + rows),)] = half
    ref[index + (slice(0, 8),)] = half[rows - 8 :]
    ref[index + (slice(8 + rows, 16 + rows),)] = half[:8]


def harmonic(here, there):
    return here * there / (here + there)


def tau_after(here, there, inside):
    return jnp.where(inside > 0.0, harmonic(here, there), here + there)


def body_kernel(k_ref, row_low, row_high, lx_ref, tau_ref, source_ref, ky_ref, kz_ref, lz_ref):
    layers, nx, ny = k_ref.shape[1:]
    cell, in_x, in_xp = [mask[:, :ny] for mask in grid_masks(nx, ny)[:3]]
    share, share_back = 0.5 + 0.5 * in_x, 0.5 + 0.5 * in_xp
    zero = jnp.zeros((nx + 8, ny), jnp.float32)
    lz_ref[0] = zero
    lz_ref[layers] = zero
    for j in range(layers):
        kx, ky, kz = [body_rows(k_ref, row_low, row_high, q, j, cell[nx:]) for q in range(3)]
        tau = tau_after(kx, moved(kx, -1, 0), in_x)
        back = moved(tau, 1, 0)
        put_half(lx_ref, (j,), tau * in_x)
        tau_ref[j] = tau + back
        source_ref[j] = tau * share - back * share_back
        ky_ref[j] = ky
        kz_ref[j] = kz
        if j > 0:
            lz_ref[j] = jnp.where(cell, harmonic(below, kz), 0.0)
        below = kz


def end_eliminate_kernel(
    table_ref, cut_ref, y_low, y_high, lx_body, tau_body, source_body, ky_body, kz_body, lz_body,
    message_ref, own_ref, lx_ref, ly_ref, lz_ref, d_ref, ratio_ref, inverse_ref,
    kx_ref, tx_ref, ky_ref, kz_ref, source_ref, centre_ref,
):
    layers, size, ny = ky_body.shape
    nx = size - 8
    sign = signed()
    cell, in_x, in_xp, in_y, in_yp = grid_masks(nx, ny)
    share_x, share_xp = 0.5 + 0.5 * in_x[:, ny:], 0.5 + 0.5 * in_xp[:, ny:]
    share_y, share_yp = 0.5 + 0.5 * in_y, 0.5 + 0.5 * in_yp
    side_x, side_in = in_x[:, ny:], cell[:, ny:]
    rows = slice(8, 8 + size)

    def whole(body, side):
        return jnp.concatenate([body, side], axis=1)

    beside = rim_columns(True, [table_ref[q] for q in range(3)], y_low, y_high, cell)
    for j in range(layers):
        put_half(kx_ref, (j,), beside(0, j))
        ky_ref[j] = whole(ky_body[j], beside(1, j))
        kz_ref[j] = beside(2, j)
    lz_ref[0] = jnp.zeros((size, 2 * ny), jnp.float32)
    lz_ref[layers] = jnp.zeros((size, 2 * ny), jnp.float32)
    for j in range(layers):
        tau = tau_after(kx_ref[j, rows, :], kx_ref[j, slice(9, 9 + size), :], side_x)
        put_half(tx_ref, (j,), tau)
        put_half(lx_ref, (j, 1), tau * side_x)
        lx_ref[j, 0] = lx_body[j]
        ky = ky_ref[j]
        ky_ref[j] = tau_after(ky, moved(ky, -1, 1), in_y)
        if j < layers - 1:
            side = jnp.where(side_in, harmonic(kz_ref[j], kz_ref[j + 1]), 0.0)
            lz_ref[j + 1] = whole(lz_body[j + 1], side)
    for j in range(layers):
        tau, back = tx_ref[j, rows, :], tx_ref[j, slice(7, 7 + size), :]
        source_ref[0, j] = whole(source_body[j], tau * share_x - back * share_xp)
        centre = whole(tau_body[j], tau + back)
        tau = ky_ref[j]
        back = moved(tau, 1, 1)
        ly_ref[j] = tau * in_y
        source_ref[1, j] = tau * share_y - back * share_yp
        centre = centre + (tau + back)
        centre = centre + (whole(kz_body[0], kz_ref[0]) if j == 0 else lz_ref[j])
        if j < layers - 1:
            centre = centre + lz_ref[j + 1]
        centre_ref[j] = jnp.where(cell, centre, 1.0)
    for j in range(layers):
        flow_z = -0.5 * whole(kz_body[0], kz_ref[0]) if j == 0 else -lz_ref[j]
        if j < layers - 1:
            flow_z = flow_z + lz_ref[j + 1]
        forward = [source_ref[0, j], source_ref[1, j], sign * flow_z]
        pivot = centre_ref[j]
        if j > 0:
            pivot = pivot - coupling * ratio
            forward = [a + coupling * d for a, d in zip(forward, value)]
        if j < layers - 1:
            inverse = 1.0 / pivot
            coupling = lz_ref[j + 1] * (1.0 - both_halves(cut_ref, j + 1))
            ratio = coupling * inverse
            value = [a * inverse for a in forward]
            inverse_ref[j] = inverse
            ratio_ref[j] = ratio
            for f in range(3):
                d_ref[f, j] = value[f]
    slabs = [pivot, 0.5 * whole(kz_body[layers - 1], kz_ref[layers - 1])] + forward
    for q, slab in enumerate(slabs):
        own_ref[q] = slab
    Message(LAST_COUNT, 2, nx, ny).write(message_ref, slabs)


def expand_kernel(
    cut_ref, lx_ref, ly_ref, lz_ref, d_ref, ratio_ref, base_ref, phi_ref, part_ref
):
    layers = ly_ref.shape[0]
    zero = jnp.zeros(ly_ref.shape[1:], jnp.float32)
    phi, base = zero + 1.0, [zero] * 3
    put(phi_ref, (layers - 1,), phi)
    for f in range(3):
        put(base_ref, (f, layers - 1), zero)
    for j in range(layers - 2, -1, -1):
        ratio = ratio_ref[j]
        phi = ratio * phi
        put(phi_ref, (j,), phi)
        for f in range(3):
            base[f] = d_ref[f, j] + ratio * base[f]
            put(base_ref, (f, j), base[f])
    along_x = along_y = along_z = zero
    parts = [zero] * 3
    for j in range(layers):
        phi = get(phi_ref, (j,))
        along_x = along_x + (get(lx_ref, (j,)) * phi) * get(phi_ref, (j,), 1)
        along_y = along_y + (ly_ref[j] * phi) * moved(phi, -1, 1)
        cut_low = lz_ref[j] * both_halves(cut_ref, j)
        if j < layers - 1:
            cut_high = lz_ref[j + 1] * both_halves(cut_ref, j + 1)
            along_z = along_z + (cut_high * phi) * get(phi_ref, (j + 1,))
        for f in range(3):
            right = beside_sum(base_ref, (f, j), lx_ref, ly_ref, j)
            if j > 0:
                right = right + cut_low * get(base_ref, (f, j - 1))
            if j < layers - 1:
                right = right + cut_high * get(base_ref, (f, j + 1))
            parts[f] = parts[f] + phi * right
    for n, slab in enumerate(parts + [along_x, along_y, 2.0 * along_z]):
        part_ref[n] = slab


def end_join_kernel(layers, cut_ref, own_ref, message_ref, part_ref, next_ref, near_ref):
    nx, ny = slab_size(own_ref)
    own = [own_ref[q] for q in range(LAST_COUNT)]
    other = Message(LAST_COUNT, 2, nx, ny).read(message_ref)
    sign = signed()
    cut = both_halves(cut_ref, layers)
    link, flow, tau = face(own[1], other[1])
    coupling = link * (1.0 - cut)
    inverse_other = 1.0 / (other[0] + tau)
    step = coupling * inverse_other
    inverse = 1.0 / (own[0] + tau - coupling * step)
    right_own = own[2:4] + [own[4] + sign * flow]
    right_other = other[2:4] + [other[4] - sign * flow]
    cut_near = link * cut
    along_x, along_y, along_z = [part_ref[3 + n] for n in range(3)]
    slabs = []
    for f in range(3):
        near = (right_own[f] + step * right_other[f]) * inverse
        beyond = right_other[f] * inverse_other + step * near
        near_ref[f], near_ref[3 + f] = near, beyond
        right = part_ref[f] + stencil(near, along_x, along_y)
        slabs.append(right + (along_z * near + cut_near * beyond))
        near_ref[6 + f] = slabs[f]
    near_ref[9], near_ref[10], near_ref[11], near_ref[12] = step, inverse, inverse_other, link
    Message(3, 1, nx, ny).write(next_ref, slabs)


def correct_kernel(
    cut_ref, near_ref, lx_ref, ly_ref, lz_ref, ratio_ref, inverse_ref, base_ref, phi_ref,
    first_ref, change_ref, d_ref,
):
    layers = ly_ref.shape[0]
    for j in range(layers):
        phi = get(phi_ref, (j,))
        for f in range(3):
            put(first_ref, (f, j), get(base_ref, (f, j)) + phi * near_ref[f])
    for j in range(layers - 1):
        cut_low = lz_ref[j] * both_halves(cut_ref, j)
        cut_high = lz_ref[j + 1] * both_halves(cut_ref, j + 1)
        inverse = inverse_ref[j]
        if j > 0:
            coupling = lz_ref[j] * (1.0 - both_halves(cut_ref, j))
        for f in range(3):
            right = beside_sum(first_ref, (f, j), lx_ref, ly_ref, j)
            right = right + cut_high * get(first_ref, (f, j + 1))
            if j > 0:
                right = right + cut_low * get(first_ref, (f, j - 1)) + coupling * d_ref[f, j - 1]
            d_ref[f, j] = right * inverse
    change = [jnp.zeros(ly_ref.shape[1:], jnp.float32)] * 3
    for f in range(3):
        change_ref[f, layers - 1] = change[f]
    for j in range(layers - 2, -1, -1):
        ratio = ratio_ref[j]
        for f in range(3):
            change[f] = d_ref[f, j] + ratio * change[f]
            change_ref[f, j] = change[f]


def end_final_kernel(
    cut_ref, message_ref, near_ref, lx_ref, ly_ref, lz_ref, phi_ref, first_ref, base_ref,
    pressure_out, residual_out, change_ref, pressure_ref, residual_ref, sems,
):
    layers = ly_ref.shape[0]
    nz = layers // 2
    nx, ny = slab_size(ly_ref)
    high = is_high(0)
    start = jnp.where(high, nz - own_start(nz), own_start(nz))
    beside_other = start > 0
    other = Message(3, 1, nx, ny).read(message_ref)
    step, inverse, inverse_other, link_near = [near_ref[9 + n] for n in range(4)]
    near = [(near_ref[6 + f] + step * other[f]) * inverse for f in range(3)]
    for i in range(-1, nz + 1):
        j = jnp.clip(start + i, 0, layers - 1)
        phi = get(phi_ref, (j,))
        for f in range(3):
            change = base_ref[f, j] + phi * near[f]
            if i == -1:
                change = jnp.where(beside_other, change, 0.0)
            if i == nz:
                beyond = other[f] * inverse_other + step * near[f]
                change = jnp.where(beside_other, beyond, change)
            put(change_ref, (f, i + 1), change)
    lane = iotas(nx, ny)[1]
    first_lane, last_lane = lane == 0, lane == ny - 1

    def body(ref, index, shift=0):
        return ref[index + (0, slice(8 + shift, 8 + shift + nx))]

    def edge(ref, index):
        return ref[index + (1, slice(8, 8 + nx))]

    copies = []
    for i in range(nz):
        j = start + i
        z = jnp.where(high, nz - 1 - i, i)
        link_high = lz_ref[j + 1][:nx, :ny]
        if i == nz - 1:
            link_high = jnp.where(beside_other, link_near[:nx, :ny], link_high)
        cut_low = lz_ref[j][:nx, :ny] * cut_ref[pl.ds(j, 1), :]
        cut_high = link_high * cut_ref[pl.ds(j + 1, 1), :]
        link_x, link_xp = body(lx_ref, (j,)), body(lx_ref, (j,), -1)
        link_y = ly_ref[j][:nx]
        link_yp = moved(jnp.where(last_lane, link_y[:, ny:], link_y[:, :ny]), 1, 1)
        for f in range(3):
            at = (f, i + 1)
            here, side = body(change_ref, at), edge(change_ref, at)
            left_out = (
                link_x * body(change_ref, at, 1)
                + link_xp * body(change_ref, at, -1)
                + link_y[:, :ny] * moved(jnp.where(first_lane, side, here), -1, 1)
                + link_yp * moved(jnp.where(last_lane, side, here), 1, 1)
            )
            beyond = cut_low * body(change_ref, (f, i)) + cut_high * body(change_ref, (f, i + 2))
            pressure_ref[f, z] = body(first_ref, (f, j)) + here
            residual_ref[f, z] = left_out + beyond
        if (i + 1) % CHUNK == 0:
            part = (slice(None), pl.ds(jnp.where(high, nz - 1 - i, i + 1 - CHUNK), CHUNK))
            for n, (buffer, out) in enumerate(
                ((pressure_ref, pressure_out), (residual_ref, residual_out))
            ):
                copy = pltpu.make_async_copy(
                    buffer.at[part], out.at[part], sems.at[n, i // CHUNK]
                )
                copy.start()
                copies.append(copy)
    for copy in copies:
        copy.wait()


def kernel_call(kernel, outputs, operands, scratch=(), smem=0, cost=None, space=pltpu.VMEM):
    specs = [pl.BlockSpec(memory_space=pltpu.SMEM)] * smem
    specs += [pl.BlockSpec(memory_space=pltpu.VMEM)] * (len(operands) - smem)
    return pl.pallas_call(
        kernel,
        out_shape=[jax.ShapeDtypeStruct(s, t) for s, t in outputs],
        in_specs=specs,
        out_specs=[pl.BlockSpec(memory_space=space)] * len(outputs),
        scratch_shapes=list(scratch),
        compiler_params=pltpu.CompilerParams(vmem_limit_bytes=32 * 2**20),
        cost_estimate=cost,
    )(*operands)


def swapped(values, stage):
    size = lax.axis_size("gz")
    return lax.ppermute(values, "gz", [(i, i ^ 2**stage) for i in range(size)])


def ring(values, axis, distance):
    size = lax.axis_size(axis)
    return lax.ppermute(values, axis, [(i, (i + distance) % size) for i in range(size)])


def slanted(values, x_distance):
    nx, nz = lax.axis_size("gx"), lax.axis_size("gz")
    route = []
    for i in range(nx):
        for k in range(nz):
            route.append((i * nz + k, (i + x_distance) % nx * nz + (k ^ 1)))
    return lax.ppermute(values, ("gx", "gz"), route)


def per_device(facies, perm_table, line_breaks):
    nz, nx, ny = facies.shape
    stages = (lax.axis_size("gz") - 1).bit_length() - 1
    i32, f32 = jnp.int32, jnp.float32
    two = lax.axis_size("gx") == 2
    layers = 2 * nz
    cut_rows = -(-(layers + 1 + 2 * stages) // 8) * 8
    sides = 1 if two else 2
    other = swapped(facies, 0)
    facies, *rows = kernel_call(
        pack_kernel,
        [((nz, nx, ny), i32)] + [((nz * 4, ny), i32)] * sides,
        [facies],
    )
    if two:
        rims = [ring(rows[0], "gx", 1), slanted(rows[0], 1)]
    else:
        rims = [ring(rows[1], "gx", 1), ring(rows[0], "gx", -1)]
        rims += [slanted(rows[1], 1), slanted(rows[0], -1)]
    k, table, cuts = kernel_call(
        functools.partial(prepare_kernel, stages),
        [((3, nz, nx, ny), f32), ((3, 8, ny), f32), ((cut_rows, ny), f32)],
        [perm_table, line_breaks, facies],
        smem=2,
        cost=pl.CostEstimate(flops=10**7, bytes_accessed=10**6, transcendentals=0),
    )
    strip, *rows = kernel_call(
        merge_kernel,
        [((2 * nx + 16, ny), i32)] + [((layers * 4, ny), i32)] * sides,
        [facies, other] + rims,
    )
    k, *rows = kernel_call(
        functools.partial(prepare_other_kernel, sides, stages == 1),
        [((3, layers, nx, ny), f32)] + [((3, layers * 4, ny), f32)] * sides,
        [table, k, other] + rows,
        cost=pl.CostEstimate(flops=10**7, bytes_accessed=10**6, transcendentals=0),
    )
    y_low, y_high = ring(strip, "gy", 1), ring(strip, "gy", -1)
    sizes = nz, nx, ny
    operands = [table, cuts, k, rows[0], rows[-1], y_low, y_high]
    return (sweep_ends if stages == 1 else sweep_tree)(sizes, stages, operands)


def sweep_ends(sizes, stages, operands):
    nz, nx, ny = sizes
    layers, f32 = 2 * nz, jnp.float32
    slab, tall = (nx + 8, 2 * ny), (2, nx + 24, ny)

    def slabs(*count):
        return (count + slab, f32)

    def talls(*count):
        return (count + tall, f32)

    def message_of(count, halo):
        return ((Message(count, halo, nx, ny).rows, ny), f32)

    def filler(flops):
        return pl.CostEstimate(flops=flops, bytes_accessed=10**6, transcendentals=0)

    half, tall_half = (nx + 8, ny), (nx + 24, ny)
    table, cuts, k, row_low, row_high, y_low, y_high = operands
    body = kernel_call(
        body_kernel,
        [((layers,) + tall_half, f32)] + [((layers,) + half, f32)] * 4
        + [((layers + 1,) + half, f32)],
        [k, row_low, row_high],
        cost=filler(10**7),
    )
    message, own, lx, ly, lz, d, ratio, inverse = kernel_call(
        end_eliminate_kernel,
        [message_of(LAST_COUNT, 2), slabs(LAST_COUNT), talls(layers), slabs(layers),
         slabs(layers + 1), slabs(3, layers), slabs(layers), slabs(layers)],
        [table, cuts, y_low, y_high] + list(body),
        [pltpu.VMEM((layers,) + tall_half, f32), pltpu.VMEM((layers,) + tall_half, f32),
         pltpu.VMEM(*slabs(layers)), pltpu.VMEM((layers,) + half, f32),
         pltpu.VMEM(*slabs(2, layers)), pltpu.VMEM(*slabs(layers))],
    )
    other = swapped(message, stages)
    base, phi, parts = kernel_call(
        expand_kernel,
        [talls(3, layers), talls(layers), slabs(6)],
        [cuts, lx, ly, lz, d, ratio],
        cost=filler(10**7),
    )
    message, near = kernel_call(
        functools.partial(end_join_kernel, layers),
        [message_of(3, 1), slabs(13)],
        [cuts, own, other, parts],
    )
    other = swapped(message, stages)
    first, change = kernel_call(
        correct_kernel,
        [talls(3, layers), slabs(3, layers)],
        [cuts, near, lx, ly, lz, ratio, inverse, base, phi],
        [pltpu.VMEM(*slabs(3, layers))],
        cost=filler(10**7),
    )
    out = ((3, nz, nx, ny), f32)
    return tuple(kernel_call(
        end_final_kernel,
        [out, out],
        [cuts, other, near, lx, ly, lz, phi, first, change],
        [pltpu.VMEM(*talls(3, nz + 2)), pltpu.VMEM(*out), pltpu.VMEM(*out),
         pltpu.SemaphoreType.DMA((2, nz // CHUNK))],
        space=pl.ANY,
    ))


def sweep_tree(sizes, stages, operands):
    nz, nx, ny = sizes
    layers, f32 = 2 * nz, jnp.float32
    cuts = operands[1]
    slab = (nx + 8, 2 * ny)
    one, three = ((layers,) + slab, f32), ((3, layers) + slab, f32)

    def slabs(count):
        return ((count,) + slab, f32)

    def message_of(count, halo):
        return ((Message(count, halo, nx, ny).rows, ny), f32)

    message, own, pair, lx, ly, lz, d, e, inverse = kernel_call(
        functools.partial(eliminate_kernel, stages),
        [message_of(LAST_COUNT if stages == 1 else FIRST_COUNT, 2)]
        + [slabs(FIRST_COUNT), slabs(PAIR_COUNT)]
        + [one] * 3 + [three, one, one],
        operands,
        [pltpu.VMEM(s, f32) for s in (three[0], one[0], (2,) + one[0], one[0])],
    )
    siblings, factors, group = [], [], own
    for s in range(stages - 1):
        last = s == stages - 2
        outputs = [slabs(FIRST_COUNT), slabs(7), message_of(LAST_COUNT if last else FIRST_COUNT, 2)]
        sibling, factor, message, *joined = kernel_call(
            functools.partial(join_kernel, s, last, layers + 1),
            outputs + ([] if last else [slabs(FIRST_COUNT)]),
            [cuts, group, swapped(message, s + 1)],
        )
        siblings.append(sibling)
        factors.append(factor)
        group = None if last else joined[0]
    fields = ((3, layers + 2) + slab, f32)
    message, own, rights, d2, kept, ends, first = kernel_call(
        functools.partial(middle_kernel, stages),
        [message_of(3 if stages == 1 else SECOND_COUNT, 1), slabs(SECOND_COUNT), slabs(6), three,
         slabs(2 * stages + 5), slabs(3), fields],
        [cuts, own, pair] + siblings + [swapped(message, stages)]
        + [lx, ly, lz, d, e, inverse],
    )
    siblings, group = [], own
    for s in range(stages - 1):
        last = s == stages - 2
        outputs = [slabs(SECOND_COUNT), message_of(3 if last else SECOND_COUNT, 1)]
        sibling, message, *joined = kernel_call(
            functools.partial(join_again_kernel, s, last),
            outputs + ([] if last else [slabs(SECOND_COUNT)]),
            [group, swapped(message, s + 1), factors[s]],
        )
        siblings.append(sibling)
        group = None if last else joined[0]
    out = ((3, nz, nx, ny), f32)
    pressure, residual = kernel_call(
        functools.partial(final_kernel, stages),
        [out, out],
        [cuts, own, pair] + siblings + [swapped(message, stages)]
        + [lx, ly, lz, first, rights, d2, e, inverse, kept, ends],
        [pltpu.VMEM((3, nz + 2) + slab, f32)]
        + [pltpu.VMEM((3, nz, nx, ny), f32)] * 2
        + [pltpu.SemaphoreType.DMA((2, nz // CHUNK))],
        space=pl.ANY,
    )
    return pressure, residual


def solution(mesh):
    return jax.shard_map(
        per_device,
        mesh=mesh,
        in_specs=(P("gz", "gx", "gy"), P(), P()),
        out_specs=(P(None, "gz", "gx", "gy"), P(None, "gz", "gx", "gy")),
        check_vma=False,
    )
```

```python
import functools

import jax
import jax.numpy as jnp
from jax import lax
from jax.experimental import pallas as pl
from jax.experimental.pallas import tpu as pltpu
from jax.sharding import PartitionSpec as P


WIDE = 3
FIRST_COUNT = 11
LAST_COUNT = 5
SECOND_COUNT = 6
PAIR_COUNT = 16
CHUNK = 4


def moved(values, amount, axis):
    size = values.shape[axis]
    amount = amount % size
    if amount == 0:
        return values
    return pltpu.roll(values, amount, axis)


def flag(condition):
    return condition.astype(jnp.float32)


def iotas(rows, lanes):
    return tuple(lax.broadcasted_iota(jnp.int32, (rows, lanes), d) for d in (0, 1))


def choose(condition, first, second):
    return [jnp.where(condition, a, b) for a, b in zip(first, second)]


def flipped(flips):
    return is_high(0) if flips else False


def is_high(stage):
    return (lax.axis_index("gz") >> (stage + 1)) % 2 == 1


def own_start(nz):
    return (lax.axis_index("gz") % 2) * nz


def pack_kernel(facies_ref, copy_ref, *row_refs):
    nz, nx, ny = facies_ref.shape
    copy_ref[...] = facies_ref[...]
    row = iotas(8, ny)[0]
    for z in range(0, nz, 2):
        pair = [facies_ref[z], facies_ref[z + 1]]
        first = jnp.where(row < 4, pair[0][:8], moved(pair[1][:8], 4, 0))
        last = jnp.where(row < 4, moved(pair[0][nx - 8 :], 4, 0), pair[1][nx - 8 :])
        spot = slice(4 * z, 4 * z + 8)
        if len(row_refs) == 1:
            row_refs[0][spot, :] = jnp.where(lax.axis_index("gx") == 0, last, first)
        else:
            row_refs[0][spot, :] = first
            row_refs[1][spot, :] = last


def rim_tile(low, high, layer):
    row = iotas(8, low.shape[1])[0]
    if layer % 2 == 0:
        return jnp.where(row < 4, high, moved(low, 4, 0))
    return jnp.where(row < 4, moved(high, 4, 0), low)


def merge_kernel(own_ref, other_ref, *refs):
    sides = (len(refs) - 1) // 3
    ins, strip_ref, row_refs = refs[: 2 * sides], refs[2 * sides], refs[2 * sides + 1 :]
    nz, nx, ny = own_ref.shape
    swap = own_start(nz) > 0
    lane = lax.broadcasted_iota(jnp.int32, (nx + 8, ny), 1)
    for b in range(2):
        own = swap == (b == 1)
        for n, ref in enumerate(row_refs):
            ref[4 * nz * b : 4 * nz * (b + 1), :] = jnp.where(own, ins[n][...], ins[sides + n][...])
        strip = jnp.zeros((nx + 8, ny), jnp.int32)
        for z in range(nz):
            start = 4 * nz * b + z // 2 * 8
            low, high = [ref[start : start + 8, :] for ref in (row_refs[0], row_refs[-1])]
            layer = jnp.where(own, own_ref[z], other_ref[z])
            layer = jnp.concatenate([layer, rim_tile(low, high, z)], axis=0)
            strip = jnp.where(lane // 8 == z, moved(layer, 8 * z + WIDE, 1), strip)
        strip_ref[b * (nx + 8) : (b + 1) * (nx + 8), :] = strip


def lookup(table, index):
    rows = [
        jnp.take_along_axis(table, index[r : r + 8], axis=1) for r in range(0, index.shape[0], 8)
    ]
    return jnp.concatenate(rows, axis=0)


def prepare_kernel(stages, table, breaks, facies_ref, k_ref, table_ref, cut_ref):
    nz, nx, ny = facies_ref.shape
    lane = iotas(8, ny)[1]
    tables = []
    for q in range(3):
        values = jnp.zeros((8, ny), jnp.float32)
        for label in range(table.shape[1]):
            values = jnp.where(lane == label, table[q, label], values)
        if stages == 1:
            values = 2.0 * values
        table_ref[q] = values
        tables.append(values)
    for z in range(nz):
        for q in range(3):
            k_ref[q, z] = lookup(tables[q], facies_ref[z])
    pair = lax.axis_index("gz") // 2
    layers = [pair * 2 * nz + r - 1 for r in range(2 * nz + 1)]
    if stages == 1:
        high = is_high(0)
        layers = [
            pair * 2 * nz + jnp.where(high, 2 * nz - 1 - r, r - 1) for r in range(2 * nz + 1)
        ]
    for s in range(stages if stages > 1 else 0):
        base, size = (pair >> (s + 1)) << (s + 1), 2**s
        layers.append((base + size) * 2 * nz - 1)
        layers.append(jnp.where(is_high(s), base, base + 2 * size) * 2 * nz - 1)
    for r, layer in enumerate(layers):
        cut = breaks[jnp.clip(layer, 0, breaks.shape[0] - 1)].astype(jnp.float32)
        cut_ref[r : r + 1, :] = jnp.full((1, ny), cut, jnp.float32)


def prepare_other_kernel(sides, flips, table_ref, own_ref, other_ref, *refs):
    rows, k_ref, row_refs = refs[:sides], refs[sides], refs[sides + 1 :]
    nz, _, ny = other_ref.shape
    start, flip = own_start(nz), flipped(flips)

    def spot(at, count):
        return jnp.where(flip, count - 1 - at, at)

    for q in range(3):
        for z in range(nz):
            k_ref[q, spot(start + z, 2 * nz)] = own_ref[q, z]
            k_ref[q, spot(nz - start + z, 2 * nz)] = lookup(table_ref[q], other_ref[z])
        for n in range(sides):
            for t in range(nz):
                tile = lookup(table_ref[q], rows[n][8 * t : 8 * t + 8, :])
                tile = jnp.where(flip, moved(tile, 4, 0), tile)
                row_refs[n][q, pl.ds(pl.multiple_of(8 * spot(t, nz), 8), 8), :] = tile


def face(a, b):
    product = a * b
    total = a + b
    harmonic = 2.0 * product / total
    inside = product > 0.0
    link = jnp.where(inside, harmonic, 0.0)
    flow = jnp.where(inside, harmonic, total)
    tau = jnp.where(inside, harmonic, 2.0 * total)
    return link, flow, tau


class Message:
    def __init__(self, count, halo, nx, ny):
        self.count, self.halo, self.nx, self.ny = count, halo, nx, ny
        self.one_sided = lax.axis_size("gx") == 2
        self.rows_each = halo if self.one_sided else 2 * halo
        self.per_tile = 8 // self.rows_each
        self.tiles = -(-count // self.per_tile)
        self.abreast = ny // (2 * halo * count)
        strips = -(-(nx // 8 + 1) // self.abreast)
        self.sides = count * nx + 8 * strips
        self.rows = self.sides + 8 * self.tiles

    def strip(self, t, q):
        start = self.count * self.nx + 8 * (t // self.abreast)
        shift = 2 * self.halo * (self.count * (t % self.abreast) + q) + self.halo
        return slice(start, start + 8), shift

    def tile(self, q):
        start = self.sides + 8 * (q // self.per_tile)
        return slice(start, start + 8)

    def side_moved(self, tile, q, sign):
        part = q % self.per_tile
        if not self.one_sided:
            return moved(tile, sign * (self.rows_each * part + self.halo), 0)
        first = lax.axis_index("gx") == 0
        out = jnp.where(
            first,
            moved(tile, sign * self.halo * part, 0),
            moved(tile, sign * self.halo * (part + 1), 0),
        )
        if sign > 0:
            return out
        row = iotas(8, self.ny)[0]
        return jnp.where(jnp.where(first, row, 7 - row) < self.halo, out, 1.0)

    def write(self, ref, slabs):
        nx, ny, halo = self.nx, self.ny, self.halo
        row, lane = iotas(8, ny)
        strips = {}
        for t in range(nx // 8 + 1):
            for q, slab in enumerate(slabs):
                spot, shift = self.strip(t, q)
                turned = moved(slab[8 * t : 8 * t + 8, ny:], shift, 1)
                held = strips.get(spot.start, turned)
                strips[spot.start] = jnp.where(lane < shift - halo, held, turned)
        for start, strip in strips.items():
            ref[start : start + 8, :] = strip
        for q, slab in enumerate(slabs):
            ref[q * nx : (q + 1) * nx, :] = slab[:nx, :ny]
            turned = self.side_moved(slab[nx:, :ny], q, 1)
            part = q % self.per_tile
            tile = turned if part == 0 else jnp.where(row < self.rows_each * part, tile, turned)
            if part == self.per_tile - 1 or q == self.count - 1:
                ref[self.tile(q), :] = tile

    def read(self, ref):
        nx = self.nx
        slabs = []
        for q in range(self.count):
            side = self.side_moved(ref[self.tile(q), :], q, -1)
            body = jnp.concatenate([ref[q * nx : (q + 1) * nx, :], side], axis=0)
            beside = []
            for t in range(nx // 8 + 1):
                spot, shift = self.strip(t, q)
                beside.append(moved(ref[spot, :], -shift, 1))
            slabs.append(jnp.concatenate([body, jnp.concatenate(beside, axis=0)], axis=1))
        return slabs


def open_after(cut_ref, r):
    cut = 1.0 - cut_ref[r : r + 1, :]
    return jnp.concatenate([cut, cut], axis=1)


def slab_size(ref):
    return ref.shape[-2] - 8, ref.shape[-1] // 2


def join(low, high, opened):
    ends = link, flow, tau = face(low[4], high[3])
    coupling = link * opened
    inverse = 1.0 / (low[2] + tau)
    step = coupling * inverse
    last_inverse = 1.0 / (high[0] + tau - coupling * step)
    outer = low[1] * inverse
    weight = step * low[1]
    weight_low, weight_high = weight * last_inverse, high[1] * last_inverse
    right_low = low[8:10] + [low[10] + flow]
    right_high = high[5:7] + [high[7] - flow]
    s_uu = low[0] - outer * low[1] - weight * weight_low
    s_uv = -weight * weight_high
    s_vv = high[2] - high[1] * weight_high
    factors = [outer, step, weight_low, weight_high, inverse, last_inverse]
    g_u, g_v, middle = join_right(factors, low[5:8], right_low, right_high, high[8:11])
    return [s_uu, s_uv, s_vv, low[3], high[4]] + g_u + g_v, factors, right_low + middle, ends


def join_right(factors, low_u, low_v, high_u, high_v):
    outer, step, weight_low, weight_high = factors[:4]
    middle = [b + step * a for a, b in zip(low_v, high_u)]
    g_u = [g - outer * a - weight_low * m for g, a, m in zip(low_u, low_v, middle)]
    g_v = [g - weight_high * m for g, m in zip(high_v, middle)]
    return g_u, g_v, middle


def join_inner(factors, right_low, middle, first, last):
    outer, step, weight_low, weight_high, inverse, last_inverse = factors
    high = last_inverse * middle - weight_low * first - weight_high * last
    return inverse * right_low - outer * first + step * high, high


def reduce_end(slabs, top):
    s_uu, s_uv, s_vv, k_u, k_v = slabs[:5]
    far_s, near_s = choose(top, [s_vv, s_uu], [s_uu, s_vv])
    far_k, near_k = choose(top, [k_v, k_u], [k_u, k_v])
    sign = jnp.where(top, 1.0, -1.0)
    factor = s_uv / (far_s + 2.0 * far_k)
    g_u, g_v = slabs[5:8], slabs[8:11]
    far_g, near_g = choose(top, g_v, g_u), choose(top, g_u, g_v)
    far_g[2] = far_g[2] + far_k * sign
    return [near_s - s_uv * factor, near_k] + [n - factor * g for n, g in zip(near_g, far_g)], factor


def reduce_end_right(factor, g_u, g_v, top):
    far_g, near_g = choose(top, g_v, g_u), choose(top, g_u, g_v)
    return [n - factor * g for n, g in zip(near_g, far_g)]


def grid_masks(nx, ny):
    at_x, at_y = lax.axis_index("gx"), lax.axis_index("gy")
    has_x_low, has_x_high = at_x > 0, at_x < lax.axis_size("gx") - 1
    has_y_low, has_y_high = at_y > 0, at_y < lax.axis_size("gy") - 1
    row, lane = iotas(nx + 8, 2 * ny)
    x_in = (row < nx) | ((row < nx + WIDE) & has_x_high) | ((row >= nx + 8 - WIDE) & has_x_low)
    y_in = (lane < ny) | ((lane < ny + WIDE) & has_y_high)
    y_in = y_in | ((lane >= 2 * ny - WIDE) & has_y_low)
    cell = x_in & y_in
    valid = flag(cell)
    in_x, in_xp = valid * moved(valid, -1, 0), valid * moved(valid, 1, 0)
    in_y, in_yp = valid * moved(valid, -1, 1), valid * moved(valid, 1, 1)
    return cell, in_x, in_xp, in_y, in_yp


def rim_columns(flips, tables, y_low, y_high, cell):
    ny = cell.shape[1] // 2
    size = cell.shape[0]
    strip_in = cell[:, ny:]
    lane = iotas(size, ny)[1]
    strips = []
    for b in range(2):
        part = slice(b * size, (b + 1) * size)
        strips.append(jnp.where(lane % 8 < WIDE, y_low[part, :], y_high[part, :]))
    flip, nz = flipped(flips), ny // 8
    if flips:
        strips = choose(flip, strips[::-1], strips)
    strips = [[lookup(table, strip) for table in tables] for strip in strips]

    def beside(q, at):
        z, strip = at % nz, strips[at // nz][q]
        if flips:
            turned = pltpu.roll(strip, ny - WIDE - 8 * jnp.where(flip, nz - 1 - z, z), 1)
        else:
            turned = moved(strip, -(8 * z + WIDE), 1)
        return jnp.where(strip_in, turned, 0.0)

    return beside


def body_rows(k_ref, low_ref, high_ref, q, at, row_in):
    spot = slice(at // 2 * 8, at // 2 * 8 + 8)
    side = rim_tile(low_ref[q, spot, :], high_ref[q, spot, :], at)
    return jnp.concatenate([k_ref[q, at], jnp.where(row_in, side, 0.0)], axis=0)


def flow_after(here, there, inside):
    total = here + there
    return jnp.where(inside > 0.0, 2.0 * (here * there) / total, total)


def tau_and_source(flow, back, inside, inside_back):
    return flow * (2.0 - inside) + back * (2.0 - inside_back), flow - back


def eliminate_kernel(
    stages, table_ref, cut_ref, k_ref, row_low, row_high, y_low, y_high,
    message_ref, own_ref, pair_ref, lx_ref, ly_ref, lz_ref, d_ref, e_ref, inverse_ref,
    all_ref, flow_ref, source_ref, centre_ref,
):
    layers, nx, ny = k_ref.shape[1:]
    nz = layers // 2
    cell, in_x, in_xp, in_y, in_yp = grid_masks(nx, ny)
    beside = rim_columns(False, [table_ref[q] for q in range(3)], y_low, y_high, cell)
    for at in range(layers):
        for q in range(3):
            body = body_rows(k_ref, row_low, row_high, q, at, cell[nx:, :ny])
            all_ref[q, at] = jnp.concatenate([body, beside(q, at)], axis=1)
    for at in range(layers):
        kx, ky = all_ref[0, at], all_ref[1, at]
        flow_x = flow_after(kx, moved(kx, -1, 0), in_x)
        flow_ref[at] = flow_after(ky, moved(ky, -1, 1), in_y)
        lx_ref[at] = flow_x * in_x
        centre_ref[at], source_ref[0, at] = tau_and_source(
            flow_x, moved(flow_x, 1, 0), in_x, in_xp
        )
        if at % nz < nz - 1:
            kz, above = all_ref[2, at], all_ref[2, at + 1]
            lz_ref[at] = jnp.where(cell, 2.0 * (kz * above) / (kz + above), 0.0)
    for at in range(layers):
        flow_y = flow_ref[at]
        ly_ref[at] = flow_y * in_y
        tau_y, source_ref[1, at] = tau_and_source(
            flow_y, moved(flow_y, 1, 1), in_y, in_yp
        )
        centre = centre_ref[at] + tau_y
        if at % nz > 0:
            centre = centre + lz_ref[at - 1]
        if at % nz < nz - 1:
            centre = centre + lz_ref[at]
        centre_ref[at] = jnp.where(cell, centre, 1.0)

    states = [{}, {}]
    for z in range(nz):
        for b in range(2):
            at, v = b * nz + z, states[b]
            centre = centre_ref[at]
            sources = [source_ref[0, at], source_ref[1, at]]
            if z == 0:
                v["source"] = sources + [lz_ref[at]]
                v["s_uu"], v["g_u"] = centre, v["source"]
            elif z == nz - 1:
                sources = sources + [-lz_ref[at - 1]]
                v["s_vv"] = centre - v["coupling"] * v["ratio"]
                v["s_uv"] = -v["coupling"] * v["spike"]
                v["g_v"] = [a + v["coupling"] * d for a, d in zip(sources, v["value"])]
            else:
                forward = sources + [lz_ref[at] - lz_ref[at - 1]]
                if z == 1:
                    pivot, numerator = centre, v["coupling"]
                else:
                    pivot = centre - v["coupling"] * v["ratio"]
                    forward = [a + v["coupling"] * d for a, d in zip(forward, v["value"])]
                    numerator = v["coupling"] * v["spike"]
                inverse = 1.0 / pivot
                v["value"] = [a * inverse for a in forward]
                v["spike"] = numerator * inverse
                v["s_uu"] = v["s_uu"] - numerator * v["spike"]
                v["g_u"] = [g + v["spike"] * a for g, a in zip(v["g_u"], forward)]
                inverse_ref[at] = inverse
                e_ref[at] = v["spike"]
                for f in range(3):
                    d_ref[f, at] = v["value"][f]
            if z < nz - 1:
                v["coupling"] = lz_ref[at] * open_after(cut_ref, at + 1)
                if z > 0:
                    v["ratio"] = v["coupling"] * inverse

    def block(b):
        v = states[b]
        k_ends = [all_ref[2, b * nz], all_ref[2, b * nz + nz - 1]]
        return [v["s_uu"], v["s_uv"], v["s_vv"]] + k_ends + v["g_u"] + v["g_v"]

    slabs, factors, rights, ends = join(block(0), block(1), open_after(cut_ref, nz))
    for q, slab in enumerate(slabs):
        own_ref[q] = slab
    for n, slab in enumerate(factors + rights + list(ends)):
        pair_ref[n] = slab
    if stages == 1:
        slabs, pair_ref[PAIR_COUNT - 1] = reduce_end(slabs, is_high(0))
    Message(len(slabs), 2, nx, ny).write(message_ref, slabs)


def join_kernel(stage, last, base, cut_ref, own_ref, message_ref, sibling_ref, factor_ref, next_ref, *joined):
    nx, ny = slab_size(own_ref)
    own = [own_ref[q] for q in range(FIRST_COUNT)]
    sibling = Message(FIRST_COUNT, 2, nx, ny).read(message_ref)
    for q, slab in enumerate(sibling):
        sibling_ref[q] = slab
    high = is_high(stage)
    slabs, factors, _, _ = join(
        choose(high, sibling, own),
        choose(high, own, sibling),
        open_after(cut_ref, base + 2 * stage),
    )
    for n, values in enumerate(factors):
        factor_ref[n] = values
    if last:
        slabs, factor_ref[6] = reduce_end(slabs, is_high(stage + 1))
    else:
        for q, slab in enumerate(slabs):
            joined[0][q] = slab
    Message(len(slabs), 2, nx, ny).write(next_ref, slabs)


def join_again_kernel(stage, last, own_ref, message_ref, factor_ref, sibling_ref, next_ref, *joined):
    nx, ny = slab_size(own_ref)
    own = [own_ref[q] for q in range(SECOND_COUNT)]
    sibling = Message(SECOND_COUNT, 1, nx, ny).read(message_ref)
    for q, slab in enumerate(sibling):
        sibling_ref[q] = slab
    above = is_high(stage)
    low, high = choose(above, sibling, own), choose(above, own, sibling)
    factors = [factor_ref[n] for n in range(6)]
    g_u, g_v, _ = join_right(factors, low[:3], low[3:], high[:3], high[3:])
    slabs = g_u + g_v
    if last:
        slabs = reduce_end_right(factor_ref[6], g_u, g_v, is_high(stage + 1))
    else:
        for q, slab in enumerate(slabs):
            joined[0][q] = slab
    Message(len(slabs), 1, nx, ny).write(next_ref, slabs)


def stencil(slab, link_x, link_y):
    return (
        link_x * moved(slab, -1, 0)
        + moved(link_x * slab, 1, 0)
        + (link_y * moved(slab, -1, 1) + moved(link_y * slab, 1, 1))
    )


def beyond_cuts(cut_ref, at, link_low, link_high):
    low, high = cut_ref[pl.ds(at, 1), :], cut_ref[pl.ds(at + 1, 1), :]
    return (
        link_low * jnp.concatenate([low, low], axis=1),
        link_high * jnp.concatenate([high, high], axis=1),
    )


def left_out(field_ref, f, at, link_x, link_y, cuts):
    return stencil(field_ref[f, at + 1], link_x, link_y) + (
        cuts[0] * field_ref[f, at] + cuts[1] * field_ref[f, at + 2]
    )


def middle_kernel(stages, cut_ref, *refs):
    own_ref, pair_ref, siblings, message_ref = refs[0], refs[1], refs[2 : stages + 1], refs[stages + 1]
    refs = refs[stages + 2 :]
    lx_ref, ly_ref, lz_ref, d_ref, e_ref, inverse_ref = refs[:6]
    next_ref, own2_ref, right_ref, d2_ref, factor_ref, end_ref, first_ref = refs[6:]
    layers = lx_ref.shape[0]
    nz = layers // 2
    nx, ny = slab_size(lx_ref)
    own = [own_ref[q] for q in range(FIRST_COUNT)]
    slots = []

    def keep(values):
        factor_ref[len(slots)] = values
        slots.append(None)

    def attach(state, sign, row, pivot, right, k):
        beside, k_beside, rights, exists = state[0], state[1], state[2:5], state[5]
        link, flow, tau = face(k_beside * exists, k)
        coupling = link * open_after(cut_ref, row)
        rights = rights[:2] + [rights[2] + sign * flow]
        inverse = 1.0 / (beside + tau)
        step = coupling * inverse
        right = [a + step * b for a, b in zip(right, rights)]
        right[2] = right[2] - sign * flow
        return pivot + tau - coupling * step, right, step, inverse, rights, (link, flow, tau)

    far = Message(LAST_COUNT, 2, nx, ny).read(message_ref)
    top = is_high(stages - 1)
    below, above = far + [flag(top)], far + [flag(jnp.logical_not(top))]
    for s in range(stages - 2, -1, -1):
        up = is_high(s)
        block = [siblings[s][q] for q in range(FIRST_COUNT)]
        sign = jnp.where(up, 1.0, -1.0)
        state = choose(up, below, above)
        far_s, far_k, near_s, near_k = choose(
            up, [block[0], block[3], block[2], block[4]], [block[2], block[4], block[0], block[3]]
        )
        far_g = choose(up, block[5:8], block[8:11])
        near_g = choose(up, block[8:11], block[5:8])
        row = layers + 2 + 2 * s
        pivot, right, step, _, _, _ = attach(state, sign, row, far_s, far_g, far_k)
        factor = block[1] / pivot
        keep(step)
        keep(factor)
        state = [near_s - block[1] * factor, near_k]
        state += [n - factor * r for n, r in zip(near_g, right)] + [jnp.float32(1.0)]
        below, above = choose(up, state, below), choose(up, above, state)

    pivot_u, right_u, step_b, inverse_b, rights_b, ends_b = attach(
        below, 1.0, 0, own[0], own[5:8], own[3]
    )
    pivot_v, right_v, step_a, inverse_a, rights_a, ends_a = attach(
        above, -1.0, layers, own[2], own[8:11], own[4]
    )
    held_b, held_a = inverse_b * below[5], inverse_a * above[5]
    inverse_u = 1.0 / pivot_u
    factor = own[1] * inverse_u
    inverse_v = 1.0 / (pivot_v - own[1] * factor)
    for values in (step_b, held_b, step_a, held_a, inverse_u, factor, inverse_v):
        keep(values)
    pair = [pair_ref[n] for n in range(PAIR_COUNT)]
    inner = pair[:6]
    ends = [ends_b[0], pair[12], ends_a[0]]
    for n, values in enumerate(ends):
        end_ref[n] = values

    for f in range(3):
        last = (right_v[f] - factor * right_u[f]) * inverse_v
        first_u = right_u[f] * inverse_u - factor * last
        low_v, high_u = join_inner(inner, pair[6 + f], pair[9 + f], first_u, last)
        first_ref[f, 0] = rights_b[f] * held_b + step_b * first_u
        first_ref[f, layers + 1] = rights_a[f] * held_a + step_a * last
        first_ref[f, 1] = first_u
        first_ref[f, nz] = low_v
        first_ref[f, nz + 1] = high_u
        first_ref[f, layers] = last
    for z in range(nz - 2, 0, -1):
        for at in (z, nz + z):
            ratio = lz_ref[at] * open_after(cut_ref, at + 1) * inverse_ref[at]
            spike = e_ref[at]
            for f in range(3):
                first_ref[f, at + 1] = (
                    d_ref[f, at]
                    + spike * first_ref[f, 1 + at - z]
                    + ratio * first_ref[f, at + 2]
                )

    def block(b):
        for z in range(nz):
            at = b * nz + z
            cuts = beyond_cuts(
                cut_ref, at,
                ends[b] if z == 0 else lz_ref[at - 1],
                ends[b + 1] if z == nz - 1 else lz_ref[at],
            )
            right = [left_out(first_ref, f, at, lx_ref[at], ly_ref[at], cuts) for f in range(3)]
            if z == 0:
                g_u = list(right)
            else:
                if z == 1:
                    forward = right
                else:
                    forward = [right[f] + coupling * value[f] for f in range(3)]
                if z < nz - 1:
                    inverse, spike = inverse_ref[at], e_ref[at]
                    value = [forward[f] * inverse for f in range(3)]
                    g_u = [g_u[f] + spike * forward[f] for f in range(3)]
                    for f in range(3):
                        d2_ref[f, at] = value[f]
                    coupling = lz_ref[at] * open_after(cut_ref, at + 1)
        return g_u, forward

    (low_u, low_v), (high_u, high_v) = block(0), block(1)
    g_u, g_v, middle = join_right(inner, low_u, low_v, high_u, high_v)
    for n, slab in enumerate(low_v + middle):
        right_ref[n] = slab
    for q, slab in enumerate(g_u + g_v):
        own2_ref[q] = slab
    slabs = g_u + g_v
    if stages == 1:
        slabs = reduce_end_right(pair[PAIR_COUNT - 1], g_u, g_v, is_high(0))
    Message(len(slabs), 1, nx, ny).write(next_ref, slabs)


def final_kernel(stages, cut_ref, *refs):
    own_ref, pair_ref, siblings, message_ref = refs[0], refs[1], refs[2 : stages + 1], refs[stages + 1]
    refs = refs[stages + 2 :]
    lx_ref, ly_ref, lz_ref, first_ref, right_ref, d2_ref, e_ref, inverse_ref = refs[:8]
    factor_ref, end_ref, pressure_out, residual_out = refs[8:12]
    change_ref, pressure_ref, residual_ref, sems = refs[12:]
    nz = lx_ref.shape[0] // 2
    nx, ny = slab_size(lx_ref)
    own = [own_ref[q] for q in range(SECOND_COUNT)]
    slots = []

    def kept():
        slots.append(None)
        return factor_ref[len(slots) - 1]

    below = above = Message(3, 1, nx, ny).read(message_ref)
    for s in range(stages - 2, -1, -1):
        up = is_high(s)
        block = [siblings[s][q] for q in range(SECOND_COUNT)]
        state = choose(up, below, above)
        far_g = choose(up, block[:3], block[3:])
        near_g = choose(up, block[3:], block[:3])
        step, factor = kept(), kept()
        right = [a + step * b for a, b in zip(far_g, state)]
        state = [n - factor * r for n, r in zip(near_g, right)]
        below, above = choose(up, state, below), choose(up, above, state)
    step_b, held_b, step_a, held_a = kept(), kept(), kept(), kept()
    inverse_u, factor, inverse_v = kept(), kept(), kept()
    inner = [pair_ref[n] for n in range(6)]
    start = own_start(nz)
    high = start > 0
    for f in range(3):
        right_u = own[f] + step_b * below[f]
        right_v = own[3 + f] + step_a * above[f]
        last = (right_v - factor * right_u) * inverse_v
        first = right_u * inverse_u - factor * last
        low_v, high_u = join_inner(inner, right_ref[f], right_ref[3 + f], first, last)
        beyond_b = below[f] * held_b + step_b * first
        beyond_a = above[f] * held_a + step_a * last
        values = choose(high, [low_v, high_u, last, beyond_a], [beyond_b, first, low_v, high_u])
        for at, slab in zip((0, 1, nz, nz + 1), values):
            change_ref[f, at] = slab
    ends = choose(high, [end_ref[1], end_ref[2]], [end_ref[0], end_ref[1]])
    for z in range(nz - 2, 0, -1):
        at = start + z
        opened = 1.0 - cut_ref[pl.ds(at + 1, 1), :]
        opened = jnp.concatenate([opened, opened], axis=1)
        ratio = lz_ref[at] * opened * inverse_ref[at]
        spike = e_ref[at]
        for f in range(3):
            change_ref[f, z + 1] = (
                d2_ref[f, at] + spike * change_ref[f, 1] + ratio * change_ref[f, z + 2]
            )
    own_part = (slice(0, nx), slice(0, ny))
    copies = []
    for z in range(nz):
        at = start + z
        cuts = beyond_cuts(
            cut_ref, at,
            ends[0] if z == 0 else lz_ref[at - 1],
            ends[1] if z == nz - 1 else lz_ref[at],
        )
        link_x, link_y = lx_ref[at], ly_ref[at]
        for f in range(3):
            pressure_ref[f, z] = (first_ref[f, at + 1] + change_ref[f, z + 1])[own_part]
            residual_ref[f, z] = left_out(change_ref, f, z, link_x, link_y, cuts)[own_part]
        if (z + 1) % CHUNK == 0:
            part = (slice(None), slice(z + 1 - CHUNK, z + 1))
            for n, (buffer, out) in enumerate(
                ((pressure_ref, pressure_out), (residual_ref, residual_out))
            ):
                copy = pltpu.make_async_copy(
                    buffer.at[part], out.at[part], sems.at[n, z // CHUNK]
                )
                copy.start()
                copies.append(copy)
    for copy in copies:
        copy.wait()


def put(ref, index, slab):
    rows, ny = slab.shape[0], slab.shape[1] // 2
    for h in range(2):
        half = slab[:, h * ny : (h + 1) * ny]
        ref[index + (h, slice(8, 8 + rows))] = half
        ref[index + (h, slice(0, 8))] = half[rows - 8 :]
        ref[index + (h, slice(8 + rows, 16 + rows))] = half[:8]


def get(ref, index, shift=0):
    rows = ref.shape[-2] - 16
    halves = [ref[index + (h, slice(8 + shift, 8 + shift + rows))] for h in range(2)]
    return jnp.concatenate(halves, axis=1)


def blank(slab):
    rows, ny = slab.shape[0] - 8, slab.shape[1] // 2
    side = jnp.concatenate([slab[:rows, ny:], jnp.zeros((8, ny), jnp.float32)], axis=0)
    return jnp.concatenate([slab[:, :ny], side], axis=1)


def signed():
    return jnp.where(is_high(0), -1.0, 1.0)


def both_halves(ref, r):
    values = ref[pl.ds(r, 1), :]
    return jnp.concatenate([values, values], axis=1)


def beside_sum(field_ref, index, lx_ref, ly_ref, j):
    here, link_y = get(field_ref, index), ly_ref[j]
    return (
        get(lx_ref, (j,)) * moved(here, -1, 0)
        + get(lx_ref, (j,), -1) * moved(here, 1, 0)
        + (link_y * moved(here, -1, 1) + moved(link_y * here, 1, 1))
    )


def put_half(ref, index, half):
    rows = half.shape[0]
    ref[index + (slice(8, 8 + rows),)] = half
    ref[index + (slice(0, 8),)] = half[rows - 8 :]
    ref[index + (slice(8 + rows, 16 + rows),)] = half[:8]


def harmonic(here, there):
    return here * there / (here + there)


def tau_after(here, there, inside):
    return jnp.where(inside > 0.0, harmonic(here, there), here + there)


def body_kernel(k_ref, row_low, row_high, lx_ref, tau_ref, source_ref, ky_ref, kz_ref, lz_ref):
    layers, nx, ny = k_ref.shape[1:]
    cell, in_x, in_xp = [mask[:, :ny] for mask in grid_masks(nx, ny)[:3]]
    share, share_back = 0.5 + 0.5 * in_x, 0.5 + 0.5 * in_xp
    zero = jnp.zeros((nx + 8, ny), jnp.float32)
    lz_ref[0] = zero
    lz_ref[layers] = zero
    for j in range(layers):
        kx, ky, kz = [body_rows(k_ref, row_low, row_high, q, j, cell[nx:]) for q in range(3)]
        tau = tau_after(kx, moved(kx, -1, 0), in_x)
        back = moved(tau, 1, 0)
        put_half(lx_ref, (j,), tau * in_x)
        tau_ref[j] = tau + back
        source_ref[j] = tau * share - back * share_back
        ky_ref[j] = ky
        kz_ref[j] = kz
        if j > 0:
            lz_ref[j] = jnp.where(cell, harmonic(below, kz), 0.0)
        below = kz


def end_eliminate_kernel(
    table_ref, cut_ref, y_low, y_high, lx_body, tau_body, source_body, ky_body, kz_body, lz_body,
    message_ref, own_ref, lx_ref, ly_ref, lz_ref, d_ref, ratio_ref, inverse_ref,
    kx_ref, tx_ref, ky_ref, kz_ref, source_ref, centre_ref,
):
    layers, size, ny = ky_body.shape
    nx = size - 8
    sign = signed()
    cell, in_x, in_xp, in_y, in_yp = grid_masks(nx, ny)
    share_x, share_xp = 0.5 + 0.5 * in_x[:, ny:], 0.5 + 0.5 * in_xp[:, ny:]
    share_y, share_yp = 0.5 + 0.5 * in_y, 0.5 + 0.5 * in_yp
    side_x, side_in = in_x[:, ny:], cell[:, ny:]
    rows = slice(8, 8 + size)

    def whole(body, side):
        return jnp.concatenate([body, side], axis=1)

    beside = rim_columns(True, [table_ref[q] for q in range(3)], y_low, y_high, cell)
    for j in range(layers):
        put_half(kx_ref, (j,), beside(0, j))
        ky_ref[j] = whole(ky_body[j], beside(1, j))
        kz_ref[j] = beside(2, j)
    lz_ref[0] = jnp.zeros((size, 2 * ny), jnp.float32)
    lz_ref[layers] = jnp.zeros((size, 2 * ny), jnp.float32)
    for j in range(layers):
        tau = tau_after(kx_ref[j, rows, :], kx_ref[j, slice(9, 9 + size), :], side_x)
        put_half(tx_ref, (j,), tau)
        put_half(lx_ref, (j, 1), tau * side_x)
        lx_ref[j, 0] = lx_body[j]
        ky = ky_ref[j]
        ky_ref[j] = tau_after(ky, moved(ky, -1, 1), in_y)
        if j < layers - 1:
            side = jnp.where(side_in, harmonic(kz_ref[j], kz_ref[j + 1]), 0.0)
            lz_ref[j + 1] = whole(lz_body[j + 1], side)
    for j in range(layers):
        tau, back = tx_ref[j, rows, :], tx_ref[j, slice(7, 7 + size), :]
        source_ref[0, j] = whole(source_body[j], tau * share_x - back * share_xp)
        centre = whole(tau_body[j], tau + back)
        tau = ky_ref[j]
        back = moved(tau, 1, 1)
        ly_ref[j] = tau * in_y
        source_ref[1, j] = tau * share_y - back * share_yp
        centre = centre + (tau + back)
        centre = centre + (whole(kz_body[0], kz_ref[0]) if j == 0 else lz_ref[j])
        if j < layers - 1:
            centre = centre + lz_ref[j + 1]
        centre_ref[j] = jnp.where(cell, centre, 1.0)
    for j in range(layers):
        flow_z = -0.5 * whole(kz_body[0], kz_ref[0]) if j == 0 else -lz_ref[j]
        if j < layers - 1:
            flow_z = flow_z + lz_ref[j + 1]
        forward = [source_ref[0, j], source_ref[1, j], sign * flow_z]
        pivot = centre_ref[j]
        if j > 0:
            pivot = pivot - coupling * ratio
            forward = [a + coupling * d for a, d in zip(forward, value)]
        if j < layers - 1:
            inverse = 1.0 / pivot
            coupling = lz_ref[j + 1] * (1.0 - both_halves(cut_ref, j + 1))
            ratio = coupling * inverse
            value = [a * inverse for a in forward]
            inverse_ref[j] = inverse
            ratio_ref[j] = ratio
            for f in range(3):
                d_ref[f, j] = value[f]
    slabs = [pivot, 0.5 * whole(kz_body[layers - 1], kz_ref[layers - 1])] + forward
    for q, slab in enumerate(slabs):
        own_ref[q] = slab
    Message(LAST_COUNT, 2, nx, ny).write(message_ref, slabs)


def expand_kernel(
    cut_ref, lx_ref, ly_ref, lz_ref, d_ref, ratio_ref, base_ref, phi_ref, part_ref
):
    layers = ly_ref.shape[0]
    zero = jnp.zeros(ly_ref.shape[1:], jnp.float32)
    phi, base = zero + 1.0, [zero] * 3
    put(phi_ref, (layers - 1,), phi)
    for f in range(3):
        put(base_ref, (f, layers - 1), zero)
    for j in range(layers - 2, -1, -1):
        ratio = ratio_ref[j]
        phi = ratio * phi
        put(phi_ref, (j,), phi)
        for f in range(3):
            base[f] = d_ref[f, j] + ratio * base[f]
            put(base_ref, (f, j), base[f])
    along_x = along_y = along_z = zero
    parts = [zero] * 3
    for j in range(layers):
        phi = get(phi_ref, (j,))
        along_x = along_x + (get(lx_ref, (j,)) * phi) * get(phi_ref, (j,), 1)
        along_y = along_y + (ly_ref[j] * phi) * moved(phi, -1, 1)
        cut_low = lz_ref[j] * both_halves(cut_ref, j)
        if j < layers - 1:
            cut_high = lz_ref[j + 1] * both_halves(cut_ref, j + 1)
            along_z = along_z + (cut_high * phi) * get(phi_ref, (j + 1,))
        for f in range(3):
            right = beside_sum(base_ref, (f, j), lx_ref, ly_ref, j)
            if j > 0:
                right = right + cut_low * get(base_ref, (f, j - 1))
            if j < layers - 1:
                right = right + cut_high * get(base_ref, (f, j + 1))
            parts[f] = blank(parts[f] + phi * right)
    for n, slab in enumerate(parts + [along_x, along_y, 2.0 * along_z]):
        part_ref[n] = slab


def end_join_kernel(layers, cut_ref, own_ref, message_ref, part_ref, next_ref, near_ref):
    nx, ny = slab_size(own_ref)
    own = [own_ref[q] for q in range(LAST_COUNT)]
    other = Message(LAST_COUNT, 2, nx, ny).read(message_ref)
    sign = signed()
    cut = both_halves(cut_ref, layers)
    link, flow, tau = face(own[1], other[1])
    coupling = link * (1.0 - cut)
    inverse_other = 1.0 / (other[0] + tau)
    step = coupling * inverse_other
    inverse = 1.0 / (own[0] + tau - coupling * step)
    right_own = own[2:4] + [own[4] + sign * flow]
    right_other = other[2:4] + [other[4] - sign * flow]
    cut_near = link * cut
    along_x, along_y, along_z = [part_ref[3 + n] for n in range(3)]
    slabs = []
    for f in range(3):
        near = (right_own[f] + step * right_other[f]) * inverse
        beyond = right_other[f] * inverse_other + step * near
        near_ref[f], near_ref[3 + f] = near, beyond
        right = part_ref[f] + stencil(near, along_x, along_y)
        slabs.append(right + (along_z * near + cut_near * beyond))
        near_ref[6 + f] = slabs[f]
    near_ref[9], near_ref[10], near_ref[11], near_ref[12] = step, inverse, inverse_other, link
    Message(3, 1, nx, ny).write(next_ref, slabs)


def correct_kernel(
    cut_ref, near_ref, lx_ref, ly_ref, lz_ref, ratio_ref, inverse_ref, base_ref, phi_ref,
    first_ref, change_ref, d_ref,
):
    layers = ly_ref.shape[0]
    for j in range(layers):
        phi = get(phi_ref, (j,))
        for f in range(3):
            put(first_ref, (f, j), get(base_ref, (f, j)) + phi * near_ref[f])
    for j in range(layers - 1):
        cut_low = lz_ref[j] * both_halves(cut_ref, j)
        cut_high = lz_ref[j + 1] * both_halves(cut_ref, j + 1)
        inverse = inverse_ref[j]
        if j > 0:
            coupling = lz_ref[j] * (1.0 - both_halves(cut_ref, j))
        for f in range(3):
            right = beside_sum(first_ref, (f, j), lx_ref, ly_ref, j)
            right = right + cut_high * get(first_ref, (f, j + 1))
            if j > 0:
                right = right + cut_low * get(first_ref, (f, j - 1)) + coupling * d_ref[f, j - 1]
            d_ref[f, j] = blank(right * inverse)
    change = [jnp.zeros(ly_ref.shape[1:], jnp.float32)] * 3
    for f in range(3):
        change_ref[f, layers - 1] = change[f]
    for j in range(layers - 2, -1, -1):
        ratio = ratio_ref[j]
        for f in range(3):
            change[f] = blank(d_ref[f, j] + ratio * change[f])
            change_ref[f, j] = change[f]


def end_final_kernel(
    cut_ref, message_ref, near_ref, lx_ref, ly_ref, lz_ref, phi_ref, first_ref, base_ref,
    pressure_out, residual_out, change_ref, pressure_ref, residual_ref, sems,
):
    layers = ly_ref.shape[0]
    nz = layers // 2
    nx, ny = slab_size(ly_ref)
    high = is_high(0)
    start = jnp.where(high, nz - own_start(nz), own_start(nz))
    beside_other = start > 0
    other = Message(3, 1, nx, ny).read(message_ref)
    step, inverse, inverse_other, link_near = [near_ref[9 + n] for n in range(4)]
    near = [(near_ref[6 + f] + step * other[f]) * inverse for f in range(3)]
    for i in range(-1, nz + 1):
        j = jnp.clip(start + i, 0, layers - 1)
        phi = get(phi_ref, (j,))
        for f in range(3):
            change = base_ref[f, j] + phi * near[f]
            if i == -1:
                change = jnp.where(beside_other, change, 0.0)
            if i == nz:
                beyond = other[f] * inverse_other + step * near[f]
                change = jnp.where(beside_other, beyond, change)
            put(change_ref, (f, i + 1), blank(change))
    lane = iotas(nx, ny)[1]
    first_lane, last_lane = lane == 0, lane == ny - 1

    def body(ref, index, shift=0):
        return ref[index + (0, slice(8 + shift, 8 + shift + nx))]

    def edge(ref, index):
        return ref[index + (1, slice(8, 8 + nx))]

    copies = []
    for i in range(nz):
        j = start + i
        z = jnp.where(high, nz - 1 - i, i)
        link_high = lz_ref[j + 1][:nx, :ny]
        if i == nz - 1:
            link_high = jnp.where(beside_other, link_near[:nx, :ny], link_high)
        cut_low = lz_ref[j][:nx, :ny] * cut_ref[pl.ds(j, 1), :]
        cut_high = link_high * cut_ref[pl.ds(j + 1, 1), :]
        link_x, link_xp = body(lx_ref, (j,)), body(lx_ref, (j,), -1)
        link_y = ly_ref[j][:nx]
        link_yp = moved(jnp.where(last_lane, link_y[:, ny:], link_y[:, :ny]), 1, 1)
        for f in range(3):
            at = (f, i + 1)
            here, side = body(change_ref, at), edge(change_ref, at)
            left_out = (
                link_x * body(change_ref, at, 1)
                + link_xp * body(change_ref, at, -1)
                + link_y[:, :ny] * moved(jnp.where(first_lane, side, here), -1, 1)
                + link_yp * moved(jnp.where(last_lane, side, here), 1, 1)
            )
            beyond = cut_low * body(change_ref, (f, i)) + cut_high * body(change_ref, (f, i + 2))
            pressure_ref[f, z] = body(first_ref, (f, j)) + here
            residual_ref[f, z] = left_out + beyond
        if (i + 1) % CHUNK == 0:
            part = (slice(None), pl.ds(jnp.where(high, nz - 1 - i, i + 1 - CHUNK), CHUNK))
            for n, (buffer, out) in enumerate(
                ((pressure_ref, pressure_out), (residual_ref, residual_out))
            ):
                copy = pltpu.make_async_copy(
                    buffer.at[part], out.at[part], sems.at[n, i // CHUNK]
                )
                copy.start(priority=n)
                copies.append(copy)
    for copy in copies:
        copy.wait()


def kernel_call(kernel, outputs, operands, scratch=(), smem=0, cost=None, space=pltpu.VMEM):
    specs = [pl.BlockSpec(memory_space=pltpu.SMEM)] * smem
    specs += [pl.BlockSpec(memory_space=pltpu.VMEM)] * (len(operands) - smem)
    return pl.pallas_call(
        kernel,
        out_shape=[jax.ShapeDtypeStruct(s, t) for s, t in outputs],
        in_specs=specs,
        out_specs=[pl.BlockSpec(memory_space=space)] * len(outputs),
        scratch_shapes=list(scratch),
        compiler_params=pltpu.CompilerParams(vmem_limit_bytes=32 * 2**20),
        cost_estimate=cost,
    )(*operands)


def swapped(values, stage):
    size = lax.axis_size("gz")
    return lax.ppermute(values, "gz", [(i, i ^ 2**stage) for i in range(size)])


def ring(values, axis, distance):
    size = lax.axis_size(axis)
    return lax.ppermute(values, axis, [(i, (i + distance) % size) for i in range(size)])


def slanted(values, x_distance):
    nx, nz = lax.axis_size("gx"), lax.axis_size("gz")
    route = []
    for i in range(nx):
        for k in range(nz):
            route.append((i * nz + k, (i + x_distance) % nx * nz + (k ^ 1)))
    return lax.ppermute(values, ("gx", "gz"), route)


def per_device(facies, perm_table, line_breaks):
    nz, nx, ny = facies.shape
    stages = (lax.axis_size("gz") - 1).bit_length() - 1
    i32, f32 = jnp.int32, jnp.float32
    two = lax.axis_size("gx") == 2
    layers = 2 * nz
    cut_rows = -(-(layers + 1 + 2 * stages) // 8) * 8
    sides = 1 if two else 2
    other = swapped(facies, 0)
    facies, *rows = kernel_call(
        pack_kernel,
        [((nz, nx, ny), i32)] + [((nz * 4, ny), i32)] * sides,
        [facies],
    )
    if two:
        rims = [ring(rows[0], "gx", 1), slanted(rows[0], 1)]
    else:
        rims = [ring(rows[1], "gx", 1), ring(rows[0], "gx", -1)]
        rims += [slanted(rows[1], 1), slanted(rows[0], -1)]
    k, table, cuts = kernel_call(
        functools.partial(prepare_kernel, stages),
        [((3, nz, nx, ny), f32), ((3, 8, ny), f32), ((cut_rows, ny), f32)],
        [perm_table, line_breaks, facies],
        smem=2,
        cost=pl.CostEstimate(flops=10**7, bytes_accessed=10**6, transcendentals=0),
    )
    strip, *rows = kernel_call(
        merge_kernel,
        [((2 * nx + 16, ny), i32)] + [((layers * 4, ny), i32)] * sides,
        [facies, other] + rims,
    )
    k, *rows = kernel_call(
        functools.partial(prepare_other_kernel, sides, stages == 1),
        [((3, layers, nx, ny), f32)] + [((3, layers * 4, ny), f32)] * sides,
        [table, k, other] + rows,
        cost=pl.CostEstimate(flops=10**7, bytes_accessed=10**6, transcendentals=0),
    )
    y_low, y_high = ring(strip, "gy", 1), ring(strip, "gy", -1)
    sizes = nz, nx, ny
    operands = [table, cuts, k, rows[0], rows[-1], y_low, y_high]
    return (sweep_ends if stages == 1 else sweep_tree)(sizes, stages, operands)


def sweep_ends(sizes, stages, operands):
    nz, nx, ny = sizes
    layers, f32 = 2 * nz, jnp.float32
    slab, tall = (nx + 8, 2 * ny), (2, nx + 24, ny)

    def slabs(*count):
        return (count + slab, f32)

    def talls(*count):
        return (count + tall, f32)

    def message_of(count, halo):
        return ((Message(count, halo, nx, ny).rows, ny), f32)

    def filler(flops):
        return pl.CostEstimate(flops=flops, bytes_accessed=10**6, transcendentals=0)

    half, tall_half = (nx + 8, ny), (nx + 24, ny)
    table, cuts, k, row_low, row_high, y_low, y_high = operands
    body = kernel_call(
        body_kernel,
        [((layers,) + tall_half, f32)] + [((layers,) + half, f32)] * 4
        + [((layers + 1,) + half, f32)],
        [k, row_low, row_high],
        cost=filler(10**7),
    )
    message, own, lx, ly, lz, d, ratio, inverse = kernel_call(
        end_eliminate_kernel,
        [message_of(LAST_COUNT, 2), slabs(LAST_COUNT), talls(layers), slabs(layers),
         slabs(layers + 1), slabs(3, layers), slabs(layers), slabs(layers)],
        [table, cuts, y_low, y_high] + list(body),
        [pltpu.VMEM((layers,) + tall_half, f32), pltpu.VMEM((layers,) + tall_half, f32),
         pltpu.VMEM(*slabs(layers)), pltpu.VMEM((layers,) + half, f32),
         pltpu.VMEM(*slabs(2, layers)), pltpu.VMEM(*slabs(layers))],
    )
    other = swapped(message, stages)
    base, phi, parts = kernel_call(
        expand_kernel,
        [talls(3, layers), talls(layers), slabs(6)],
        [cuts, lx, ly, lz, d, ratio],
        cost=filler(10**7),
    )
    message, near = kernel_call(
        functools.partial(end_join_kernel, layers),
        [message_of(3, 1), slabs(13)],
        [cuts, own, other, parts],
    )
    other = swapped(message, stages)
    first, change = kernel_call(
        correct_kernel,
        [talls(3, layers), slabs(3, layers)],
        [cuts, near, lx, ly, lz, ratio, inverse, base, phi],
        [pltpu.VMEM(*slabs(3, layers))],
        cost=filler(10**7),
    )
    out = ((3, nz, nx, ny), f32)
    return tuple(kernel_call(
        end_final_kernel,
        [out, out],
        [cuts, other, near, lx, ly, lz, phi, first, change],
        [pltpu.VMEM(*talls(3, nz + 2)), pltpu.VMEM(*out), pltpu.VMEM(*out),
         pltpu.SemaphoreType.DMA((2, nz // CHUNK))],
        space=pl.ANY,
    ))


def sweep_tree(sizes, stages, operands):
    nz, nx, ny = sizes
    layers, f32 = 2 * nz, jnp.float32
    cuts = operands[1]
    slab = (nx + 8, 2 * ny)
    one, three = ((layers,) + slab, f32), ((3, layers) + slab, f32)

    def slabs(count):
        return ((count,) + slab, f32)

    def message_of(count, halo):
        return ((Message(count, halo, nx, ny).rows, ny), f32)

    message, own, pair, lx, ly, lz, d, e, inverse = kernel_call(
        functools.partial(eliminate_kernel, stages),
        [message_of(LAST_COUNT if stages == 1 else FIRST_COUNT, 2)]
        + [slabs(FIRST_COUNT), slabs(PAIR_COUNT)]
        + [one] * 3 + [three, one, one],
        operands,
        [pltpu.VMEM(s, f32) for s in (three[0], one[0], (2,) + one[0], one[0])],
    )
    siblings, factors, group = [], [], own
    for s in range(stages - 1):
        last = s == stages - 2
        outputs = [slabs(FIRST_COUNT), slabs(7), message_of(LAST_COUNT if last else FIRST_COUNT, 2)]
        sibling, factor, message, *joined = kernel_call(
            functools.partial(join_kernel, s, last, layers + 1),
            outputs + ([] if last else [slabs(FIRST_COUNT)]),
            [cuts, group, swapped(message, s + 1)],
        )
        siblings.append(sibling)
        factors.append(factor)
        group = None if last else joined[0]
    fields = ((3, layers + 2) + slab, f32)
    message, own, rights, d2, kept, ends, first = kernel_call(
        functools.partial(middle_kernel, stages),
        [message_of(3 if stages == 1 else SECOND_COUNT, 1), slabs(SECOND_COUNT), slabs(6), three,
         slabs(2 * stages + 5), slabs(3), fields],
        [cuts, own, pair] + siblings + [swapped(message, stages)]
        + [lx, ly, lz, d, e, inverse],
    )
    siblings, group = [], own
    for s in range(stages - 1):
        last = s == stages - 2
        outputs = [slabs(SECOND_COUNT), message_of(3 if last else SECOND_COUNT, 1)]
        sibling, message, *joined = kernel_call(
            functools.partial(join_again_kernel, s, last),
            outputs + ([] if last else [slabs(SECOND_COUNT)]),
            [group, swapped(message, s + 1), factors[s]],
        )
        siblings.append(sibling)
        group = None if last else joined[0]
    out = ((3, nz, nx, ny), f32)
    pressure, residual = kernel_call(
        functools.partial(final_kernel, stages),
        [out, out],
        [cuts, own, pair] + siblings + [swapped(message, stages)]
        + [lx, ly, lz, first, rights, d2, e, inverse, kept, ends],
        [pltpu.VMEM((3, nz + 2) + slab, f32)]
        + [pltpu.VMEM((3, nz, nx, ny), f32)] * 2
        + [pltpu.SemaphoreType.DMA((2, nz // CHUNK))],
        space=pl.ANY,
    )
    return pressure, residual


def solution(mesh):
    return jax.shard_map(
        per_device,
        mesh=mesh,
        in_specs=(P("gz", "gx", "gy"), P(), P()),
        out_specs=(P(None, "gz", "gx", "gy"), P(None, "gz", "gx", "gy")),
        check_vma=False,
    )
```

```python
import functools

import jax
import jax.numpy as jnp
from jax import lax
from jax.experimental import pallas as pl
from jax.experimental.pallas import tpu as pltpu
from jax.sharding import PartitionSpec as P


WIDE = 3
FIRST_COUNT = 11
LAST_COUNT = 5
SECOND_COUNT = 6
PAIR_COUNT = 16
CHUNK = 4


def moved(values, amount, axis):
    size = values.shape[axis]
    amount = amount % size
    if amount == 0:
        return values
    return pltpu.roll(values, amount, axis)


def flag(condition):
    return condition.astype(jnp.float32)


def iotas(rows, lanes):
    return tuple(lax.broadcasted_iota(jnp.int32, (rows, lanes), d) for d in (0, 1))


def choose(condition, first, second):
    return [jnp.where(condition, a, b) for a, b in zip(first, second)]


def flipped(flips):
    return is_high(0) if flips else False


def is_high(stage):
    return (lax.axis_index("gz") >> (stage + 1)) % 2 == 1


def own_start(nz):
    return (lax.axis_index("gz") % 2) * nz


def pack_kernel(facies_ref, copy_ref, *row_refs):
    nz, nx, ny = facies_ref.shape
    copy_ref[...] = facies_ref[...]
    row = iotas(8, ny)[0]
    for z in range(0, nz, 2):
        pair = [facies_ref[z], facies_ref[z + 1]]
        first = jnp.where(row < 4, pair[0][:8], moved(pair[1][:8], 4, 0))
        last = jnp.where(row < 4, moved(pair[0][nx - 8 :], 4, 0), pair[1][nx - 8 :])
        spot = slice(4 * z, 4 * z + 8)
        if len(row_refs) == 1:
            row_refs[0][spot, :] = jnp.where(lax.axis_index("gx") == 0, last, first)
        else:
            row_refs[0][spot, :] = first
            row_refs[1][spot, :] = last


def rim_tile(low, high, layer):
    row = iotas(8, low.shape[1])[0]
    if layer % 2 == 0:
        return jnp.where(row < 4, high, moved(low, 4, 0))
    return jnp.where(row < 4, moved(high, 4, 0), low)


def merge_kernel(own_ref, other_ref, *refs):
    sides = (len(refs) - 1) // 3
    ins, strip_ref, row_refs = refs[: 2 * sides], refs[2 * sides], refs[2 * sides + 1 :]
    nz, nx, ny = own_ref.shape
    swap = own_start(nz) > 0
    lane = lax.broadcasted_iota(jnp.int32, (nx + 8, ny), 1)
    for b in range(2):
        own = swap == (b == 1)
        for n, ref in enumerate(row_refs):
            ref[4 * nz * b : 4 * nz * (b + 1), :] = jnp.where(own, ins[n][...], ins[sides + n][...])
        strip = jnp.zeros((nx + 8, ny), jnp.int32)
        for z in range(nz):
            start = 4 * nz * b + z // 2 * 8
            low, high = [ref[start : start + 8, :] for ref in (row_refs[0], row_refs[-1])]
            layer = jnp.where(own, own_ref[z], other_ref[z])
            layer = jnp.concatenate([layer, rim_tile(low, high, z)], axis=0)
            strip = jnp.where(lane // 8 == z, moved(layer, 8 * z + WIDE, 1), strip)
        strip_ref[b * (nx + 8) : (b + 1) * (nx + 8), :] = strip


def lookup(table, index):
    rows = [
        jnp.take_along_axis(table, index[r : r + 8], axis=1) for r in range(0, index.shape[0], 8)
    ]
    return jnp.concatenate(rows, axis=0)


def prepare_kernel(stages, labels, scalars, facies_ref, k_ref, table_ref, cut_ref):
    nz, nx, ny = facies_ref.shape
    lane = iotas(8, ny)[1]
    tables = []
    for q in range(3):
        values = jnp.zeros((8, ny), jnp.float32)
        for label in range(labels):
            values = jnp.where(lane == label, scalars[q * labels + label], values)
        if stages == 1:
            values = 2.0 * values
        table_ref[q] = values
        tables.append(values)
    for z in range(nz):
        for q in range(3):
            k_ref[q, z] = lookup(tables[q], facies_ref[z])
    pair = lax.axis_index("gz") // 2
    layers = [pair * 2 * nz + r - 1 for r in range(2 * nz + 1)]
    if stages == 1:
        high = is_high(0)
        layers = [
            pair * 2 * nz + jnp.where(high, 2 * nz - 1 - r, r - 1) for r in range(2 * nz + 1)
        ]
    for s in range(stages if stages > 1 else 0):
        base, size = (pair >> (s + 1)) << (s + 1), 2**s
        layers.append((base + size) * 2 * nz - 1)
        layers.append(jnp.where(is_high(s), base, base + 2 * size) * 2 * nz - 1)
    for r, layer in enumerate(layers):
        last = scalars.shape[0] - 1 - 3 * labels
        cut = scalars[3 * labels + jnp.clip(layer, 0, last)]
        cut_ref[r : r + 1, :] = jnp.full((1, ny), cut, jnp.float32)


def prepare_other_kernel(sides, flips, table_ref, own_ref, other_ref, *refs):
    rows, k_ref, row_refs = refs[:sides], refs[sides], refs[sides + 1 :]
    nz, _, ny = other_ref.shape
    start, flip = own_start(nz), flipped(flips)

    def spot(at, count):
        return jnp.where(flip, count - 1 - at, at)

    for q in range(3):
        for z in range(nz):
            k_ref[q, spot(start + z, 2 * nz)] = own_ref[q, z]
            k_ref[q, spot(nz - start + z, 2 * nz)] = lookup(table_ref[q], other_ref[z])
        for n in range(sides):
            for t in range(nz):
                tile = lookup(table_ref[q], rows[n][8 * t : 8 * t + 8, :])
                tile = jnp.where(flip, moved(tile, 4, 0), tile)
                row_refs[n][q, pl.ds(pl.multiple_of(8 * spot(t, nz), 8), 8), :] = tile


def face(a, b):
    product = a * b
    total = a + b
    harmonic = 2.0 * product / total
    inside = product > 0.0
    link = jnp.where(inside, harmonic, 0.0)
    flow = jnp.where(inside, harmonic, total)
    tau = jnp.where(inside, harmonic, 2.0 * total)
    return link, flow, tau


class Message:
    def __init__(self, count, halo, nx, ny):
        self.count, self.halo, self.nx, self.ny = count, halo, nx, ny
        self.one_sided = lax.axis_size("gx") == 2
        self.rows_each = halo if self.one_sided else 2 * halo
        self.per_tile = 8 // self.rows_each
        self.tiles = -(-count // self.per_tile)
        self.abreast = ny // (2 * halo * count)
        strips = -(-(nx // 8 + 1) // self.abreast)
        self.sides = count * nx + 8 * strips
        self.rows = self.sides + 8 * self.tiles

    def strip(self, t, q):
        start = self.count * self.nx + 8 * (t // self.abreast)
        shift = 2 * self.halo * (self.count * (t % self.abreast) + q) + self.halo
        return slice(start, start + 8), shift

    def tile(self, q):
        start = self.sides + 8 * (q // self.per_tile)
        return slice(start, start + 8)

    def side_moved(self, tile, q, sign):
        part = q % self.per_tile
        if not self.one_sided:
            return moved(tile, sign * (self.rows_each * part + self.halo), 0)
        first = lax.axis_index("gx") == 0
        out = jnp.where(
            first,
            moved(tile, sign * self.halo * part, 0),
            moved(tile, sign * self.halo * (part + 1), 0),
        )
        if sign > 0:
            return out
        row = iotas(8, self.ny)[0]
        return jnp.where(jnp.where(first, row, 7 - row) < self.halo, out, 1.0)

    def write(self, ref, slabs):
        nx, ny, halo = self.nx, self.ny, self.halo
        row, lane = iotas(8, ny)
        strips = {}
        for t in range(nx // 8 + 1):
            for q, slab in enumerate(slabs):
                spot, shift = self.strip(t, q)
                turned = moved(slab[8 * t : 8 * t + 8, ny:], shift, 1)
                held = strips.get(spot.start, turned)
                strips[spot.start] = jnp.where(lane < shift - halo, held, turned)
        for start, strip in strips.items():
            ref[start : start + 8, :] = strip
        for q, slab in enumerate(slabs):
            ref[q * nx : (q + 1) * nx, :] = slab[:nx, :ny]
            turned = self.side_moved(slab[nx:, :ny], q, 1)
            part = q % self.per_tile
            tile = turned if part == 0 else jnp.where(row < self.rows_each * part, tile, turned)
            if part == self.per_tile - 1 or q == self.count - 1:
                ref[self.tile(q), :] = tile

    def read(self, ref):
        nx = self.nx
        slabs = []
        for q in range(self.count):
            side = self.side_moved(ref[self.tile(q), :], q, -1)
            body = jnp.concatenate([ref[q * nx : (q + 1) * nx, :], side], axis=0)
            beside = []
            for t in range(nx // 8 + 1):
                spot, shift = self.strip(t, q)
                beside.append(moved(ref[spot, :], -shift, 1))
            slabs.append(jnp.concatenate([body, jnp.concatenate(beside, axis=0)], axis=1))
        return slabs


def open_after(cut_ref, r):
    cut = 1.0 - cut_ref[r : r + 1, :]
    return jnp.concatenate([cut, cut], axis=1)


def slab_size(ref):
    return ref.shape[-2] - 8, ref.shape[-1] // 2


def join(low, high, opened):
    ends = link, flow, tau = face(low[4], high[3])
    coupling = link * opened
    inverse = 1.0 / (low[2] + tau)
    step = coupling * inverse
    last_inverse = 1.0 / (high[0] + tau - coupling * step)
    outer = low[1] * inverse
    weight = step * low[1]
    weight_low, weight_high = weight * last_inverse, high[1] * last_inverse
    right_low = low[8:10] + [low[10] + flow]
    right_high = high[5:7] + [high[7] - flow]
    s_uu = low[0] - outer * low[1] - weight * weight_low
    s_uv = -weight * weight_high
    s_vv = high[2] - high[1] * weight_high
    factors = [outer, step, weight_low, weight_high, inverse, last_inverse]
    g_u, g_v, middle = join_right(factors, low[5:8], right_low, right_high, high[8:11])
    return [s_uu, s_uv, s_vv, low[3], high[4]] + g_u + g_v, factors, right_low + middle, ends


def join_right(factors, low_u, low_v, high_u, high_v):
    outer, step, weight_low, weight_high = factors[:4]
    middle = [b + step * a for a, b in zip(low_v, high_u)]
    g_u = [g - outer * a - weight_low * m for g, a, m in zip(low_u, low_v, middle)]
    g_v = [g - weight_high * m for g, m in zip(high_v, middle)]
    return g_u, g_v, middle


def join_inner(factors, right_low, middle, first, last):
    outer, step, weight_low, weight_high, inverse, last_inverse = factors
    high = last_inverse * middle - weight_low * first - weight_high * last
    return inverse * right_low - outer * first + step * high, high


def reduce_end(slabs, top):
    s_uu, s_uv, s_vv, k_u, k_v = slabs[:5]
    far_s, near_s = choose(top, [s_vv, s_uu], [s_uu, s_vv])
    far_k, near_k = choose(top, [k_v, k_u], [k_u, k_v])
    sign = jnp.where(top, 1.0, -1.0)
    factor = s_uv / (far_s + 2.0 * far_k)
    g_u, g_v = slabs[5:8], slabs[8:11]
    far_g, near_g = choose(top, g_v, g_u), choose(top, g_u, g_v)
    far_g[2] = far_g[2] + far_k * sign
    return [near_s - s_uv * factor, near_k] + [n - factor * g for n, g in zip(near_g, far_g)], factor


def reduce_end_right(factor, g_u, g_v, top):
    far_g, near_g = choose(top, g_v, g_u), choose(top, g_u, g_v)
    return [n - factor * g for n, g in zip(near_g, far_g)]


def grid_masks(nx, ny):
    at_x, at_y = lax.axis_index("gx"), lax.axis_index("gy")
    has_x_low, has_x_high = at_x > 0, at_x < lax.axis_size("gx") - 1
    has_y_low, has_y_high = at_y > 0, at_y < lax.axis_size("gy") - 1
    row, lane = iotas(nx + 8, 2 * ny)
    x_in = (row < nx) | ((row < nx + WIDE) & has_x_high) | ((row >= nx + 8 - WIDE) & has_x_low)
    y_in = (lane < ny) | ((lane < ny + WIDE) & has_y_high)
    y_in = y_in | ((lane >= 2 * ny - WIDE) & has_y_low)
    cell = x_in & y_in
    valid = flag(cell)
    in_x, in_xp = valid * moved(valid, -1, 0), valid * moved(valid, 1, 0)
    in_y, in_yp = valid * moved(valid, -1, 1), valid * moved(valid, 1, 1)
    return cell, in_x, in_xp, in_y, in_yp


def rim_columns(flips, tables, y_low, y_high, cell):
    ny = cell.shape[1] // 2
    size = cell.shape[0]
    strip_in = cell[:, ny:]
    lane = iotas(size, ny)[1]
    strips = []
    for b in range(2):
        part = slice(b * size, (b + 1) * size)
        strips.append(jnp.where(lane % 8 < WIDE, y_low[part, :], y_high[part, :]))
    flip, nz = flipped(flips), ny // 8
    if flips:
        strips = choose(flip, strips[::-1], strips)
    strips = [[lookup(table, strip) for table in tables] for strip in strips]

    def beside(q, at):
        z, strip = at % nz, strips[at // nz][q]
        if flips:
            turned = pltpu.roll(strip, ny - WIDE - 8 * jnp.where(flip, nz - 1 - z, z), 1)
        else:
            turned = moved(strip, -(8 * z + WIDE), 1)
        return jnp.where(strip_in, turned, 0.0)

    return beside


def body_rows(k_ref, low_ref, high_ref, q, at, row_in):
    spot = slice(at // 2 * 8, at // 2 * 8 + 8)
    side = rim_tile(low_ref[q, spot, :], high_ref[q, spot, :], at)
    return jnp.concatenate([k_ref[q, at], jnp.where(row_in, side, 0.0)], axis=0)


def flow_after(here, there, inside):
    total = here + there
    return jnp.where(inside > 0.0, 2.0 * (here * there) / total, total)


def tau_and_source(flow, back, inside, inside_back):
    return flow * (2.0 - inside) + back * (2.0 - inside_back), flow - back


def eliminate_kernel(
    stages, table_ref, cut_ref, k_ref, row_low, row_high, y_low, y_high,
    message_ref, own_ref, pair_ref, lx_ref, ly_ref, lz_ref, d_ref, e_ref, inverse_ref,
    all_ref, flow_ref, source_ref, centre_ref,
):
    layers, nx, ny = k_ref.shape[1:]
    nz = layers // 2
    cell, in_x, in_xp, in_y, in_yp = grid_masks(nx, ny)
    beside = rim_columns(False, [table_ref[q] for q in range(3)], y_low, y_high, cell)
    for at in range(layers):
        for q in range(3):
            body = body_rows(k_ref, row_low, row_high, q, at, cell[nx:, :ny])
            all_ref[q, at] = jnp.concatenate([body, beside(q, at)], axis=1)
    for at in range(layers):
        kx, ky = all_ref[0, at], all_ref[1, at]
        flow_x = flow_after(kx, moved(kx, -1, 0), in_x)
        flow_ref[at] = flow_after(ky, moved(ky, -1, 1), in_y)
        lx_ref[at] = flow_x * in_x
        centre_ref[at], source_ref[0, at] = tau_and_source(
            flow_x, moved(flow_x, 1, 0), in_x, in_xp
        )
        if at % nz < nz - 1:
            kz, above = all_ref[2, at], all_ref[2, at + 1]
            lz_ref[at] = jnp.where(cell, 2.0 * (kz * above) / (kz + above), 0.0)
    for at in range(layers):
        flow_y = flow_ref[at]
        ly_ref[at] = flow_y * in_y
        tau_y, source_ref[1, at] = tau_and_source(
            flow_y, moved(flow_y, 1, 1), in_y, in_yp
        )
        centre = centre_ref[at] + tau_y
        if at % nz > 0:
            centre = centre + lz_ref[at - 1]
        if at % nz < nz - 1:
            centre = centre + lz_ref[at]
        centre_ref[at] = jnp.where(cell, centre, 1.0)

    states = [{}, {}]
    for z in range(nz):
        for b in range(2):
            at, v = b * nz + z, states[b]
            centre = centre_ref[at]
            sources = [source_ref[0, at], source_ref[1, at]]
            if z == 0:
                v["source"] = sources + [lz_ref[at]]
                v["s_uu"], v["g_u"] = centre, v["source"]
            elif z == nz - 1:
                sources = sources + [-lz_ref[at - 1]]
                v["s_vv"] = centre - v["coupling"] * v["ratio"]
                v["s_uv"] = -v["coupling"] * v["spike"]
                v["g_v"] = [a + v["coupling"] * d for a, d in zip(sources, v["value"])]
            else:
                forward = sources + [lz_ref[at] - lz_ref[at - 1]]
                if z == 1:
                    pivot, numerator = centre, v["coupling"]
                else:
                    pivot = centre - v["coupling"] * v["ratio"]
                    forward = [a + v["coupling"] * d for a, d in zip(forward, v["value"])]
                    numerator = v["coupling"] * v["spike"]
                inverse = 1.0 / pivot
                v["value"] = [a * inverse for a in forward]
                v["spike"] = numerator * inverse
                v["s_uu"] = v["s_uu"] - numerator * v["spike"]
                v["g_u"] = [g + v["spike"] * a for g, a in zip(v["g_u"], forward)]
                inverse_ref[at] = inverse
                e_ref[at] = v["spike"]
                for f in range(3):
                    d_ref[f, at] = v["value"][f]
            if z < nz - 1:
                v["coupling"] = lz_ref[at] * open_after(cut_ref, at + 1)
                if z > 0:
                    v["ratio"] = v["coupling"] * inverse

    def block(b):
        v = states[b]
        k_ends = [all_ref[2, b * nz], all_ref[2, b * nz + nz - 1]]
        return [v["s_uu"], v["s_uv"], v["s_vv"]] + k_ends + v["g_u"] + v["g_v"]

    slabs, factors, rights, ends = join(block(0), block(1), open_after(cut_ref, nz))
    for q, slab in enumerate(slabs):
        own_ref[q] = slab
    for n, slab in enumerate(factors + rights + list(ends)):
        pair_ref[n] = slab
    if stages == 1:
        slabs, pair_ref[PAIR_COUNT - 1] = reduce_end(slabs, is_high(0))
    Message(len(slabs), 2, nx, ny).write(message_ref, slabs)


def join_kernel(stage, last, base, cut_ref, own_ref, message_ref, sibling_ref, factor_ref, next_ref, *joined):
    nx, ny = slab_size(own_ref)
    own = [own_ref[q] for q in range(FIRST_COUNT)]
    sibling = Message(FIRST_COUNT, 2, nx, ny).read(message_ref)
    for q, slab in enumerate(sibling):
        sibling_ref[q] = slab
    high = is_high(stage)
    slabs, factors, _, _ = join(
        choose(high, sibling, own),
        choose(high, own, sibling),
        open_after(cut_ref, base + 2 * stage),
    )
    for n, values in enumerate(factors):
        factor_ref[n] = values
    if last:
        slabs, factor_ref[6] = reduce_end(slabs, is_high(stage + 1))
    else:
        for q, slab in enumerate(slabs):
            joined[0][q] = slab
    Message(len(slabs), 2, nx, ny).write(next_ref, slabs)


def join_again_kernel(stage, last, own_ref, message_ref, factor_ref, sibling_ref, next_ref, *joined):
    nx, ny = slab_size(own_ref)
    own = [own_ref[q] for q in range(SECOND_COUNT)]
    sibling = Message(SECOND_COUNT, 1, nx, ny).read(message_ref)
    for q, slab in enumerate(sibling):
        sibling_ref[q] = slab
    above = is_high(stage)
    low, high = choose(above, sibling, own), choose(above, own, sibling)
    factors = [factor_ref[n] for n in range(6)]
    g_u, g_v, _ = join_right(factors, low[:3], low[3:], high[:3], high[3:])
    slabs = g_u + g_v
    if last:
        slabs = reduce_end_right(factor_ref[6], g_u, g_v, is_high(stage + 1))
    else:
        for q, slab in enumerate(slabs):
            joined[0][q] = slab
    Message(len(slabs), 1, nx, ny).write(next_ref, slabs)


def stencil(slab, link_x, link_y):
    return (
        link_x * moved(slab, -1, 0)
        + moved(link_x * slab, 1, 0)
        + (link_y * moved(slab, -1, 1) + moved(link_y * slab, 1, 1))
    )


def beyond_cuts(cut_ref, at, link_low, link_high):
    low, high = cut_ref[pl.ds(at, 1), :], cut_ref[pl.ds(at + 1, 1), :]
    return (
        link_low * jnp.concatenate([low, low], axis=1),
        link_high * jnp.concatenate([high, high], axis=1),
    )


def left_out(field_ref, f, at, link_x, link_y, cuts):
    return stencil(field_ref[f, at + 1], link_x, link_y) + (
        cuts[0] * field_ref[f, at] + cuts[1] * field_ref[f, at + 2]
    )


def middle_kernel(stages, cut_ref, *refs):
    own_ref, pair_ref, siblings, message_ref = refs[0], refs[1], refs[2 : stages + 1], refs[stages + 1]
    refs = refs[stages + 2 :]
    lx_ref, ly_ref, lz_ref, d_ref, e_ref, inverse_ref = refs[:6]
    next_ref, own2_ref, right_ref, d2_ref, factor_ref, end_ref, first_ref = refs[6:]
    layers = lx_ref.shape[0]
    nz = layers // 2
    nx, ny = slab_size(lx_ref)
    own = [own_ref[q] for q in range(FIRST_COUNT)]
    slots = []

    def keep(values):
        factor_ref[len(slots)] = values
        slots.append(None)

    def attach(state, sign, row, pivot, right, k):
        beside, k_beside, rights, exists = state[0], state[1], state[2:5], state[5]
        link, flow, tau = face(k_beside * exists, k)
        coupling = link * open_after(cut_ref, row)
        rights = rights[:2] + [rights[2] + sign * flow]
        inverse = 1.0 / (beside + tau)
        step = coupling * inverse
        right = [a + step * b for a, b in zip(right, rights)]
        right[2] = right[2] - sign * flow
        return pivot + tau - coupling * step, right, step, inverse, rights, (link, flow, tau)

    far = Message(LAST_COUNT, 2, nx, ny).read(message_ref)
    top = is_high(stages - 1)
    below, above = far + [flag(top)], far + [flag(jnp.logical_not(top))]
    for s in range(stages - 2, -1, -1):
        up = is_high(s)
        block = [siblings[s][q] for q in range(FIRST_COUNT)]
        sign = jnp.where(up, 1.0, -1.0)
        state = choose(up, below, above)
        far_s, far_k, near_s, near_k = choose(
            up, [block[0], block[3], block[2], block[4]], [block[2], block[4], block[0], block[3]]
        )
        far_g = choose(up, block[5:8], block[8:11])
        near_g = choose(up, block[8:11], block[5:8])
        row = layers + 2 + 2 * s
        pivot, right, step, _, _, _ = attach(state, sign, row, far_s, far_g, far_k)
        factor = block[1] / pivot
        keep(step)
        keep(factor)
        state = [near_s - block[1] * factor, near_k]
        state += [n - factor * r for n, r in zip(near_g, right)] + [jnp.float32(1.0)]
        below, above = choose(up, state, below), choose(up, above, state)

    pivot_u, right_u, step_b, inverse_b, rights_b, ends_b = attach(
        below, 1.0, 0, own[0], own[5:8], own[3]
    )
    pivot_v, right_v, step_a, inverse_a, rights_a, ends_a = attach(
        above, -1.0, layers, own[2], own[8:11], own[4]
    )
    held_b, held_a = inverse_b * below[5], inverse_a * above[5]
    inverse_u = 1.0 / pivot_u
    factor = own[1] * inverse_u
    inverse_v = 1.0 / (pivot_v - own[1] * factor)
    for values in (step_b, held_b, step_a, held_a, inverse_u, factor, inverse_v):
        keep(values)
    pair = [pair_ref[n] for n in range(PAIR_COUNT)]
    inner = pair[:6]
    ends = [ends_b[0], pair[12], ends_a[0]]
    for n, values in enumerate(ends):
        end_ref[n] = values

    for f in range(3):
        last = (right_v[f] - factor * right_u[f]) * inverse_v
        first_u = right_u[f] * inverse_u - factor * last
        low_v, high_u = join_inner(inner, pair[6 + f], pair[9 + f], first_u, last)
        first_ref[f, 0] = rights_b[f] * held_b + step_b * first_u
        first_ref[f, layers + 1] = rights_a[f] * held_a + step_a * last
        first_ref[f, 1] = first_u
        first_ref[f, nz] = low_v
        first_ref[f, nz + 1] = high_u
        first_ref[f, layers] = last
    for z in range(nz - 2, 0, -1):
        for at in (z, nz + z):
            ratio = lz_ref[at] * open_after(cut_ref, at + 1) * inverse_ref[at]
            spike = e_ref[at]
            for f in range(3):
                first_ref[f, at + 1] = (
                    d_ref[f, at]
                    + spike * first_ref[f, 1 + at - z]
                    + ratio * first_ref[f, at + 2]
                )

    def block(b):
        for z in range(nz):
            at = b * nz + z
            cuts = beyond_cuts(
                cut_ref, at,
                ends[b] if z == 0 else lz_ref[at - 1],
                ends[b + 1] if z == nz - 1 else lz_ref[at],
            )
            right = [left_out(first_ref, f, at, lx_ref[at], ly_ref[at], cuts) for f in range(3)]
            if z == 0:
                g_u = list(right)
            else:
                if z == 1:
                    forward = right
                else:
                    forward = [right[f] + coupling * value[f] for f in range(3)]
                if z < nz - 1:
                    inverse, spike = inverse_ref[at], e_ref[at]
                    value = [forward[f] * inverse for f in range(3)]
                    g_u = [g_u[f] + spike * forward[f] for f in range(3)]
                    for f in range(3):
                        d2_ref[f, at] = value[f]
                    coupling = lz_ref[at] * open_after(cut_ref, at + 1)
        return g_u, forward

    (low_u, low_v), (high_u, high_v) = block(0), block(1)
    g_u, g_v, middle = join_right(inner, low_u, low_v, high_u, high_v)
    for n, slab in enumerate(low_v + middle):
        right_ref[n] = slab
    for q, slab in enumerate(g_u + g_v):
        own2_ref[q] = slab
    slabs = g_u + g_v
    if stages == 1:
        slabs = reduce_end_right(pair[PAIR_COUNT - 1], g_u, g_v, is_high(0))
    Message(len(slabs), 1, nx, ny).write(next_ref, slabs)


def final_kernel(stages, cut_ref, *refs):
    own_ref, pair_ref, siblings, message_ref = refs[0], refs[1], refs[2 : stages + 1], refs[stages + 1]
    refs = refs[stages + 2 :]
    lx_ref, ly_ref, lz_ref, first_ref, right_ref, d2_ref, e_ref, inverse_ref = refs[:8]
    factor_ref, end_ref, pressure_out, residual_out = refs[8:12]
    change_ref, pressure_ref, residual_ref, sems = refs[12:]
    nz = lx_ref.shape[0] // 2
    nx, ny = slab_size(lx_ref)
    own = [own_ref[q] for q in range(SECOND_COUNT)]
    slots = []

    def kept():
        slots.append(None)
        return factor_ref[len(slots) - 1]

    below = above = Message(3, 1, nx, ny).read(message_ref)
    for s in range(stages - 2, -1, -1):
        up = is_high(s)
        block = [siblings[s][q] for q in range(SECOND_COUNT)]
        state = choose(up, below, above)
        far_g = choose(up, block[:3], block[3:])
        near_g = choose(up, block[3:], block[:3])
        step, factor = kept(), kept()
        right = [a + step * b for a, b in zip(far_g, state)]
        state = [n - factor * r for n, r in zip(near_g, right)]
        below, above = choose(up, state, below), choose(up, above, state)
    step_b, held_b, step_a, held_a = kept(), kept(), kept(), kept()
    inverse_u, factor, inverse_v = kept(), kept(), kept()
    inner = [pair_ref[n] for n in range(6)]
    start = own_start(nz)
    high = start > 0
    for f in range(3):
        right_u = own[f] + step_b * below[f]
        right_v = own[3 + f] + step_a * above[f]
        last = (right_v - factor * right_u) * inverse_v
        first = right_u * inverse_u - factor * last
        low_v, high_u = join_inner(inner, right_ref[f], right_ref[3 + f], first, last)
        beyond_b = below[f] * held_b + step_b * first
        beyond_a = above[f] * held_a + step_a * last
        values = choose(high, [low_v, high_u, last, beyond_a], [beyond_b, first, low_v, high_u])
        for at, slab in zip((0, 1, nz, nz + 1), values):
            change_ref[f, at] = slab
    ends = choose(high, [end_ref[1], end_ref[2]], [end_ref[0], end_ref[1]])
    for z in range(nz - 2, 0, -1):
        at = start + z
        opened = 1.0 - cut_ref[pl.ds(at + 1, 1), :]
        opened = jnp.concatenate([opened, opened], axis=1)
        ratio = lz_ref[at] * opened * inverse_ref[at]
        spike = e_ref[at]
        for f in range(3):
            change_ref[f, z + 1] = (
                d2_ref[f, at] + spike * change_ref[f, 1] + ratio * change_ref[f, z + 2]
            )
    own_part = (slice(0, nx), slice(0, ny))
    copies = []
    for z in range(nz):
        at = start + z
        cuts = beyond_cuts(
            cut_ref, at,
            ends[0] if z == 0 else lz_ref[at - 1],
            ends[1] if z == nz - 1 else lz_ref[at],
        )
        link_x, link_y = lx_ref[at], ly_ref[at]
        for f in range(3):
            pressure_ref[f, z] = (first_ref[f, at + 1] + change_ref[f, z + 1])[own_part]
            residual_ref[f, z] = left_out(change_ref, f, z, link_x, link_y, cuts)[own_part]
        if (z + 1) % CHUNK == 0:
            part = (slice(None), slice(z + 1 - CHUNK, z + 1))
            for n, (buffer, out) in enumerate(
                ((pressure_ref, pressure_out), (residual_ref, residual_out))
            ):
                copy = pltpu.make_async_copy(
                    buffer.at[part], out.at[part], sems.at[n, z // CHUNK]
                )
                copy.start()
                copies.append(copy)
    for copy in copies:
        copy.wait()


def put(ref, index, slab):
    rows, ny = slab.shape[0], slab.shape[1] // 2
    for h in range(2):
        half = slab[:, h * ny : (h + 1) * ny]
        ref[index + (h, slice(8, 8 + rows))] = half
        ref[index + (h, slice(0, 8))] = half[rows - 8 :]
        ref[index + (h, slice(8 + rows, 16 + rows))] = half[:8]


def get(ref, index, shift=0):
    rows = ref.shape[-2] - 16
    halves = [ref[index + (h, slice(8 + shift, 8 + shift + rows))] for h in range(2)]
    return jnp.concatenate(halves, axis=1)


def signed():
    return jnp.where(is_high(0), -1.0, 1.0)


def both_halves(ref, r):
    values = ref[pl.ds(r, 1), :]
    return jnp.concatenate([values, values], axis=1)


def beside_sum(field_ref, index, lx_ref, ly_ref, j):
    here, link_y = get(field_ref, index), ly_ref[j]
    return (
        get(lx_ref, (j,)) * get(field_ref, index, 1)
        + get(lx_ref, (j,), -1) * get(field_ref, index, -1)
        + (link_y * moved(here, -1, 1) + moved(link_y * here, 1, 1))
    )


def put_half(ref, index, half):
    rows = half.shape[0]
    ref[index + (slice(8, 8 + rows),)] = half
    ref[index + (slice(0, 8),)] = half[rows - 8 :]
    ref[index + (slice(8 + rows, 16 + rows),)] = half[:8]


def harmonic(here, there):
    return here * there / (here + there)


def tau_after(here, there, inside):
    return jnp.where(inside > 0.0, harmonic(here, there), here + there)


def body_kernel(k_ref, row_low, row_high, lx_ref, tau_ref, source_ref, ky_ref, kz_ref, lz_ref):
    layers, nx, ny = k_ref.shape[1:]
    cell, in_x, in_xp = [mask[:, :ny] for mask in grid_masks(nx, ny)[:3]]
    share, share_back = 0.5 + 0.5 * in_x, 0.5 + 0.5 * in_xp
    zero = jnp.zeros((nx + 8, ny), jnp.float32)
    lz_ref[0] = zero
    lz_ref[layers] = zero
    for j in range(layers):
        kx, ky, kz = [body_rows(k_ref, row_low, row_high, q, j, cell[nx:]) for q in range(3)]
        tau = tau_after(kx, moved(kx, -1, 0), in_x)
        back = moved(tau, 1, 0)
        put_half(lx_ref, (j,), tau * in_x)
        tau_ref[j] = tau + back
        source_ref[j] = tau * share - back * share_back
        ky_ref[j] = ky
        kz_ref[j] = kz
        if j > 0:
            lz_ref[j] = jnp.where(cell, harmonic(below, kz), 0.0)
        below = kz


def end_eliminate_kernel(
    table_ref, cut_ref, y_low, y_high, lx_body, tau_body, source_body, ky_body, kz_body, lz_body,
    message_ref, own_ref, lx_ref, ly_ref, lz_ref, d_ref, ratio_ref, inverse_ref,
    kx_ref, tx_ref, ky_ref, kz_ref, source_ref, centre_ref,
):
    layers, size, ny = ky_body.shape
    nx = size - 8
    sign = signed()
    cell, in_x, in_xp, in_y, in_yp = grid_masks(nx, ny)
    share_x, share_xp = 0.5 + 0.5 * in_x[:, ny:], 0.5 + 0.5 * in_xp[:, ny:]
    share_y, share_yp = 0.5 + 0.5 * in_y, 0.5 + 0.5 * in_yp
    side_x, side_in = in_x[:, ny:], cell[:, ny:]
    rows = slice(8, 8 + size)

    def whole(body, side):
        return jnp.concatenate([body, side], axis=1)

    beside = rim_columns(True, [table_ref[q] for q in range(3)], y_low, y_high, cell)
    for j in range(layers):
        put_half(kx_ref, (j,), beside(0, j))
        ky_ref[j] = whole(ky_body[j], beside(1, j))
        kz_ref[j] = beside(2, j)
    lz_ref[0] = jnp.zeros((size, 2 * ny), jnp.float32)
    lz_ref[layers] = jnp.zeros((size, 2 * ny), jnp.float32)
    for j in range(layers):
        tau = tau_after(kx_ref[j, rows, :], kx_ref[j, slice(9, 9 + size), :], side_x)
        put_half(tx_ref, (j,), tau)
        put_half(lx_ref, (j, 1), tau * side_x)
        lx_ref[j, 0] = lx_body[j]
        ky = ky_ref[j]
        ky_ref[j] = tau_after(ky, moved(ky, -1, 1), in_y)
        if j < layers - 1:
            side = jnp.where(side_in, harmonic(kz_ref[j], kz_ref[j + 1]), 0.0)
            lz_ref[j + 1] = whole(lz_body[j + 1], side)
    for j in range(layers):
        tau, back = tx_ref[j, rows, :], tx_ref[j, slice(7, 7 + size), :]
        source_ref[0, j] = whole(source_body[j], tau * share_x - back * share_xp)
        centre = whole(tau_body[j], tau + back)
        tau = ky_ref[j]
        back = moved(tau, 1, 1)
        ly_ref[j] = tau * in_y
        source_ref[1, j] = tau * share_y - back * share_yp
        centre = centre + (tau + back)
        centre = centre + (whole(kz_body[0], kz_ref[0]) if j == 0 else lz_ref[j])
        if j < layers - 1:
            centre = centre + lz_ref[j + 1]
        centre_ref[j] = jnp.where(cell, centre, 1.0)
    for j in range(layers):
        flow_z = -0.5 * whole(kz_body[0], kz_ref[0]) if j == 0 else -lz_ref[j]
        if j < layers - 1:
            flow_z = flow_z + lz_ref[j + 1]
        forward = [source_ref[0, j], source_ref[1, j], sign * flow_z]
        pivot = centre_ref[j]
        if j > 0:
            pivot = pivot - coupling * ratio
            forward = [a + coupling * d for a, d in zip(forward, value)]
        if j < layers - 1:
            inverse = 1.0 / pivot
            coupling = lz_ref[j + 1] * (1.0 - both_halves(cut_ref, j + 1))
            ratio = coupling * inverse
            value = [a * inverse for a in forward]
            inverse_ref[j] = inverse
            ratio_ref[j] = ratio
            for f in range(3):
                d_ref[f, j] = value[f]
    slabs = [pivot, 0.5 * whole(kz_body[layers - 1], kz_ref[layers - 1])] + forward
    for q, slab in enumerate(slabs):
        own_ref[q] = slab
    Message(LAST_COUNT, 2, nx, ny).write(message_ref, slabs)


def expand_kernel(
    cut_ref, lx_ref, ly_ref, lz_ref, d_ref, ratio_ref, base_ref, phi_ref, part_ref
):
    layers = ly_ref.shape[0]
    zero = jnp.zeros(ly_ref.shape[1:], jnp.float32)
    phi, base = zero + 1.0, [zero] * 3
    put(phi_ref, (layers - 1,), phi)
    for f in range(3):
        put(base_ref, (f, layers - 1), zero)
    for j in range(layers - 2, -1, -1):
        ratio = ratio_ref[j]
        phi = ratio * phi
        put(phi_ref, (j,), phi)
        for f in range(3):
            base[f] = d_ref[f, j] + ratio * base[f]
            put(base_ref, (f, j), base[f])
    along_x = along_y = along_z = zero
    parts = [zero] * 3
    for j in range(layers):
        phi = get(phi_ref, (j,))
        along_x = along_x + (get(lx_ref, (j,)) * phi) * get(phi_ref, (j,), 1)
        along_y = along_y + (ly_ref[j] * phi) * moved(phi, -1, 1)
        cut_low = lz_ref[j] * both_halves(cut_ref, j)
        if j < layers - 1:
            cut_high = lz_ref[j + 1] * both_halves(cut_ref, j + 1)
            along_z = along_z + (cut_high * phi) * get(phi_ref, (j + 1,))
        for f in range(3):
            right = beside_sum(base_ref, (f, j), lx_ref, ly_ref, j)
            if j > 0:
                right = right + cut_low * get(base_ref, (f, j - 1))
            if j < layers - 1:
                right = right + cut_high * get(base_ref, (f, j + 1))
            parts[f] = parts[f] + phi * right
    for n, slab in enumerate(parts + [along_x, along_y, 2.0 * along_z]):
        part_ref[n] = slab


def end_join_kernel(layers, cut_ref, own_ref, message_ref, part_ref, next_ref, near_ref):
    nx, ny = slab_size(own_ref)
    own = [own_ref[q] for q in range(LAST_COUNT)]
    other = Message(LAST_COUNT, 2, nx, ny).read(message_ref)
    sign = signed()
    cut = both_halves(cut_ref, layers)
    link, flow, tau = face(own[1], other[1])
    coupling = link * (1.0 - cut)
    inverse_other = 1.0 / (other[0] + tau)
    step = coupling * inverse_other
    inverse = 1.0 / (own[0] + tau - coupling * step)
    right_own = own[2:4] + [own[4] + sign * flow]
    right_other = other[2:4] + [other[4] - sign * flow]
    cut_near = link * cut
    along_x, along_y, along_z = [part_ref[3 + n] for n in range(3)]
    slabs = []
    for f in range(3):
        near = (right_own[f] + step * right_other[f]) * inverse
        beyond = right_other[f] * inverse_other + step * near
        near_ref[f], near_ref[3 + f] = near, beyond
        right = part_ref[f] + stencil(near, along_x, along_y)
        slabs.append(right + (along_z * near + cut_near * beyond))
        near_ref[6 + f] = slabs[f]
    near_ref[9], near_ref[10], near_ref[11], near_ref[12] = step, inverse, inverse_other, link
    Message(3, 1, nx, ny).write(next_ref, slabs)


def correct_kernel(
    cut_ref, near_ref, lx_ref, ly_ref, lz_ref, ratio_ref, inverse_ref, base_ref, phi_ref,
    first_ref, change_ref, d_ref,
):
    layers = ly_ref.shape[0]
    for j in range(layers):
        phi = get(phi_ref, (j,))
        for f in range(3):
            put(first_ref, (f, j), get(base_ref, (f, j)) + phi * near_ref[f])
    for j in range(layers - 1):
        cut_low = lz_ref[j] * both_halves(cut_ref, j)
        cut_high = lz_ref[j + 1] * both_halves(cut_ref, j + 1)
        inverse = inverse_ref[j]
        if j > 0:
            coupling = lz_ref[j] * (1.0 - both_halves(cut_ref, j))
        for f in range(3):
            right = beside_sum(first_ref, (f, j), lx_ref, ly_ref, j)
            right = right + cut_high * get(first_ref, (f, j + 1))
            if j > 0:
                right = right + cut_low * get(first_ref, (f, j - 1)) + coupling * d_ref[f, j - 1]
            d_ref[f, j] = right * inverse
    change = [jnp.zeros(ly_ref.shape[1:], jnp.float32)] * 3
    for f in range(3):
        change_ref[f, layers - 1] = change[f]
    for j in range(layers - 2, -1, -1):
        ratio = ratio_ref[j]
        for f in range(3):
            change[f] = d_ref[f, j] + ratio * change[f]
            change_ref[f, j] = change[f]


def end_final_kernel(
    cut_ref, message_ref, near_ref, lx_ref, ly_ref, lz_ref, phi_ref, first_ref, base_ref,
    pressure_out, residual_out, change_ref, pressure_ref, residual_ref, sems,
):
    layers = ly_ref.shape[0]
    nz = layers // 2
    nx, ny = slab_size(ly_ref)
    high = is_high(0)
    start = jnp.where(high, nz - own_start(nz), own_start(nz))
    beside_other = start > 0
    other = Message(3, 1, nx, ny).read(message_ref)
    step, inverse, inverse_other, link_near = [near_ref[9 + n] for n in range(4)]
    near = [(near_ref[6 + f] + step * other[f]) * inverse for f in range(3)]
    for i in range(-1, nz + 1):
        j = jnp.clip(start + i, 0, layers - 1)
        phi = get(phi_ref, (j,))
        for f in range(3):
            change = base_ref[f, j] + phi * near[f]
            if i == -1:
                change = jnp.where(beside_other, change, 0.0)
            if i == nz:
                beyond = other[f] * inverse_other + step * near[f]
                change = jnp.where(beside_other, beyond, change)
            put(change_ref, (f, i + 1), change)
    lane = iotas(nx, ny)[1]
    first_lane, last_lane = lane == 0, lane == ny - 1

    def body(ref, index, shift=0):
        return ref[index + (0, slice(8 + shift, 8 + shift + nx))]

    def edge(ref, index):
        return ref[index + (1, slice(8, 8 + nx))]

    copies = []
    for i in range(nz):
        j = start + i
        z = jnp.where(high, nz - 1 - i, i)
        link_high = lz_ref[j + 1][:nx, :ny]
        if i == nz - 1:
            link_high = jnp.where(beside_other, link_near[:nx, :ny], link_high)
        cut_low = lz_ref[j][:nx, :ny] * cut_ref[pl.ds(j, 1), :]
        cut_high = link_high * cut_ref[pl.ds(j + 1, 1), :]
        link_x, link_xp = body(lx_ref, (j,)), body(lx_ref, (j,), -1)
        link_y = ly_ref[j][:nx]
        link_yp = moved(jnp.where(last_lane, link_y[:, ny:], link_y[:, :ny]), 1, 1)
        for f in range(3):
            at = (f, i + 1)
            here, side = body(change_ref, at), edge(change_ref, at)
            left_out = (
                link_x * body(change_ref, at, 1)
                + link_xp * body(change_ref, at, -1)
                + link_y[:, :ny] * moved(jnp.where(first_lane, side, here), -1, 1)
                + link_yp * moved(jnp.where(last_lane, side, here), 1, 1)
            )
            beyond = cut_low * body(change_ref, (f, i)) + cut_high * body(change_ref, (f, i + 2))
            pressure_ref[f, z] = body(first_ref, (f, j)) + here
            residual_ref[f, z] = left_out + beyond
        if (i + 1) % CHUNK == 0:
            part = (slice(None), pl.ds(jnp.where(high, nz - 1 - i, i + 1 - CHUNK), CHUNK))
            for n, (buffer, out) in enumerate(
                ((pressure_ref, pressure_out), (residual_ref, residual_out))
            ):
                copy = pltpu.make_async_copy(
                    buffer.at[part], out.at[part], sems.at[n, i // CHUNK]
                )
                copy.start()
                copies.append(copy)
    for copy in copies:
        copy.wait()


def kernel_call(kernel, outputs, operands, scratch=(), smem=0, cost=None, space=pltpu.VMEM):
    specs = [pl.BlockSpec(memory_space=pltpu.SMEM)] * smem
    specs += [pl.BlockSpec(memory_space=pltpu.VMEM)] * (len(operands) - smem)
    return pl.pallas_call(
        kernel,
        out_shape=[jax.ShapeDtypeStruct(s, t) for s, t in outputs],
        in_specs=specs,
        out_specs=[pl.BlockSpec(memory_space=space)] * len(outputs),
        scratch_shapes=list(scratch),
        compiler_params=pltpu.CompilerParams(vmem_limit_bytes=32 * 2**20),
        cost_estimate=cost,
    )(*operands)


def swapped(values, stage):
    size = lax.axis_size("gz")
    return lax.ppermute(values, "gz", [(i, i ^ 2**stage) for i in range(size)])


def ring(values, axis, distance):
    size = lax.axis_size(axis)
    return lax.ppermute(values, axis, [(i, (i + distance) % size) for i in range(size)])


def slanted(values, x_distance):
    nx, nz = lax.axis_size("gx"), lax.axis_size("gz")
    route = []
    for i in range(nx):
        for k in range(nz):
            route.append((i * nz + k, (i + x_distance) % nx * nz + (k ^ 1)))
    return lax.ppermute(values, ("gx", "gz"), route)


def per_device(facies, perm_table, line_breaks):
    nz, nx, ny = facies.shape
    stages = (lax.axis_size("gz") - 1).bit_length() - 1
    i32, f32 = jnp.int32, jnp.float32
    two = lax.axis_size("gx") == 2
    layers = 2 * nz
    cut_rows = -(-(layers + 1 + 2 * stages) // 8) * 8
    sides = 1 if two else 2
    other = swapped(facies, 0)
    facies, *rows = kernel_call(
        pack_kernel,
        [((nz, nx, ny), i32)] + [((nz * 4, ny), i32)] * sides,
        [facies],
    )
    if two:
        rims = [ring(rows[0], "gx", 1), slanted(rows[0], 1)]
    else:
        rims = [ring(rows[1], "gx", 1), ring(rows[0], "gx", -1)]
        rims += [slanted(rows[1], 1), slanted(rows[0], -1)]
    scalars = jnp.concatenate([perm_table.reshape(-1), line_breaks.astype(f32)])
    k, table, cuts = kernel_call(
        functools.partial(prepare_kernel, stages, perm_table.shape[1]),
        [((3, nz, nx, ny), f32), ((3, 8, ny), f32), ((cut_rows, ny), f32)],
        [scalars, facies],
        smem=1,
        cost=pl.CostEstimate(flops=10**7, bytes_accessed=10**6, transcendentals=0),
    )
    strip, *rows = kernel_call(
        merge_kernel,
        [((2 * nx + 16, ny), i32)] + [((layers * 4, ny), i32)] * sides,
        [facies, other] + rims,
    )
    k, *rows = kernel_call(
        functools.partial(prepare_other_kernel, sides, stages == 1),
        [((3, layers, nx, ny), f32)] + [((3, layers * 4, ny), f32)] * sides,
        [table, k, other] + rows,
        cost=pl.CostEstimate(flops=10**7, bytes_accessed=10**6, transcendentals=0),
    )
    y_low, y_high = ring(strip, "gy", 1), ring(strip, "gy", -1)
    sizes = nz, nx, ny
    operands = [table, cuts, k, rows[0], rows[-1], y_low, y_high]
    return (sweep_ends if stages == 1 else sweep_tree)(sizes, stages, operands)


def sweep_ends(sizes, stages, operands):
    nz, nx, ny = sizes
    layers, f32 = 2 * nz, jnp.float32
    slab, tall = (nx + 8, 2 * ny), (2, nx + 24, ny)

    def slabs(*count):
        return (count + slab, f32)

    def talls(*count):
        return (count + tall, f32)

    def message_of(count, halo):
        return ((Message(count, halo, nx, ny).rows, ny), f32)

    def filler(flops):
        return pl.CostEstimate(flops=flops, bytes_accessed=10**6, transcendentals=0)

    half, tall_half = (nx + 8, ny), (nx + 24, ny)
    table, cuts, k, row_low, row_high, y_low, y_high = operands
    body = kernel_call(
        body_kernel,
        [((layers,) + tall_half, f32)] + [((layers,) + half, f32)] * 4
        + [((layers + 1,) + half, f32)],
        [k, row_low, row_high],
        cost=filler(10**7),
    )
    message, own, lx, ly, lz, d, ratio, inverse = kernel_call(
        end_eliminate_kernel,
        [message_of(LAST_COUNT, 2), slabs(LAST_COUNT), talls(layers), slabs(layers),
         slabs(layers + 1), slabs(3, layers), slabs(layers), slabs(layers)],
        [table, cuts, y_low, y_high] + list(body),
        [pltpu.VMEM((layers,) + tall_half, f32), pltpu.VMEM((layers,) + tall_half, f32),
         pltpu.VMEM(*slabs(layers)), pltpu.VMEM((layers,) + half, f32),
         pltpu.VMEM(*slabs(2, layers)), pltpu.VMEM(*slabs(layers))],
    )
    other = swapped(message, stages)
    base, phi, parts = kernel_call(
        expand_kernel,
        [talls(3, layers), talls(layers), slabs(6)],
        [cuts, lx, ly, lz, d, ratio],
        cost=filler(10**7),
    )
    message, near = kernel_call(
        functools.partial(end_join_kernel, layers),
        [message_of(3, 1), slabs(13)],
        [cuts, own, other, parts],
    )
    other = swapped(message, stages)
    first, change = kernel_call(
        correct_kernel,
        [talls(3, layers), slabs(3, layers)],
        [cuts, near, lx, ly, lz, ratio, inverse, base, phi],
        [pltpu.VMEM(*slabs(3, layers))],
        cost=filler(10**7),
    )
    out = ((3, nz, nx, ny), f32)
    return tuple(kernel_call(
        end_final_kernel,
        [out, out],
        [cuts, other, near, lx, ly, lz, phi, first, change],
        [pltpu.VMEM(*talls(3, nz + 2)), pltpu.VMEM(*out), pltpu.VMEM(*out),
         pltpu.SemaphoreType.DMA((2, nz // CHUNK))],
        space=pl.ANY,
    ))


def sweep_tree(sizes, stages, operands):
    nz, nx, ny = sizes
    layers, f32 = 2 * nz, jnp.float32
    cuts = operands[1]
    slab = (nx + 8, 2 * ny)
    one, three = ((layers,) + slab, f32), ((3, layers) + slab, f32)

    def slabs(count):
        return ((count,) + slab, f32)

    def message_of(count, halo):
        return ((Message(count, halo, nx, ny).rows, ny), f32)

    message, own, pair, lx, ly, lz, d, e, inverse = kernel_call(
        functools.partial(eliminate_kernel, stages),
        [message_of(LAST_COUNT if stages == 1 else FIRST_COUNT, 2)]
        + [slabs(FIRST_COUNT), slabs(PAIR_COUNT)]
        + [one] * 3 + [three, one, one],
        operands,
        [pltpu.VMEM(s, f32) for s in (three[0], one[0], (2,) + one[0], one[0])],
    )
    siblings, factors, group = [], [], own
    for s in range(stages - 1):
        last = s == stages - 2
        outputs = [slabs(FIRST_COUNT), slabs(7), message_of(LAST_COUNT if last else FIRST_COUNT, 2)]
        sibling, factor, message, *joined = kernel_call(
            functools.partial(join_kernel, s, last, layers + 1),
            outputs + ([] if last else [slabs(FIRST_COUNT)]),
            [cuts, group, swapped(message, s + 1)],
        )
        siblings.append(sibling)
        factors.append(factor)
        group = None if last else joined[0]
    fields = ((3, layers + 2) + slab, f32)
    message, own, rights, d2, kept, ends, first = kernel_call(
        functools.partial(middle_kernel, stages),
        [message_of(3 if stages == 1 else SECOND_COUNT, 1), slabs(SECOND_COUNT), slabs(6), three,
         slabs(2 * stages + 5), slabs(3), fields],
        [cuts, own, pair] + siblings + [swapped(message, stages)]
        + [lx, ly, lz, d, e, inverse],
    )
    siblings, group = [], own
    for s in range(stages - 1):
        last = s == stages - 2
        outputs = [slabs(SECOND_COUNT), message_of(3 if last else SECOND_COUNT, 1)]
        sibling, message, *joined = kernel_call(
            functools.partial(join_again_kernel, s, last),
            outputs + ([] if last else [slabs(SECOND_COUNT)]),
            [group, swapped(message, s + 1), factors[s]],
        )
        siblings.append(sibling)
        group = None if last else joined[0]
    out = ((3, nz, nx, ny), f32)
    pressure, residual = kernel_call(
        functools.partial(final_kernel, stages),
        [out, out],
        [cuts, own, pair] + siblings + [swapped(message, stages)]
        + [lx, ly, lz, first, rights, d2, e, inverse, kept, ends],
        [pltpu.VMEM((3, nz + 2) + slab, f32)]
        + [pltpu.VMEM((3, nz, nx, ny), f32)] * 2
        + [pltpu.SemaphoreType.DMA((2, nz // CHUNK))],
        space=pl.ANY,
    )
    return pressure, residual


def solution(mesh):
    return jax.shard_map(
        per_device,
        mesh=mesh,
        in_specs=(P("gz", "gx", "gy"), P(), P()),
        out_specs=(P(None, "gz", "gx", "gy"), P(None, "gz", "gx", "gy")),
        check_vma=False,
    )
```
